32 devices in a mesh: seq: 4 (over y, x), fsdp: 8 (over z, core).
Axes of the slice: x: 2, y: 2, z: 4, core: 2. Of those that a mesh axis runs over, the one named last changes fastest.
Arguments:
- tokens: bfloat16 [8, 2048, 768], P('fsdp', 'seq'), may hold values from -6 to 6
- cotangent: bfloat16 [8, 2048, 768], P('fsdp', 'seq'), may hold values from -6 to 6
- doc_starts: int32 [8, 4], P('fsdp'), may hold values from 0 to 2047, as said below
- routes: int32 [8, 2048], P('fsdp', 'seq'), may hold values from 0 to 3, as said below
- bucket_table: int32 [2048], replicated, may hold values from 0 to 31, as said below
- w_query: bfloat16 [768, 768], P('fsdp'), may hold values from -0.21875 to 0.21875
- w_key: bfloat16 [768, 768], P('fsdp'), may hold values from -0.21875 to 0.21875
- w_value: bfloat16 [768, 768], P('fsdp'), may hold values from -0.21875 to 0.21875
- w_output: bfloat16 [768, 768], P('fsdp'), may hold values from -1.75 to 1.75
- w_router: bfloat16 [768, 4], P('fsdp'), may hold values from -0.21875 to 0.21875
- gain_attn: bfloat16 [768], P('fsdp'), may hold values from 0.099609375 to 1.8984375
- gain_moe: bfloat16 [768], P('fsdp'), may hold values from 0.099609375 to 1.8984375
- rel_bias: bfloat16 [12, 32], P('seq'), may hold values from -4 to 4
- expert_in: bfloat16 [8, 768, 1536], P('fsdp', None, 'seq'), may hold values from -0.21875 to 0.21875
- expert_out: bfloat16 [8, 1536, 768], P('fsdp', 'seq'), may hold values from -0.4375 to 0.4375
Outputs:
- output: bfloat16 [8, 2048, 768], P('fsdp', 'seq')
- input_grad: float32 [8, 2048, 768], P('fsdp', 'seq')
- grad_query: float32 [768, 768], P('fsdp', 'seq')
- grad_key: float32 [768, 768], P('fsdp', 'seq')
- grad_value: float32 [768, 768], P('fsdp', 'seq')
- grad_output: float32 [768, 768], P('fsdp', 'seq')
- grad_router: float32 [768, 4], P('fsdp', 'seq')
- grad_gain_attn: float32 [768], P('fsdp')
- grad_gain_moe: float32 [768], P('fsdp')
- grad_rel_bias: float32 [12, 32], P('seq')
- grad_expert_in: float32 [8, 768, 1536], P('fsdp', None, 'seq')
- grad_expert_out: float32 [8, 1536, 768], P('fsdp', 'seq')
The draws below stay inside these ranges and needn't reach their ends.
Inputs may be any that keep to these rules, and one draw needn't show every extreme that they name: `doc_starts`: each sequence's 4 starts rise strictly from 0. Among the 1 sequence of one index of fsdp, one, drawn from the seed, has a document that begins before position 512 and ends after position 1536. `routes`: within positions k * 512 to (k + 1) * 512 - 1 of a sequence, no expert is named more than 256 times; one expert, the same for all these blocks of a draw, is named exactly 256 times in every block. `bucket_table`: 0 at distance 0, rising by 0 or 1 from one distance to the next, and 31 from distance 2 * 32 - 2 on.
All inputs are finite; a program needn't handle non-finite values.
Results may differ from the reference program's by a relative error of at most 0.014.
Values may be sent and summed in bfloat16 or wider, within the bound.
No kernel may reach another device: no remote copies, remote signals or barrier semaphores. Data moves between devices by JAX's collectives and lax.ppermute only.
A program may use at most 256 MiB of HBM per device.

```python
import jax
import jax.numpy as jnp
from jax import lax

D = 768
HEADS = 12
HEAD = 64
FF = 3072
BUCKETS = 32
LENGTH = 2048
SEQS = 1
DOCS = 4
EXPERTS = 4
SPAN = 512
SEQS_ALL = 8
MOST = 256
N_SEQ = 4


def draw_doc_starts(key, part):
    key = jax.random.fold_in(key, 11)
    pick_key, free_key, long_key = jax.random.split(key, 3)
    groups = SEQS_ALL // SEQS
    chosen = jax.random.randint(pick_key, (groups,), 0, SEQS)
    is_long = jnp.arange(SEQS_ALL, dtype=jnp.int32) % SEQS == jnp.repeat(chosen, SEQS)

    def free_row(row_key):
        picked = jax.random.permutation(row_key, jnp.arange(1, LENGTH, dtype=jnp.int32))[:DOCS - 1]
        return jnp.concatenate([jnp.zeros((1,), jnp.int32), jnp.sort(picked)])

    def long_row(row_key):
        early_key, late_key = jax.random.split(row_key)
        early_start = jax.random.randint(early_key, (1,), 1, SPAN).astype(jnp.int32)
        late_starts = jax.random.permutation(late_key, jnp.arange(3 * SPAN + 1, LENGTH, dtype=jnp.int32))[:DOCS - 2]
        return jnp.concatenate([jnp.zeros((1,), jnp.int32), early_start, jnp.sort(late_starts)])
    free_rows = jax.vmap(free_row)(jax.random.split(free_key, SEQS_ALL))
    long_rows = jax.vmap(long_row)(jax.random.split(long_key, SEQS_ALL))
    return jnp.where(is_long[:, None], long_rows, free_rows).astype(jnp.int32)


def draw_routes(key, part):
    key = jax.random.fold_in(key, 23)
    busy_key, block_key = jax.random.split(key)
    busiest = jax.random.randint(busy_key, (), 0, EXPERTS).astype(jnp.int32)
    block_total = SEQS_ALL * (LENGTH // SPAN)
    tickets = (busiest + 1 + jnp.arange((EXPERTS - 1) * MOST, dtype=jnp.int32) // MOST) % EXPERTS

    def one_block(row_key):
        pool_key, order_key = jax.random.split(row_key)
        others = jax.random.permutation(pool_key, tickets)[:SPAN - MOST]
        filled = jnp.concatenate([jnp.full((MOST,), busiest, jnp.int32), others])
        return jax.random.permutation(order_key, filled)
    blocks_drawn = jax.vmap(one_block)(jax.random.split(block_key, block_total))
    return blocks_drawn.reshape(SEQS_ALL, LENGTH).astype(jnp.int32)


def draw_bucket_table(key, part):
    key = jax.random.fold_in(key, 37)
    reach = 2 * BUCKETS - 2
    rising = jax.random.permutation(key, jnp.arange(1, reach + 1, dtype=jnp.int32))[:BUCKETS - 1]
    steps_up = jnp.zeros((LENGTH,), jnp.int32).at[rising].set(1)
    return jnp.cumsum(steps_up).astype(jnp.int32)


def level_of(key, shape, shards, low, largest):
    factor_of = 1.0
    for dim, shards_of in shards:
        steps = jax.random.uniform(jax.random.fold_in(jax.random.fold_in(key, 6), dim), (shards_of,), jnp.float32, low / len(shards), largest / len(shards))
        factor_of = factor_of * jnp.repeat(jnp.exp(steps), shape[dim] // shards_of).reshape((-1,) + (1,) * (len(shape) - 1 - dim))
    return factor_of


def noise(stream_key, shape, width, most, cuts=(), held_as=jnp.bfloat16):
    factor_of = level_of(stream_key, shape, cuts, -0.22, 0.18) if cuts else 1.0
    array = jax.random.normal(stream_key, shape, jnp.float32) * width * factor_of
    return jnp.minimum(jnp.maximum(array, -most), most).astype(held_as)


def setup_inputs(seed: int = 0) -> dict:
    arg_keys = jax.random.split(jax.random.key(seed), 16)
    return {
        "tokens": noise(arg_keys[0], (SEQS_ALL, LENGTH, D), 1.0, 6.0, ((0, 8), (1, 4))),
        "cotangent": noise(arg_keys[1], (SEQS_ALL, LENGTH, D), 1.0, 6.0, ((0, 8), (1, 4))),
        "doc_starts": draw_doc_starts(jax.random.fold_in(arg_keys[15], 71), 0),
        "routes": draw_routes(jax.random.fold_in(arg_keys[15], 71), 0),
        "bucket_table": draw_bucket_table(jax.random.fold_in(arg_keys[15], 71), 0),
        "w_query": noise(arg_keys[5], (D, D), D ** -0.5, 0.21875, ((0, 8),)),
        "w_key": noise(arg_keys[6], (D, D), D ** -0.5, 0.21875, ((0, 8),)),
        "w_value": noise(arg_keys[7], (D, D), D ** -0.5, 0.21875, ((0, 8),)),
        "w_output": noise(arg_keys[8], (D, D), (D // 64) ** -0.5, 1.75, ((0, 8),)),
        "w_router": noise(arg_keys[9], (D, EXPERTS), D ** -0.5, 0.21875, ((0, 8),)),
        "gain_attn": jnp.clip(1.0 + 0.18 * jax.random.normal(arg_keys[10], (D,), jnp.float32), 0.099609375, 1.8984375).astype(jnp.bfloat16),
        "gain_moe": jnp.clip(1.0 + 0.18 * jax.random.normal(arg_keys[11], (D,), jnp.float32), 0.099609375, 1.8984375).astype(jnp.bfloat16),
        "rel_bias": noise(arg_keys[12], (HEADS, BUCKETS), 1.0, 4.0, ((0, 4),)),
        "expert_in": noise(arg_keys[13], (2 * EXPERTS, D, FF // 2), D ** -0.5, 0.21875, ((0, 8), (2, 4))),
        "expert_out": noise(arg_keys[14], (2 * EXPERTS, FF // 2, D), (max(1, FF // (EXPERTS * EXPERTS))) ** -0.5, 0.4375, ((0, 8), (1, 4))),
    }


HIGH = lax.Precision.HIGHEST
EPS = 1e-06

@jax.custom_vjp
def low(v):
    return lax.optimization_barrier(v.astype(jnp.bfloat16)).astype(jnp.float32)

@jax.custom_vjp
def low_back(v):
    return v

def low_keep(v):
    return (low(v), None)

def low_pass(kept, grad):
    return (grad,)

def back_keep(v):
    return (v, None)

def back_low(kept, grad):
    return (low(grad),)
low.defvjp(low_keep, low_pass)
low_back.defvjp(back_keep, back_low)

def layer_sequence(params, inputs, route_row, start_row, bucket_table):
    query_w, key_w, value_w, output_w, router_w, gain_one, gain_two, rel_table, in_experts, out_experts = params
    length = inputs.shape[0]
    scale_one = lax.rsqrt(lax.optimization_barrier(jnp.mean(inputs * inputs, axis=-1, keepdims=True)) + EPS)
    normed_one = low(inputs * scale_one * gain_one)

    def project(weight_matrix):
        heads_flat = low(low_back(jnp.dot(normed_one, weight_matrix, precision=HIGH)))
        return heads_flat.reshape(length, HEADS, HEAD).transpose(1, 0, 2)
    queries = project(query_w)
    key_heads = project(key_w)
    values = project(value_w)
    position = jnp.arange(length, dtype=jnp.int32)
    doc_ids = (lax.optimization_barrier(jnp.sum((start_row[None, :] <= position[:, None]).astype(jnp.int32), axis=1)) - 1).astype(jnp.int32)
    row_count = min(512, length)

    def attend(block_index):
        offset = block_index * row_count
        query_block = lax.dynamic_slice_in_dim(queries, offset, row_count, 1)
        query_pos = offset + jnp.arange(row_count, dtype=jnp.int32)
        query_docs = lax.dynamic_slice_in_dim(doc_ids, offset, row_count, 0)
        products = low_back(jnp.einsum('hqd,hkd->hqk', query_block, key_heads, precision=HIGH))
        distance = jnp.clip(query_pos[:, None] - position[None, :], 0, length - 1)
        biases = rel_table[:, bucket_table[distance]]
        allowed = (query_docs[:, None] == doc_ids[None, :]) & (position[None, :] <= query_pos[:, None])
        scores = jnp.where(allowed[None], products * 0.125 + biases, -jnp.inf)
        maxima = lax.optimization_barrier(jnp.max(scores, axis=-1, keepdims=True))
        expons = jnp.exp(scores - maxima)
        weights = low(expons / lax.optimization_barrier(jnp.sum(expons, axis=-1, keepdims=True)))
        return jnp.einsum('hqk,hkd->hqd', weights, values, precision=HIGH)
    attended = lax.map(jax.checkpoint(attend), jnp.arange(length // row_count, dtype=jnp.int32))
    attended = attended.transpose(1, 0, 2, 3).reshape(HEADS, length, HEAD).transpose(1, 0, 2).reshape(length, D)
    mixed_heads = low(low_back(attended))
    branch = low_back(jnp.dot(mixed_heads, output_w, precision=HIGH))
    hidden_state = inputs + branch
    scale_two = lax.rsqrt(lax.optimization_barrier(jnp.mean(hidden_state * hidden_state, axis=-1, keepdims=True)) + EPS)
    normed_two = low(hidden_state * scale_two * gain_two)
    logits = low_back(jnp.dot(normed_two, router_w, precision=HIGH))
    shifted = jnp.exp(logits - lax.optimization_barrier(jnp.max(logits, axis=-1, keepdims=True)))
    router_probs = shifted / lax.optimization_barrier(jnp.sum(shifted, axis=-1, keepdims=True))
    chosen = route_row[:, None] == jnp.arange(EXPERTS, dtype=jnp.int32)[None, :]
    gate_values = lax.optimization_barrier(jnp.sum(router_probs * chosen.astype(jnp.float32), axis=1))
    counts = lax.optimization_barrier(jnp.sum(chosen.astype(jnp.int32), axis=0)).astype(jnp.int32)
    begins = (jnp.cumsum(counts) - counts).astype(jnp.int32)
    ordering = jnp.argsort(route_row, stable=True).astype(jnp.int32)
    lanes = jnp.arange(N_SEQ * MOST, dtype=jnp.int32)
    where_at = jnp.clip(begins[:, None] + lanes[None, :], 0, length - 1).astype(jnp.int32)
    valid = lanes[None, :] < counts[:, None]
    picks = jnp.where(valid, ordering[where_at], length).astype(jnp.int32)
    padded = jnp.concatenate([normed_two, jnp.zeros((1, D), jnp.float32)], axis=0)
    gathered = padded[picks]
    halves_in = in_experts.reshape(EXPERTS, 2, D, FF // 2)
    halves_out = out_experts.reshape(EXPERTS, 2, FF // 2, D)
    summed = jnp.zeros((EXPERTS, N_SEQ * MOST, D), jnp.float32)
    for half_index in range(2):
        arrived = low_back(gathered)
        hidden_pre = low_back(jnp.einsum('ecd,edf->ecf', arrived, halves_in[:, half_index], precision=HIGH))
        activated = low(jax.nn.gelu(hidden_pre, approximate=True))
        summed = summed + low(jnp.einsum('ecf,efd->ecd', activated, halves_out[:, half_index], precision=HIGH))
    scattered = jnp.zeros((length + 1, D), jnp.float32).at[picks].add(summed)[:length]
    expert_rows = low_back(scattered)
    return hidden_state + gate_values[:, None] * expert_rows

def reference(tokens, cotangent, doc_starts, routes, bucket_table, w_query, w_key, w_value, w_output, w_router, gain_attn, gain_moe, rel_bias, expert_in, expert_out):
    params = tuple((matrix.astype(jnp.float32) for matrix in (w_query, w_key, w_value, w_output, w_router, gain_attn, gain_moe, rel_bias, expert_in, expert_out)))
    inputs_all = tokens.astype(jnp.float32)
    upstream_all = cotangent.astype(jnp.float32)
    starting = tuple((jnp.zeros_like(matrix) for matrix in params))

    def one_sequence(carry, packed):
        inputs, upstream, start_row, route_row = packed

        def forward(weights, sequence):
            return layer_sequence(weights, sequence, route_row, start_row, bucket_table)
        result, pullback = jax.vjp(forward, params, inputs)
        weight_grads, input_grads = pullback(upstream)
        carry = tuple((before + adding for before, adding in zip(carry, weight_grads)))
        return (carry, (result, input_grads))
    totals, (results, input_grads) = lax.scan(one_sequence, starting, (inputs_all, upstream_all, doc_starts, routes))
    return (results.astype(jnp.bfloat16), input_grads, totals[0], totals[1], totals[2], totals[3], totals[4], totals[5], totals[6], totals[7], totals[8], totals[9])
```

```python
import functools

import jax
import jax.numpy as jnp
from jax import lax
from jax.experimental import pallas as pl
from jax.experimental.pallas import tpu as pltpu
from jax.sharding import PartitionSpec as P

EPS = 1e-06
HIGH = lax.Precision.HIGHEST
BIG = 1e30
TILE = 256
LANES = 128
BF = jnp.bfloat16
F32 = jnp.float32


def contract(left, right, left_dim, right_dim):
    return lax.dot_general(
        left, right, (((left_dim,), (right_dim,)), ((), ())), preferred_element_type=F32
    )


def doc_rows(starts_ref, length, docs):
    pos = lax.broadcasted_iota(jnp.int32, (1, length), 1)
    doc = jnp.zeros((1, length), jnp.int32) - 1
    for index in range(docs):
        doc = doc + (starts_ref[0, index] <= pos).astype(jnp.int32)
    row = lax.broadcasted_iota(jnp.int32, (8, length), 0)
    same = row == doc
    return jnp.where(same, 1.0, 0.0), jnp.where(same, 0.0, jnp.where(row < docs, -BIG, 0.0))


def forward_kernel(
    head, tile, docs, starts_ref, bias_ref, q_ref, k_ref, v_ref, o_ref, lse_ref,
    kaug, qaug, vaug, band, scores,
):
    length = q_ref.shape[1]
    span = o_ref.shape[2]
    doc_q, doc_k = doc_rows(starts_ref, length, docs)
    qaug[:head, :] = (q_ref[...].astype(F32) * 0.125).astype(BF)
    qaug[head : head + 16, :] = jnp.concatenate([doc_q, jnp.zeros((8, length), F32)], 0).astype(BF)
    qaug[head + 16 :, :] = jnp.zeros((qaug.shape[0] - head - 16, length), BF)
    tail = jnp.zeros((LANES - head - 8, tile), F32)
    for block in range(length // tile):
        cols = slice(block * tile, (block + 1) * tile)
        full = jnp.concatenate([k_ref[:, cols].astype(F32), doc_k[:, cols], tail], 0)
        kaug[cols, :] = full.T.astype(BF)
    vaug[:head, :] = v_ref[...]
    extra = lax.broadcasted_iota(jnp.int32, (vaug.shape[0] - head, length), 0)
    vaug[head:, :] = jnp.where(extra == 0, 1.0, 0.0).astype(BF)
    circle = pltpu.roll(
        jnp.broadcast_to(bias_ref[0], (tile, tile)), 0, 1, stride=1, stride_axis=0
    )
    key_row = lax.broadcasted_iota(jnp.int32, (tile, tile), 0)
    query_col = lax.broadcasted_iota(jnp.int32, (tile, tile), 1)
    band[:tile, :] = jnp.where(key_row > query_col, circle, 0.0)
    band[tile:, :] = jnp.where(key_row <= query_col, circle, -BIG)
    for i in range(length // tile):
        cols = slice(i * tile, (i + 1) * tile)
        queries = qaug[:, cols]
        peak = None
        for j in range(i + 1):
            rows = slice(j * tile, (j + 1) * tile)
            part = contract(kaug[rows, :], queries, 1, 0)
            if j == i:
                part = part + band[tile:, :]
            elif j == i - 1:
                part = part + band[:tile, :]
            scores[rows, :] = part
            most = jnp.max(part.reshape(tile // 8, 8, tile), axis=0)
            peak = most if peak is None else jnp.maximum(peak, most)
        peak = jnp.max(peak, axis=0, keepdims=True)
        summed = jnp.zeros((vaug.shape[0], tile), F32)
        for j in range(i + 1):
            rows = slice(j * tile, (j + 1) * tile)
            expons = jnp.exp(scores[rows, :] - peak).astype(BF)
            summed = summed + contract(vaug[:, rows], expons, 1, 0)
        total = summed[head : head + 1, :]
        start = (i * tile) % span
        o_ref[i * tile // span, :, start : start + tile] = (summed[:head, :] / total).astype(BF)
        lse_ref[0, :, cols] = peak + jnp.log(total)


def attend_forward(qkv_t, starts, bias_f, heads, head, spans):
    length = qkv_t.shape[1]
    docs = starts.shape[1]
    span = length // spans

    def rows_of(part):
        return pl.BlockSpec((head, length), lambda h: (part * heads + h, 0))

    return pl.pallas_call(
        functools.partial(forward_kernel, head, TILE, docs),
        grid=(heads,),
        in_specs=[
            pl.BlockSpec(memory_space=pltpu.SMEM),
            pl.BlockSpec((1, 1, TILE), lambda h: (h, 0, 0)),
            rows_of(0),
            rows_of(1),
            rows_of(2),
        ],
        out_specs=[
            pl.BlockSpec((spans, head, span), lambda h: (0, h, 0)),
            pl.BlockSpec((1, 1, length), lambda h: (h, 0, 0)),
        ],
        out_shape=[
            jax.ShapeDtypeStruct((spans, heads * head, span), BF),
            jax.ShapeDtypeStruct((heads, 1, length), F32),
        ],
        scratch_shapes=[
            pltpu.VMEM((length, LANES), BF),
            pltpu.VMEM((LANES, length), BF),
            pltpu.VMEM((head + 16, length), BF),
            pltpu.VMEM((2 * TILE, TILE), F32),
            pltpu.VMEM((length, TILE), F32),
        ],
        compiler_params=pltpu.CompilerParams(vmem_limit_bytes=40 * 2**20),
        name="attend_forward",
    )(starts, bias_f, qkv_t, qkv_t, qkv_t)


def backward_kernel(
    head, tile, docs, starts_ref, bias_ref, q_ref, k_ref, v_ref, do_ref, o_ref, lse_ref,
    grads_ref, dist_ref, qaug, doaug, kaug, vaug, scaled, band, dq_sum, diagonal,
):
    length = q_ref.shape[1]
    span = o_ref.shape[2]
    doc_q, doc_k = doc_rows(starts_ref, length, docs)
    sub = lax.broadcasted_iota(jnp.int32, (8, tile), 0)

    def minus_split(row):
        row = -row
        high = row.astype(BF).astype(F32)
        rest = row - high
        mid = rest.astype(BF).astype(F32)
        return jnp.where(
            sub == 0, high, jnp.where(sub == 1, mid, jnp.where(sub == 2, rest - mid, 0.0))
        )

    ones3 = jnp.where(lax.broadcasted_iota(jnp.int32, (8, length), 0) < 3, 1.0, 0.0)
    zeros8 = jnp.zeros((8, length), F32)
    blocks = length // tile
    tail = jnp.zeros((LANES - head - 16, tile), F32)
    for block in range(blocks):
        cols = slice(block * tile, (block + 1) * tile)
        begin = (block * tile) % span
        inner = slice(begin, begin + tile)
        upstream = do_ref[block * tile // span, :, inner].astype(F32)
        attended = o_ref[block * tile // span, :, inner].astype(F32)
        centre = jnp.sum(upstream * attended, axis=0, keepdims=True)
        query = q_ref[:, cols].astype(F32) * 0.125
        scaled[:, cols] = query.astype(BF)
        full = jnp.concatenate([query, doc_q[:, cols], minus_split(lse_ref[0, :, cols]), tail], 0)
        qaug[cols, :] = full.T.astype(BF)
        full = jnp.concatenate([upstream, minus_split(centre), zeros8[:, cols], tail], 0)
        doaug[cols, :] = full.T.astype(BF)
    kaug[:head, :] = k_ref[...]
    kaug[head : head + 16, :] = jnp.concatenate([doc_k, ones3], 0).astype(BF)
    kaug[head + 16 :, :] = jnp.zeros((LANES - head - 16, length), BF)
    vaug[:head, :] = v_ref[...]
    vaug[head : head + 16, :] = jnp.concatenate([ones3, zeros8], 0).astype(BF)
    vaug[head + 16 :, :] = jnp.zeros((LANES - head - 16, length), BF)
    circle = pltpu.roll(
        jnp.broadcast_to(bias_ref[0], (tile, tile)), 0, 1, stride=1, stride_axis=0
    )
    query_row = lax.broadcasted_iota(jnp.int32, (tile, tile), 0)
    key_col = lax.broadcasted_iota(jnp.int32, (tile, tile), 1)
    band[:tile, :] = jnp.where(key_col <= query_row, circle, -BIG)
    band[tile:, :] = jnp.where(key_col > query_row, circle, 0.0)
    diagonal[...] = jnp.zeros_like(diagonal)
    for j in range(blocks):
        keys = slice(j * tile, (j + 1) * tile)
        dk = jnp.zeros((head, tile), F32)
        dv = jnp.zeros((head, tile), F32)
        for i in range(j, blocks):
            rows = slice(i * tile, (i + 1) * tile)
            begin = (i * tile) % span
            upstream = do_ref[i * tile // span, :, begin : begin + tile]
            part = contract(qaug[rows, :], kaug[:, keys], 1, 0)
            if i == j:
                part = part + band[:tile, :]
            elif i == j + 1:
                part = part + band[tile:, :]
            probs = jnp.exp(part)
            grads = probs * contract(doaug[rows, :], vaug[:, keys], 1, 0)
            if i == j:
                diagonal[...] += grads
            elif i == j + 1:
                diagonal[...] += jnp.where(key_col > query_row, grads, 0.0)
            weights = probs.astype(BF)
            short = grads.astype(BF)
            dv = dv + contract(upstream, weights, 1, 0)
            dk = dk + contract(scaled[:, rows], short, 1, 0)
            dq = contract(kaug[:head, keys], short, 1, 1)
            if j == 0:
                dq_sum[:, rows] = dq
            else:
                dq_sum[:, rows] += dq
        begin = (j * tile) % span
        inner = slice(begin, begin + tile)
        grads_ref[j * tile // span, 1, 0, :, inner] = dk.astype(BF)
        grads_ref[j * tile // span, 2, 0, :, inner] = dv.astype(BF)
        grads_ref[j * tile // span, 0, 0, :, inner] = (dq_sum[:, keys] * 0.125).astype(BF)
    skew = diagonal[...]
    step = 1
    while step < tile:
        skew = jnp.where((query_row & step) != 0, pltpu.roll(skew, tile - step, 1), skew)
        step *= 2
    dist_ref[0] = jnp.sum(skew, axis=0, keepdims=True)


def attend_backward(qkv_t, upstream, attended, lse, starts, bias_g, heads, head):
    length = qkv_t.shape[1]
    docs = starts.shape[1]
    spans, _, span = attended.shape

    def rows_of(part):
        return pl.BlockSpec((head, length), lambda h: (part * heads + h, 0))

    by_span = pl.BlockSpec((spans, head, span), lambda h: (0, h, 0))
    return pl.pallas_call(
        functools.partial(backward_kernel, head, TILE, docs),
        grid=(heads,),
        in_specs=[
            pl.BlockSpec(memory_space=pltpu.SMEM),
            pl.BlockSpec((1, 1, TILE), lambda h: (h, 0, 0)),
            rows_of(0),
            rows_of(1),
            rows_of(2),
            by_span,
            by_span,
            pl.BlockSpec((1, 1, length), lambda h: (h, 0, 0)),
        ],
        out_specs=[
            pl.BlockSpec((spans, 3, 1, head, span), lambda h: (0, 0, h, 0, 0)),
            pl.BlockSpec((1, 1, TILE), lambda h: (h, 0, 0)),
        ],
        out_shape=[
            jax.ShapeDtypeStruct((spans, 3, heads, head, span), BF),
            jax.ShapeDtypeStruct((heads, 1, TILE), F32),
        ],
        scratch_shapes=[
            pltpu.VMEM((length, LANES), BF),
            pltpu.VMEM((length, LANES), BF),
            pltpu.VMEM((LANES, length), BF),
            pltpu.VMEM((LANES, length), BF),
            pltpu.VMEM((head, length), BF),
            pltpu.VMEM((2 * TILE, TILE), F32),
            pltpu.VMEM((head, length), F32),
            pltpu.VMEM((TILE, TILE), F32),
        ],
        compiler_params=pltpu.CompilerParams(vmem_limit_bytes=40 * 2**20),
        name="attend_backward",
    )(starts, bias_g, qkv_t, qkv_t, qkv_t, upstream, attended, lse)


def all_to_all(blocks, axis, groups=None):
    return lax.all_to_all(
        blocks, axis, split_axis=0, concat_axis=0, tiled=True, axis_index_groups=groups
    )


def pair_swap(block, axis, mask):
    count = lax.axis_size(axis)
    return lax.ppermute(block, axis, [(i, i ^ mask) for i in range(count)])


def gather_four(rows, axis):
    me = lax.axis_index(axis)
    half = rows.shape[0] // 2
    near = pair_swap(rows, axis, 1)
    far = pair_swap(rows, axis, 2)
    across = jnp.concatenate(
        [pair_swap(near[:half], axis, 2), pair_swap(far[half:], axis, 1)], axis=0
    )
    whole = jnp.zeros((4,) + rows.shape, rows.dtype)
    for mask, part in enumerate((rows, near, far, across)):
        whole = lax.dynamic_update_index_in_dim(whole, part, me ^ mask, 0)
    return whole


def per_device(
    tokens, cotangent, doc_starts, routes, bucket_table, w_query, w_key, w_value, w_output,
    w_router, gain_attn, gain_moe, rel_bias, expert_in, expert_out,
):
    _, span, width = tokens.shape
    seq_count = lax.axis_size("seq")
    fsdp_count = lax.axis_size("fsdp")
    seq_me = lax.axis_index("seq")
    length = span * seq_count
    heads, buckets = rel_bias.shape
    local = width // seq_count
    head = local // heads
    experts = w_router.shape[1]
    rows_here = w_query.shape[0]
    quarter = expert_in.shape[2]
    half = quarter * seq_count

    own_cols = [
        lax.dynamic_slice_in_dim(matrix, seq_me * local, local, 1)
        for matrix in (w_query, w_key, w_value)
    ]
    slab = jnp.concatenate(own_cols + [w_router, gain_attn[:, None], gain_moe[:, None]], axis=1)
    slab_width = slab.shape[1]
    slab = jnp.pad(slab, ((0, 0), (0, -slab_width % LANES)))
    x_all = gather_four(tokens[0], "seq").reshape(length, width)
    slab = lax.all_gather(slab, "fsdp", axis=0, tiled=True)
    w_heads = slab[:, : 3 * local]
    full_router = slab[:, 3 * local : 3 * local + experts]
    gain_one = slab[:, 3 * local + experts].astype(F32)
    gain_two = slab[:, 3 * local + experts + 1].astype(F32)
    full_output = lax.all_gather(w_output, "fsdp", axis=0, tiled=True)
    packed = jnp.stack([w_query, w_key, w_value], axis=1).reshape(rows_here, 3, seq_count, local)
    packed = packed.transpose(0, 2, 1, 3).reshape(rows_here, 3 * width)
    w_all = lax.all_gather(packed, "fsdp", axis=0, tiled=True)
    gathered_in = lax.all_gather(expert_in[0], "seq", axis=0, tiled=False)
    gathered_out = lax.all_gather(expert_out[0], "seq", axis=0, tiled=True)
    own_in = gathered_in.transpose(1, 0, 2).reshape(width, half)
    own_out = gathered_out

    route = routes[0]
    chosen = (route[:, None] == jnp.arange(experts, dtype=jnp.int32)[None, :]).astype(F32)
    before = (
        jnp.arange(span, dtype=jnp.int32)[:, None] > jnp.arange(span, dtype=jnp.int32)[None, :]
    ).astype(BF)
    ranks = jnp.dot(before, chosen.astype(BF), preferred_element_type=F32)
    capacity = max(2, 2 * span // experts)
    slot = route * capacity + jnp.sum(ranks * chosen, axis=1).astype(jnp.int32)
    place = (jnp.arange(experts * capacity, dtype=jnp.int32)[:, None] == slot[None, :]).astype(BF)
    cores = 2
    groups = [list(range(core, fsdp_count, cores)) for core in range(cores)]

    def to_experts(rows):
        slots = jnp.dot(place, rows, preferred_element_type=F32).astype(BF)
        return all_to_all(slots.reshape(experts, capacity, width), "fsdp", groups).reshape(
            experts * capacity, width
        )

    def to_tokens(slots):
        back = all_to_all(slots.reshape(experts, capacity, width), "fsdp", groups)
        return contract(place, back.reshape(experts * capacity, width), 0, 0)

    arrived_up = to_experts(cotangent[0])

    x_wide = x_all.astype(F32)
    scale_all = lax.rsqrt(jnp.mean(x_wide * x_wide, axis=-1, keepdims=True) + EPS)
    n1_all = (x_wide * scale_all * gain_one).astype(BF)
    qkv_t = contract(w_heads, n1_all, 0, 1).astype(BF)
    table = jnp.concatenate([bucket_table[:TILE], bucket_table[:1], bucket_table[1:TILE][::-1]])
    onehot = (table[:, None] == jnp.arange(buckets, dtype=jnp.int32)[None, :]).astype(F32)
    rel = rel_bias.astype(F32)
    by_distance = jnp.dot(rel - rel[:, buckets - 1 :], onehot.T, precision=HIGH)
    attended, lse = attend_forward(
        qkv_t, doc_starts, by_distance[:, None, :TILE], heads, head, seq_count
    )
    mixed_t = all_to_all(attended, "seq").reshape(width, span)

    x = tokens[0].astype(F32)
    hidden = x + contract(mixed_t, full_output, 0, 0)
    scale_moe = lax.rsqrt(jnp.mean(hidden * hidden, axis=-1, keepdims=True) + EPS)
    normed_moe = hidden * scale_moe
    n2 = (normed_moe * gain_two).astype(BF)

    def router(rows):
        logits = jnp.dot(rows, full_router, preferred_element_type=F32)
        shifted = jnp.exp(logits - jnp.max(logits, axis=-1, keepdims=True))
        return shifted / jnp.sum(shifted, axis=-1, keepdims=True)

    probs = router(n2)
    gate = jnp.sum(probs * chosen, axis=1)

    other_in, other_out = pair_swap((own_in, own_out), "fsdp", 1)
    whole_in = jnp.concatenate([own_in, other_in], axis=1)
    whole_out = jnp.concatenate([own_out, other_out], axis=0)
    arrived = to_experts(n2)
    expert_me = lax.axis_index("fsdp") // cores
    gate_here = jnp.sum(
        router(arrived)
        * (jnp.arange(experts, dtype=jnp.int32)[None, :] == expert_me).astype(F32),
        axis=1,
        keepdims=True,
    )
    dy = (gate_here * arrived_up.astype(F32)).astype(BF)
    pre = jnp.dot(arrived, whole_in, preferred_element_type=F32)
    act, pull = jax.vjp(lambda values: jax.nn.gelu(values, approximate=True), pre)
    act = act.astype(BF)
    expert_rows = to_tokens(jnp.dot(act, whole_out, preferred_element_type=F32).astype(BF))
    pre_grads = pull(contract(dy, whole_out, 1, 1))[0].astype(BF)
    moe_grads = to_tokens(contract(pre_grads, whole_in, 1, 1).astype(BF))
    grad_out = contract(act, dy, 0, 0)
    grad_in = contract(arrived, pre_grads, 0, 0)
    got_in = pair_swap(grad_in[:, half:].astype(BF), "fsdp", 1)
    got_out = pair_swap(grad_out[half:].astype(BF), "fsdp", 1)
    settled_in = (grad_in[:, :half] + got_in.astype(F32)).astype(BF)
    settled_out = (grad_out[:half] + got_out.astype(F32)).astype(BF)
    settled_in = settled_in.reshape(width, seq_count, quarter).transpose(1, 0, 2)
    grad_expert_in = jnp.sum(all_to_all(settled_in, "seq").astype(F32), axis=0)
    grad_expert_out = jnp.sum(
        all_to_all(settled_out.reshape(seq_count, quarter, width), "seq").astype(F32), axis=0
    )

    output = (hidden + gate[:, None] * expert_rows).astype(BF)
    upstream = cotangent[0].astype(F32)
    gate_grads = jnp.sum(upstream * expert_rows, axis=1)
    logit_grads = (probs * (chosen * gate_grads[:, None] - (gate * gate_grads)[:, None])).astype(BF)
    grad_router = contract(n2, logit_grads, 0, 0)
    moe_grads = moe_grads + contract(logit_grads, full_router, 1, 1)
    grad_gain_moe = jnp.sum(moe_grads * normed_moe, axis=0)
    scaled_moe = moe_grads * gain_two
    hidden_grads = upstream + scale_moe * (
        scaled_moe - normed_moe * jnp.mean(scaled_moe * normed_moe, axis=-1, keepdims=True)
    )
    branch_grads = hidden_grads.astype(BF)
    grad_output = contract(mixed_t, branch_grads, 1, 0)
    mixed_grads = contract(full_output, branch_grads, 1, 1).astype(BF)
    moved = all_to_all(mixed_grads.reshape(seq_count, local, span), "seq")
    head_grads, distances = attend_backward(
        qkv_t, moved, attended, lse, doc_starts, by_distance[:, None, TILE:], heads, head
    )
    head_grads = head_grads.reshape(seq_count, 3 * local, span)
    below = jnp.dot(distances[:, 0], onehot[TILE:, : buckets - 1], precision=HIGH)
    grad_rel = jnp.concatenate([below, -jnp.sum(below, axis=1, keepdims=True)], axis=1)
    back = all_to_all(head_grads, "seq").reshape(3 * width, span)
    dn1 = contract(back, w_all, 0, 1)
    n1_spans = n1_all.reshape(seq_count, span, width)
    grad_heads = jnp.einsum("std,set->de", n1_spans, head_grads, preferred_element_type=F32)
    scale_attn = lax.rsqrt(jnp.mean(x * x, axis=-1, keepdims=True) + EPS)
    normed_attn = x * scale_attn
    grad_gain_attn = jnp.sum(dn1 * normed_attn, axis=0)
    scaled_attn = dn1 * gain_one
    input_grads = hidden_grads + scale_attn * (
        scaled_attn - normed_attn * jnp.mean(scaled_attn * normed_attn, axis=-1, keepdims=True)
    )

    output_parts = grad_output.reshape(width, seq_count, local).transpose(1, 0, 2).astype(BF)
    output_part = jnp.sum(all_to_all(output_parts, "seq").astype(F32), axis=0)
    summed = lax.psum_scatter(
        jnp.concatenate([grad_heads, output_part], axis=1), "fsdp", scatter_dimension=0, tiled=True
    )
    rel_place = lax.dynamic_update_slice_in_dim(
        jnp.zeros((seq_count * heads, buckets), F32), grad_rel, seq_me * heads, 0
    )
    small = jnp.concatenate(
        [grad_router.reshape(-1), grad_gain_attn, grad_gain_moe, rel_place.reshape(-1)]
    )
    small = lax.psum(small, ("seq", "fsdp"))
    at = width * experts
    fsdp_me = lax.axis_index("fsdp")
    sum_router = lax.dynamic_slice(
        small[:at].reshape(width, experts),
        (fsdp_me * rows_here, seq_me * (experts // seq_count)),
        (rows_here, experts // seq_count),
    )
    sum_gain_attn = lax.dynamic_slice_in_dim(small[at : at + width], fsdp_me * rows_here, rows_here)
    at += width
    sum_gain_moe = lax.dynamic_slice_in_dim(small[at : at + width], fsdp_me * rows_here, rows_here)
    at += width
    sum_rel = lax.dynamic_slice_in_dim(
        small[at:].reshape(seq_count * heads, buckets), seq_me * heads, heads, 0
    )
    return (
        output[None],
        input_grads[None],
        summed[:, :local],
        summed[:, local : 2 * local],
        summed[:, 2 * local : 3 * local],
        summed[:, 3 * local :],
        sum_router,
        sum_gain_attn,
        sum_gain_moe,
        sum_rel,
        grad_expert_in[None],
        grad_expert_out[None],
    )


def solution(mesh):
    rows = P("fsdp", "seq", None)
    weight = P("fsdp", None)
    shared = P("fsdp", "seq")
    return jax.shard_map(
        per_device,
        mesh=mesh,
        in_specs=(
            rows, rows, weight, shared, P(), weight, weight, weight, weight, weight,
            P("fsdp"), P("fsdp"), P("seq", None), P("fsdp", None, "seq"), rows,
        ),
        out_specs=(
            rows, rows, shared, shared, shared, shared, shared, P("fsdp"), P("fsdp"),
            P("seq", None), P("fsdp", None, "seq"), rows,
        ),
        check_vma=False,
    )
```

```python
import functools

import jax
import jax.numpy as jnp
from jax import lax
from jax.experimental import pallas as pl
from jax.experimental.pallas import tpu as pltpu
from jax.sharding import PartitionSpec as P

EPS = 1e-06
HIGH = lax.Precision.HIGHEST
BIG = 1e30
TILE = 256
LANES = 128
BF = jnp.bfloat16
F32 = jnp.float32


def contract(left, right, left_dim, right_dim):
    return lax.dot_general(
        left, right, (((left_dim,), (right_dim,)), ((), ())), preferred_element_type=F32
    )


def doc_rows(starts_ref, length, docs):
    pos = lax.broadcasted_iota(jnp.int32, (1, length), 1)
    doc = jnp.zeros((1, length), jnp.int32) - 1
    for index in range(docs):
        doc = doc + (starts_ref[0, index] <= pos).astype(jnp.int32)
    row = lax.broadcasted_iota(jnp.int32, (8, length), 0)
    same = row == doc
    return jnp.where(same, 1.0, 0.0), jnp.where(same, 0.0, jnp.where(row < docs, -BIG, 0.0))


def forward_kernel(
    head, tile, docs, starts_ref, bias_ref, q_ref, k_ref, v_ref, o_ref, lse_ref,
    kaug, qaug, vaug, band, scores,
):
    length = q_ref.shape[1]
    span = o_ref.shape[2]
    doc_q, doc_k = doc_rows(starts_ref, length, docs)
    qaug[:head, :] = (q_ref[...].astype(F32) * 0.125).astype(BF)
    qaug[head : head + 16, :] = jnp.concatenate([doc_q, jnp.zeros((8, length), F32)], 0).astype(BF)
    qaug[head + 16 :, :] = jnp.zeros((qaug.shape[0] - head - 16, length), BF)
    tail = jnp.zeros((LANES - head - 8, tile), F32)
    for block in range(length // tile):
        cols = slice(block * tile, (block + 1) * tile)
        full = jnp.concatenate([k_ref[:, cols].astype(F32), doc_k[:, cols], tail], 0)
        kaug[cols, :] = full.T.astype(BF)
    vaug[:head, :] = v_ref[...]
    extra = lax.broadcasted_iota(jnp.int32, (vaug.shape[0] - head, length), 0)
    vaug[head:, :] = jnp.where(extra == 0, 1.0, 0.0).astype(BF)
    circle = pltpu.roll(
        jnp.broadcast_to(bias_ref[0], (tile, tile)), 0, 1, stride=1, stride_axis=0
    )
    key_row = lax.broadcasted_iota(jnp.int32, (tile, tile), 0)
    query_col = lax.broadcasted_iota(jnp.int32, (tile, tile), 1)
    band[:tile, :] = jnp.where(key_row > query_col, circle, 0.0)
    band[tile:, :] = jnp.where(key_row <= query_col, circle, -BIG)
    for i in range(length // tile):
        cols = slice(i * tile, (i + 1) * tile)
        queries = qaug[:, cols]
        peak = None
        for j in range(i + 1):
            rows = slice(j * tile, (j + 1) * tile)
            part = contract(kaug[rows, :], queries, 1, 0)
            if j == i:
                part = part + band[tile:, :]
            elif j == i - 1:
                part = part + band[:tile, :]
            scores[rows, :] = part
            most = jnp.max(part.reshape(tile // 8, 8, tile), axis=0)
            peak = most if peak is None else jnp.maximum(peak, most)
        peak = jnp.max(peak, axis=0, keepdims=True)
        summed = jnp.zeros((vaug.shape[0], tile), F32)
        for j in range(i + 1):
            rows = slice(j * tile, (j + 1) * tile)
            expons = jnp.exp(scores[rows, :] - peak).astype(BF)
            summed = summed + contract(vaug[:, rows], expons, 1, 0)
        total = summed[head : head + 1, :]
        start = (i * tile) % span
        o_ref[i * tile // span, :, start : start + tile] = (summed[:head, :] / total).astype(BF)
        lse_ref[0, :, cols] = peak + jnp.log(total)


def attend_forward(qkv_t, starts, bias_f, heads, head, spans):
    length = qkv_t.shape[1]
    docs = starts.shape[1]
    span = length // spans

    def rows_of(part):
        return pl.BlockSpec((head, length), lambda h: (3 * h + part, 0))

    return pl.pallas_call(
        functools.partial(forward_kernel, head, TILE, docs),
        grid=(heads,),
        in_specs=[
            pl.BlockSpec(memory_space=pltpu.SMEM),
            pl.BlockSpec((1, 1, TILE), lambda h: (h, 0, 0)),
            rows_of(0),
            rows_of(1),
            rows_of(2),
        ],
        out_specs=[
            pl.BlockSpec((spans, head, span), lambda h: (0, h, 0)),
            pl.BlockSpec((1, 1, length), lambda h: (h, 0, 0)),
        ],
        out_shape=[
            jax.ShapeDtypeStruct((spans, heads * head, span), BF),
            jax.ShapeDtypeStruct((heads, 1, length), F32),
        ],
        scratch_shapes=[
            pltpu.VMEM((length, LANES), BF),
            pltpu.VMEM((LANES, length), BF),
            pltpu.VMEM((head + 16, length), BF),
            pltpu.VMEM((2 * TILE, TILE), F32),
            pltpu.VMEM((length, TILE), F32),
        ],
        compiler_params=pltpu.CompilerParams(vmem_limit_bytes=40 * 2**20),
        name="attend_forward",
    )(starts, bias_f, qkv_t, qkv_t, qkv_t)


def backward_kernel(
    count, head, offset, tile, docs, starts_ref, me_ref, bias_ref, q_ref, k_ref, v_ref, do_ref, o_ref,
    lse_ref, n1_ref, slab_ref, grads_ref, dist_ref, weight_ref, qaug, doaug, kaug, vaug, scaled,
    band, dq_sum, diagonal, grads,
):
    length = q_ref.shape[1]
    span = o_ref.shape[2]
    doc_q, doc_k = doc_rows(starts_ref, length, docs)
    sub = lax.broadcasted_iota(jnp.int32, (8, tile), 0)

    def minus_split(row):
        row = -row
        high = row.astype(BF).astype(F32)
        rest = row - high
        mid = rest.astype(BF).astype(F32)
        return jnp.where(
            sub == 0, high, jnp.where(sub == 1, mid, jnp.where(sub == 2, rest - mid, 0.0))
        )

    ones3 = jnp.where(lax.broadcasted_iota(jnp.int32, (8, length), 0) < 3, 1.0, 0.0)
    zeros8 = jnp.zeros((8, length), F32)
    blocks = length // tile
    tail = jnp.zeros((LANES - head - 16, tile), F32)
    for block in range(blocks):
        cols = slice(block * tile, (block + 1) * tile)
        begin = (block * tile) % span
        inner = slice(begin, begin + tile)
        upstream = do_ref[block * tile // span, :, inner].astype(F32)
        attended = o_ref[block * tile // span, :, inner].astype(F32)
        centre = jnp.sum(upstream * attended, axis=0, keepdims=True)
        query = q_ref[:, cols].astype(F32) * 0.125
        scaled[:, cols] = query.astype(BF)
        full = jnp.concatenate([query, doc_q[:, cols], minus_split(lse_ref[0, :, cols]), tail], 0)
        qaug[cols, :] = full.T.astype(BF)
        full = jnp.concatenate([upstream, minus_split(centre), zeros8[:, cols], tail], 0)
        doaug[cols, :] = full.T.astype(BF)
    kaug[:head, :] = k_ref[...]
    kaug[head : head + 16, :] = jnp.concatenate([doc_k, ones3], 0).astype(BF)
    kaug[head + 16 :, :] = jnp.zeros((LANES - head - 16, length), BF)
    vaug[:head, :] = v_ref[...]
    vaug[head : head + 16, :] = jnp.concatenate([ones3, zeros8], 0).astype(BF)
    vaug[head + 16 :, :] = jnp.zeros((LANES - head - 16, length), BF)
    circle = pltpu.roll(
        jnp.broadcast_to(bias_ref[0], (tile, tile)), 0, 1, stride=1, stride_axis=0
    )
    query_row = lax.broadcasted_iota(jnp.int32, (tile, tile), 0)
    key_col = lax.broadcasted_iota(jnp.int32, (tile, tile), 1)
    band[:tile, :] = jnp.where(key_col <= query_row, circle, -BIG)
    band[tile:, :] = jnp.where(key_col > query_row, circle, 0.0)
    diagonal[...] = jnp.zeros_like(diagonal)
    for j in range(blocks):
        keys = slice(j * tile, (j + 1) * tile)
        dk = jnp.zeros((head, tile), F32)
        dv = jnp.zeros((head, tile), F32)
        for i in range(j, blocks):
            rows = slice(i * tile, (i + 1) * tile)
            begin = (i * tile) % span
            upstream = do_ref[i * tile // span, :, begin : begin + tile]
            part = contract(qaug[rows, :], kaug[:, keys], 1, 0)
            if i == j:
                part = part + band[:tile, :]
            elif i == j + 1:
                part = part + band[tile:, :]
            probs = jnp.exp(part)
            score_grads = probs * contract(doaug[rows, :], vaug[:, keys], 1, 0)
            if i == j:
                diagonal[...] += score_grads
            elif i == j + 1:
                diagonal[...] += jnp.where(key_col > query_row, score_grads, 0.0)
            weights = probs.astype(BF)
            short = score_grads.astype(BF)
            dv = dv + contract(upstream, weights, 1, 0)
            dk = dk + contract(scaled[:, rows], short, 1, 0)
            dq = contract(kaug[:head, keys], short, 1, 1)
            if j == 0:
                dq_sum[:, rows] = dq
            else:
                dq_sum[:, rows] += dq
        begin = (j * tile) % span
        inner = slice(begin, begin + tile)
        together = jnp.concatenate([dq_sum[:, keys] * 0.125, dk, dv], axis=0).astype(BF)
        grads[:, keys] = together
        grads_ref[(j * tile // span) ^ me_ref[0], :, inner] = together
    products = contract(grads[...], n1_ref[...], 1, 0).T
    own = slab_ref[:, offset : offset + 3 * head]
    for later in range(1, count):
        begin = offset + 3 * head * later
        own = jnp.where(pl.program_id(0) == later, slab_ref[:, begin : begin + 3 * head], own)
    share = jnp.sum(products * own.astype(F32), axis=1, keepdims=True)
    rows, columns = weight_ref.shape
    weight_ref[...] = jnp.concatenate(
        [products, share, jnp.zeros((rows, columns - 3 * head - 1), F32)], axis=1
    ).astype(BF)
    skew = diagonal[...]
    step = 1
    while step < tile:
        skew = jnp.where((query_row & step) != 0, pltpu.roll(skew, tile - step, 1), skew)
        step *= 2
    dist_ref[0] = jnp.sum(skew, axis=0, keepdims=True)


def attend_backward(
    first, count, qkv_t, upstream, attended, lse, starts, me, bias_g, n1, slab, heads, head
):
    length = qkv_t.shape[1]
    docs = starts.shape[1]
    spans, _, span = attended.shape
    width = n1.shape[1]

    def rows_of(part):
        return pl.BlockSpec((head, length), lambda h: (3 * (first + h) + part, 0))

    by_span = pl.BlockSpec((spans, head, span), lambda h: (0, first + h, 0))
    smem = pl.BlockSpec(memory_space=pltpu.SMEM)
    columns = 3 * head + 1
    columns += -columns % LANES
    return pl.pallas_call(
        functools.partial(backward_kernel, count, head, 3 * first * head, TILE, docs),
        grid=(count,),
        in_specs=[
            smem,
            smem,
            pl.BlockSpec((1, 1, TILE), lambda h: (first + h, 0, 0)),
            rows_of(0),
            rows_of(1),
            rows_of(2),
            by_span,
            by_span,
            pl.BlockSpec((1, 1, length), lambda h: (first + h, 0, 0)),
            pl.BlockSpec(n1.shape, lambda h: (0, 0)),
            pl.BlockSpec(slab.shape, lambda h: (0, 0)),
        ],
        out_specs=[
            pl.BlockSpec((spans, 3 * head, span), lambda h: (0, h, 0)),
            pl.BlockSpec((1, 1, TILE), lambda h: (h, 0, 0)),
            pl.BlockSpec((width, columns), lambda h: (0, h)),
        ],
        out_shape=[
            jax.ShapeDtypeStruct((spans, count * 3 * head, span), BF),
            jax.ShapeDtypeStruct((count, 1, TILE), F32),
            jax.ShapeDtypeStruct((width, count * columns), BF),
        ],
        scratch_shapes=[
            pltpu.VMEM((length, LANES), BF),
            pltpu.VMEM((length, LANES), BF),
            pltpu.VMEM((LANES, length), BF),
            pltpu.VMEM((LANES, length), BF),
            pltpu.VMEM((head, length), BF),
            pltpu.VMEM((2 * TILE, TILE), F32),
            pltpu.VMEM((head, length), F32),
            pltpu.VMEM((TILE, TILE), F32),
            pltpu.VMEM((3 * head, length), BF),
        ],
        compiler_params=pltpu.CompilerParams(vmem_limit_bytes=48 * 2**20),
        name="attend_backward",
    )(starts, me, bias_g, qkv_t, qkv_t, qkv_t, upstream, attended, lse, n1, slab)


def pack_kernel(spans, head, me_ref, q_ref, k_ref, v_ref, router_ref, one_ref, two_ref, slab_ref):
    rows, width = q_ref.shape
    local = width // spans
    for span in range(spans):

        @pl.when(me_ref[0] == span)
        def _():
            pieces = []
            for at in range(span * local, (span + 1) * local, head):
                pieces += [ref[:, at : at + head] for ref in (q_ref, k_ref, v_ref)]
            slab_ref[:, : 3 * local] = jnp.concatenate(pieces, axis=1)

    top = [ref[...].astype(F32) for ref in (router_ref, one_ref, two_ref)]
    used = sum(part.shape[0] for part in top)
    free = slab_ref.shape[1] - 3 * local
    tail = jnp.concatenate(top + [jnp.zeros((free - used, rows), F32)], axis=0)
    tail = jnp.concatenate([tail, jnp.zeros((free, LANES - rows), F32)], axis=1)
    slab_ref[:, 3 * local :] = tail.T[:rows].astype(BF)


def pack_slab(me, w_query, w_key, w_value, w_router, gain_attn, gain_moe, spans, head):
    rows, width = w_query.shape
    columns = 3 * width // spans + w_router.shape[1] + 2
    columns += -columns % LANES
    return pl.pallas_call(
        functools.partial(pack_kernel, spans, head),
        in_specs=[pl.BlockSpec(memory_space=pltpu.SMEM)]
        + [pl.BlockSpec(memory_space=pltpu.VMEM)] * 6,
        out_specs=pl.BlockSpec(memory_space=pltpu.VMEM),
        out_shape=jax.ShapeDtypeStruct((rows, columns), BF),
        name="pack_slab",
    )(me, w_query, w_key, w_value, w_router.T, gain_attn[None], gain_moe[None])


def share_kernel(spans, me_ref, slab_ref, *refs):
    grad_refs, out_refs = refs[:-spans], refs[-spans:]
    for mask in range(spans):
        grads = jnp.concatenate([ref[mask] for ref in grad_refs], axis=0)
        out_refs[mask][...] = contract(grads, slab_ref[:, : grads.shape[0]], 0, 1).astype(BF)


def share_rows(me, slab, grads):
    spans, _, span = grads[0].shape
    vmem = pl.BlockSpec(memory_space=pltpu.VMEM)
    return pl.pallas_call(
        functools.partial(share_kernel, spans),
        in_specs=[pl.BlockSpec(memory_space=pltpu.SMEM)] + [vmem] * (1 + len(grads)),
        out_specs=[vmem] * spans,
        out_shape=[jax.ShapeDtypeStruct((span, slab.shape[0]), BF)] * spans,
        compiler_params=pltpu.CompilerParams(vmem_limit_bytes=50 * 2**20),
        name="share_rows",
    )(me, slab, *grads)


def out_kernel(x_ref, gain_ref, grads_ref, *refs):
    share_refs, out_ref = refs[:-1], refs[-1]
    dn = sum(ref[...].astype(F32) for ref in share_refs)
    x = x_ref[...].astype(F32)
    scale = lax.rsqrt(jnp.mean(x * x, axis=1, keepdims=True) + EPS)
    normed = x * scale
    scaled = dn * gain_ref[...]
    out_ref[...] = grads_ref[...] + scale * (
        scaled - normed * jnp.mean(scaled * normed, axis=1, keepdims=True)
    )


def rows_out(x, gain, grads, shares):
    span, width = x.shape
    part = span // 4
    rows = pl.BlockSpec((part, width), lambda i: (i, 0))
    return pl.pallas_call(
        out_kernel,
        grid=(4,),
        in_specs=[rows, pl.BlockSpec((1, width), lambda i: (0, 0)), rows] + [rows] * len(shares),
        out_specs=rows,
        out_shape=jax.ShapeDtypeStruct(x.shape, F32),
        compiler_params=pltpu.CompilerParams(vmem_limit_bytes=50 * 2**20),
        name="rows_out",
    )(x, gain, grads, *shares)


def project_kernel(wide, count_old, at_ref, x_ref, slab_ref, gain_ref, *refs):
    if len(refs) == count_old + 5:
        in_ref, w_ref = refs[0], refs[1]
        packed_ref = refs[-1]
        refs = refs[2:-1]
        width, quarter = in_ref.shape
        packed_ref[:width, :] = in_ref[...]
        for at in range(0, width, quarter):
            packed_ref[width + at : width + at + quarter, :] = w_ref[:, at : at + quarter]
    n1_ref, qkv_ref = refs[count_old:]
    x = x_ref[...].astype(F32)
    scale = lax.rsqrt(jnp.mean(x * x, axis=1, keepdims=True) + EPS)
    n1 = (x * scale * gain_ref[...]).astype(BF)
    n1_ref[...] = n1
    qkv_ref[...] = contract(slab_ref[:, :wide], n1, 0, 1).astype(BF)


def project(at, rows, slab, gain, wide, spans, old, expert=()):
    span, width = rows.shape
    packed = [jax.ShapeDtypeStruct((2 * width, array.shape[1]), BF) for array in expert[:1]]
    first = 4 + len(expert)

    def whole(array):
        return pl.BlockSpec(array.shape, lambda i, at: (0, 0))

    return pl.pallas_call(
        functools.partial(project_kernel, wide, len(old)),
        grid_spec=pltpu.PrefetchScalarGridSpec(
            num_scalar_prefetch=1,
            grid=(1,),
            in_specs=[whole(array) for array in (rows, slab, gain, *expert)]
            + [pl.BlockSpec(memory_space=pl.ANY)] * len(old),
            out_specs=[
                pl.BlockSpec((span, width), lambda i, at: (at[0], 0)),
                pl.BlockSpec((wide, span), lambda i, at: (0, at[0])),
            ]
            + [whole(array) for array in packed],
        ),
        out_shape=[
            jax.ShapeDtypeStruct((spans * span, width), BF),
            jax.ShapeDtypeStruct((wide, spans * span), BF),
        ]
        + packed,
        input_output_aliases={first + index: index for index in range(len(old))},
        compiler_params=pltpu.CompilerParams(vmem_limit_bytes=40 * 2**20),
        name="project",
    )(at, rows, slab, gain, *expert, *old)


def place_of(slot_ref, part, part_rows):
    slots = lax.broadcasted_iota(jnp.int32, (part_rows, slot_ref.shape[1]), 0) + part * part_rows
    return jnp.where(slots == slot_ref[...], 1.0, 0.0).astype(BF)


def normed_rows(hidden, gain):
    scale = lax.rsqrt(jnp.mean(hidden * hidden, axis=1, keepdims=True) + EPS)
    normed = hidden * scale
    return scale, normed, (normed * gain).astype(BF)


def router_probs(rows, router, experts):
    logits = contract(rows, router, 1, 0)
    lane = lax.broadcasted_iota(jnp.int32, logits.shape, 1)
    logits = jnp.where(lane < experts, logits, -BIG)
    shifted = jnp.exp(logits - jnp.max(logits, axis=1, keepdims=True))
    return shifted / jnp.sum(shifted, axis=1, keepdims=True)


def into_kernel(parts, x_ref, mixed_ref, top_ref, low_ref, gain_ref, slot_ref, hidden_ref, *part_refs):
    out_ref = part_refs[-1]
    half, columns = top_ref.shape[1:]
    for begin, ref in ((0, top_ref), (half, low_ref)):
        for core in range(2):
            out_ref[begin : begin + half, core * columns : (core + 1) * columns] = ref[core]
    hidden = x_ref[...].astype(F32) + contract(mixed_ref[...], out_ref[...], 0, 0)
    hidden_ref[...] = hidden
    _, _, n2 = normed_rows(hidden, gain_ref[...])
    for part in range(parts):
        rows = part_refs[part].shape[0]
        part_refs[part][...] = contract(place_of(slot_ref, part, rows), n2, 1, 0).astype(BF)


def rows_into_experts(x, mixed, output_halves, gain, slot, parts, part_rows):
    span, width = x.shape
    if len(output_halves) == 1:
        blocks = output_halves[0].reshape(2, width // 2, 2, width // 2).transpose(0, 2, 1, 3)
        output_halves = [blocks[0], blocks[1]]
    vmem = pl.BlockSpec(memory_space=pltpu.VMEM)
    return pl.pallas_call(
        functools.partial(into_kernel, parts),
        in_specs=[vmem] * 6,
        out_specs=[vmem] * (2 + parts),
        out_shape=[jax.ShapeDtypeStruct((span, width), F32)]
        + [jax.ShapeDtypeStruct((part_rows, width), BF)] * parts
        + [jax.ShapeDtypeStruct((width, width), BF)],
        compiler_params=pltpu.CompilerParams(vmem_limit_bytes=50 * 2**20),
        name="rows_into_experts",
    )(x, mixed, *output_halves, gain, slot)


def back_kernel(
    parts, experts, spans, hidden_ref, up_ref, mixed_ref, out_ref, gain_ref, router_ref, chosen_ref,
    slot_ref, *refs
):
    part_refs = refs[:parts]
    output_ref, grads_ref, early_ref, do_ref = refs[parts:]
    rows = part_refs[0].shape[0] // 2
    y = None
    dn = None
    for part in range(parts):
        place = place_of(slot_ref, part, rows)
        one = contract(place, part_refs[part][:rows, :], 0, 0)
        two = contract(place, part_refs[part][rows:, :], 0, 0)
        y = one if y is None else y + one
        dn = two if dn is None else dn + two
    hidden = hidden_ref[...]
    gain = gain_ref[...]
    scale, normed, n2 = normed_rows(hidden, gain)
    probs = router_probs(n2, router_ref[...], experts)
    chosen = chosen_ref[...]
    gate = jnp.sum(probs * chosen, axis=1, keepdims=True)
    output_ref[...] = (hidden + gate * y).astype(BF)
    upstream = up_ref[...].astype(F32)
    gate_grads = jnp.sum(upstream * y, axis=1, keepdims=True)
    logit_grads = (probs * (chosen * gate_grads - gate * gate_grads)).astype(BF)
    grad_router = contract(n2, logit_grads, 0, 0)
    dn = dn + contract(logit_grads, router_ref[...], 1, 1)
    grad_gain = jnp.sum(dn * normed, axis=0, keepdims=True)
    scaled = dn * gain
    grads = upstream + scale * (scaled - normed * jnp.mean(scaled * normed, axis=1, keepdims=True))
    grads_ref[...] = grads
    short = grads.astype(BF)
    width = out_ref.shape[0]
    local = width // spans
    share = experts // spans
    column = jnp.broadcast_to(grad_gain, (8, width)).T[:, :1]
    free = early_ref.shape[2] - local - share - 1
    for span in range(spans):
        tail = [grad_router[:, span * share : (span + 1) * share], column, jnp.zeros((width, free), F32)]
        early_ref[span, :, local:] = jnp.concatenate(tail, axis=1).astype(BF)
    do_ref[...] = contract(out_ref[...], short, 1, 1).astype(BF)
    grad_output = contract(mixed_ref[...], short, 1, 0).astype(BF)
    for span in range(spans):
        early_ref[span, :, :local] = grad_output[:, span * local : (span + 1) * local]


def rows_from_experts(
    hidden, upstream, mixed, full_output, gain, router, chosen, slot, back, experts, spans
):
    span, width = hidden.shape
    columns = width // spans + experts // spans + 1
    columns += -columns % LANES
    vmem = pl.BlockSpec(memory_space=pltpu.VMEM)
    return pl.pallas_call(
        functools.partial(back_kernel, len(back), experts, spans),
        in_specs=[vmem] * (8 + len(back)),
        out_specs=[vmem] * 4,
        out_shape=[
            jax.ShapeDtypeStruct((span, width), BF),
            jax.ShapeDtypeStruct((span, width), F32),
            jax.ShapeDtypeStruct((spans, width, columns), BF),
            jax.ShapeDtypeStruct((width, span), BF),
        ],
        compiler_params=pltpu.CompilerParams(vmem_limit_bytes=50 * 2**20),
        name="rows_from_experts",
    )(hidden, upstream, mixed, full_output, gain, router, chosen, slot, *back)


def expert_kernel(experts, inputs, count_old, me_ref, core_ref, router_ref, *refs):
    x_refs = refs[:inputs]
    up_refs = refs[inputs : 2 * inputs]
    own_ref, near_ref, far_ref, in_ref, out_ref = refs[2 * inputs : 2 * inputs + 5]
    ours_ref, parts_ref, act_ref, pre_ref, dy_ref, keep_ref = refs[2 * inputs + 5 + count_old :]
    count, width = x_refs[0].shape
    rows = count // 2
    first = core_ref[0] == 0
    quarter = own_ref.shape[1]
    ins = [own_ref[:width, :], near_ref[:width, :], far_ref[:width, :], in_ref[...]]
    outs = [
        jnp.concatenate([ref[at : at + quarter, :] for at in range(begin, begin + width, quarter)], 1)
        for ref, begin in ((own_ref, width), (near_ref, width), (far_ref, width), (out_ref, 0))
    ]
    pairs = [
        (jnp.concatenate(ins[b : b + 2], axis=1), jnp.concatenate(outs[b : b + 2], axis=0))
        for b in (0, 2)
    ]
    for index in range(inputs):
        here = slice(index * count, (index + 1) * count)
        x = x_refs[index][...]
        probs = router_probs(x, router_ref[...], experts)
        lane = lax.broadcasted_iota(jnp.int32, probs.shape, 1)
        gate = jnp.sum(jnp.where(lane == me_ref[0], probs, 0.0), axis=1, keepdims=True)
        dy_ref[here, :] = (gate * up_refs[index][...].astype(F32)).astype(BF)
        keep_ref[here, :] = x
        y_sum = None
        for pair, (w_in, w_out) in enumerate(pairs):
            cols = slice(2 * pair * quarter, 2 * (pair + 1) * quarter)
            pre = contract(x_refs[index][...], w_in, 1, 0)
            root = 0.7978845608028654
            square = pre * pre
            tanh = jnp.tanh(pre * (root + (root * 0.044715) * square))
            half = 0.5 + 0.5 * tanh
            act = (pre * half).astype(BF)
            slope = half + (pre * half) * (1.0 - tanh) * (root + (root * 0.134145) * square)
            act_ref[here, cols] = act
            pre_grads = (contract(dy_ref[here, :], w_out, 1, 1) * slope).astype(BF)
            pre_ref[here, cols] = pre_grads
            y = contract(act, w_out, 1, 0)
            dn = contract(pre_grads, w_in, 1, 1)
            y_sum = y if y_sum is None else y_sum + y
            dn_sum = dn if pair == 0 else dn_sum + dn
        for some, total in ((slice(0, rows), y_sum), (slice(rows, count), dn_sum)):
            one, two = total[:rows], total[rows:]
            ours_ref[index, some, :] = jnp.where(first, one, two).astype(BF)
            parts_ref[index, some, :] = jnp.where(first, two, one).astype(BF)


def expert_part(part, parts, me, core, rows, upstream, router, weights, old, experts):
    inputs = len(rows)
    count, width = rows[0].shape
    hidden = 4 * weights[0].shape[1]
    here = count * inputs
    total = here * parts
    first = 3 + 2 * inputs + len(weights)
    kept = [pl.BlockSpec((here, size), lambda i: (part, 0)) for size in (hidden, hidden, width, width)]
    whole = [
        pl.BlockSpec(array.shape, lambda i: (0, 0)) for array in (router, *rows, *upstream, *weights)
    ]
    return pl.pallas_call(
        functools.partial(expert_kernel, experts, inputs, len(old)),
        grid=(1,),
        in_specs=[pl.BlockSpec(memory_space=pltpu.SMEM)] * 2
        + whole
        + [pl.BlockSpec(memory_space=pl.ANY)] * len(old),
        out_specs=[pl.BlockSpec((inputs, count, width), lambda i: (0, 0, 0))] * 2 + kept,
        out_shape=[jax.ShapeDtypeStruct((inputs, count, width), BF)] * 2
        + [
            jax.ShapeDtypeStruct((total, size), BF) for size in (hidden, hidden, width, width)
        ],
        input_output_aliases={first + index: 2 + index for index in range(len(old))},
        compiler_params=pltpu.CompilerParams(vmem_limit_bytes=56 * 2**20),
        name="expert_part",
    )(me, core, router, *rows, *upstream, *weights, *old)


def add_kernel(shares, *refs):
    parts = len(refs) - 2 * shares
    for index in range(parts):
        share, at = divmod(index, parts // shares)
        mine, theirs = refs[2 * share], refs[2 * share + 1]
        refs[2 * shares + index][...] = (mine[at].astype(F32) + theirs[at].astype(F32)).astype(BF)


def add_halves(pairs):
    inputs, rows, width = pairs[0][0].shape
    vmem = pl.BlockSpec(memory_space=pltpu.VMEM)
    flat = [array for pair in pairs for array in pair]
    return pl.pallas_call(
        functools.partial(add_kernel, len(pairs)),
        in_specs=[vmem] * len(flat),
        out_specs=[vmem] * (inputs * len(pairs)),
        out_shape=[jax.ShapeDtypeStruct((rows, width), BF)] * (inputs * len(pairs)),
        compiler_params=pltpu.CompilerParams(vmem_limit_bytes=50 * 2**20),
        name="add_halves",
    )(*flat)


def expert_grads_kernel(act_ref, pre_ref, dy_ref, x_ref, one_ref, two_ref, keep_one, keep_two):
    width = x_ref.shape[1]
    quarter = act_ref.shape[1]
    mask = pl.program_id(0)
    grad_in = contract(x_ref[...], pre_ref[...], 0, 0)
    grad_out = contract(act_ref[...], dy_ref[...], 0, 0)
    grad_out = jnp.concatenate(
        [grad_out[:, at : at + quarter] for at in range(0, width, quarter)], axis=0
    )
    for index, at in enumerate((1, 3)):

        @pl.when(mask == at)
        def _():
            one_ref[index] = grad_in.astype(BF)

    for index, at in enumerate((2, 3)):

        @pl.when(mask == at)
        def _():
            two_ref[index] = grad_out.astype(BF)

    for index, at in enumerate((0, 2)):

        @pl.when(mask == at)
        def _():
            keep_one[index] = grad_in

    for index, at in enumerate((0, 1)):

        @pl.when(mask == at)
        def _():
            keep_two[index] = grad_out


def expert_grads(kept, quarter):
    act, pre, dy, rows = kept
    total, width = dy.shape
    hidden = pl.BlockSpec((total, quarter), lambda f: (0, f))
    whole = pl.BlockSpec((total, width), lambda f: (0, 0))
    pair = pl.BlockSpec((2, width, quarter), lambda f: (0, 0, 0))
    return pl.pallas_call(
        expert_grads_kernel,
        grid=(act.shape[1] // quarter,),
        in_specs=[hidden, hidden, whole, whole],
        out_specs=[pair] * 4,
        out_shape=[jax.ShapeDtypeStruct((2, width, quarter), BF)] * 2
        + [jax.ShapeDtypeStruct((2, width, quarter), F32)] * 2,
        compiler_params=pltpu.CompilerParams(vmem_limit_bytes=50 * 2**20),
        name="expert_grads",
    )(act, pre, dy, rows)


def settle_kernel(keep_one, keep_two, got_one, got_two, one_ref, two_ref):
    one_ref[...] = (keep_one[0].astype(F32) + got_one[0].astype(F32)).astype(BF)
    two_ref[...] = (keep_two[0].astype(F32) + got_two[0].astype(F32)).astype(BF)


def settle_step(keep_one, keep_two, got_one, got_two):
    _, width, quarter = keep_one.shape
    second = pl.BlockSpec((1, width, quarter), lambda i: (1, 0, 0))
    whole = pl.BlockSpec((width, quarter), lambda i: (0, 0))
    return pl.pallas_call(
        settle_kernel,
        grid=(1,),
        in_specs=[second] * 4,
        out_specs=[whole] * 2,
        out_shape=[jax.ShapeDtypeStruct((width, quarter), BF)] * 2,
        compiler_params=pltpu.CompilerParams(vmem_limit_bytes=50 * 2**20),
        name="settle_step",
    )(keep_one, keep_two, got_one, got_two)


def all_to_all(blocks, axis, groups=None):
    return lax.all_to_all(
        blocks, axis, split_axis=0, concat_axis=0, tiled=True, axis_index_groups=groups
    )


def pair_swap(block, axis, mask):
    count = lax.axis_size(axis)
    return lax.ppermute(block, axis, [(i, i ^ mask) for i in range(count)])


def tied(values, *others):
    return lax.optimization_barrier((values, others))[0]


def gather_pairs(rows, axis, groups, pairs, after):
    count = lax.axis_size(axis)
    if count > 8:
        return [lax.all_gather(rows, axis, axis=0, tiled=True)]
    core = lax.axis_index(axis) % 2
    columns = rows.shape[1] // 2
    low, high = rows[:, :columns], rows[:, columns:]
    mine = jnp.where(core == 0, low, high)
    got = pair_swap(jnp.where(core == 0, high, low), axis, 1)
    chip = jnp.where(core == 0, jnp.stack([mine, got]), jnp.stack([got, mine]))
    whole = all_to_all(jnp.broadcast_to(chip[None], (count // 2,) + chip.shape), axis, groups)
    whole = tied(whole.reshape(2, count * rows.shape[0] // 2, columns), after)
    return [
        lax.all_gather(part, axis, axis=0, tiled=False, axis_index_groups=pairs) for part in whole
    ]


def scatter_sums(rows, axis, groups):
    count = lax.axis_size(axis)
    here = rows.shape[0] // count
    if count > 8:
        blocks = all_to_all(rows.reshape(count, here, rows.shape[1]), axis)
        return jnp.sum(blocks.astype(F32), axis=0)
    core = lax.axis_index(axis) % 2
    split = rows.reshape(count // 2, 2, here, rows.shape[1])
    mine = lax.dynamic_index_in_dim(split, core, 1, keepdims=False)
    other = pair_swap(lax.dynamic_index_in_dim(split, 1 - core, 1, keepdims=False), axis, 1)
    chip = (mine.astype(F32) + other.astype(F32)).astype(BF)
    return jnp.sum(all_to_all(chip, axis, groups).astype(F32), axis=0)


def per_device(
    tokens, cotangent, doc_starts, routes, bucket_table, w_query, w_key, w_value, w_output,
    w_router, gain_attn, gain_moe, rel_bias, expert_in, expert_out,
):
    _, span, width = tokens.shape
    seq_count = lax.axis_size("seq")
    fsdp_count = lax.axis_size("fsdp")
    seq_me = lax.axis_index("seq")
    fsdp_me = lax.axis_index("fsdp")
    heads, buckets = rel_bias.shape
    local = width // seq_count
    head = local // heads
    experts = w_router.shape[1]
    rows_here = w_query.shape[0]
    quarter = expert_in.shape[2]
    cores = 2
    groups = [list(range(core, fsdp_count, cores)) for core in range(cores)]
    x = tokens[0]
    seq_index = seq_me.astype(jnp.int32)[None]
    expert_index = (fsdp_me // cores).astype(jnp.int32)[None]
    core_index = (fsdp_me % cores).astype(jnp.int32)[None]

    near = pair_swap(x, "seq", 1)
    far = pair_swap(x, "seq", 2)
    slab = pack_slab(
        seq_index, w_query, w_key, w_value, w_router, gain_attn, gain_moe, seq_count, head
    )
    slab = lax.all_gather(slab, "fsdp", axis=0, tiled=True)
    half = span // 2
    slab, near_half, far_half = lax.optimization_barrier((slab, near[:half], far[half:]))
    across = [pair_swap(near_half, "seq", 2), pair_swap(far_half, "seq", 1)]
    tail = slab[:, 3 * local :]
    full_router = jnp.pad(tail[:, :experts], ((0, 0), (0, -experts % LANES)))
    gains = tail[:, experts : experts + 2].astype(F32).T
    gain_one, gain_two = gains[:1], gains[1:2]
    own_gain = gain_attn.astype(F32)

    expert_me = fsdp_me // cores
    few = experts <= 4
    route = routes[0]
    chosen = (route[:, None] == jnp.arange(LANES, dtype=jnp.int32)[None, :]).astype(F32)
    before = (
        jnp.arange(span, dtype=jnp.int32)[:, None] > jnp.arange(span, dtype=jnp.int32)[None, :]
    ).astype(BF)
    ranks = jnp.dot(before, chosen.astype(BF), preferred_element_type=F32)
    capacity = max(2, 2 * span // experts)
    target = route ^ expert_me if few else route
    slot = target * capacity + jnp.sum(ranks * chosen, axis=1).astype(jnp.int32)
    slot = slot[None]
    part_count = 4
    part_rows = experts * capacity // part_count

    def exchange(parts):
        if few:
            return [parts[0]] + [
                pair_swap(parts[mask], "fsdp", cores * mask) for mask in range(1, part_count)
            ]
        blocks = jnp.concatenate(parts, axis=0).reshape(experts, capacity, width)
        blocks = all_to_all(blocks, "fsdp", groups).reshape(part_count, part_rows, width)
        return [blocks[part] for part in range(part_count)]

    upstream_parts = []
    old = ()
    for mask, part in enumerate((x, near, far)):
        old = project(
            (seq_me ^ mask).astype(jnp.int32)[None], part, slab, gain_one, 3 * local, seq_count, old,
            () if mask < 2 else (expert_in[0], expert_out[0]),
        )
    weights = tied(old[2], across)
    w_near = pair_swap(weights, "seq", 1)
    w_far = pair_swap(weights, "seq", 2)
    up_rows, old = lax.optimization_barrier((cotangent[0], old[:2]))
    w_output = tied(w_output, slab)
    for part in range(part_count):
        place = (part * part_rows + jnp.arange(part_rows, dtype=jnp.int32))[:, None] == slot
        upstream_parts.append(
            jnp.dot(place.astype(BF), up_rows, preferred_element_type=F32).astype(BF)
        )
    upstream_parts = exchange(upstream_parts)
    n1_all, qkv_t = project(
        (seq_me ^ 3).astype(jnp.int32)[None], jnp.concatenate(across, axis=0), slab, gain_one,
        3 * local, seq_count, old,
    )
    table = jnp.concatenate([bucket_table[:TILE], bucket_table[:1], bucket_table[1:TILE][::-1]])
    onehot = (table[:, None] == jnp.arange(buckets, dtype=jnp.int32)[None, :]).astype(F32)
    rel = rel_bias.astype(F32)
    by_distance = jnp.dot(rel - rel[:, buckets - 1 :], onehot.T, precision=HIGH)
    attended, lse = attend_forward(
        qkv_t, doc_starts, by_distance[:, None, :TILE], heads, head, seq_count
    )
    mixed = all_to_all(attended, "seq").reshape(width, span)
    pairs = [list(range(at, at + cores)) for at in range(0, fsdp_count, cores)]
    output_halves = gather_pairs(w_output, "fsdp", groups, pairs, attended)

    def of_chip(rows):
        return lax.all_gather(rows, "fsdp", axis=0, tiled=True, axis_index_groups=pairs)

    upstream_parts = [of_chip(part) for part in upstream_parts]
    mixed, output_halves, upstream_parts, w_near, w_far = lax.optimization_barrier(
        (mixed, output_halves, upstream_parts, w_near, w_far)
    )

    hidden, *parts, full_output = rows_into_experts(
        x, mixed, output_halves, gain_two, slot, part_count, part_rows
    )
    w_near, w_far, parts = lax.optimization_barrier((w_near, w_far, parts))
    w_across = [pair_swap(w_near[:width], "seq", 2), pair_swap(w_far[width:], "seq", 1)]
    weights = [weights, w_near, w_far] + w_across
    arrived = exchange(parts)
    kept = ()
    pairs_of_shares = []
    steps = part_count // 2
    for part in range(steps):
        some = slice(part * part_count // steps, (part + 1) * part_count // steps)
        rows = arrived[some]
        if part:
            rows = tied(rows, kept)
        ours, theirs, *kept = expert_part(
            part, steps, expert_index, core_index, [of_chip(part) for part in rows],
            upstream_parts[some],
            full_router, weights, kept, experts,
        )
        pairs_of_shares.append((ours, pair_swap(theirs, "fsdp", 1)))
    back = add_halves(pairs_of_shares)
    kept = tied(kept, back)
    if few:
        back = exchange(back)
    else:
        ys = exchange([rows[:part_rows] for rows in back])
        dns = exchange([rows[part_rows:] for rows in back])
        back = [jnp.concatenate(rows, axis=0) for rows in zip(ys, dns)]
    one, two, keep_one, keep_two = expert_grads(kept, quarter)
    back = tied(back, one, two)
    got_one = pair_swap(one, "seq", 1)
    got_two = pair_swap(two, "seq", 2)

    output, hidden_grads, early, mixed_grads = rows_from_experts(
        hidden, cotangent[0], mixed, full_output, gain_two, full_router, chosen, slot, back,
        experts, seq_count,
    )
    moved = all_to_all(mixed_grads.reshape(seq_count, local, span), "seq")
    moved, got_one, got_two = lax.optimization_barrier((moved, got_one, got_two))
    settled_sum = [keep[0] + got[0].astype(F32) for keep, got in ((keep_one, got_one), (keep_two, got_two))]
    one, two = settle_step(keep_one, keep_two, got_one, got_two)
    moved, one, two = lax.optimization_barrier((moved, one, two))
    got_one = pair_swap(one, "seq", 2)
    got_two = pair_swap(two, "seq", 1)
    early = all_to_all(tied(early, moved), "seq")
    head_grads, distances, weight_grads = attend_backward(
        0, heads, qkv_t, moved, attended, lse, doc_starts, seq_index,
        by_distance[:, None, TILE:], n1_all, slab, heads, head,
    )
    head_grads, got_one, got_two = lax.optimization_barrier((head_grads, got_one, got_two))
    shares = share_rows(seq_index, slab, [head_grads])
    weight_grads, distances, early = tied((weight_grads, distances, early), shares)
    shares = [shares[0]] + [
        pair_swap(shares[mask], "seq", mask) for mask in range(1, seq_count)
    ]
    grad_expert_in, grad_expert_out = [
        total + got.astype(F32) for total, got in zip(settled_sum, (got_one, got_two))
    ]
    grad_expert_out = jnp.concatenate(
        [grad_expert_out[at : at + quarter] for at in range(0, width, quarter)], axis=1
    )
    below = jnp.dot(distances[:, 0], onehot[TILE:, : buckets - 1], precision=HIGH)
    grad_rel = jnp.concatenate([below, -jnp.sum(below, axis=1, keepdims=True)], axis=1)
    input_grads = rows_out(x, gain_one, hidden_grads, shares)

    share = experts // seq_count
    early = jnp.sum(early.astype(F32), axis=0).astype(BF)
    rel_count = heads * buckets
    fits = rows_here >= rel_count
    if fits:
        column = jnp.pad(grad_rel.reshape(rel_count), (0, rows_here - rel_count))
        column = jnp.tile(column, fsdp_count)[:, None].astype(BF)
        at = local + share + 1
        early = jnp.concatenate([early[:, :at], column, early[:, at + 1 :]], axis=1)
    columns = weight_grads.shape[1] // heads
    summed = scatter_sums(jnp.concatenate([weight_grads, early], axis=1), "fsdp", groups)
    by_head = [summed[:, at : at + columns] for at in range(0, heads * columns, columns)]
    summed = summed[:, heads * columns :]
    sum_gain_attn = sum(part[:, 3 * head] for part in by_head) / own_gain
    sum_gain_attn = sum_gain_attn + sum(
        pair_swap(sum_gain_attn, "seq", mask) for mask in range(1, seq_count)
    )
    if fits:
        sum_rel = summed[:rel_count, local + share + 1].reshape(heads, buckets)
    else:
        sum_rel = lax.psum(grad_rel, "fsdp")
    heads_sum = [
        jnp.concatenate([part[:, at : at + head] for part in by_head], axis=1)
        for at in range(0, 3 * head, head)
    ]
    return (
        output[None],
        input_grads[None],
        heads_sum[0],
        heads_sum[1],
        heads_sum[2],
        summed[:, :local],
        summed[:, local : local + share],
        sum_gain_attn,
        summed[:, local + share],
        sum_rel,
        grad_expert_in[None],
        grad_expert_out[None],
    )


def solution(mesh):
    rows = P("fsdp", "seq", None)
    weight = P("fsdp", None)
    shared = P("fsdp", "seq")
    return jax.shard_map(
        per_device,
        mesh=mesh,
        in_specs=(
            rows, rows, weight, shared, P(), weight, weight, weight, weight, weight,
            P("fsdp"), P("fsdp"), P("seq", None), P("fsdp", None, "seq"), rows,
        ),
        out_specs=(
            rows, rows, shared, shared, shared, shared, shared, P("fsdp"), P("fsdp"),
            P("seq", None), P("fsdp", None, "seq"), rows,
        ),
        check_vma=False,
    )
```

```python
import functools

import jax
import jax.numpy as jnp
from jax import lax
from jax.experimental import pallas as pl
from jax.experimental.pallas import tpu as pltpu
from jax.sharding import PartitionSpec as P

EPS = 1e-06
HIGH = lax.Precision.HIGHEST
BIG = 1e30
TILE = 256
LANES = 128
BF = jnp.bfloat16
F32 = jnp.float32


def contract(left, right, left_dim, right_dim):
    return lax.dot_general(
        left, right, (((left_dim,), (right_dim,)), ((), ())), preferred_element_type=F32
    )


def doc_rows(starts_ref, length, docs):
    pos = lax.broadcasted_iota(jnp.int32, (1, length), 1)
    doc = jnp.zeros((1, length), jnp.int32) - 1
    for index in range(docs):
        doc = doc + (starts_ref[0, index] <= pos).astype(jnp.int32)
    row = lax.broadcasted_iota(jnp.int32, (8, length), 0)
    same = row == doc
    return jnp.where(same, 1.0, 0.0), jnp.where(same, 0.0, jnp.where(row < docs, -BIG, 0.0))


def bias_circle(rel_ref, bucket_ref, head, tile):
    last = rel_ref.shape[1] - 1
    bucket = bucket_ref[...]
    row = jnp.zeros(bucket.shape, F32)
    for index in range(last):
        row = jnp.where(bucket == index, rel_ref[head, index] - rel_ref[head, last], row)
    return pltpu.roll(jnp.broadcast_to(row, (tile, tile)), 0, 1, stride=1, stride_axis=0)


def forward_kernel(
    head, tile, docs, starts_ref, rel_ref, bucket_ref, q_ref, k_ref, v_ref, o_ref, lse_ref,
    kaug, qaug, vaug, band, scores,
):
    length = q_ref.shape[1]
    span = o_ref.shape[2]
    doc_q, doc_k = doc_rows(starts_ref, length, docs)
    qaug[:head, :] = (q_ref[...].astype(F32) * 0.125).astype(BF)
    qaug[head : head + 16, :] = jnp.concatenate([doc_q, jnp.zeros((8, length), F32)], 0).astype(BF)
    qaug[head + 16 :, :] = jnp.zeros((qaug.shape[0] - head - 16, length), BF)
    tail = jnp.zeros((LANES - head - 8, tile), F32)
    for block in range(length // tile):
        cols = slice(block * tile, (block + 1) * tile)
        full = jnp.concatenate([k_ref[:, cols].astype(F32), doc_k[:, cols], tail], 0)
        kaug[cols, :] = full.T.astype(BF)
    vaug[:head, :] = v_ref[...]
    extra = lax.broadcasted_iota(jnp.int32, (vaug.shape[0] - head, length), 0)
    vaug[head:, :] = jnp.where(extra == 0, 1.0, 0.0).astype(BF)
    circle = bias_circle(rel_ref, bucket_ref, pl.program_id(0), tile)
    key_row = lax.broadcasted_iota(jnp.int32, (tile, tile), 0)
    query_col = lax.broadcasted_iota(jnp.int32, (tile, tile), 1)
    band[:tile, :] = jnp.where(key_row > query_col, circle, 0.0)
    band[tile:, :] = jnp.where(key_row <= query_col, circle, -BIG)
    for i in range(length // tile):
        cols = slice(i * tile, (i + 1) * tile)
        queries = qaug[:, cols]
        peak = None
        for j in range(i + 1):
            rows = slice(j * tile, (j + 1) * tile)
            part = contract(kaug[rows, :], queries, 1, 0)
            if j == i:
                part = part + band[tile:, :]
            elif j == i - 1:
                part = part + band[:tile, :]
            scores[rows, :] = part
            most = jnp.max(part.reshape(tile // 8, 8, tile), axis=0)
            peak = most if peak is None else jnp.maximum(peak, most)
        peak = jnp.max(peak, axis=0, keepdims=True)
        summed = jnp.zeros((vaug.shape[0], tile), F32)
        for j in range(i + 1):
            rows = slice(j * tile, (j + 1) * tile)
            expons = jnp.exp(scores[rows, :] - peak).astype(BF)
            summed = summed + contract(vaug[:, rows], expons, 1, 0)
        total = summed[head : head + 1, :]
        start = (i * tile) % span
        o_ref[i * tile // span, :, start : start + tile] = (summed[:head, :] / total).astype(BF)
        lse_ref[0, :, cols] = peak + jnp.log(total)


def attend_forward(qkv_t, starts, rel, bucket, heads, head, spans):
    length = qkv_t.shape[1]
    docs = starts.shape[1]
    span = length // spans

    def rows_of(part):
        return pl.BlockSpec((head, length), lambda h: (3 * h + part, 0))

    return pl.pallas_call(
        functools.partial(forward_kernel, head, TILE, docs),
        grid=(heads,),
        in_specs=[
            pl.BlockSpec(memory_space=pltpu.SMEM),
            pl.BlockSpec(memory_space=pltpu.SMEM),
            pl.BlockSpec((1, TILE), lambda h: (0, 0)),
            rows_of(0),
            rows_of(1),
            rows_of(2),
        ],
        out_specs=[
            pl.BlockSpec((spans, head, span), lambda h: (0, h, 0)),
            pl.BlockSpec((1, 1, length), lambda h: (h, 0, 0)),
        ],
        out_shape=[
            jax.ShapeDtypeStruct((spans, heads * head, span), BF),
            jax.ShapeDtypeStruct((heads, 1, length), F32),
        ],
        scratch_shapes=[
            pltpu.VMEM((length, LANES), BF),
            pltpu.VMEM((LANES, length), BF),
            pltpu.VMEM((head + 16, length), BF),
            pltpu.VMEM((2 * TILE, TILE), F32),
            pltpu.VMEM((length, TILE), F32),
        ],
        compiler_params=pltpu.CompilerParams(vmem_limit_bytes=40 * 2**20),
        name="attend_forward",
    )(starts, rel, bucket, qkv_t, qkv_t, qkv_t)


def backward_kernel(
    count, head, offset, tile, docs, starts_ref, me_ref, rel_ref, bucket_ref, q_ref, k_ref, v_ref, do_ref, o_ref,
    lse_ref, n1_ref, slab_ref, grads_ref, dist_ref, weight_ref, qaug, doaug, kaug, vaug, scaled,
    band, dq_sum, diagonal, grads,
):
    length = q_ref.shape[1]
    span = o_ref.shape[2]
    doc_q, doc_k = doc_rows(starts_ref, length, docs)
    sub = lax.broadcasted_iota(jnp.int32, (8, tile), 0)

    def minus_split(row):
        row = -row
        high = row.astype(BF).astype(F32)
        rest = row - high
        mid = rest.astype(BF).astype(F32)
        return jnp.where(
            sub == 0, high, jnp.where(sub == 1, mid, jnp.where(sub == 2, rest - mid, 0.0))
        )

    ones3 = jnp.where(lax.broadcasted_iota(jnp.int32, (8, length), 0) < 3, 1.0, 0.0)
    zeros8 = jnp.zeros((8, length), F32)
    blocks = length // tile
    tail = jnp.zeros((LANES - head - 16, tile), F32)
    for block in range(blocks):
        cols = slice(block * tile, (block + 1) * tile)
        begin = (block * tile) % span
        inner = slice(begin, begin + tile)
        upstream = do_ref[block * tile // span, :, inner].astype(F32)
        attended = o_ref[block * tile // span, :, inner].astype(F32)
        centre = jnp.sum(upstream * attended, axis=0, keepdims=True)
        query = q_ref[:, cols].astype(F32) * 0.125
        scaled[:, cols] = query.astype(BF)
        full = jnp.concatenate([query, doc_q[:, cols], minus_split(lse_ref[0, :, cols]), tail], 0)
        qaug[cols, :] = full.T.astype(BF)
        full = jnp.concatenate([upstream, minus_split(centre), zeros8[:, cols], tail], 0)
        doaug[cols, :] = full.T.astype(BF)
    kaug[:head, :] = k_ref[...]
    kaug[head : head + 16, :] = jnp.concatenate([doc_k, ones3], 0).astype(BF)
    kaug[head + 16 :, :] = jnp.zeros((LANES - head - 16, length), BF)
    vaug[:head, :] = v_ref[...]
    vaug[head : head + 16, :] = jnp.concatenate([ones3, zeros8], 0).astype(BF)
    vaug[head + 16 :, :] = jnp.zeros((LANES - head - 16, length), BF)
    circle = bias_circle(rel_ref, bucket_ref, pl.program_id(0) + offset // (3 * head), tile).T
    query_row = lax.broadcasted_iota(jnp.int32, (tile, tile), 0)
    key_col = lax.broadcasted_iota(jnp.int32, (tile, tile), 1)
    band[:tile, :] = jnp.where(key_col <= query_row, circle, -BIG)
    band[tile:, :] = jnp.where(key_col > query_row, circle, 0.0)
    diagonal[...] = jnp.zeros_like(diagonal)
    for j in range(blocks):
        keys = slice(j * tile, (j + 1) * tile)
        dk = jnp.zeros((head, tile), F32)
        dv = jnp.zeros((head, tile), F32)
        for i in range(j, blocks):
            rows = slice(i * tile, (i + 1) * tile)
            begin = (i * tile) % span
            upstream = do_ref[i * tile // span, :, begin : begin + tile]
            part = contract(qaug[rows, :], kaug[:, keys], 1, 0)
            if i == j:
                part = part + band[:tile, :]
            elif i == j + 1:
                part = part + band[tile:, :]
            probs = jnp.exp(part)
            score_grads = probs * contract(doaug[rows, :], vaug[:, keys], 1, 0)
            if i == j:
                diagonal[...] += score_grads
            elif i == j + 1:
                diagonal[...] += jnp.where(key_col > query_row, score_grads, 0.0)
            weights = probs.astype(BF)
            short = score_grads.astype(BF)
            dv = dv + contract(upstream, weights, 1, 0)
            dk = dk + contract(scaled[:, rows], short, 1, 0)
            dq = contract(kaug[:head, keys], short, 1, 1)
            if j == 0:
                dq_sum[:, rows] = dq
            else:
                dq_sum[:, rows] += dq
        begin = (j * tile) % span
        inner = slice(begin, begin + tile)
        together = jnp.concatenate([dq_sum[:, keys] * 0.125, dk, dv], axis=0).astype(BF)
        grads[:, keys] = together
        grads_ref[(j * tile // span) ^ me_ref[0], :, inner] = together
    products = contract(grads[...], n1_ref[...], 1, 0).T
    own = slab_ref[:, offset : offset + 3 * head]
    for later in range(1, count):
        begin = offset + 3 * head * later
        own = jnp.where(pl.program_id(0) == later, slab_ref[:, begin : begin + 3 * head], own)
    share = jnp.sum(products * own.astype(F32), axis=1, keepdims=True)
    rows, columns = weight_ref.shape
    weight_ref[...] = jnp.concatenate(
        [products, share, jnp.zeros((rows, columns - 3 * head - 1), F32)], axis=1
    ).astype(BF)
    skew = diagonal[...].T
    step = 1
    while step < tile:
        skew = jnp.where((query_row & step) != 0, pltpu.roll(skew, tile - step, 1), skew)
        step *= 2
    dist_ref[0] = jnp.sum(skew, axis=0, keepdims=True)


def attend_backward(
    first, count, qkv_t, upstream, attended, lse, starts, me, rel, bucket, n1, slab, heads, head
):
    length = qkv_t.shape[1]
    docs = starts.shape[1]
    spans, _, span = attended.shape
    width = n1.shape[1]

    def rows_of(part):
        return pl.BlockSpec((head, length), lambda h: (3 * (first + h) + part, 0))

    by_span = pl.BlockSpec((spans, head, span), lambda h: (0, first + h, 0))
    smem = pl.BlockSpec(memory_space=pltpu.SMEM)
    columns = 3 * head + 1
    columns += -columns % LANES
    return pl.pallas_call(
        functools.partial(backward_kernel, count, head, 3 * first * head, TILE, docs),
        grid=(count,),
        in_specs=[
            smem,
            smem,
            smem,
            pl.BlockSpec((1, TILE), lambda h: (0, 0)),
            rows_of(0),
            rows_of(1),
            rows_of(2),
            by_span,
            by_span,
            pl.BlockSpec((1, 1, length), lambda h: (first + h, 0, 0)),
            pl.BlockSpec(n1.shape, lambda h: (0, 0)),
            pl.BlockSpec(slab.shape, lambda h: (0, 0)),
        ],
        out_specs=[
            pl.BlockSpec((spans, 3 * head, span), lambda h: (0, h, 0)),
            pl.BlockSpec((1, 1, TILE), lambda h: (h, 0, 0)),
            pl.BlockSpec((width, columns), lambda h: (0, h)),
        ],
        out_shape=[
            jax.ShapeDtypeStruct((spans, count * 3 * head, span), BF),
            jax.ShapeDtypeStruct((count, 1, TILE), F32),
            jax.ShapeDtypeStruct((width, count * columns), BF),
        ],
        scratch_shapes=[
            pltpu.VMEM((length, LANES), BF),
            pltpu.VMEM((length, LANES), BF),
            pltpu.VMEM((LANES, length), BF),
            pltpu.VMEM((LANES, length), BF),
            pltpu.VMEM((head, length), BF),
            pltpu.VMEM((2 * TILE, TILE), F32),
            pltpu.VMEM((head, length), F32),
            pltpu.VMEM((TILE, TILE), F32),
            pltpu.VMEM((3 * head, length), BF),
        ],
        compiler_params=pltpu.CompilerParams(vmem_limit_bytes=48 * 2**20),
        name="attend_backward",
    )(starts, me, rel, bucket, qkv_t, qkv_t, qkv_t, upstream, attended, lse, n1, slab)


def pack_kernel(spans, head, me_ref, q_ref, k_ref, v_ref, router_ref, one_ref, two_ref, slab_ref):
    rows, width = q_ref.shape
    local = width // spans
    for span in range(spans):

        @pl.when(me_ref[0] == span)
        def _():
            pieces = []
            for at in range(span * local, (span + 1) * local, head):
                pieces += [ref[:, at : at + head] for ref in (q_ref, k_ref, v_ref)]
            slab_ref[:, : 3 * local] = jnp.concatenate(pieces, axis=1)

    top = [ref[...].astype(F32) for ref in (router_ref, one_ref, two_ref)]
    used = sum(part.shape[0] for part in top)
    free = slab_ref.shape[1] - 3 * local
    tail = jnp.concatenate(top + [jnp.zeros((free - used, rows), F32)], axis=0)
    tail = jnp.concatenate([tail, jnp.zeros((free, LANES - rows), F32)], axis=1)
    slab_ref[:, 3 * local :] = tail.T[:rows].astype(BF)


def pack_slab(me, w_query, w_key, w_value, w_router, gain_attn, gain_moe, spans, head):
    rows, width = w_query.shape
    columns = 3 * width // spans + w_router.shape[1] + 2
    columns += -columns % LANES
    return pl.pallas_call(
        functools.partial(pack_kernel, spans, head),
        in_specs=[pl.BlockSpec(memory_space=pltpu.SMEM)]
        + [pl.BlockSpec(memory_space=pltpu.VMEM)] * 6,
        out_specs=pl.BlockSpec(memory_space=pltpu.VMEM),
        out_shape=jax.ShapeDtypeStruct((rows, columns), BF),
        name="pack_slab",
    )(me, w_query, w_key, w_value, w_router.T, gain_attn[None], gain_moe[None])


def share_kernel(spans, me_ref, slab_ref, *refs):
    grad_refs, out_refs = refs[:-spans], refs[-spans:]
    for mask in range(spans):
        grads = jnp.concatenate([ref[mask] for ref in grad_refs], axis=0)
        out_refs[mask][...] = contract(grads, slab_ref[:, : grads.shape[0]], 0, 1).astype(BF)


def share_rows(me, slab, grads):
    spans, _, span = grads[0].shape
    vmem = pl.BlockSpec(memory_space=pltpu.VMEM)
    return pl.pallas_call(
        functools.partial(share_kernel, spans),
        in_specs=[pl.BlockSpec(memory_space=pltpu.SMEM)] + [vmem] * (1 + len(grads)),
        out_specs=[vmem] * spans,
        out_shape=[jax.ShapeDtypeStruct((span, slab.shape[0]), BF)] * spans,
        compiler_params=pltpu.CompilerParams(vmem_limit_bytes=50 * 2**20),
        name="share_rows",
    )(me, slab, *grads)


def out_kernel(x_ref, gain_ref, grads_ref, *refs):
    share_refs, out_ref = refs[:-1], refs[-1]
    dn = sum(ref[...].astype(F32) for ref in share_refs)
    x = x_ref[...].astype(F32)
    scale = lax.rsqrt(jnp.mean(x * x, axis=1, keepdims=True) + EPS)
    normed = x * scale
    scaled = dn * gain_ref[...]
    out_ref[...] = grads_ref[...] + scale * (
        scaled - normed * jnp.mean(scaled * normed, axis=1, keepdims=True)
    )


def rows_out(x, gain, grads, shares):
    span, width = x.shape
    part = span // 4
    rows = pl.BlockSpec((part, width), lambda i: (i, 0))
    return pl.pallas_call(
        out_kernel,
        grid=(4,),
        in_specs=[rows, pl.BlockSpec((1, width), lambda i: (0, 0)), rows] + [rows] * len(shares),
        out_specs=rows,
        out_shape=jax.ShapeDtypeStruct(x.shape, F32),
        compiler_params=pltpu.CompilerParams(vmem_limit_bytes=50 * 2**20),
        cost_estimate=pl.CostEstimate(flops=0, bytes_accessed=32 * 2**20, transcendentals=0),
        name="rows_out",
    )(x, gain, grads, *shares)


def project_kernel(wide, pieces, count_old, at_ref, *refs):
    x_refs, slab_ref, gain_ref, refs = refs[:pieces], refs[pieces], refs[pieces + 1], refs[pieces + 2 :]
    if len(refs) == count_old + 5:
        in_ref, w_ref = refs[0], refs[1]
        packed_ref = refs[-1]
        refs = refs[2:-1]
        width, quarter = in_ref.shape
        packed_ref[:width, :] = in_ref[...]
        for at in range(0, width, quarter):
            packed_ref[width + at : width + at + quarter, :] = w_ref[:, at : at + quarter]
    n1_ref, qkv_ref = refs[count_old:]
    x = jnp.concatenate([ref[...].astype(F32) for ref in x_refs], axis=0)
    scale = lax.rsqrt(jnp.mean(x * x, axis=1, keepdims=True) + EPS)
    n1 = (x * scale * gain_ref[...]).astype(BF)
    n1_ref[...] = n1
    qkv_ref[...] = contract(slab_ref[:, :wide], n1, 0, 1).astype(BF)


def project(at, rows, slab, gain, wide, spans, old, expert=()):
    width = rows[0].shape[1]
    span = sum(piece.shape[0] for piece in rows)
    packed = [jax.ShapeDtypeStruct((2 * width, array.shape[1]), BF) for array in expert[:1]]
    first = 3 + len(rows) + len(expert)

    def whole(array):
        return pl.BlockSpec(array.shape, lambda i, at: (0, 0))

    return pl.pallas_call(
        functools.partial(project_kernel, wide, len(rows), len(old)),
        grid_spec=pltpu.PrefetchScalarGridSpec(
            num_scalar_prefetch=1,
            grid=(1,),
            in_specs=[whole(array) for array in (*rows, slab, gain, *expert)]
            + [pl.BlockSpec(memory_space=pl.ANY)] * len(old),
            out_specs=[
                pl.BlockSpec((span, width), lambda i, at: (at[0], 0)),
                pl.BlockSpec((wide, span), lambda i, at: (0, at[0])),
            ]
            + [whole(array) for array in packed],
        ),
        out_shape=[
            jax.ShapeDtypeStruct((spans * span, width), BF),
            jax.ShapeDtypeStruct((wide, spans * span), BF),
        ]
        + packed,
        input_output_aliases={first + index: index for index in range(len(old))},
        compiler_params=pltpu.CompilerParams(vmem_limit_bytes=40 * 2**20),
        name="project",
    )(at, *rows, slab, gain, *expert, *old)


def place_of(slot_ref, part, part_rows):
    slots = lax.broadcasted_iota(jnp.int32, (part_rows, slot_ref.shape[1]), 0) + part * part_rows
    return jnp.where(slots == slot_ref[...], 1.0, 0.0).astype(BF)


def normed_rows(hidden, gain):
    scale = lax.rsqrt(jnp.mean(hidden * hidden, axis=1, keepdims=True) + EPS)
    normed = hidden * scale
    return scale, normed, (normed * gain).astype(BF)


def router_probs(rows, router, experts):
    logits = contract(rows, router, 1, 0)
    lane = lax.broadcasted_iota(jnp.int32, logits.shape, 1)
    logits = jnp.where(lane < experts, logits, -BIG)
    shifted = jnp.exp(logits - jnp.max(logits, axis=1, keepdims=True))
    return shifted / jnp.sum(shifted, axis=1, keepdims=True)


def slots_kernel(rows_ref, slot_ref, *part_refs):
    for part, ref in enumerate(part_refs):
        ref[...] = contract(place_of(slot_ref, part, ref.shape[0]), rows_ref[...], 1, 0).astype(BF)


def into_slots(rows, slot, parts, part_rows):
    vmem = pl.BlockSpec(memory_space=pltpu.VMEM)
    return pl.pallas_call(
        slots_kernel,
        in_specs=[vmem] * 2,
        out_specs=[vmem] * parts,
        out_shape=[jax.ShapeDtypeStruct((part_rows, rows.shape[1]), BF)] * parts,
        name="into_slots",
    )(rows, slot)


def into_kernel(parts, x_ref, mixed_ref, top_ref, low_ref, gain_ref, slot_ref, hidden_ref, *part_refs):
    out_ref = part_refs[-1]
    half, columns = top_ref.shape[1:]
    for begin, ref in ((0, top_ref), (half, low_ref)):
        for core in range(2):
            out_ref[begin : begin + half, core * columns : (core + 1) * columns] = ref[core]
    hidden = x_ref[...].astype(F32) + contract(mixed_ref[...], out_ref[...], 0, 0)
    hidden_ref[...] = hidden
    _, _, n2 = normed_rows(hidden, gain_ref[...])
    for part in range(parts):
        rows = part_refs[part].shape[0]
        part_refs[part][...] = contract(place_of(slot_ref, part, rows), n2, 1, 0).astype(BF)


def rows_into_experts(x, mixed, output_halves, gain, slot, parts, part_rows):
    span, width = x.shape
    if len(output_halves) == 1:
        blocks = output_halves[0].reshape(2, width // 2, 2, width // 2).transpose(0, 2, 1, 3)
        output_halves = [blocks[0], blocks[1]]
    vmem = pl.BlockSpec(memory_space=pltpu.VMEM)
    return pl.pallas_call(
        functools.partial(into_kernel, parts),
        in_specs=[vmem] * 6,
        out_specs=[vmem] * (2 + parts),
        out_shape=[jax.ShapeDtypeStruct((span, width), F32)]
        + [jax.ShapeDtypeStruct((part_rows, width), BF)] * parts
        + [jax.ShapeDtypeStruct((width, width), BF)],
        compiler_params=pltpu.CompilerParams(vmem_limit_bytes=50 * 2**20),
        name="rows_into_experts",
    )(x, mixed, *output_halves, gain, slot)


def back_kernel(hidden_ref, up_ref, out_ref, gain_ref, slot_ref, *refs):
    part_refs = refs[:-3]
    grads_ref, do_ref, grad_gain_ref = refs[-3:]
    dn = None
    for part, part_ref in enumerate(part_refs):
        rows = contract(place_of(slot_ref, part, part_ref.shape[0]), part_ref[...], 0, 0)
        dn = rows if dn is None else dn + rows
    gain = gain_ref[...]
    scale, normed, _ = normed_rows(hidden_ref[...], gain)
    grad_gain_ref[...] = jnp.sum(dn * normed, axis=0, keepdims=True)
    scaled = dn * gain
    grads = up_ref[...].astype(F32) + scale * (
        scaled - normed * jnp.mean(scaled * normed, axis=1, keepdims=True)
    )
    grads_ref[...] = grads
    do_ref[...] = contract(out_ref[...], grads.astype(BF), 1, 1).astype(BF)


def rows_from_experts(hidden, upstream, full_output, gain, slot, back):
    span, width = hidden.shape
    vmem = pl.BlockSpec(memory_space=pltpu.VMEM)
    return pl.pallas_call(
        back_kernel,
        in_specs=[vmem] * (5 + len(back)),
        out_specs=[vmem] * 3,
        out_shape=[
            jax.ShapeDtypeStruct((span, width), F32),
            jax.ShapeDtypeStruct((width, span), BF),
            jax.ShapeDtypeStruct((1, width), F32),
        ],
        compiler_params=pltpu.CompilerParams(vmem_limit_bytes=50 * 2**20),
        name="rows_from_experts",
    )(hidden, upstream, full_output, gain, slot, *back)


def early_kernel(experts, spans, grads_ref, mixed_ref, router_ref, gain_ref, early_ref):
    grad_output = contract(mixed_ref[...], grads_ref[...].astype(BF), 1, 0)
    width = grad_output.shape[1]
    local = width // spans
    share = experts // spans
    column = jnp.broadcast_to(gain_ref[...], (8, width)).T[:, :1]
    free = early_ref.shape[2] - local - share - 1
    grad_router = router_ref[...]
    for span in range(spans):
        early_ref[span] = jnp.concatenate(
            [
                grad_output[:, span * local : (span + 1) * local],
                grad_router[:, span * share : (span + 1) * share],
                column,
                jnp.zeros((width, free), F32),
            ],
            axis=1,
        ).astype(BF)


def early_sums(grads, mixed, grad_router, grad_gain, experts, spans):
    width = grads.shape[1]
    columns = width // spans + experts // spans + 1
    columns += -columns % LANES
    vmem = pl.BlockSpec(memory_space=pltpu.VMEM)
    return pl.pallas_call(
        functools.partial(early_kernel, experts, spans),
        in_specs=[vmem] * 4,
        out_specs=vmem,
        out_shape=jax.ShapeDtypeStruct((spans, width, columns), BF),
        compiler_params=pltpu.CompilerParams(vmem_limit_bytes=50 * 2**20),
        name="early_sums",
    )(grads, mixed, grad_router, grad_gain)


def sums_kernel(heads, buckets, at, fsdp_count, weights_ref, early_ref, dist_ref, bucket_ref, out_ref):
    width = weights_ref.shape[0]
    columns = weights_ref.shape[1]
    early = early_ref[0].astype(F32)
    for span in range(1, early_ref.shape[0]):
        early = early + early_ref[span].astype(F32)
    index = lax.broadcasted_iota(jnp.int32, (buckets, bucket_ref.shape[1]), 0)
    onehot = jnp.where(index == bucket_ref[...], 1.0, 0.0)
    dist = jnp.concatenate([dist_ref[head] for head in range(heads)], axis=0)
    dist = jnp.concatenate([dist, jnp.zeros((8 - heads, dist.shape[1]), F32)], axis=0)
    rel = lax.dot_general(
        dist, onehot, (((1,), (1,)), ((), ())), precision=HIGH, preferred_element_type=F32
    )
    last = lax.broadcasted_iota(jnp.int32, rel.shape, 1) == buckets - 1
    rel = jnp.where(last, 0.0, rel)
    rel = jnp.where(last, -jnp.sum(rel, axis=1, keepdims=True), rel)
    rows_here = width // fsdp_count
    if heads * buckets == rows_here:
        column = jnp.concatenate([rel.T[:, head : head + 1] for head in range(heads)], axis=0)
        column = jnp.concatenate([column] * fsdp_count, axis=0)
        lane = lax.broadcasted_iota(jnp.int32, early.shape, 1)
        early = jnp.where(lane == at, column, early)
    out_ref[:, :columns] = weights_ref[...]
    out_ref[:, columns:] = early.astype(BF)


def all_sums(weight_grads, early, distances, bucket, buckets, at, fsdp_count):
    width, columns = weight_grads.shape
    vmem = pl.BlockSpec(memory_space=pltpu.VMEM)
    return pl.pallas_call(
        functools.partial(sums_kernel, distances.shape[0], buckets, at, fsdp_count),
        in_specs=[vmem] * 4,
        out_specs=vmem,
        out_shape=jax.ShapeDtypeStruct((width, columns + early.shape[2]), BF),
        compiler_params=pltpu.CompilerParams(vmem_limit_bytes=50 * 2**20),
        name="all_sums",
    )(weight_grads, early, distances, bucket)


def final_kernel(experts, hidden_ref, gain_ref, router_ref, chosen_ref, slot_ref, *refs):
    part_refs, output_ref = refs[:-1], refs[-1]
    hidden = hidden_ref[...]
    _, _, n2 = normed_rows(hidden, gain_ref[...])
    probs = router_probs(n2, router_ref[...], experts)
    gate = jnp.sum(probs * chosen_ref[...], axis=1, keepdims=True)
    y = None
    for part, part_ref in enumerate(part_refs):
        rows = contract(place_of(slot_ref, part, part_ref.shape[0]), part_ref[...], 0, 0)
        y = rows if y is None else y + rows
    output_ref[...] = (hidden + gate * y).astype(BF)


def final_output(hidden, gain, router, chosen, slot, parts, experts):
    vmem = pl.BlockSpec(memory_space=pltpu.VMEM)
    return pl.pallas_call(
        functools.partial(final_kernel, experts),
        in_specs=[vmem] * (5 + len(parts)),
        out_specs=vmem,
        out_shape=jax.ShapeDtypeStruct(hidden.shape, BF),
        compiler_params=pltpu.CompilerParams(vmem_limit_bytes=50 * 2**20),
        name="final_output",
    )(hidden, gain, router, chosen, slot, *parts)


def expert_kernel(experts, inputs, count_old, me_ref, core_ref, router_ref, *refs):
    x_refs, up_refs = refs[:inputs], refs[inputs : 2 * inputs]
    own_hbm, near_hbm, far_hbm, in_hbm, out_hbm = refs[2 * inputs : 2 * inputs + 5]
    refs = refs[2 * inputs + 5 + count_old :]
    ours_ref, theirs_ref, act_ref, pre_ref, dy_ref, w_ref, y_sum, dn_sum, sems = refs
    count, width = x_refs[0].shape
    rows = count // 2
    quarter = w_ref.shape[2]
    first = core_ref[0] == 0
    part, pair = pl.program_id(0), pl.program_id(1)
    copies = [
        [
            pltpu.make_async_copy(own_hbm, w_ref.at[0], sems.at[0]),
            pltpu.make_async_copy(near_hbm, w_ref.at[1], sems.at[1]),
        ],
        [
            pltpu.make_async_copy(far_hbm, w_ref.at[2], sems.at[2]),
            pltpu.make_async_copy(in_hbm, w_ref.at[3, pl.ds(0, width)], sems.at[3]),
            pltpu.make_async_copy(out_hbm, w_ref.at[3, pl.ds(width, width)], sems.at[4]),
        ],
    ]

    @pl.when((part == 0) & (pair == 0))
    def _():
        for copy in copies[0] + copies[1]:
            copy.start()

    def parted(index):
        x = x_refs[index][...]

        @pl.when(pair == 0)
        def _():
            probs = router_probs(x, router_ref[...], experts)
            lane = lax.broadcasted_iota(jnp.int32, probs.shape, 1)
            gate = jnp.sum(jnp.where(lane == me_ref[0], probs, 0.0), axis=1, keepdims=True)
            dy_ref[...] = (gate * up_refs[index][...].astype(F32)).astype(BF)

        def blocks(half):
            if index == 0:
                for copy in copies[half]:
                    copy.wait()
            w_in = jnp.concatenate([w_ref[2 * half + b, :width, :] for b in range(2)], axis=1)
            w_out = jnp.concatenate(
                [
                    jnp.concatenate(
                        [
                            w_ref[2 * half + b, at : at + quarter, :]
                            for at in range(width, 2 * width, quarter)
                        ],
                        axis=1,
                    )
                    for b in range(2)
                ],
                axis=0,
            )
            pre = contract(x, w_in, 1, 0)
            root = 0.7978845608028654
            square = pre * pre
            tanh = jnp.tanh(pre * (root + (root * 0.044715) * square))
            upper = 0.5 + 0.5 * tanh
            act = (pre * upper).astype(BF)
            slope = upper + (pre * upper) * (1.0 - tanh) * (root + (root * 0.134145) * square)
            act_ref[...] = act
            pre_grads = (contract(dy_ref[...], w_out, 1, 1) * slope).astype(BF)
            pre_ref[...] = pre_grads
            y = contract(act, w_out, 1, 0)
            dn = contract(pre_grads, w_in, 1, 1)
            if half == 0:
                y_sum[...] = y
                dn_sum[...] = dn
                return
            for some, total in (
                (slice(0, rows), y_sum[...] + y),
                (slice(rows, count), dn_sum[...] + dn),
            ):
                one, two = total[:rows], total[rows:]
                ours_ref[0, some, :] = jnp.where(first, one, two).astype(BF)
                theirs_ref[0, some, :] = jnp.where(first, two, one).astype(BF)

        for half in range(2):
            pl.when(pair == half)(functools.partial(blocks, half))

    for index in range(inputs):
        pl.when(part == index)(functools.partial(parted, index))


def expert_part(part, parts, me, core, rows, upstream, router, weights, old, experts):
    inputs = len(rows)
    count, width = rows[0].shape
    quarter = weights[0].shape[1]
    hidden = 4 * quarter
    total = count * inputs * parts
    begin = part * inputs
    first = 3 + 2 * inputs + len(weights)
    smem = pl.BlockSpec(memory_space=pltpu.SMEM)
    hbm = pl.BlockSpec(memory_space=pl.ANY)
    share = pl.BlockSpec((1, count, width), lambda i, j: (i, 0, 0))
    inner = pl.BlockSpec((count, 2 * quarter), lambda i, j: (begin + i, j))
    return pl.pallas_call(
        functools.partial(expert_kernel, experts, inputs, len(old)),
        grid=(inputs, 2),
        in_specs=[smem] * 2
        + [
            pl.BlockSpec(array.shape, lambda i, j: (0, 0))
            for array in (router, *rows, *upstream)
        ]
        + [hbm] * (len(weights) + len(old)),
        out_specs=[share] * 2
        + [inner] * 2
        + [pl.BlockSpec((count, width), lambda i, j: (begin + i, 0))],
        out_shape=[jax.ShapeDtypeStruct((inputs, count, width), BF)] * 2
        + [jax.ShapeDtypeStruct((total, size), BF) for size in (hidden, hidden, width)],
        scratch_shapes=[
            pltpu.VMEM((4, 2 * width, quarter), BF),
            pltpu.VMEM((count, width), F32),
            pltpu.VMEM((count, width), F32),
            pltpu.SemaphoreType.DMA((5,)),
        ],
        input_output_aliases={first + index: 2 + index for index in range(len(old))},
        compiler_params=pltpu.CompilerParams(vmem_limit_bytes=56 * 2**20),
        name="expert_part",
    )(me, core, router, *rows, *upstream, *weights, *old)


def combine_kernel(inputs, experts, me_ref, core_ref, ours_ref, theirs_ref, router_ref, *refs):
    x_refs, up_refs, refs = refs[:inputs], refs[inputs : 2 * inputs], refs[2 * inputs :]
    y_refs, dn_refs, grad_ref = refs[:inputs], refs[inputs : 2 * inputs], refs[-1]
    rows = y_refs[0].shape[0]
    router = router_ref[...]
    mine = pl.ds(pl.multiple_of(core_ref[0] * rows, 16), rows)
    grad_router = None
    for index in range(inputs):
        x = x_refs[index][mine, :]
        y = ours_ref[index, :rows, :].astype(F32) + theirs_ref[index, :rows, :].astype(F32)
        dn = ours_ref[index, rows:, :].astype(F32) + theirs_ref[index, rows:, :].astype(F32)
        probs = router_probs(x, router, experts)
        lane = lax.broadcasted_iota(jnp.int32, probs.shape, 1)
        chosen = jnp.where(lane == me_ref[0], 1.0, 0.0)
        gate = jnp.sum(probs * chosen, axis=1, keepdims=True)
        gate_grads = jnp.sum(up_refs[index][mine, :].astype(F32) * y, axis=1, keepdims=True)
        logit_grads = (probs * (chosen * gate_grads - gate * gate_grads)).astype(BF)
        product = contract(x, logit_grads, 0, 0)
        grad_router = product if grad_router is None else grad_router + product
        y_refs[index][...] = y.astype(BF)
        dn_refs[index][...] = (dn + contract(logit_grads, router, 1, 1)).astype(BF)
    grad_ref[...] = grad_router


def combine_halves(me, core, ours, theirs, router, rows, upstream, experts):
    inputs, count, width = ours.shape
    smem = pl.BlockSpec(memory_space=pltpu.SMEM)
    vmem = pl.BlockSpec(memory_space=pltpu.VMEM)
    results = pl.pallas_call(
        functools.partial(combine_kernel, inputs, experts),
        in_specs=[smem, smem] + [vmem] * (3 + 2 * inputs),
        out_specs=[vmem] * (2 * inputs + 1),
        out_shape=[jax.ShapeDtypeStruct((count // 2, width), BF)] * (2 * inputs)
        + [jax.ShapeDtypeStruct(router.shape, F32)],
        compiler_params=pltpu.CompilerParams(vmem_limit_bytes=50 * 2**20),
        name="combine_halves",
    )(me, core, ours, theirs, router, *rows, *upstream)
    return results[:inputs], results[inputs : 2 * inputs], results[-1]


def expert_grads_kernel(act_ref, pre_ref, dy_ref, *refs):
    x_refs = refs[:-4]
    one_ref, two_ref, keep_one, keep_two = refs[-4:]
    width = dy_ref.shape[1]
    quarter = act_ref.shape[1]
    mask = pl.program_id(0)
    rows = jnp.concatenate([ref[...] for ref in x_refs], axis=0)
    grad_in = contract(rows, pre_ref[...], 0, 0)
    grad_out = contract(act_ref[...], dy_ref[...], 0, 0)
    grad_out = jnp.concatenate(
        [grad_out[:, at : at + quarter] for at in range(0, width, quarter)], axis=0
    )
    for at in (1, 3):

        @pl.when(mask == at)
        def _():
            one_ref[0] = grad_in.astype(BF)

    for at in (2, 3):

        @pl.when(mask == at)
        def _():
            two_ref[0] = grad_out.astype(BF)

    for at in (0, 2):

        @pl.when(mask == at)
        def _():
            keep_one[0] = grad_in

    for at in (0, 1):

        @pl.when(mask == at)
        def _():
            keep_two[0] = grad_out


def expert_grads(kept, rows, quarter):
    act, pre, dy = kept
    total, width = dy.shape
    hidden = pl.BlockSpec((total, quarter), lambda f: (0, f))

    def whole(array):
        return pl.BlockSpec(array.shape, lambda f: (0, 0))

    def block(place):
        return pl.BlockSpec((1, width, quarter), lambda f: (place(f), 0, 0))

    return pl.pallas_call(
        expert_grads_kernel,
        grid=(act.shape[1] // quarter,),
        in_specs=[hidden, hidden, whole(dy)] + [whole(part) for part in rows],
        out_specs=[
            block(lambda f: f // 2),
            block(lambda f: jnp.maximum(f - 2, 0)),
            block(lambda f: f // 2),
            block(lambda f: jnp.minimum(f, 1)),
        ],
        out_shape=[jax.ShapeDtypeStruct((2, width, quarter), BF)] * 2
        + [jax.ShapeDtypeStruct((2, width, quarter), F32)] * 2,
        compiler_params=pltpu.CompilerParams(vmem_limit_bytes=50 * 2**20),
        name="expert_grads",
    )(act, pre, dy, *rows)


def settle_kernel(keep_one, keep_two, got_one, got_two, one_ref, two_ref):
    one_ref[...] = (keep_one[0].astype(F32) + got_one[0].astype(F32)).astype(BF)
    two_ref[...] = (keep_two[0].astype(F32) + got_two[0].astype(F32)).astype(BF)


def settle_step(keep_one, keep_two, got_one, got_two):
    _, width, quarter = keep_one.shape
    second = pl.BlockSpec((1, width, quarter), lambda i: (1, 0, 0))
    whole = pl.BlockSpec((width, quarter), lambda i: (0, 0))
    return pl.pallas_call(
        settle_kernel,
        grid=(1,),
        in_specs=[second] * 4,
        out_specs=[whole] * 2,
        out_shape=[jax.ShapeDtypeStruct((width, quarter), BF)] * 2,
        compiler_params=pltpu.CompilerParams(vmem_limit_bytes=50 * 2**20),
        name="settle_step",
    )(keep_one, keep_two, got_one, got_two)


def all_to_all(blocks, axis, groups=None):
    return lax.all_to_all(
        blocks, axis, split_axis=0, concat_axis=0, tiled=True, axis_index_groups=groups
    )


def pair_swap(block, axis, mask):
    count = lax.axis_size(axis)
    return lax.ppermute(block, axis, [(i, i ^ mask) for i in range(count)])


def tied(values, *others):
    return lax.optimization_barrier((values, others))[0]


def gather_pairs(rows, axis, groups, pairs, after):
    count = lax.axis_size(axis)
    if count > 8:
        return [lax.all_gather(rows, axis, axis=0, tiled=True)]
    core = lax.axis_index(axis) % 2
    columns = rows.shape[1] // 2
    low, high = rows[:, :columns], rows[:, columns:]
    mine = jnp.where(core == 0, low, high)
    got = pair_swap(jnp.where(core == 0, high, low), axis, 1)
    chip = jnp.where(core == 0, jnp.stack([mine, got]), jnp.stack([got, mine]))
    whole = all_to_all(jnp.broadcast_to(chip[None], (count // 2,) + chip.shape), axis, groups)
    whole = tied(whole.reshape(2, count * rows.shape[0] // 2, columns), after)
    return [
        lax.all_gather(part, axis, axis=0, tiled=False, axis_index_groups=pairs) for part in whole
    ]


def per_device(
    tokens, cotangent, doc_starts, routes, bucket_table, w_query, w_key, w_value, w_output,
    w_router, gain_attn, gain_moe, rel_bias, expert_in, expert_out,
):
    _, span, width = tokens.shape
    seq_count = lax.axis_size("seq")
    fsdp_count = lax.axis_size("fsdp")
    seq_me = lax.axis_index("seq")
    fsdp_me = lax.axis_index("fsdp")
    heads, buckets = rel_bias.shape
    local = width // seq_count
    head = local // heads
    experts = w_router.shape[1]
    rows_here = w_query.shape[0]
    quarter = expert_in.shape[2]
    cores = 2
    groups = [list(range(core, fsdp_count, cores)) for core in range(cores)]
    x = tokens[0]
    seq_index = seq_me.astype(jnp.int32)[None]
    expert_index = (fsdp_me // cores).astype(jnp.int32)[None]
    core_index = (fsdp_me % cores).astype(jnp.int32)[None]

    near = pair_swap(x, "seq", 1)
    far = pair_swap(x, "seq", 2)
    slab = pack_slab(
        seq_index, w_query, w_key, w_value, w_router, gain_attn, gain_moe, seq_count, head
    )
    slab = lax.all_gather(slab, "fsdp", axis=0, tiled=True)
    half = span // 2
    slab, near_half, far_half = lax.optimization_barrier((slab, near[:half], far[half:]))
    across = [pair_swap(near_half, "seq", 2), pair_swap(far_half, "seq", 1)]
    tail = slab[:, 3 * local :]
    full_router = jnp.pad(tail[:, :experts], ((0, 0), (0, -experts % LANES)))
    gains = tail[:, experts : experts + 2].astype(F32).T
    gain_one, gain_two = gains[:1], gains[1:2]
    own_gain = gain_attn.astype(F32)

    expert_me = fsdp_me // cores
    few = experts <= 4
    route, bucket_table, rel_bias = tied((routes[0], bucket_table[:TILE], rel_bias), slab)
    chosen = (route[:, None] == jnp.arange(LANES, dtype=jnp.int32)[None, :]).astype(F32)
    before = (
        jnp.arange(span, dtype=jnp.int32)[:, None] > jnp.arange(span, dtype=jnp.int32)[None, :]
    ).astype(BF)
    ranks = jnp.dot(before, chosen.astype(BF), preferred_element_type=F32)
    capacity = max(2, 2 * span // experts)
    target = route ^ expert_me if few else route
    slot = target * capacity + jnp.sum(ranks * chosen, axis=1).astype(jnp.int32)
    slot = slot[None]
    part_count = 4
    part_rows = experts * capacity // part_count

    def exchange(parts):
        if few:
            return [parts[0]] + [
                pair_swap(parts[mask], "fsdp", cores * mask) for mask in range(1, part_count)
            ]
        blocks = jnp.concatenate(parts, axis=0).reshape(experts, capacity, width)
        blocks = all_to_all(blocks, "fsdp", groups).reshape(part_count, part_rows, width)
        return [blocks[part] for part in range(part_count)]

    old = ()
    for mask, part in enumerate((x, near, far)):
        old = project(
            (seq_me ^ mask).astype(jnp.int32)[None], (part,), slab, gain_one, 3 * local, seq_count, old,
            () if mask < 2 else (expert_in[0], expert_out[0]),
        )
    weights = tied(old[2], across)
    w_near = pair_swap(weights, "seq", 1)
    w_far = pair_swap(weights, "seq", 2)
    up_rows, old = lax.optimization_barrier((cotangent[0], old[:2]))
    w_output = tied(w_output, slab)
    upstream_parts = into_slots(up_rows, slot, part_count, part_rows)
    upstream_parts = exchange(upstream_parts)
    n1_all, qkv_t = project(
        (seq_me ^ 3).astype(jnp.int32)[None], across, slab, gain_one, 3 * local, seq_count, old,
    )
    rel = rel_bias.astype(F32)
    bucket = bucket_table[None]
    attended, lse = attend_forward(
        qkv_t, doc_starts, rel, bucket, heads, head, seq_count
    )
    mixed = all_to_all(attended, "seq").reshape(width, span)
    pairs = [list(range(at, at + cores)) for at in range(0, fsdp_count, cores)]
    output_halves = gather_pairs(w_output, "fsdp", groups, pairs, (attended, upstream_parts))

    def of_chip(rows):
        return lax.all_gather(rows, "fsdp", axis=0, tiled=True, axis_index_groups=pairs)

    mixed, output_halves, upstream_parts, w_near, w_far = lax.optimization_barrier(
        (mixed, output_halves, upstream_parts, w_near, w_far)
    )

    hidden, *parts, full_output = rows_into_experts(
        x, mixed, output_halves, gain_two, slot, part_count, part_rows
    )
    w_near, w_far, parts = lax.optimization_barrier((w_near, w_far, parts))
    w_across = [pair_swap(w_near[:width], "seq", 2), pair_swap(w_far[width:], "seq", 1)]
    weights = [weights, w_near, w_far] + w_across
    arrived = exchange(parts)
    kept = ()
    chip_rows, ys, back = [], [], []
    grad_router = None
    steps = part_count // 2
    for part in range(steps):
        some = slice(part * part_count // steps, (part + 1) * part_count // steps)
        rows, some_up = arrived[some], upstream_parts[some]
        some_up = [of_chip(one) for one in tied(some_up, kept if part else parts)]
        if part:
            rows, some_up = lax.optimization_barrier((rows, some_up))
        rows = [of_chip(one) for one in rows]
        chip_rows += rows
        ours, theirs, *kept = expert_part(
            part, steps, expert_index, core_index, rows, some_up, full_router, weights, kept,
            experts,
        )
        some_ys, dns, product = combine_halves(
            expert_index, core_index, ours, pair_swap(theirs, "fsdp", 1), full_router, rows,
            some_up, experts,
        )
        ys += some_ys
        back += dns
        grad_router = product if grad_router is None else grad_router + product
    kept = tied(kept, back)
    back = exchange(back)
    one, two, keep_one, keep_two = expert_grads(kept, chip_rows, quarter)
    back = tied(back, one, two)
    got_one = pair_swap(one, "seq", 1)
    got_two = pair_swap(two, "seq", 2)

    hidden_grads, mixed_grads, grad_gain = rows_from_experts(
        hidden, cotangent[0], full_output, gain_two, slot, back
    )
    ys = exchange(tied(ys, mixed_grads))
    early = early_sums(hidden_grads, mixed, grad_router, grad_gain, experts, seq_count)
    moved = all_to_all(mixed_grads.reshape(seq_count, local, span), "seq")
    settled_sum = [keep[0] + got[0].astype(F32) for keep, got in ((keep_one, got_one), (keep_two, got_two))]
    one, two = settle_step(keep_one, keep_two, got_one, got_two)
    got_one = pair_swap(one, "seq", 2)
    got_two = pair_swap(two, "seq", 1)
    early = all_to_all(tied(early, moved), "seq")
    head_grads, distances, weight_grads = attend_backward(
        0, heads, qkv_t, moved, attended, lse, doc_starts, seq_index,
        rel, bucket, n1_all, slab, heads, head,
    )
    head_grads, distances, weight_grads, got_one, got_two, ys = lax.optimization_barrier(
        (head_grads, distances, weight_grads, got_one, got_two, ys)
    )
    output = final_output(hidden, gain_two, full_router, chosen, slot, ys, experts)
    shares = share_rows(seq_index, slab, [head_grads])
    shares = [shares[0]] + [
        pair_swap(shares[mask], "seq", mask) for mask in range(1, seq_count)
    ]
    grad_expert_in, grad_expert_out = [
        total + got.astype(F32) for total, got in zip(settled_sum, (got_one, got_two))
    ]
    grad_expert_out = jnp.concatenate(
        [grad_expert_out[at : at + quarter] for at in range(0, width, quarter)], axis=1
    )
    input_grads = rows_out(x, gain_one, hidden_grads, shares)

    share = experts // seq_count
    rel_count = heads * buckets
    sums = all_sums(weight_grads, early, distances, bucket, buckets, local + share + 1, fsdp_count)
    columns = weight_grads.shape[1] // heads
    summed = all_to_all(sums.reshape(fsdp_count, rows_here, sums.shape[1]), "fsdp")
    summed = jnp.sum(summed.astype(F32), axis=0)
    by_head = [summed[:, at : at + columns] for at in range(0, heads * columns, columns)]
    summed = summed[:, heads * columns :]
    sum_gain_attn = sum(part[:, 3 * head] for part in by_head) / own_gain
    sum_gain_attn = sum_gain_attn + sum(
        pair_swap(sum_gain_attn, "seq", mask) for mask in range(1, seq_count)
    )
    if rows_here == rel_count:
        sum_rel = summed[:rel_count, local + share + 1].reshape(heads, buckets)
    else:
        onehot = bucket_table[:, None] == jnp.arange(buckets - 1, dtype=jnp.int32)[None, :]
        below = jnp.dot(distances[:, 0], onehot.astype(F32), precision=HIGH)
        grad_rel = jnp.concatenate([below, -jnp.sum(below, axis=1, keepdims=True)], axis=1)
        sum_rel = lax.psum(grad_rel, "fsdp")
    heads_sum = [
        jnp.concatenate([part[:, at : at + head] for part in by_head], axis=1)
        for at in range(0, 3 * head, head)
    ]
    return (
        output[None],
        input_grads[None],
        heads_sum[0],
        heads_sum[1],
        heads_sum[2],
        summed[:, :local],
        summed[:, local : local + share],
        sum_gain_attn,
        summed[:, local + share],
        sum_rel,
        grad_expert_in[None],
        grad_expert_out[None],
    )


def solution(mesh):
    rows = P("fsdp", "seq", None)
    weight = P("fsdp", None)
    shared = P("fsdp", "seq")
    return jax.shard_map(
        per_device,
        mesh=mesh,
        in_specs=(
            rows, rows, weight, shared, P(), weight, weight, weight, weight, weight,
            P("fsdp"), P("fsdp"), P("seq", None), P("fsdp", None, "seq"), rows,
        ),
        out_specs=(
            rows, rows, shared, shared, shared, shared, shared, P("fsdp"), P("fsdp"),
            P("seq", None), P("fsdp", None, "seq"), rows,
        ),
        check_vma=False,
    )
```

```python
import functools

import jax
import jax.numpy as jnp
from jax import lax
from jax.experimental import pallas as pl
from jax.experimental.pallas import tpu as pltpu
from jax.sharding import PartitionSpec as P

EPS = 1e-06
HIGH = lax.Precision.HIGHEST
BIG = 1e30
TILE = 256
LANES = 128
CHUNK = 1024
BF = jnp.bfloat16
F32 = jnp.float32


def contract(left, right, left_dim, right_dim):
    return lax.dot_general(
        left, right, (((left_dim,), (right_dim,)), ((), ())), preferred_element_type=F32
    )


def doc_rows(starts_ref, length, docs):
    pos = lax.broadcasted_iota(jnp.int32, (1, length), 1)
    doc = jnp.zeros((1, length), jnp.int32) - 1
    for index in range(docs):
        doc = doc + (starts_ref[0, index] <= pos).astype(jnp.int32)
    row = lax.broadcasted_iota(jnp.int32, (8, length), 0)
    same = row == doc
    return jnp.where(same, 1.0, 0.0), jnp.where(same, 0.0, jnp.where(row < docs, -BIG, 0.0))


def bias_circle(rel_ref, bucket_ref, head, tile):
    last = rel_ref.shape[1] - 1
    bucket = bucket_ref[...]
    row = jnp.zeros(bucket.shape, F32)
    for index in range(last):
        row = jnp.where(bucket == index, rel_ref[head, index] - rel_ref[head, last], row)
    return pltpu.roll(jnp.broadcast_to(row, (tile, tile)), 0, 1, stride=1, stride_axis=0)


def forward_kernel(
    head, tile, docs, starts_ref, rel_ref, bucket_ref, q_ref, k_ref, v_ref, o_ref, lse_ref,
    kaug, qaug, vaug, band, scores,
):
    length = q_ref.shape[1]
    span = o_ref.shape[2]
    doc_q, doc_k = doc_rows(starts_ref, length, docs)
    qaug[:head, :] = (q_ref[...].astype(F32) * 0.125).astype(BF)
    qaug[head : head + 16, :] = jnp.concatenate([doc_q, jnp.zeros((8, length), F32)], 0).astype(BF)
    qaug[head + 16 :, :] = jnp.zeros((qaug.shape[0] - head - 16, length), BF)
    tail = jnp.zeros((LANES - head - 8, tile), F32)
    for block in range(length // tile):
        cols = slice(block * tile, (block + 1) * tile)
        full = jnp.concatenate([k_ref[:, cols].astype(F32), doc_k[:, cols], tail], 0)
        kaug[cols, :] = full.T.astype(BF)
    vaug[:head, :] = v_ref[...]
    extra = lax.broadcasted_iota(jnp.int32, (vaug.shape[0] - head, length), 0)
    vaug[head:, :] = jnp.where(extra == 0, 1.0, 0.0).astype(BF)
    circle = bias_circle(rel_ref, bucket_ref, pl.program_id(0), tile)
    key_row = lax.broadcasted_iota(jnp.int32, (tile, tile), 0)
    query_col = lax.broadcasted_iota(jnp.int32, (tile, tile), 1)
    band[:tile, :] = jnp.where(key_row > query_col, circle, 0.0)
    band[tile:, :] = jnp.where(key_row <= query_col, circle, -BIG)
    for i in range(length // tile):
        cols = slice(i * tile, (i + 1) * tile)
        queries = qaug[:, cols]
        peak = None
        for j in range(i + 1):
            rows = slice(j * tile, (j + 1) * tile)
            part = contract(kaug[rows, :], queries, 1, 0)
            if j == i:
                part = part + band[tile:, :]
            elif j == i - 1:
                part = part + band[:tile, :]
            scores[rows, :] = part
            most = jnp.max(part.reshape(tile // 8, 8, tile), axis=0)
            peak = most if peak is None else jnp.maximum(peak, most)
        peak = jnp.max(peak, axis=0, keepdims=True)
        summed = jnp.zeros((vaug.shape[0], tile), F32)
        for j in range(i + 1):
            rows = slice(j * tile, (j + 1) * tile)
            expons = jnp.exp(scores[rows, :] - peak).astype(BF)
            summed = summed + contract(vaug[:, rows], expons, 1, 0)
        total = summed[head : head + 1, :]
        start = (i * tile) % span
        o_ref[i * tile // span, :, start : start + tile] = (summed[:head, :] / total).astype(BF)
        lse_ref[0, :, cols] = peak + jnp.log(total)


def attend_forward(qkv_t, starts, rel, bucket, heads, head, spans):
    length = qkv_t.shape[1]
    docs = starts.shape[1]
    span = length // spans

    def rows_of(part):
        return pl.BlockSpec((head, length), lambda h: (3 * h + part, 0))

    return pl.pallas_call(
        functools.partial(forward_kernel, head, TILE, docs),
        grid=(heads,),
        in_specs=[
            pl.BlockSpec(memory_space=pltpu.SMEM),
            pl.BlockSpec(memory_space=pltpu.SMEM),
            pl.BlockSpec((1, TILE), lambda h: (0, 0)),
            rows_of(0),
            rows_of(1),
            rows_of(2),
        ],
        out_specs=[
            pl.BlockSpec((spans, head, span), lambda h: (0, h, 0)),
            pl.BlockSpec((1, 1, length), lambda h: (h, 0, 0)),
        ],
        out_shape=[
            jax.ShapeDtypeStruct((spans, heads * head, span), BF),
            jax.ShapeDtypeStruct((heads, 1, length), F32),
        ],
        scratch_shapes=[
            pltpu.VMEM((length, LANES), BF),
            pltpu.VMEM((LANES, length), BF),
            pltpu.VMEM((head + 16, length), BF),
            pltpu.VMEM((2 * TILE, TILE), F32),
            pltpu.VMEM((length, TILE), F32),
        ],
        compiler_params=pltpu.CompilerParams(vmem_limit_bytes=40 * 2**20),
        name="attend_forward",
    )(starts, rel, bucket, qkv_t, qkv_t, qkv_t)


def backward_kernel(
    count, head, offset, tile, docs, starts_ref, me_ref, rel_ref, bucket_ref, q_ref, k_ref, v_ref, do_ref, o_ref,
    lse_ref, n1_ref, slab_ref, grads_ref, dist_ref, weight_ref, qaug, doaug, kaug, vaug, scaled,
    band, dq_sum, diagonal, grads, upstream_all,
):
    length = q_ref.shape[1]
    span = o_ref.shape[2]
    doc_q, doc_k = doc_rows(starts_ref, length, docs)
    sub = lax.broadcasted_iota(jnp.int32, (8, tile), 0)

    def minus_split(row):
        row = -row
        high = row.astype(BF).astype(F32)
        rest = row - high
        mid = rest.astype(BF).astype(F32)
        return jnp.where(
            sub == 0, high, jnp.where(sub == 1, mid, jnp.where(sub == 2, rest - mid, 0.0))
        )

    ones3 = jnp.where(lax.broadcasted_iota(jnp.int32, (8, length), 0) < 3, 1.0, 0.0)
    zeros8 = jnp.zeros((8, length), F32)
    blocks = length // tile
    tail = jnp.zeros((LANES - head - 16, tile), F32)
    for block in range(blocks):
        cols = slice(block * tile, (block + 1) * tile)
        begin = (block * tile) % span
        inner = slice(begin, begin + tile)
        upstream_all[:, cols] = do_ref[block * tile // span, :, inner]
        upstream = do_ref[block * tile // span, :, inner].astype(F32)
        attended = o_ref[block * tile // span, :, inner].astype(F32)
        centre = jnp.sum(upstream * attended, axis=0, keepdims=True)
        query = q_ref[:, cols].astype(F32) * 0.125
        scaled[:, cols] = query.astype(BF)
        full = jnp.concatenate([query, doc_q[:, cols], minus_split(lse_ref[0, :, cols]), tail], 0)
        qaug[cols, :] = full.T.astype(BF)
        full = jnp.concatenate([upstream, minus_split(centre), zeros8[:, cols], tail], 0)
        doaug[cols, :] = full.T.astype(BF)
    kaug[:head, :] = k_ref[...]
    kaug[head : head + 16, :] = jnp.concatenate([doc_k, ones3], 0).astype(BF)
    kaug[head + 16 :, :] = jnp.zeros((LANES - head - 16, length), BF)
    vaug[:head, :] = v_ref[...]
    vaug[head : head + 16, :] = jnp.concatenate([ones3, zeros8], 0).astype(BF)
    vaug[head + 16 :, :] = jnp.zeros((LANES - head - 16, length), BF)
    circle = bias_circle(rel_ref, bucket_ref, pl.program_id(0) + offset // (3 * head), tile).T
    query_row = lax.broadcasted_iota(jnp.int32, (tile, tile), 0)
    key_col = lax.broadcasted_iota(jnp.int32, (tile, tile), 1)
    band[:tile, :] = jnp.where(key_col <= query_row, circle, -BIG)
    band[tile:, :] = jnp.where(key_col > query_row, circle, 0.0)
    diagonal[...] = jnp.zeros_like(diagonal)
    for j in range(blocks):
        keys = slice(j * tile, (j + 1) * tile)
        dk = jnp.zeros((head, tile), F32)
        dv = jnp.zeros((head, tile), F32)
        at = j * tile
        while at < length:
            end = min(length, (at // CHUNK + 1) * CHUNK)
            rows = slice(at, end)
            part = contract(qaug[rows, :], kaug[:, keys], 1, 0)
            near = max(0, min(end, (j + 2) * tile) - at)
            if near:
                top = at - j * tile
                part = jnp.concatenate(
                    [part[:near] + band[top : top + near, :]] + ([part[near:]] if at + near < end else []),
                    axis=0,
                )
            probs = jnp.exp(part)
            score_grads = probs * contract(doaug[rows, :], vaug[:, keys], 1, 0)
            if at == j * tile:
                diagonal[...] += score_grads[:tile]
            if at <= (j + 1) * tile < end:
                begin = (j + 1) * tile - at
                diagonal[...] += jnp.where(
                    key_col > query_row, score_grads[begin : begin + tile], 0.0
                )
            weights = probs.astype(BF)
            short = score_grads.astype(BF)
            dv = dv + contract(upstream_all[:, rows], weights, 1, 0)
            dk = dk + contract(scaled[:, rows], short, 1, 0)
            dq = contract(kaug[:head, keys], short, 1, 1)
            if j == 0:
                dq_sum[:, rows] = dq
            else:
                dq_sum[:, rows] += dq
            at = end
        begin = (j * tile) % span
        inner = slice(begin, begin + tile)
        together = jnp.concatenate([dq_sum[:, keys] * 0.125, dk, dv], axis=0).astype(BF)
        grads[:, keys] = together
        grads_ref[(j * tile // span) ^ me_ref[0], :, inner] = together
    products = contract(grads[...], n1_ref[...], 1, 0).T
    own = slab_ref[:, offset : offset + 3 * head]
    for later in range(1, count):
        begin = offset + 3 * head * later
        own = jnp.where(pl.program_id(0) == later, slab_ref[:, begin : begin + 3 * head], own)
    share = jnp.sum(products * own.astype(F32), axis=1, keepdims=True)
    rows, columns = weight_ref.shape
    weight_ref[...] = jnp.concatenate(
        [products, share, jnp.zeros((rows, columns - 3 * head - 1), F32)], axis=1
    ).astype(BF)
    skew = diagonal[...].T
    step = 1
    while step < tile:
        skew = jnp.where((query_row & step) != 0, pltpu.roll(skew, tile - step, 1), skew)
        step *= 2
    dist_ref[0] = jnp.sum(skew, axis=0, keepdims=True)


def attend_backward(
    first, count, qkv_t, upstream, attended, lse, starts, me, rel, bucket, n1, slab, heads, head
):
    length = qkv_t.shape[1]
    docs = starts.shape[1]
    spans, _, span = attended.shape
    width = n1.shape[1]

    def rows_of(part):
        return pl.BlockSpec((head, length), lambda h: (3 * (first + h) + part, 0))

    by_span = pl.BlockSpec((spans, head, span), lambda h: (0, first + h, 0))
    smem = pl.BlockSpec(memory_space=pltpu.SMEM)
    columns = 3 * head + 1
    columns += -columns % LANES
    return pl.pallas_call(
        functools.partial(backward_kernel, count, head, 3 * first * head, TILE, docs),
        grid=(count,),
        in_specs=[
            smem,
            smem,
            smem,
            pl.BlockSpec((1, TILE), lambda h: (0, 0)),
            rows_of(0),
            rows_of(1),
            rows_of(2),
            by_span,
            by_span,
            pl.BlockSpec((1, 1, length), lambda h: (first + h, 0, 0)),
            pl.BlockSpec(n1.shape, lambda h: (0, 0)),
            pl.BlockSpec(slab.shape, lambda h: (0, 0)),
        ],
        out_specs=[
            pl.BlockSpec((spans, 3 * head, span), lambda h: (0, h, 0)),
            pl.BlockSpec((1, 1, TILE), lambda h: (h, 0, 0)),
            pl.BlockSpec((width, columns), lambda h: (0, h)),
        ],
        out_shape=[
            jax.ShapeDtypeStruct((spans, count * 3 * head, span), BF),
            jax.ShapeDtypeStruct((count, 1, TILE), F32),
            jax.ShapeDtypeStruct((width, count * columns), BF),
        ],
        scratch_shapes=[
            pltpu.VMEM((length, LANES), BF),
            pltpu.VMEM((length, LANES), BF),
            pltpu.VMEM((LANES, length), BF),
            pltpu.VMEM((LANES, length), BF),
            pltpu.VMEM((head, length), BF),
            pltpu.VMEM((2 * TILE, TILE), F32),
            pltpu.VMEM((head, length), F32),
            pltpu.VMEM((TILE, TILE), F32),
            pltpu.VMEM((3 * head, length), BF),
            pltpu.VMEM((head, length), BF),
        ],
        compiler_params=pltpu.CompilerParams(vmem_limit_bytes=48 * 2**20),
        name="attend_backward",
    )(starts, me, rel, bucket, qkv_t, qkv_t, qkv_t, upstream, attended, lse, n1, slab)


def pack_kernel(spans, head, me_ref, q_ref, k_ref, v_ref, router_ref, one_ref, two_ref, slab_ref):
    rows, width = q_ref.shape
    local = width // spans
    for span in range(spans):

        @pl.when(me_ref[0] == span)
        def _():
            pieces = []
            for at in range(span * local, (span + 1) * local, head):
                pieces += [ref[:, at : at + head] for ref in (q_ref, k_ref, v_ref)]
            slab_ref[:, : 3 * local] = jnp.concatenate(pieces, axis=1)

    top = [ref[...].astype(F32) for ref in (router_ref, one_ref, two_ref)]
    used = sum(part.shape[0] for part in top)
    free = slab_ref.shape[1] - 3 * local
    tail = jnp.concatenate(top + [jnp.zeros((free - used, rows), F32)], axis=0)
    tail = jnp.concatenate([tail, jnp.zeros((free, LANES - rows), F32)], axis=1)
    slab_ref[:, 3 * local :] = tail.T[:rows].astype(BF)


def pack_slab(me, w_query, w_key, w_value, w_router, gain_attn, gain_moe, spans, head):
    rows, width = w_query.shape
    columns = 3 * width // spans + w_router.shape[1] + 2
    columns += -columns % LANES
    return pl.pallas_call(
        functools.partial(pack_kernel, spans, head),
        in_specs=[pl.BlockSpec(memory_space=pltpu.SMEM)]
        + [pl.BlockSpec(memory_space=pltpu.VMEM)] * 6,
        out_specs=pl.BlockSpec(memory_space=pltpu.VMEM),
        out_shape=jax.ShapeDtypeStruct((rows, columns), BF),
        name="pack_slab",
    )(me, w_query, w_key, w_value, w_router.T, gain_attn[None], gain_moe[None])


def share_kernel(spans, me_ref, slab_ref, *refs):
    grad_refs, out_refs = refs[:-spans], refs[-spans:]
    for mask in range(spans):
        grads = jnp.concatenate([ref[mask] for ref in grad_refs], axis=0)
        out_refs[mask][...] = contract(grads, slab_ref[:, : grads.shape[0]], 0, 1).astype(BF)


def share_rows(me, slab, grads):
    spans, _, span = grads[0].shape
    vmem = pl.BlockSpec(memory_space=pltpu.VMEM)
    return pl.pallas_call(
        functools.partial(share_kernel, spans),
        in_specs=[pl.BlockSpec(memory_space=pltpu.SMEM)] + [vmem] * (1 + len(grads)),
        out_specs=[vmem] * spans,
        out_shape=[jax.ShapeDtypeStruct((span, slab.shape[0]), BF)] * spans,
        compiler_params=pltpu.CompilerParams(vmem_limit_bytes=50 * 2**20),
        name="share_rows",
    )(me, slab, *grads)


def out_kernel(x_ref, gain_ref, grads_ref, *refs):
    share_refs, out_ref = refs[:-1], refs[-1]
    dn = sum(ref[...].astype(F32) for ref in share_refs)
    x = x_ref[...].astype(F32)
    scale = lax.rsqrt(jnp.mean(x * x, axis=1, keepdims=True) + EPS)
    normed = x * scale
    scaled = dn * gain_ref[...]
    out_ref[...] = grads_ref[...] + scale * (
        scaled - normed * jnp.mean(scaled * normed, axis=1, keepdims=True)
    )


def rows_out(x, gain, grads, shares):
    span, width = x.shape
    part = span // 4
    rows = pl.BlockSpec((part, width), lambda i: (i, 0))
    return pl.pallas_call(
        out_kernel,
        grid=(4,),
        in_specs=[rows, pl.BlockSpec((1, width), lambda i: (0, 0)), rows] + [rows] * len(shares),
        out_specs=rows,
        out_shape=jax.ShapeDtypeStruct(x.shape, F32),
        compiler_params=pltpu.CompilerParams(vmem_limit_bytes=50 * 2**20),
        cost_estimate=pl.CostEstimate(flops=0, bytes_accessed=32 * 2**20, transcendentals=0),
        name="rows_out",
    )(x, gain, grads, *shares)


def project_kernel(wide, pieces, count_old, at_ref, *refs):
    x_refs, slab_ref, gain_ref, refs = refs[:pieces], refs[pieces], refs[pieces + 1], refs[pieces + 2 :]
    if len(refs) == count_old + 5:
        in_ref, w_ref = refs[0], refs[1]
        packed_ref = refs[-1]
        refs = refs[2:-1]
        width, quarter = in_ref.shape
        packed_ref[:width, :] = in_ref[...]
        for at in range(0, width, quarter):
            packed_ref[width + at : width + at + quarter, :] = w_ref[:, at : at + quarter]
    n1_ref, qkv_ref = refs[count_old:]
    x = jnp.concatenate([ref[...].astype(F32) for ref in x_refs], axis=0)
    scale = lax.rsqrt(jnp.mean(x * x, axis=1, keepdims=True) + EPS)
    n1 = (x * scale * gain_ref[...]).astype(BF)
    n1_ref[...] = n1
    qkv_ref[...] = contract(slab_ref[:, :wide], n1, 0, 1).astype(BF)


def project(at, rows, slab, gain, wide, spans, old, expert=()):
    width = rows[0].shape[1]
    span = sum(piece.shape[0] for piece in rows)
    packed = [jax.ShapeDtypeStruct((2 * width, array.shape[1]), BF) for array in expert[:1]]
    first = 3 + len(rows) + len(expert)

    def whole(array):
        return pl.BlockSpec(array.shape, lambda i, at: (0, 0))

    return pl.pallas_call(
        functools.partial(project_kernel, wide, len(rows), len(old)),
        grid_spec=pltpu.PrefetchScalarGridSpec(
            num_scalar_prefetch=1,
            grid=(1,),
            in_specs=[whole(array) for array in (*rows, slab, gain, *expert)]
            + [pl.BlockSpec(memory_space=pl.ANY)] * len(old),
            out_specs=[
                pl.BlockSpec((span, width), lambda i, at: (at[0], 0)),
                pl.BlockSpec((wide, span), lambda i, at: (0, at[0])),
            ]
            + [whole(array) for array in packed],
        ),
        out_shape=[
            jax.ShapeDtypeStruct((spans * span, width), BF),
            jax.ShapeDtypeStruct((wide, spans * span), BF),
        ]
        + packed,
        input_output_aliases={first + index: index for index in range(len(old))},
        compiler_params=pltpu.CompilerParams(vmem_limit_bytes=40 * 2**20),
        name="project",
    )(at, *rows, slab, gain, *expert, *old)


def place_of(slot_ref, part, part_rows):
    slots = lax.broadcasted_iota(jnp.int32, (part_rows, slot_ref.shape[1]), 0) + part * part_rows
    return jnp.where(slots == slot_ref[...], 1.0, 0.0).astype(BF)


def normed_rows(hidden, gain):
    scale = lax.rsqrt(jnp.mean(hidden * hidden, axis=1, keepdims=True) + EPS)
    normed = hidden * scale
    return scale, normed, (normed * gain).astype(BF)


def router_probs(rows, router, experts):
    logits = contract(rows, router, 1, 0)
    lane = lax.broadcasted_iota(jnp.int32, logits.shape, 1)
    logits = jnp.where(lane < experts, logits, -BIG)
    shifted = jnp.exp(logits - jnp.max(logits, axis=1, keepdims=True))
    return shifted / jnp.sum(shifted, axis=1, keepdims=True)


def slots_kernel(rows_ref, slot_ref, *part_refs):
    for part, ref in enumerate(part_refs):
        ref[...] = contract(place_of(slot_ref, part, ref.shape[0]), rows_ref[...], 1, 0).astype(BF)


def into_slots(rows, slot, parts, part_rows):
    vmem = pl.BlockSpec(memory_space=pltpu.VMEM)
    return pl.pallas_call(
        slots_kernel,
        in_specs=[vmem] * 2,
        out_specs=[vmem] * parts,
        out_shape=[jax.ShapeDtypeStruct((part_rows, rows.shape[1]), BF)] * parts,
        name="into_slots",
    )(rows, slot)


def into_kernel(parts, x_ref, mixed_ref, top_ref, low_ref, gain_ref, slot_ref, hidden_ref, *part_refs):
    out_ref = part_refs[-1]
    half, columns = top_ref.shape[1:]
    for begin, ref in ((0, top_ref), (half, low_ref)):
        for core in range(2):
            out_ref[begin : begin + half, core * columns : (core + 1) * columns] = ref[core]
    hidden = x_ref[...].astype(F32) + contract(mixed_ref[...], out_ref[...], 0, 0)
    hidden_ref[...] = hidden
    _, _, n2 = normed_rows(hidden, gain_ref[...])
    for part in range(parts):
        rows = part_refs[part].shape[0]
        part_refs[part][...] = contract(place_of(slot_ref, part, rows), n2, 1, 0).astype(BF)


def rows_into_experts(x, mixed, output_halves, gain, slot, parts, part_rows):
    span, width = x.shape
    if len(output_halves) == 1:
        blocks = output_halves[0].reshape(2, width // 2, 2, width // 2).transpose(0, 2, 1, 3)
        output_halves = [blocks[0], blocks[1]]
    vmem = pl.BlockSpec(memory_space=pltpu.VMEM)
    return pl.pallas_call(
        functools.partial(into_kernel, parts),
        in_specs=[vmem] * 6,
        out_specs=[vmem] * (2 + parts),
        out_shape=[jax.ShapeDtypeStruct((span, width), F32)]
        + [jax.ShapeDtypeStruct((part_rows, width), BF)] * parts
        + [jax.ShapeDtypeStruct((width, width), BF)],
        compiler_params=pltpu.CompilerParams(vmem_limit_bytes=50 * 2**20),
        name="rows_into_experts",
    )(x, mixed, *output_halves, gain, slot)


def back_kernel(hidden_ref, up_ref, out_ref, gain_ref, slot_ref, *refs):
    part_refs = refs[:-3]
    grads_ref, do_ref, grad_gain_ref = refs[-3:]
    dn = None
    for part, part_ref in enumerate(part_refs):
        rows = contract(place_of(slot_ref, part, part_ref.shape[0]), part_ref[...], 0, 0)
        dn = rows if dn is None else dn + rows
    gain = gain_ref[...]
    scale, normed, _ = normed_rows(hidden_ref[...], gain)
    grad_gain_ref[...] = jnp.sum(dn * normed, axis=0, keepdims=True)
    scaled = dn * gain
    grads = up_ref[...].astype(F32) + scale * (
        scaled - normed * jnp.mean(scaled * normed, axis=1, keepdims=True)
    )
    grads_ref[...] = grads
    do_ref[...] = contract(out_ref[...], grads.astype(BF), 1, 1).astype(BF)


def rows_from_experts(hidden, upstream, full_output, gain, slot, back):
    span, width = hidden.shape
    vmem = pl.BlockSpec(memory_space=pltpu.VMEM)
    return pl.pallas_call(
        back_kernel,
        in_specs=[vmem] * (5 + len(back)),
        out_specs=[vmem] * 3,
        out_shape=[
            jax.ShapeDtypeStruct((span, width), F32),
            jax.ShapeDtypeStruct((width, span), BF),
            jax.ShapeDtypeStruct((1, width), F32),
        ],
        compiler_params=pltpu.CompilerParams(vmem_limit_bytes=50 * 2**20),
        name="rows_from_experts",
    )(hidden, upstream, full_output, gain, slot, *back)


def early_kernel(experts, spans, grads_ref, mixed_ref, gain_ref, *refs):
    router_refs, early_ref = refs[:-1], refs[-1]
    grad_output = contract(mixed_ref[...], grads_ref[...].astype(BF), 1, 0)
    width = grad_output.shape[1]
    local = width // spans
    share = experts // spans
    column = jnp.broadcast_to(gain_ref[...], (8, width)).T[:, :1]
    free = early_ref.shape[2] - local - share - 1
    grad_router = sum(ref[...] for ref in router_refs)
    for span in range(spans):
        early_ref[span] = jnp.concatenate(
            [
                grad_output[:, span * local : (span + 1) * local],
                grad_router[:, span * share : (span + 1) * share],
                column,
                jnp.zeros((width, free), F32),
            ],
            axis=1,
        ).astype(BF)


def early_sums(grads, mixed, grad_router, grad_gain, experts, spans):
    width = grads.shape[1]
    columns = width // spans + experts // spans + 1
    columns += -columns % LANES
    vmem = pl.BlockSpec(memory_space=pltpu.VMEM)
    return pl.pallas_call(
        functools.partial(early_kernel, experts, spans),
        in_specs=[vmem] * (3 + len(grad_router)),
        out_specs=vmem,
        out_shape=jax.ShapeDtypeStruct((spans, width, columns), BF),
        compiler_params=pltpu.CompilerParams(vmem_limit_bytes=50 * 2**20),
        name="early_sums",
    )(grads, mixed, grad_gain, *grad_router)


def sums_kernel(heads, head_size, buckets, at, fsdp_count, weights_ref, early_ref, dist_ref, bucket_ref, out_ref):
    width = weights_ref.shape[0]
    columns = weights_ref.shape[1]
    early = early_ref[0].astype(F32)
    for span in range(1, early_ref.shape[0]):
        early = early + early_ref[span].astype(F32)
    index = lax.broadcasted_iota(jnp.int32, (buckets, bucket_ref.shape[1]), 0)
    onehot = jnp.where(index == bucket_ref[...], 1.0, 0.0)
    dist = jnp.concatenate([dist_ref[head] for head in range(heads)], axis=0)
    dist = jnp.concatenate([dist, jnp.zeros((8 - heads, dist.shape[1]), F32)], axis=0)
    rel = lax.dot_general(
        dist, onehot, (((1,), (1,)), ((), ())), precision=HIGH, preferred_element_type=F32
    )
    last = lax.broadcasted_iota(jnp.int32, rel.shape, 1) == buckets - 1
    rel = jnp.where(last, 0.0, rel)
    rel = jnp.where(last, -jnp.sum(rel, axis=1, keepdims=True), rel)
    rows_here = width // fsdp_count
    if heads * buckets == rows_here:
        column = jnp.concatenate([rel.T[:, head : head + 1] for head in range(heads)], axis=0)
        column = jnp.concatenate([column] * fsdp_count, axis=0)
        lane = lax.broadcasted_iota(jnp.int32, early.shape, 1)
        early = jnp.where(lane == at, column, early)
    columns //= heads
    used = 3 * head_size
    parts = [weights_ref[:, head * columns : head * columns + used] for head in range(heads)]
    shares = [
        weights_ref[:, head * columns + used : head * columns + used + 1] for head in range(heads)
    ]
    parts = parts + [early.astype(BF)[:, : at + 1]] + shares
    free = out_ref.shape[1] - sum(part.shape[1] for part in parts)
    out_ref[...] = jnp.concatenate(parts + [jnp.zeros((width, free), BF)], axis=1)


def all_sums(weight_grads, early, distances, bucket, head, buckets, at, fsdp_count):
    width = weight_grads.shape[0]
    heads = distances.shape[0]
    total = heads * (3 * head + 1) + at + 1
    total += -total % LANES
    vmem = pl.BlockSpec(memory_space=pltpu.VMEM)
    return pl.pallas_call(
        functools.partial(sums_kernel, heads, head, buckets, at, fsdp_count),
        in_specs=[vmem] * 4,
        out_specs=vmem,
        out_shape=jax.ShapeDtypeStruct((width, total), BF),
        compiler_params=pltpu.CompilerParams(vmem_limit_bytes=50 * 2**20),
        name="all_sums",
    )(weight_grads, early, distances, bucket)


def final_kernel(experts, hidden_ref, gain_ref, router_ref, chosen_ref, slot_ref, *refs):
    part_refs, output_ref = refs[:-1], refs[-1]
    hidden = hidden_ref[...]
    _, _, n2 = normed_rows(hidden, gain_ref[...])
    probs = router_probs(n2, router_ref[...], experts)
    gate = jnp.sum(probs * chosen_ref[...], axis=1, keepdims=True)
    y = None
    for part, part_ref in enumerate(part_refs):
        rows = contract(place_of(slot_ref, part, part_ref.shape[0]), part_ref[...], 0, 0)
        y = rows if y is None else y + rows
    output_ref[...] = (hidden + gate * y).astype(BF)


def final_output(hidden, gain, router, chosen, slot, parts, experts):
    vmem = pl.BlockSpec(memory_space=pltpu.VMEM)
    return pl.pallas_call(
        functools.partial(final_kernel, experts),
        in_specs=[vmem] * (5 + len(parts)),
        out_specs=vmem,
        out_shape=jax.ShapeDtypeStruct(hidden.shape, BF),
        compiler_params=pltpu.CompilerParams(vmem_limit_bytes=50 * 2**20),
        name="final_output",
    )(hidden, gain, router, chosen, slot, *parts)


def expert_kernel(experts, inputs, count_old, me_ref, core_ref, router_ref, *refs):
    x_refs, up_refs = refs[:inputs], refs[inputs : 2 * inputs]
    own_hbm, near_hbm, far_hbm, in_hbm, out_hbm = refs[2 * inputs : 2 * inputs + 5]
    refs = refs[2 * inputs + 5 + count_old :]
    ours_ref, theirs_ref, act_ref, pre_ref, dy_ref, w_ref, y_sum, dn_sum, sems = refs
    count, width = x_refs[0].shape
    rows = count // 2
    quarter = w_ref.shape[2]
    first = core_ref[0] == 0
    part, pair = pl.program_id(0), pl.program_id(1)
    copies = [
        [
            pltpu.make_async_copy(own_hbm, w_ref.at[0], sems.at[0]),
            pltpu.make_async_copy(near_hbm, w_ref.at[1], sems.at[1]),
        ],
        [
            pltpu.make_async_copy(far_hbm, w_ref.at[2], sems.at[2]),
            pltpu.make_async_copy(in_hbm, w_ref.at[3, pl.ds(0, width)], sems.at[3]),
            pltpu.make_async_copy(out_hbm, w_ref.at[3, pl.ds(width, width)], sems.at[4]),
        ],
    ]

    @pl.when((part == 0) & (pair == 0))
    def _():
        for copy in copies[0] + copies[1]:
            copy.start()

    def parted(index):
        x = x_refs[index][...]

        @pl.when(pair == 0)
        def _():
            probs = router_probs(x, router_ref[...], experts)
            lane = lax.broadcasted_iota(jnp.int32, probs.shape, 1)
            gate = jnp.sum(jnp.where(lane == me_ref[0], probs, 0.0), axis=1, keepdims=True)
            dy_ref[...] = (gate * up_refs[index][...].astype(F32)).astype(BF)

        def blocks(half):
            if index == 0:
                for copy in copies[half]:
                    copy.wait()
            w_in = jnp.concatenate([w_ref[2 * half + b, :width, :] for b in range(2)], axis=1)
            w_out = jnp.concatenate(
                [
                    jnp.concatenate(
                        [
                            w_ref[2 * half + b, at : at + quarter, :]
                            for at in range(width, 2 * width, quarter)
                        ],
                        axis=1,
                    )
                    for b in range(2)
                ],
                axis=0,
            )
            pre = contract(x, w_in, 1, 0)
            root = 0.7978845608028654
            square = pre * pre
            tanh = jnp.tanh(pre * (root + (root * 0.044715) * square))
            upper = 0.5 + 0.5 * tanh
            act = (pre * upper).astype(BF)
            slope = upper + (pre * upper) * (1.0 - tanh) * (root + (root * 0.134145) * square)
            act_ref[...] = act
            pre_grads = (contract(dy_ref[...], w_out, 1, 1) * slope).astype(BF)
            pre_ref[...] = pre_grads
            y = contract(act, w_out, 1, 0)
            dn = contract(pre_grads, w_in, 1, 1)
            if half == 0:
                y_sum[...] = y
                dn_sum[...] = dn
                return
            for some, total in (
                (slice(0, rows), y_sum[...] + y),
                (slice(rows, count), dn_sum[...] + dn),
            ):
                one, two = total[:rows], total[rows:]
                ours_ref[0, some, :] = jnp.where(first, one, two).astype(BF)
                theirs_ref[0, some, :] = jnp.where(first, two, one).astype(BF)

        for half in range(2):
            pl.when(pair == half)(functools.partial(blocks, half))

    for index in range(inputs):
        pl.when(part == index)(functools.partial(parted, index))


def expert_part(part, parts, me, core, rows, upstream, router, weights, old, experts):
    inputs = len(rows)
    count, width = rows[0].shape
    quarter = weights[0].shape[1]
    hidden = 4 * quarter
    total = count * inputs * parts
    begin = part * inputs
    first = 3 + 2 * inputs + len(weights)
    smem = pl.BlockSpec(memory_space=pltpu.SMEM)
    hbm = pl.BlockSpec(memory_space=pl.ANY)
    share = pl.BlockSpec((1, count, width), lambda i, j: (i, 0, 0))
    inner = pl.BlockSpec((count, 2 * quarter), lambda i, j: (begin + i, j))
    return pl.pallas_call(
        functools.partial(expert_kernel, experts, inputs, len(old)),
        grid=(inputs, 2),
        in_specs=[smem] * 2
        + [
            pl.BlockSpec(array.shape, lambda i, j: (0, 0))
            for array in (router, *rows, *upstream)
        ]
        + [hbm] * (len(weights) + len(old)),
        out_specs=[share] * 2
        + [inner] * 2
        + [pl.BlockSpec((count, width), lambda i, j: (begin + i, 0))],
        out_shape=[jax.ShapeDtypeStruct((inputs, count, width), BF)] * 2
        + [jax.ShapeDtypeStruct((total, size), BF) for size in (hidden, hidden, width)],
        scratch_shapes=[
            pltpu.VMEM((4, 2 * width, quarter), BF),
            pltpu.VMEM((count, width), F32),
            pltpu.VMEM((count, width), F32),
            pltpu.SemaphoreType.DMA((5,)),
        ],
        input_output_aliases={first + index: 2 + index for index in range(len(old))},
        compiler_params=pltpu.CompilerParams(vmem_limit_bytes=56 * 2**20),
        name="expert_part",
    )(me, core, router, *rows, *upstream, *weights, *old)


def combine_kernel(inputs, experts, core_ref, me_ref, ours_ref, theirs_ref, router_ref, *refs):
    x_refs, up_refs, refs = refs[:inputs], refs[inputs : 2 * inputs], refs[2 * inputs :]
    y_refs, dn_refs, grad_ref = refs[:inputs], refs[inputs : 2 * inputs], refs[-1]
    rows = y_refs[0].shape[0]
    router = router_ref[...]
    grad_router = None
    for index in range(inputs):
        x = x_refs[index][...]
        y = ours_ref[index, :rows, :].astype(F32) + theirs_ref[index, :rows, :].astype(F32)
        dn = ours_ref[index, rows:, :].astype(F32) + theirs_ref[index, rows:, :].astype(F32)
        probs = router_probs(x, router, experts)
        lane = lax.broadcasted_iota(jnp.int32, probs.shape, 1)
        chosen = jnp.where(lane == me_ref[0], 1.0, 0.0)
        gate = jnp.sum(probs * chosen, axis=1, keepdims=True)
        gate_grads = jnp.sum(up_refs[index][...].astype(F32) * y, axis=1, keepdims=True)
        logit_grads = (probs * (chosen * gate_grads - gate * gate_grads)).astype(BF)
        product = contract(x, logit_grads, 0, 0)
        grad_router = product if grad_router is None else grad_router + product
        y_refs[index][...] = y.astype(BF)
        dn_refs[index][...] = (dn + contract(logit_grads, router, 1, 1)).astype(BF)
    grad_ref[...] = grad_router


def combine_halves(me, core, ours, theirs, router, rows, upstream, experts):
    inputs, count, width = ours.shape

    def whole(array):
        return pl.BlockSpec(array.shape, lambda i, core: (0,) * array.ndim)

    own = pl.BlockSpec((count // 2, width), lambda i, core: (core[0], 0))
    out_shape = [jax.ShapeDtypeStruct((count // 2, width), BF)] * (2 * inputs)
    out_shape.append(jax.ShapeDtypeStruct(router.shape, F32))
    results = pl.pallas_call(
        functools.partial(combine_kernel, inputs, experts),
        grid_spec=pltpu.PrefetchScalarGridSpec(
            num_scalar_prefetch=1,
            grid=(1,),
            in_specs=[pl.BlockSpec(memory_space=pltpu.SMEM)]
            + [whole(array) for array in (ours, theirs, router)]
            + [own] * (2 * inputs),
            out_specs=[
                pl.BlockSpec(array.shape, lambda i, core: (0, 0)) for array in out_shape
            ],
        ),
        out_shape=out_shape,
        compiler_params=pltpu.CompilerParams(vmem_limit_bytes=50 * 2**20),
        name="combine_halves",
    )(core, me, ours, theirs, router, *rows, *upstream)
    return results[:inputs], results[inputs : 2 * inputs], results[-1]


def expert_grads_kernel(act_ref, pre_ref, dy_ref, *refs):
    x_refs = refs[:-4]
    one_ref, two_ref, keep_one, keep_two = refs[-4:]
    width = dy_ref.shape[1]
    quarter = act_ref.shape[1]
    mask = pl.program_id(0)
    rows = jnp.concatenate([ref[...] for ref in x_refs], axis=0)
    grad_in = contract(rows, pre_ref[...], 0, 0)
    grad_out = contract(act_ref[...], dy_ref[...], 0, 0)
    grad_out = jnp.concatenate(
        [grad_out[:, at : at + quarter] for at in range(0, width, quarter)], axis=0
    )
    for at in (1, 3):

        @pl.when(mask == at)
        def _():
            one_ref[0] = grad_in.astype(BF)

    for at in (2, 3):

        @pl.when(mask == at)
        def _():
            two_ref[0] = grad_out.astype(BF)

    for at in (0, 2):

        @pl.when(mask == at)
        def _():
            keep_one[0] = grad_in

    for at in (0, 1):

        @pl.when(mask == at)
        def _():
            keep_two[0] = grad_out


def expert_grads(kept, rows, quarter):
    act, pre, dy = kept
    total, width = dy.shape
    hidden = pl.BlockSpec((total, quarter), lambda f: (0, f))

    def whole(array):
        return pl.BlockSpec(array.shape, lambda f: (0, 0))

    def block(place):
        return pl.BlockSpec((1, width, quarter), lambda f: (place(f), 0, 0))

    return pl.pallas_call(
        expert_grads_kernel,
        grid=(act.shape[1] // quarter,),
        in_specs=[hidden, hidden, whole(dy)] + [whole(part) for part in rows],
        out_specs=[
            block(lambda f: f // 2),
            block(lambda f: jnp.maximum(f - 2, 0)),
            block(lambda f: f // 2),
            block(lambda f: jnp.minimum(f, 1)),
        ],
        out_shape=[jax.ShapeDtypeStruct((2, width, quarter), BF)] * 2
        + [jax.ShapeDtypeStruct((2, width, quarter), F32)] * 2,
        compiler_params=pltpu.CompilerParams(vmem_limit_bytes=50 * 2**20),
        name="expert_grads",
    )(act, pre, dy, *rows)


def settle_kernel(keep_one, keep_two, got_one, got_two, one_ref, two_ref):
    one_ref[...] = (keep_one[0].astype(F32) + got_one[0].astype(F32)).astype(BF)
    two_ref[...] = (keep_two[0].astype(F32) + got_two[0].astype(F32)).astype(BF)


def settle_step(keep_one, keep_two, got_one, got_two):
    _, width, quarter = keep_one.shape
    second = pl.BlockSpec((1, width, quarter), lambda i: (1, 0, 0))
    whole = pl.BlockSpec((width, quarter), lambda i: (0, 0))
    return pl.pallas_call(
        settle_kernel,
        grid=(1,),
        in_specs=[second] * 4,
        out_specs=[whole] * 2,
        out_shape=[jax.ShapeDtypeStruct((width, quarter), BF)] * 2,
        compiler_params=pltpu.CompilerParams(vmem_limit_bytes=50 * 2**20),
        name="settle_step",
    )(keep_one, keep_two, got_one, got_two)


def all_to_all(blocks, axis, groups=None):
    return lax.all_to_all(
        blocks, axis, split_axis=0, concat_axis=0, tiled=True, axis_index_groups=groups
    )


def pair_swap(block, axis, mask):
    count = lax.axis_size(axis)
    return lax.ppermute(block, axis, [(i, i ^ mask) for i in range(count)])


def tied(values, *others):
    return lax.optimization_barrier((values, others))[0]


def gather_pairs(rows, axis, groups, pairs, after):
    count = lax.axis_size(axis)
    if count > 8:
        return [lax.all_gather(rows, axis, axis=0, tiled=True)]
    core = lax.axis_index(axis) % 2
    columns = rows.shape[1] // 2
    low, high = rows[:, :columns], rows[:, columns:]
    mine = jnp.where(core == 0, low, high)
    got = pair_swap(jnp.where(core == 0, high, low), axis, 1)
    chip = jnp.where(core == 0, jnp.stack([mine, got]), jnp.stack([got, mine]))
    whole = all_to_all(jnp.broadcast_to(chip[None], (count // 2,) + chip.shape), axis, groups)
    whole = tied(whole.reshape(2, count * rows.shape[0] // 2, columns), after)
    return [
        lax.all_gather(part, axis, axis=0, tiled=False, axis_index_groups=pairs) for part in whole
    ]


def scatter_sums(rows, axis, groups):
    count = lax.axis_size(axis)
    here = rows.shape[0] // count
    if count > 8:
        blocks = all_to_all(rows.reshape(count, here, rows.shape[1]), axis)
        return jnp.sum(blocks.astype(F32), axis=0)
    core = lax.axis_index(axis) % 2
    split = rows.reshape(count // 2, 2, here, rows.shape[1])
    mine = lax.dynamic_index_in_dim(split, core, 1, keepdims=False)
    other = pair_swap(lax.dynamic_index_in_dim(split, 1 - core, 1, keepdims=False), axis, 1)
    chip = (mine.astype(F32) + other.astype(F32)).astype(BF)
    return jnp.sum(all_to_all(chip, axis, groups).astype(F32), axis=0)


def per_device(
    tokens, cotangent, doc_starts, routes, bucket_table, w_query, w_key, w_value, w_output,
    w_router, gain_attn, gain_moe, rel_bias, expert_in, expert_out,
):
    _, span, width = tokens.shape
    seq_count = lax.axis_size("seq")
    fsdp_count = lax.axis_size("fsdp")
    seq_me = lax.axis_index("seq")
    fsdp_me = lax.axis_index("fsdp")
    heads, buckets = rel_bias.shape
    local = width // seq_count
    head = local // heads
    experts = w_router.shape[1]
    rows_here = w_query.shape[0]
    quarter = expert_in.shape[2]
    cores = 2
    groups = [list(range(core, fsdp_count, cores)) for core in range(cores)]
    x = tokens[0]
    seq_index = seq_me.astype(jnp.int32)[None]
    expert_index = (fsdp_me // cores).astype(jnp.int32)[None]
    core_index = (fsdp_me % cores).astype(jnp.int32)[None]

    near = pair_swap(x, "seq", 1)
    far = pair_swap(x, "seq", 2)
    slab = pack_slab(
        seq_index, w_query, w_key, w_value, w_router, gain_attn, gain_moe, seq_count, head
    )
    slab = lax.all_gather(slab, "fsdp", axis=0, tiled=True)
    half = span // 2
    slab, near_half, far_half = lax.optimization_barrier((slab, near[:half], far[half:]))
    across = [pair_swap(near_half, "seq", 2), pair_swap(far_half, "seq", 1)]
    tail = slab[:, 3 * local :]
    full_router = jnp.pad(tail[:, :experts], ((0, 0), (0, -experts % LANES)))
    gains = tail[:, experts : experts + 2].astype(F32).T
    gain_one, gain_two = gains[:1], gains[1:2]
    own_gain = gain_attn.astype(F32)

    expert_me = fsdp_me // cores
    few = experts <= 4
    route, bucket_table, rel_bias = tied((routes[0], bucket_table[:TILE], rel_bias), slab)
    chosen = (route[:, None] == jnp.arange(LANES, dtype=jnp.int32)[None, :]).astype(F32)
    before = (
        jnp.arange(span, dtype=jnp.int32)[:, None] > jnp.arange(span, dtype=jnp.int32)[None, :]
    ).astype(BF)
    ranks = jnp.dot(before, chosen.astype(BF), preferred_element_type=F32)
    capacity = max(2, 2 * span // experts)
    target = route ^ expert_me if few else route
    slot = target * capacity + jnp.sum(ranks * chosen, axis=1).astype(jnp.int32)
    slot = slot[None]
    part_count = 4
    part_rows = experts * capacity // part_count

    def exchange(parts):
        if few:
            return [parts[0]] + [
                pair_swap(parts[mask], "fsdp", cores * mask) for mask in range(1, part_count)
            ]
        blocks = jnp.concatenate(parts, axis=0).reshape(experts, capacity, width)
        blocks = all_to_all(blocks, "fsdp", groups).reshape(part_count, part_rows, width)
        return [blocks[part] for part in range(part_count)]

    old = ()
    for mask, part in enumerate((x, near, far)):
        old = project(
            (seq_me ^ mask).astype(jnp.int32)[None], (part,), slab, gain_one, 3 * local, seq_count, old,
            () if mask < 2 else (expert_in[0], expert_out[0]),
        )
    weights = tied(old[2], across)
    w_near = pair_swap(weights, "seq", 1)
    w_far = pair_swap(weights, "seq", 2)
    up_rows, old = lax.optimization_barrier((cotangent[0], old[:2]))
    w_output = tied(w_output, slab)
    upstream_parts = into_slots(up_rows, slot, part_count, part_rows)
    upstream_parts = exchange(upstream_parts)
    n1_all, qkv_t = project(
        (seq_me ^ 3).astype(jnp.int32)[None], across, slab, gain_one, 3 * local, seq_count, old,
    )
    rel = rel_bias.astype(F32)
    bucket = bucket_table[None]
    attended, lse = attend_forward(
        qkv_t, doc_starts, rel, bucket, heads, head, seq_count
    )
    mixed = all_to_all(attended, "seq").reshape(width, span)
    pairs = [list(range(at, at + cores)) for at in range(0, fsdp_count, cores)]
    output_halves = gather_pairs(w_output, "fsdp", groups, pairs, (attended, upstream_parts))

    def of_chip(rows):
        return lax.all_gather(rows, "fsdp", axis=0, tiled=True, axis_index_groups=pairs)

    mixed, output_halves, upstream_parts, w_near, w_far = lax.optimization_barrier(
        (mixed, output_halves, upstream_parts, w_near, w_far)
    )

    hidden, *parts, full_output = rows_into_experts(
        x, mixed, output_halves, gain_two, slot, part_count, part_rows
    )
    w_near, w_far, parts = lax.optimization_barrier((w_near, w_far, parts))
    w_across = [pair_swap(w_near[:width], "seq", 2), pair_swap(w_far[width:], "seq", 1)]
    weights = [weights, w_near, w_far] + w_across
    arrived = exchange(parts)
    kept = ()
    upstream_parts = [of_chip(one) for one in tied(upstream_parts, parts)]
    chip_rows, ys, back, pairs_of_shares = [], [], [], []
    grad_router = []
    steps = part_count // 2
    for part in range(steps):
        some = slice(part * part_count // steps, (part + 1) * part_count // steps)
        rows, some_up = arrived[some], upstream_parts[some]
        if part:
            rows = tied(rows, kept)
        rows = [of_chip(one) for one in rows]
        if not part:
            rows, upstream_parts = lax.optimization_barrier((rows, upstream_parts))
            some_up = upstream_parts[some]
        chip_rows += rows
        ours, theirs, *kept = expert_part(
            part, steps, expert_index, core_index, rows, some_up, full_router, weights, kept,
            experts,
        )
        pairs_of_shares.append((ours, pair_swap(theirs, "fsdp", 1), rows, some_up))
    for ours, theirs, rows, some_up in pairs_of_shares[::-1]:
        ours, theirs = tied((ours, theirs), back)
        some_ys, dns, product = combine_halves(
            expert_index, core_index, ours, theirs, full_router, rows, some_up, experts
        )
        ys = list(some_ys) + ys
        back = list(dns) + back
        grad_router.append(product)
    kept = tied(kept, back)
    back = exchange(back)
    one, two, keep_one, keep_two = expert_grads(kept, chip_rows, quarter)
    back = tied(back, one, two)
    got_one = pair_swap(one, "seq", 1)
    got_two = pair_swap(two, "seq", 2)

    hidden_grads, mixed_grads, grad_gain = rows_from_experts(
        hidden, cotangent[0], full_output, gain_two, slot, back
    )
    ys = exchange(tied(ys, mixed_grads))
    early = early_sums(hidden_grads, mixed, grad_router, grad_gain, experts, seq_count)
    moved = all_to_all(mixed_grads.reshape(seq_count, local, span), "seq")
    settled_sum = [keep[0] + got[0].astype(F32) for keep, got in ((keep_one, got_one), (keep_two, got_two))]
    one, two = settle_step(keep_one, keep_two, got_one, got_two)
    got_one = pair_swap(one, "seq", 2)
    got_two = pair_swap(two, "seq", 1)
    early = all_to_all(tied(early, moved), "seq")
    head_grads, distances, weight_grads = attend_backward(
        0, heads, qkv_t, moved, attended, lse, doc_starts, seq_index,
        rel, bucket, n1_all, slab, heads, head,
    )
    head_grads, distances, weight_grads, got_one, got_two, ys = lax.optimization_barrier(
        (head_grads, distances, weight_grads, got_one, got_two, ys)
    )
    shares = share_rows(seq_index, slab, [head_grads])
    output = final_output(hidden, gain_two, full_router, chosen, slot, ys, experts)
    shares = [shares[0]] + [
        pair_swap(shares[mask], "seq", mask) for mask in range(1, seq_count)
    ]
    grad_expert_in, grad_expert_out = [
        total + got.astype(F32) for total, got in zip(settled_sum, (got_one, got_two))
    ]
    grad_expert_out = jnp.concatenate(
        [grad_expert_out[at : at + quarter] for at in range(0, width, quarter)], axis=1
    )
    input_grads = rows_out(x, gain_one, hidden_grads, shares)

    share = experts // seq_count
    rel_count = heads * buckets
    at = local + share + 1
    sums = all_sums(weight_grads, early, distances, bucket, head, buckets, at, fsdp_count)
    summed = scatter_sums(sums, "fsdp", groups)
    by_head = [summed[:, begin : begin + 3 * head] for begin in range(0, 3 * local, 3 * head)]
    summed = summed[:, 3 * local :]
    sum_gain_attn = jnp.sum(summed[:, at + 1 : at + 1 + heads], axis=1) / own_gain
    sum_gain_attn = sum_gain_attn + sum(
        pair_swap(sum_gain_attn, "seq", mask) for mask in range(1, seq_count)
    )
    if rows_here == rel_count:
        sum_rel = summed[:rel_count, local + share + 1].reshape(heads, buckets)
    else:
        onehot = bucket_table[:, None] == jnp.arange(buckets - 1, dtype=jnp.int32)[None, :]
        below = jnp.dot(distances[:, 0], onehot.astype(F32), precision=HIGH)
        grad_rel = jnp.concatenate([below, -jnp.sum(below, axis=1, keepdims=True)], axis=1)
        sum_rel = lax.psum(grad_rel, "fsdp")
    heads_sum = [
        jnp.concatenate([part[:, at : at + head] for part in by_head], axis=1)
        for at in range(0, 3 * head, head)
    ]
    return (
        output[None],
        input_grads[None],
        heads_sum[0],
        heads_sum[1],
        heads_sum[2],
        summed[:, :local],
        summed[:, local : local + share],
        sum_gain_attn,
        summed[:, local + share],
        sum_rel,
        grad_expert_in[None],
        grad_expert_out[None],
    )


def solution(mesh):
    rows = P("fsdp", "seq", None)
    weight = P("fsdp", None)
    shared = P("fsdp", "seq")
    return jax.shard_map(
        per_device,
        mesh=mesh,
        in_specs=(
            rows, rows, weight, shared, P(), weight, weight, weight, weight, weight,
            P("fsdp"), P("fsdp"), P("seq", None), P("fsdp", None, "seq"), rows,
        ),
        out_specs=(
            rows, rows, shared, shared, shared, shared, shared, P("fsdp"), P("fsdp"),
            P("seq", None), P("fsdp", None, "seq"), rows,
        ),
        check_vma=False,
    )
```

```python
import functools

import jax
import jax.numpy as jnp
from jax import lax
from jax.experimental import pallas as pl
from jax.experimental.pallas import tpu as pltpu
from jax.sharding import PartitionSpec as P

EPS = 1e-06
HIGH = lax.Precision.HIGHEST
BIG = 1e30
TILE = 256
LANES = 128
CHUNK = 1024
BF = jnp.bfloat16
F32 = jnp.float32


def contract(left, right, left_dim, right_dim):
    return lax.dot_general(
        left, right, (((left_dim,), (right_dim,)), ((), ())), preferred_element_type=F32
    )


def doc_rows(starts_ref, length, docs):
    pos = lax.broadcasted_iota(jnp.int32, (1, length), 1)
    doc = jnp.zeros((1, length), jnp.int32) - 1
    for index in range(docs):
        doc = doc + (starts_ref[0, index] <= pos).astype(jnp.int32)
    row = lax.broadcasted_iota(jnp.int32, (8, length), 0)
    same = row == doc
    return jnp.where(same, 1.0, 0.0), jnp.where(same, 0.0, jnp.where(row < docs, -BIG, 0.0))


def bias_circle(rel_ref, bucket_ref, head, tile):
    last = rel_ref.shape[1] - 1
    bucket = bucket_ref[...]
    row = jnp.zeros(bucket.shape, F32)
    for index in range(last):
        row = jnp.where(bucket == index, rel_ref[head, index] - rel_ref[head, last], row)
    return pltpu.roll(jnp.broadcast_to(row, (tile, tile)), 0, 1, stride=1, stride_axis=0)


def forward_kernel(
    head, tile, docs, starts_ref, rel_ref, bucket_ref, q_ref, k_ref, v_ref, o_ref, lse_ref,
    kaug, qaug, vaug, band, scores,
):
    length = q_ref.shape[1]
    span = o_ref.shape[2]
    doc_q, doc_k = doc_rows(starts_ref, length, docs)
    qaug[:head, :] = (q_ref[...].astype(F32) * 0.125).astype(BF)
    qaug[head : head + 16, :] = jnp.concatenate([doc_q, jnp.zeros((8, length), F32)], 0).astype(BF)
    qaug[head + 16 :, :] = jnp.zeros((qaug.shape[0] - head - 16, length), BF)
    tail = jnp.zeros((LANES - head - 8, tile), F32)
    for block in range(length // tile):
        cols = slice(block * tile, (block + 1) * tile)
        full = jnp.concatenate([k_ref[:, cols].astype(F32), doc_k[:, cols], tail], 0)
        kaug[cols, :] = full.T.astype(BF)
    vaug[:head, :] = v_ref[...]
    extra = lax.broadcasted_iota(jnp.int32, (vaug.shape[0] - head, length), 0)
    vaug[head:, :] = jnp.where(extra == 0, 1.0, 0.0).astype(BF)
    circle = bias_circle(rel_ref, bucket_ref, pl.program_id(0), tile)
    key_row = lax.broadcasted_iota(jnp.int32, (tile, tile), 0)
    query_col = lax.broadcasted_iota(jnp.int32, (tile, tile), 1)
    band[:tile, :] = jnp.where(key_row > query_col, circle, 0.0)
    band[tile:, :] = jnp.where(key_row <= query_col, circle, -BIG)
    for i in range(length // tile):
        cols = slice(i * tile, (i + 1) * tile)
        queries = qaug[:, cols]
        peak = None
        for j in range(i + 1):
            rows = slice(j * tile, (j + 1) * tile)
            part = contract(kaug[rows, :], queries, 1, 0)
            if j == i:
                part = part + band[tile:, :]
            elif j == i - 1:
                part = part + band[:tile, :]
            scores[rows, :] = part
            most = jnp.max(part.reshape(tile // 8, 8, tile), axis=0)
            peak = most if peak is None else jnp.maximum(peak, most)
        peak = jnp.max(peak, axis=0, keepdims=True)
        summed = jnp.zeros((vaug.shape[0], tile), F32)
        for j in range(i + 1):
            rows = slice(j * tile, (j + 1) * tile)
            expons = jnp.exp(scores[rows, :] - peak).astype(BF)
            summed = summed + contract(vaug[:, rows], expons, 1, 0)
        total = summed[head : head + 1, :]
        start = (i * tile) % span
        o_ref[i * tile // span, :, start : start + tile] = (summed[:head, :] / total).astype(BF)
        lse_ref[0, :, cols] = peak + jnp.log(total)


def attend_forward(qkv_t, starts, rel, bucket, heads, head, spans):
    length = qkv_t.shape[1]
    docs = starts.shape[1]
    span = length // spans

    def rows_of(part):
        return pl.BlockSpec((head, length), lambda h: (3 * h + part, 0))

    return pl.pallas_call(
        functools.partial(forward_kernel, head, TILE, docs),
        grid=(heads,),
        in_specs=[
            pl.BlockSpec(memory_space=pltpu.SMEM),
            pl.BlockSpec(memory_space=pltpu.SMEM),
            pl.BlockSpec((1, TILE), lambda h: (0, 0)),
            rows_of(0),
            rows_of(1),
            rows_of(2),
        ],
        out_specs=[
            pl.BlockSpec((spans, head, span), lambda h: (0, h, 0)),
            pl.BlockSpec((1, 1, length), lambda h: (h, 0, 0)),
        ],
        out_shape=[
            jax.ShapeDtypeStruct((spans, heads * head, span), BF),
            jax.ShapeDtypeStruct((heads, 1, length), F32),
        ],
        scratch_shapes=[
            pltpu.VMEM((length, LANES), BF),
            pltpu.VMEM((LANES, length), BF),
            pltpu.VMEM((head + 16, length), BF),
            pltpu.VMEM((2 * TILE, TILE), F32),
            pltpu.VMEM((length, TILE), F32),
        ],
        compiler_params=pltpu.CompilerParams(vmem_limit_bytes=40 * 2**20),
        name="attend_forward",
    )(starts, rel, bucket, qkv_t, qkv_t, qkv_t)


def backward_kernel(
    count, head, offset, tile, docs, starts_ref, me_ref, rel_ref, bucket_ref, q_ref, k_ref, v_ref, do_ref, o_ref,
    lse_ref, n1_ref, slab_ref, one_ref, two_ref, three_ref, four_ref, dist_ref, weight_ref, qaug, doaug, kaug, vaug, scaled,
    band, dq_sum, diagonal, grads, upstream_all, all_grads, spare,
):
    length = q_ref.shape[1]
    span = o_ref.shape[2]
    doc_q, doc_k = doc_rows(starts_ref, length, docs)
    sub = lax.broadcasted_iota(jnp.int32, (8, tile), 0)

    def minus_split(row):
        row = -row
        high = row.astype(BF).astype(F32)
        rest = row - high
        mid = rest.astype(BF).astype(F32)
        return jnp.where(
            sub == 0, high, jnp.where(sub == 1, mid, jnp.where(sub == 2, rest - mid, 0.0))
        )

    ones3 = jnp.where(lax.broadcasted_iota(jnp.int32, (8, length), 0) < 3, 1.0, 0.0)
    zeros8 = jnp.zeros((8, length), F32)
    blocks = length // tile
    tail = jnp.zeros((LANES - head - 16, tile), F32)
    for block in range(blocks):
        cols = slice(block * tile, (block + 1) * tile)
        begin = (block * tile) % span
        inner = slice(begin, begin + tile)
        upstream_all[:, cols] = do_ref[block * tile // span, :, inner]
        upstream = do_ref[block * tile // span, :, inner].astype(F32)
        attended = o_ref[block * tile // span, :, inner].astype(F32)
        centre = jnp.sum(upstream * attended, axis=0, keepdims=True)
        query = q_ref[:, cols].astype(F32) * 0.125
        scaled[:, cols] = query.astype(BF)
        full = jnp.concatenate([query, doc_q[:, cols], minus_split(lse_ref[0, :, cols]), tail], 0)
        qaug[cols, :] = full.T.astype(BF)
        full = jnp.concatenate([upstream, minus_split(centre), zeros8[:, cols], tail], 0)
        doaug[cols, :] = full.T.astype(BF)
    kaug[:head, :] = k_ref[...]
    kaug[head : head + 16, :] = jnp.concatenate([doc_k, ones3], 0).astype(BF)
    kaug[head + 16 :, :] = jnp.zeros((LANES - head - 16, length), BF)
    vaug[:head, :] = v_ref[...]
    vaug[head : head + 16, :] = jnp.concatenate([ones3, zeros8], 0).astype(BF)
    vaug[head + 16 :, :] = jnp.zeros((LANES - head - 16, length), BF)
    circle = bias_circle(rel_ref, bucket_ref, pl.program_id(0) + offset // (3 * head), tile).T
    query_row = lax.broadcasted_iota(jnp.int32, (tile, tile), 0)
    key_col = lax.broadcasted_iota(jnp.int32, (tile, tile), 1)
    band[:tile, :] = jnp.where(key_col <= query_row, circle, -BIG)
    band[tile:, :] = jnp.where(key_col > query_row, circle, 0.0)
    diagonal[...] = jnp.zeros_like(diagonal)
    for j in range(blocks):
        keys = slice(j * tile, (j + 1) * tile)
        dk = jnp.zeros((head, tile), F32)
        dv = jnp.zeros((head, tile), F32)
        at = j * tile
        while at < length:
            end = min(length, (at // CHUNK + 1) * CHUNK)
            rows = slice(at, end)
            part = contract(qaug[rows, :], kaug[:, keys], 1, 0)
            near = max(0, min(end, (j + 2) * tile) - at)
            if near:
                top = at - j * tile
                part = jnp.concatenate(
                    [part[:near] + band[top : top + near, :]] + ([part[near:]] if at + near < end else []),
                    axis=0,
                )
            probs = jnp.exp(part)
            score_grads = probs * contract(doaug[rows, :], vaug[:, keys], 1, 0)
            if at == j * tile:
                diagonal[...] += score_grads[:tile]
            if at <= (j + 1) * tile < end:
                begin = (j + 1) * tile - at
                diagonal[...] += jnp.where(
                    key_col > query_row, score_grads[begin : begin + tile], 0.0
                )
            weights = probs.astype(BF)
            short = score_grads.astype(BF)
            dv = dv + contract(upstream_all[:, rows], weights, 1, 0)
            dk = dk + contract(scaled[:, rows], short, 1, 0)
            dq = contract(kaug[:head, keys], short, 1, 1)
            if j == 0:
                dq_sum[:, rows] = dq
            else:
                dq_sum[:, rows] += dq
            at = end
        begin = (j * tile) % span
        inner = slice(begin, begin + tile)
        together = jnp.concatenate([dq_sum[:, keys] * 0.125, dk, dv], axis=0).astype(BF)
        grads[:, keys] = together
    step = pl.program_id(0)
    share_refs = (one_ref, two_ref, three_ref, four_ref)
    own = slab_ref[:, offset : offset + 3 * head]
    for later in range(1, count):
        begin = offset + 3 * head * later
        own = jnp.where(pl.program_id(0) == later, slab_ref[:, begin : begin + 3 * head], own)
    here = pl.ds(pl.multiple_of(step * 3 * head, 16), 3 * head)
    all_grads[here, :] = grads[...]

    @pl.when(step == count - 1)
    def _():
        slab = slab_ref[:, offset : offset + 3 * head * count]
        for index in range(length // span):
            spare[index] = contract(
                all_grads[:, index * span : (index + 1) * span], slab, 0, 1
            ).astype(BF)
        for mask, ref in enumerate(share_refs):
            ref[...] = spare[me_ref[0] ^ mask]

    products = contract(grads[...], n1_ref[...], 1, 0).T
    share = jnp.sum(products * own.astype(F32), axis=1, keepdims=True)
    rows, columns = weight_ref.shape
    weight_ref[...] = jnp.concatenate(
        [products, share, jnp.zeros((rows, columns - 3 * head - 1), F32)], axis=1
    ).astype(BF)
    skew = diagonal[...].T
    step = 1
    while step < tile:
        skew = jnp.where((query_row & step) != 0, pltpu.roll(skew, tile - step, 1), skew)
        step *= 2
    dist_ref[0] = jnp.sum(skew, axis=0, keepdims=True)


def attend_backward(
    first, count, qkv_t, upstream, attended, lse, starts, me, rel, bucket, n1, slab, heads, head
):
    length = qkv_t.shape[1]
    docs = starts.shape[1]
    spans, _, span = attended.shape
    width = n1.shape[1]

    def rows_of(part):
        return pl.BlockSpec((head, length), lambda h: (3 * (first + h) + part, 0))

    by_span = pl.BlockSpec((spans, head, span), lambda h: (0, first + h, 0))
    smem = pl.BlockSpec(memory_space=pltpu.SMEM)
    columns = 3 * head + 1
    columns += -columns % LANES
    share = pl.BlockSpec((span, width), lambda h: (0, 0))
    return pl.pallas_call(
        functools.partial(backward_kernel, count, head, 3 * first * head, TILE, docs),
        grid=(count,),
        in_specs=[
            smem,
            smem,
            smem,
            pl.BlockSpec((1, TILE), lambda h: (0, 0)),
            rows_of(0),
            rows_of(1),
            rows_of(2),
            by_span,
            by_span,
            pl.BlockSpec((1, 1, length), lambda h: (first + h, 0, 0)),
            pl.BlockSpec(n1.shape, lambda h: (0, 0)),
            pl.BlockSpec(slab.shape, lambda h: (0, 0)),
        ],
        out_specs=[
            share,
            share,
            share,
            share,
            pl.BlockSpec((1, 1, TILE), lambda h: (h, 0, 0)),
            pl.BlockSpec((width, columns), lambda h: (0, h)),
        ],
        out_shape=[jax.ShapeDtypeStruct((span, width), BF)] * 4
        + [
            jax.ShapeDtypeStruct((count, 1, TILE), F32),
            jax.ShapeDtypeStruct((width, count * columns), BF),
        ],
        scratch_shapes=[
            pltpu.VMEM((length, LANES), BF),
            pltpu.VMEM((length, LANES), BF),
            pltpu.VMEM((LANES, length), BF),
            pltpu.VMEM((LANES, length), BF),
            pltpu.VMEM((head, length), BF),
            pltpu.VMEM((2 * TILE, TILE), F32),
            pltpu.VMEM((head, length), F32),
            pltpu.VMEM((TILE, TILE), F32),
            pltpu.VMEM((3 * head, length), BF),
            pltpu.VMEM((head, length), BF),
            pltpu.VMEM((count * 3 * head, length), BF),
            pltpu.VMEM((spans, span, width), BF),
        ],
        compiler_params=pltpu.CompilerParams(vmem_limit_bytes=60 * 2**20),
        name="attend_backward",
    )(starts, me, rel, bucket, qkv_t, qkv_t, qkv_t, upstream, attended, lse, n1, slab)


def pack_kernel(spans, head, me_ref, q_ref, k_ref, v_ref, router_ref, one_ref, two_ref, slab_ref):
    rows, width = q_ref.shape
    local = width // spans
    for span in range(spans):

        @pl.when(me_ref[0] == span)
        def _():
            pieces = []
            for at in range(span * local, (span + 1) * local, head):
                pieces += [ref[:, at : at + head] for ref in (q_ref, k_ref, v_ref)]
            slab_ref[:, : 3 * local] = jnp.concatenate(pieces, axis=1)

    top = [ref[...].astype(F32) for ref in (router_ref, one_ref, two_ref)]
    used = sum(part.shape[0] for part in top)
    free = slab_ref.shape[1] - 3 * local
    tail = jnp.concatenate(top + [jnp.zeros((free - used, rows), F32)], axis=0)
    tail = jnp.concatenate([tail, jnp.zeros((free, LANES - rows), F32)], axis=1)
    slab_ref[:, 3 * local :] = tail.T[:rows].astype(BF)


def pack_slab(me, w_query, w_key, w_value, w_router, gain_attn, gain_moe, spans, head):
    rows, width = w_query.shape
    columns = 3 * width // spans + w_router.shape[1] + 2
    columns += -columns % LANES
    return pl.pallas_call(
        functools.partial(pack_kernel, spans, head),
        in_specs=[pl.BlockSpec(memory_space=pltpu.SMEM)]
        + [pl.BlockSpec(memory_space=pltpu.VMEM)] * 6,
        out_specs=pl.BlockSpec(memory_space=pltpu.VMEM),
        out_shape=jax.ShapeDtypeStruct((rows, columns), BF),
        name="pack_slab",
    )(me, w_query, w_key, w_value, w_router.T, gain_attn[None], gain_moe[None])


def out_kernel(x_ref, gain_ref, grads_ref, *refs):
    share_refs, out_ref = refs[:-1], refs[-1]
    dn = sum(ref[...].astype(F32) for ref in share_refs)
    x = x_ref[...].astype(F32)
    scale = lax.rsqrt(jnp.mean(x * x, axis=1, keepdims=True) + EPS)
    normed = x * scale
    scaled = dn * gain_ref[...]
    out_ref[...] = grads_ref[...] + scale * (
        scaled - normed * jnp.mean(scaled * normed, axis=1, keepdims=True)
    )


def rows_out(x, gain, grads, shares):
    span, width = x.shape
    part = span // 4
    rows = pl.BlockSpec((part, width), lambda i: (i, 0))
    return pl.pallas_call(
        out_kernel,
        grid=(4,),
        in_specs=[rows, pl.BlockSpec((1, width), lambda i: (0, 0)), rows] + [rows] * len(shares),
        out_specs=rows,
        out_shape=jax.ShapeDtypeStruct(x.shape, F32),
        compiler_params=pltpu.CompilerParams(vmem_limit_bytes=50 * 2**20),
        name="rows_out",
    )(x, gain, grads, *shares)


def project_kernel(wide, pieces, count_old, at_ref, *refs):
    x_refs, slab_ref, gain_ref, refs = refs[:pieces], refs[pieces], refs[pieces + 1], refs[pieces + 2 :]
    if len(refs) == count_old + 5:
        in_ref, w_ref = refs[0], refs[1]
        packed_ref = refs[-1]
        refs = refs[2:-1]
        width, quarter = in_ref.shape
        packed_ref[:width, :] = in_ref[...]
        for at in range(0, width, quarter):
            packed_ref[width + at : width + at + quarter, :] = w_ref[:, at : at + quarter]
    n1_ref, qkv_ref = refs[count_old:]
    x = jnp.concatenate([ref[...].astype(F32) for ref in x_refs], axis=0)
    scale = lax.rsqrt(jnp.mean(x * x, axis=1, keepdims=True) + EPS)
    n1 = (x * scale * gain_ref[...]).astype(BF)
    n1_ref[...] = n1
    qkv_ref[...] = contract(slab_ref[:, :wide], n1, 0, 1).astype(BF)


def project(at, rows, slab, gain, wide, spans, old, expert=()):
    width = rows[0].shape[1]
    span = sum(piece.shape[0] for piece in rows)
    packed = [jax.ShapeDtypeStruct((2 * width, array.shape[1]), BF) for array in expert[:1]]
    first = 3 + len(rows) + len(expert)

    def whole(array):
        return pl.BlockSpec(array.shape, lambda i, at: (0, 0))

    return pl.pallas_call(
        functools.partial(project_kernel, wide, len(rows), len(old)),
        grid_spec=pltpu.PrefetchScalarGridSpec(
            num_scalar_prefetch=1,
            grid=(1,),
            in_specs=[whole(array) for array in (*rows, slab, gain, *expert)]
            + [pl.BlockSpec(memory_space=pl.ANY)] * len(old),
            out_specs=[
                pl.BlockSpec((span, width), lambda i, at: (at[0], 0)),
                pl.BlockSpec((wide, span), lambda i, at: (0, at[0])),
            ]
            + [whole(array) for array in packed],
        ),
        out_shape=[
            jax.ShapeDtypeStruct((spans * span, width), BF),
            jax.ShapeDtypeStruct((wide, spans * span), BF),
        ]
        + packed,
        input_output_aliases={first + index: index for index in range(len(old))},
        compiler_params=pltpu.CompilerParams(vmem_limit_bytes=40 * 2**20),
        name="project",
    )(at, *rows, slab, gain, *expert, *old)


def place_of(slot_ref, part, part_rows):
    slots = lax.broadcasted_iota(jnp.int32, (part_rows, slot_ref.shape[1]), 0) + part * part_rows
    return jnp.where(slots == slot_ref[...], 1.0, 0.0).astype(BF)


def normed_rows(hidden, gain):
    scale = lax.rsqrt(jnp.mean(hidden * hidden, axis=1, keepdims=True) + EPS)
    normed = hidden * scale
    return scale, normed, (normed * gain).astype(BF)


def router_probs(rows, router, experts):
    logits = contract(rows, router, 1, 0)
    lane = lax.broadcasted_iota(jnp.int32, logits.shape, 1)
    logits = jnp.where(lane < experts, logits, -BIG)
    shifted = jnp.exp(logits - jnp.max(logits, axis=1, keepdims=True))
    return shifted / jnp.sum(shifted, axis=1, keepdims=True)


def slots_kernel(rows_ref, slot_ref, *part_refs):
    for part, ref in enumerate(part_refs):
        ref[...] = contract(place_of(slot_ref, part, ref.shape[0]), rows_ref[...], 1, 0).astype(BF)


def into_slots(rows, slot, parts, part_rows):
    vmem = pl.BlockSpec(memory_space=pltpu.VMEM)
    return pl.pallas_call(
        slots_kernel,
        in_specs=[vmem] * 2,
        out_specs=[vmem] * parts,
        out_shape=[jax.ShapeDtypeStruct((part_rows, rows.shape[1]), BF)] * parts,
        name="into_slots",
    )(rows, slot)


def into_kernel(parts, x_ref, mixed_ref, top_ref, low_ref, gain_ref, slot_ref, hidden_ref, *part_refs):
    out_ref = part_refs[-1]
    half, columns = top_ref.shape[1:]
    for begin, ref in ((0, top_ref), (half, low_ref)):
        for core in range(2):
            out_ref[begin : begin + half, core * columns : (core + 1) * columns] = ref[core]
    hidden = x_ref[...].astype(F32) + contract(mixed_ref[...], out_ref[...], 0, 0)
    hidden_ref[...] = hidden
    _, _, n2 = normed_rows(hidden, gain_ref[...])
    for part in range(parts):
        rows = part_refs[part].shape[0]
        part_refs[part][...] = contract(place_of(slot_ref, part, rows), n2, 1, 0).astype(BF)


def rows_into_experts(x, mixed, output_halves, gain, slot, parts, part_rows):
    span, width = x.shape
    if len(output_halves) == 1:
        blocks = output_halves[0].reshape(2, width // 2, 2, width // 2).transpose(0, 2, 1, 3)
        output_halves = [blocks[0], blocks[1]]
    vmem = pl.BlockSpec(memory_space=pltpu.VMEM)
    return pl.pallas_call(
        functools.partial(into_kernel, parts),
        in_specs=[vmem] * 6,
        out_specs=[vmem] * (2 + parts),
        out_shape=[jax.ShapeDtypeStruct((span, width), F32)]
        + [jax.ShapeDtypeStruct((part_rows, width), BF)] * parts
        + [jax.ShapeDtypeStruct((width, width), BF)],
        compiler_params=pltpu.CompilerParams(vmem_limit_bytes=50 * 2**20),
        name="rows_into_experts",
    )(x, mixed, *output_halves, gain, slot)


def back_kernel(hidden_ref, up_ref, out_ref, gain_ref, slot_ref, *refs):
    part_refs = refs[:-3]
    grads_ref, do_ref, grad_gain_ref = refs[-3:]
    dn = None
    for part, part_ref in enumerate(part_refs):
        rows = contract(place_of(slot_ref, part, part_ref.shape[0]), part_ref[...], 0, 0)
        dn = rows if dn is None else dn + rows
    gain = gain_ref[...]
    scale, normed, _ = normed_rows(hidden_ref[...], gain)
    grad_gain_ref[...] = jnp.sum(dn * normed, axis=0, keepdims=True)
    scaled = dn * gain
    grads = up_ref[...].astype(F32) + scale * (
        scaled - normed * jnp.mean(scaled * normed, axis=1, keepdims=True)
    )
    grads_ref[...] = grads
    do_ref[...] = contract(out_ref[...], grads.astype(BF), 1, 1).astype(BF)


def rows_from_experts(hidden, upstream, full_output, gain, slot, back):
    span, width = hidden.shape
    vmem = pl.BlockSpec(memory_space=pltpu.VMEM)
    return pl.pallas_call(
        back_kernel,
        in_specs=[vmem] * (5 + len(back)),
        out_specs=[vmem] * 3,
        out_shape=[
            jax.ShapeDtypeStruct((span, width), F32),
            jax.ShapeDtypeStruct((width, span), BF),
            jax.ShapeDtypeStruct((1, width), F32),
        ],
        compiler_params=pltpu.CompilerParams(vmem_limit_bytes=50 * 2**20),
        name="rows_from_experts",
    )(hidden, upstream, full_output, gain, slot, *back)


def early_kernel(experts, spans, grads_ref, mixed_ref, gain_ref, *refs):
    router_refs, early_ref = refs[:-1], refs[-1]
    grad_output = contract(mixed_ref[...], grads_ref[...].astype(BF), 1, 0)
    width = grad_output.shape[1]
    local = width // spans
    share = experts // spans
    column = jnp.broadcast_to(gain_ref[...], (8, width)).T[:, :1]
    free = early_ref.shape[2] - local - share - 1
    grad_router = sum(ref[...] for ref in router_refs)
    for span in range(spans):
        early_ref[span] = jnp.concatenate(
            [
                grad_output[:, span * local : (span + 1) * local],
                grad_router[:, span * share : (span + 1) * share],
                column,
                jnp.zeros((width, free), F32),
            ],
            axis=1,
        ).astype(BF)


def early_sums(grads, mixed, grad_router, grad_gain, experts, spans):
    width = grads.shape[1]
    columns = width // spans + experts // spans + 1
    columns += -columns % LANES
    vmem = pl.BlockSpec(memory_space=pltpu.VMEM)
    return pl.pallas_call(
        functools.partial(early_kernel, experts, spans),
        in_specs=[vmem] * (3 + len(grad_router)),
        out_specs=vmem,
        out_shape=jax.ShapeDtypeStruct((spans, width, columns), BF),
        compiler_params=pltpu.CompilerParams(vmem_limit_bytes=50 * 2**20),
        name="early_sums",
    )(grads, mixed, grad_gain, *grad_router)


def sums_kernel(heads, head_size, buckets, at, fsdp_count, weights_ref, early_ref, dist_ref, bucket_ref, out_ref):
    width = weights_ref.shape[0]
    columns = weights_ref.shape[1]
    early = early_ref[0].astype(F32)
    for span in range(1, early_ref.shape[0]):
        early = early + early_ref[span].astype(F32)
    index = lax.broadcasted_iota(jnp.int32, (buckets, bucket_ref.shape[1]), 0)
    onehot = jnp.where(index == bucket_ref[...], 1.0, 0.0)
    dist = jnp.concatenate([dist_ref[head] for head in range(heads)], axis=0)
    dist = jnp.concatenate([dist, jnp.zeros((8 - heads, dist.shape[1]), F32)], axis=0)
    rel = lax.dot_general(
        dist, onehot, (((1,), (1,)), ((), ())), precision=HIGH, preferred_element_type=F32
    )
    last = lax.broadcasted_iota(jnp.int32, rel.shape, 1) == buckets - 1
    rel = jnp.where(last, 0.0, rel)
    rel = jnp.where(last, -jnp.sum(rel, axis=1, keepdims=True), rel)
    rows_here = width // fsdp_count
    if heads * buckets == rows_here:
        column = jnp.concatenate([rel.T[:, head : head + 1] for head in range(heads)], axis=0)
        column = jnp.concatenate([column] * fsdp_count, axis=0)
        lane = lax.broadcasted_iota(jnp.int32, early.shape, 1)
        early = jnp.where(lane == at, column, early)
    columns //= heads
    used = 3 * head_size
    parts = [weights_ref[:, head * columns : head * columns + used] for head in range(heads)]
    shares = [
        weights_ref[:, head * columns + used : head * columns + used + 1] for head in range(heads)
    ]
    parts = parts + [early.astype(BF)[:, : at + 1]] + shares
    free = out_ref.shape[1] - sum(part.shape[1] for part in parts)
    out_ref[...] = jnp.concatenate(parts + [jnp.zeros((width, free), BF)], axis=1)


def all_sums(weight_grads, early, distances, bucket, head, buckets, at, fsdp_count):
    width = weight_grads.shape[0]
    heads = distances.shape[0]
    total = heads * (3 * head + 1) + at + 1
    total += -total % LANES
    vmem = pl.BlockSpec(memory_space=pltpu.VMEM)
    return pl.pallas_call(
        functools.partial(sums_kernel, heads, head, buckets, at, fsdp_count),
        in_specs=[vmem] * 4,
        out_specs=vmem,
        out_shape=jax.ShapeDtypeStruct((width, total), BF),
        compiler_params=pltpu.CompilerParams(vmem_limit_bytes=50 * 2**20),
        name="all_sums",
    )(weight_grads, early, distances, bucket)


def final_kernel(experts, hidden_ref, gain_ref, router_ref, chosen_ref, slot_ref, *refs):
    part_refs, output_ref = refs[:-1], refs[-1]
    hidden = hidden_ref[...]
    _, _, n2 = normed_rows(hidden, gain_ref[...])
    probs = router_probs(n2, router_ref[...], experts)
    gate = jnp.sum(probs * chosen_ref[...], axis=1, keepdims=True)
    y = None
    for part, part_ref in enumerate(part_refs):
        rows = contract(place_of(slot_ref, part, part_ref.shape[0]), part_ref[...], 0, 0)
        y = rows if y is None else y + rows
    output_ref[...] = (hidden + gate * y).astype(BF)


def final_output(hidden, gain, router, chosen, slot, parts, experts):
    vmem = pl.BlockSpec(memory_space=pltpu.VMEM)
    return pl.pallas_call(
        functools.partial(final_kernel, experts),
        in_specs=[vmem] * (5 + len(parts)),
        out_specs=vmem,
        out_shape=jax.ShapeDtypeStruct(hidden.shape, BF),
        compiler_params=pltpu.CompilerParams(vmem_limit_bytes=50 * 2**20),
        name="final_output",
    )(hidden, gain, router, chosen, slot, *parts)


def expert_kernel(experts, inputs, count_old, me_ref, core_ref, router_ref, *refs):
    x_refs, up_refs = refs[:inputs], refs[inputs : 2 * inputs]
    own_hbm, near_hbm, far_hbm, in_hbm, out_hbm = refs[2 * inputs : 2 * inputs + 5]
    refs = refs[2 * inputs + 5 + count_old :]
    ours_ref, theirs_ref, act_ref, pre_ref, dy_ref, w_ref, y_sum, dn_sum, sems = refs
    count, width = x_refs[0].shape
    rows = count // 2
    quarter = w_ref.shape[2]
    first = core_ref[0] == 0
    part, pair = pl.program_id(0), pl.program_id(1)
    copies = [
        [
            pltpu.make_async_copy(own_hbm, w_ref.at[0], sems.at[0]),
            pltpu.make_async_copy(near_hbm, w_ref.at[1], sems.at[1]),
        ],
        [
            pltpu.make_async_copy(far_hbm, w_ref.at[2], sems.at[2]),
            pltpu.make_async_copy(in_hbm, w_ref.at[3, pl.ds(0, width)], sems.at[3]),
            pltpu.make_async_copy(out_hbm, w_ref.at[3, pl.ds(width, width)], sems.at[4]),
        ],
    ]

    @pl.when((part == 0) & (pair == 0))
    def _():
        for copy in copies[0] + copies[1]:
            copy.start()

    def parted(index):
        x = x_refs[index][...]

        @pl.when(pair == 0)
        def _():
            probs = router_probs(x, router_ref[...], experts)
            lane = lax.broadcasted_iota(jnp.int32, probs.shape, 1)
            gate = jnp.sum(jnp.where(lane == me_ref[0], probs, 0.0), axis=1, keepdims=True)
            dy_ref[...] = (gate * up_refs[index][...].astype(F32)).astype(BF)

        def blocks(half):
            if index == 0:
                for copy in copies[half]:
                    copy.wait()
            w_in = jnp.concatenate([w_ref[2 * half + b, :width, :] for b in range(2)], axis=1)
            w_out = jnp.concatenate(
                [
                    jnp.concatenate(
                        [
                            w_ref[2 * half + b, at : at + quarter, :]
                            for at in range(width, 2 * width, quarter)
                        ],
                        axis=1,
                    )
                    for b in range(2)
                ],
                axis=0,
            )
            pre = contract(x, w_in, 1, 0)
            root = 0.7978845608028654
            square = pre * pre
            tanh = jnp.tanh(pre * (root + (root * 0.044715) * square))
            upper = 0.5 + 0.5 * tanh
            act = (pre * upper).astype(BF)
            slope = upper + (pre * upper) * (1.0 - tanh) * (root + (root * 0.134145) * square)
            act_ref[...] = act
            pre_grads = (contract(dy_ref[...], w_out, 1, 1) * slope).astype(BF)
            pre_ref[...] = pre_grads
            y = contract(act, w_out, 1, 0)
            dn = contract(pre_grads, w_in, 1, 1)
            if half == 0:
                y_sum[...] = y
                dn_sum[...] = dn
                return
            for some, total in (
                (slice(0, rows), y_sum[...] + y),
                (slice(rows, count), dn_sum[...] + dn),
            ):
                one, two = total[:rows], total[rows:]
                ours_ref[0, some, :] = jnp.where(first, one, two).astype(BF)
                theirs_ref[0, some, :] = jnp.where(first, two, one).astype(BF)

        for half in range(2):
            pl.when(pair == half)(functools.partial(blocks, half))

    for index in range(inputs):
        pl.when(part == index)(functools.partial(parted, index))


def expert_part(part, parts, me, core, rows, upstream, router, weights, old, experts):
    inputs = len(rows)
    count, width = rows[0].shape
    quarter = weights[0].shape[1]
    hidden = 4 * quarter
    total = count * inputs * parts
    begin = part * inputs
    first = 3 + 2 * inputs + len(weights)
    smem = pl.BlockSpec(memory_space=pltpu.SMEM)
    hbm = pl.BlockSpec(memory_space=pl.ANY)
    share = pl.BlockSpec((1, count, width), lambda i, j: (i, 0, 0))
    inner = pl.BlockSpec((count, 2 * quarter), lambda i, j: (begin + i, j))
    return pl.pallas_call(
        functools.partial(expert_kernel, experts, inputs, len(old)),
        grid=(inputs, 2),
        in_specs=[smem] * 2
        + [
            pl.BlockSpec(array.shape, lambda i, j: (0, 0))
            for array in (router, *rows, *upstream)
        ]
        + [hbm] * (len(weights) + len(old)),
        out_specs=[share] * 2
        + [inner] * 2
        + [pl.BlockSpec((count, width), lambda i, j: (begin + i, 0))],
        out_shape=[jax.ShapeDtypeStruct((inputs, count, width), BF)] * 2
        + [jax.ShapeDtypeStruct((total, size), BF) for size in (hidden, hidden, width)],
        scratch_shapes=[
            pltpu.VMEM((4, 2 * width, quarter), BF),
            pltpu.VMEM((count, width), F32),
            pltpu.VMEM((count, width), F32),
            pltpu.SemaphoreType.DMA((5,)),
        ],
        input_output_aliases={first + index: 2 + index for index in range(len(old))},
        compiler_params=pltpu.CompilerParams(vmem_limit_bytes=56 * 2**20),
        name="expert_part",
    )(me, core, router, *rows, *upstream, *weights, *old)


def combine_kernel(inputs, experts, core_ref, me_ref, ours_ref, theirs_ref, router_ref, *refs):
    x_refs, up_refs, refs = refs[:inputs], refs[inputs : 2 * inputs], refs[2 * inputs :]
    y_refs, dn_refs, grad_ref = refs[:inputs], refs[inputs : 2 * inputs], refs[-1]
    rows = y_refs[0].shape[0]
    router = router_ref[...]
    grad_router = None
    for index in range(inputs):
        x = x_refs[index][...]
        y = ours_ref[index, :rows, :].astype(F32) + theirs_ref[index, :rows, :].astype(F32)
        dn = ours_ref[index, rows:, :].astype(F32) + theirs_ref[index, rows:, :].astype(F32)
        probs = router_probs(x, router, experts)
        lane = lax.broadcasted_iota(jnp.int32, probs.shape, 1)
        chosen = jnp.where(lane == me_ref[0], 1.0, 0.0)
        gate = jnp.sum(probs * chosen, axis=1, keepdims=True)
        gate_grads = jnp.sum(up_refs[index][...].astype(F32) * y, axis=1, keepdims=True)
        logit_grads = (probs * (chosen * gate_grads - gate * gate_grads)).astype(BF)
        product = contract(x, logit_grads, 0, 0)
        grad_router = product if grad_router is None else grad_router + product
        y_refs[index][...] = y.astype(BF)
        dn_refs[index][...] = (dn + contract(logit_grads, router, 1, 1)).astype(BF)
    grad_ref[...] = grad_router


def combine_halves(me, core, ours, theirs, router, rows, upstream, experts):
    inputs, count, width = ours.shape

    def whole(array):
        return pl.BlockSpec(array.shape, lambda i, core: (0,) * array.ndim)

    own = pl.BlockSpec((count // 2, width), lambda i, core: (core[0], 0))
    out_shape = [jax.ShapeDtypeStruct((count // 2, width), BF)] * (2 * inputs)
    out_shape.append(jax.ShapeDtypeStruct(router.shape, F32))
    results = pl.pallas_call(
        functools.partial(combine_kernel, inputs, experts),
        grid_spec=pltpu.PrefetchScalarGridSpec(
            num_scalar_prefetch=1,
            grid=(1,),
            in_specs=[pl.BlockSpec(memory_space=pltpu.SMEM)]
            + [whole(array) for array in (ours, theirs, router)]
            + [own] * (2 * inputs),
            out_specs=[
                pl.BlockSpec(array.shape, lambda i, core: (0, 0)) for array in out_shape
            ],
        ),
        out_shape=out_shape,
        compiler_params=pltpu.CompilerParams(vmem_limit_bytes=50 * 2**20),
        name="combine_halves",
    )(core, me, ours, theirs, router, *rows, *upstream)
    return results[:inputs], results[inputs : 2 * inputs], results[-1]


def expert_grads_kernel(act_ref, pre_ref, dy_ref, *refs):
    x_refs = refs[:-4]
    one_ref, two_ref, keep_one, keep_two = refs[-4:]
    width = dy_ref.shape[1]
    quarter = act_ref.shape[1]
    mask = pl.program_id(0)
    rows = jnp.concatenate([ref[...] for ref in x_refs], axis=0)
    grad_in = contract(rows, pre_ref[...], 0, 0)
    grad_out = contract(act_ref[...], dy_ref[...], 0, 0)
    grad_out = jnp.concatenate(
        [grad_out[:, at : at + quarter] for at in range(0, width, quarter)], axis=0
    )
    for at in (1, 3):

        @pl.when(mask == at)
        def _():
            one_ref[0] = grad_in.astype(BF)

    for at in (2, 3):

        @pl.when(mask == at)
        def _():
            two_ref[0] = grad_out.astype(BF)

    for at in (0, 2):

        @pl.when(mask == at)
        def _():
            keep_one[0] = grad_in

    for at in (0, 1):

        @pl.when(mask == at)
        def _():
            keep_two[0] = grad_out


def expert_grads(kept, rows, quarter):
    act, pre, dy = kept
    total, width = dy.shape
    hidden = pl.BlockSpec((total, quarter), lambda f: (0, f))

    def whole(array):
        return pl.BlockSpec(array.shape, lambda f: (0, 0))

    def block(place):
        return pl.BlockSpec((1, width, quarter), lambda f: (place(f), 0, 0))

    return pl.pallas_call(
        expert_grads_kernel,
        grid=(act.shape[1] // quarter,),
        in_specs=[hidden, hidden, whole(dy)] + [whole(part) for part in rows],
        out_specs=[
            block(lambda f: f // 2),
            block(lambda f: jnp.maximum(f - 2, 0)),
            block(lambda f: f // 2),
            block(lambda f: jnp.minimum(f, 1)),
        ],
        out_shape=[jax.ShapeDtypeStruct((2, width, quarter), BF)] * 2
        + [jax.ShapeDtypeStruct((2, width, quarter), F32)] * 2,
        compiler_params=pltpu.CompilerParams(vmem_limit_bytes=50 * 2**20),
        name="expert_grads",
    )(act, pre, dy, *rows)


def settle_kernel(keep_one, keep_two, got_one, got_two, one_ref, two_ref):
    one_ref[...] = (keep_one[0].astype(F32) + got_one[0].astype(F32)).astype(BF)
    two_ref[...] = (keep_two[0].astype(F32) + got_two[0].astype(F32)).astype(BF)


def settle_step(keep_one, keep_two, got_one, got_two):
    _, width, quarter = keep_one.shape
    second = pl.BlockSpec((1, width, quarter), lambda i: (1, 0, 0))
    whole = pl.BlockSpec((width, quarter), lambda i: (0, 0))
    return pl.pallas_call(
        settle_kernel,
        grid=(1,),
        in_specs=[second] * 4,
        out_specs=[whole] * 2,
        out_shape=[jax.ShapeDtypeStruct((width, quarter), BF)] * 2,
        compiler_params=pltpu.CompilerParams(vmem_limit_bytes=50 * 2**20),
        name="settle_step",
    )(keep_one, keep_two, got_one, got_two)


def all_to_all(blocks, axis, groups=None):
    return lax.all_to_all(
        blocks, axis, split_axis=0, concat_axis=0, tiled=True, axis_index_groups=groups
    )


def pair_swap(block, axis, mask):
    count = lax.axis_size(axis)
    return lax.ppermute(block, axis, [(i, i ^ mask) for i in range(count)])


def tied(values, *others):
    return lax.optimization_barrier((values, others))[0]


def gather_pairs(rows, axis, groups, pairs, after):
    count = lax.axis_size(axis)
    if count > 8:
        return [lax.all_gather(rows, axis, axis=0, tiled=True)]
    core = lax.axis_index(axis) % 2
    columns = rows.shape[1] // 2
    low, high = rows[:, :columns], rows[:, columns:]
    mine = jnp.where(core == 0, low, high)
    got = pair_swap(jnp.where(core == 0, high, low), axis, 1)
    chip = jnp.where(core == 0, jnp.stack([mine, got]), jnp.stack([got, mine]))
    whole = all_to_all(jnp.broadcast_to(chip[None], (count // 2,) + chip.shape), axis, groups)
    whole = tied(whole.reshape(2, count * rows.shape[0] // 2, columns), after)
    return [
        lax.all_gather(part, axis, axis=0, tiled=False, axis_index_groups=pairs) for part in whole
    ]


def scatter_sums(rows, axis, groups):
    count = lax.axis_size(axis)
    here = rows.shape[0] // count
    if count > 8:
        blocks = all_to_all(rows.reshape(count, here, rows.shape[1]), axis)
        return jnp.sum(blocks.astype(F32), axis=0)
    core = lax.axis_index(axis) % 2
    split = rows.reshape(count // 2, 2, here, rows.shape[1])
    mine = lax.dynamic_index_in_dim(split, core, 1, keepdims=False)
    other = pair_swap(lax.dynamic_index_in_dim(split, 1 - core, 1, keepdims=False), axis, 1)
    chip = (mine.astype(F32) + other.astype(F32)).astype(BF)
    return jnp.sum(all_to_all(chip, axis, groups).astype(F32), axis=0)


def per_device(
    tokens, cotangent, doc_starts, routes, bucket_table, w_query, w_key, w_value, w_output,
    w_router, gain_attn, gain_moe, rel_bias, expert_in, expert_out,
):
    _, span, width = tokens.shape
    seq_count = lax.axis_size("seq")
    fsdp_count = lax.axis_size("fsdp")
    seq_me = lax.axis_index("seq")
    fsdp_me = lax.axis_index("fsdp")
    heads, buckets = rel_bias.shape
    local = width // seq_count
    head = local // heads
    experts = w_router.shape[1]
    rows_here = w_query.shape[0]
    quarter = expert_in.shape[2]
    cores = 2
    groups = [list(range(core, fsdp_count, cores)) for core in range(cores)]
    x = tokens[0]
    seq_index = seq_me.astype(jnp.int32)[None]
    expert_index = (fsdp_me // cores).astype(jnp.int32)[None]
    core_index = (fsdp_me % cores).astype(jnp.int32)[None]

    near = pair_swap(x, "seq", 1)
    far = pair_swap(x, "seq", 2)
    slab = pack_slab(
        seq_index, w_query, w_key, w_value, w_router, gain_attn, gain_moe, seq_count, head
    )
    slab = lax.all_gather(slab, "fsdp", axis=0, tiled=True)
    half = span // 2
    slab, near_half, far_half = lax.optimization_barrier((slab, near[:half], far[half:]))
    across = [pair_swap(near_half, "seq", 2), pair_swap(far_half, "seq", 1)]
    tail = slab[:, 3 * local :]
    full_router = jnp.pad(tail[:, :experts], ((0, 0), (0, -experts % LANES)))
    gains = tail[:, experts : experts + 2].astype(F32).T
    gain_one, gain_two = gains[:1], gains[1:2]
    own_gain = gain_attn.astype(F32)

    expert_me = fsdp_me // cores
    few = experts <= 4
    route, bucket_table, rel_bias = tied((routes[0], bucket_table[:TILE], rel_bias), slab)
    chosen = (route[:, None] == jnp.arange(LANES, dtype=jnp.int32)[None, :]).astype(F32)
    before = (
        jnp.arange(span, dtype=jnp.int32)[:, None] > jnp.arange(span, dtype=jnp.int32)[None, :]
    ).astype(BF)
    ranks = jnp.dot(before, chosen.astype(BF), preferred_element_type=F32)
    capacity = max(2, 2 * span // experts)
    target = route ^ expert_me if few else route
    slot = target * capacity + jnp.sum(ranks * chosen, axis=1).astype(jnp.int32)
    slot = slot[None]
    part_count = 4
    part_rows = experts * capacity // part_count

    def exchange(parts):
        if few:
            return [parts[0]] + [
                pair_swap(parts[mask], "fsdp", cores * mask) for mask in range(1, part_count)
            ]
        blocks = jnp.concatenate(parts, axis=0).reshape(experts, capacity, width)
        blocks = all_to_all(blocks, "fsdp", groups).reshape(part_count, part_rows, width)
        return [blocks[part] for part in range(part_count)]

    old = ()
    for mask, part in enumerate((x, near, far)):
        old = project(
            (seq_me ^ mask).astype(jnp.int32)[None], (part,), slab, gain_one, 3 * local, seq_count, old,
            () if mask < 2 else (expert_in[0], expert_out[0]),
        )
    weights = tied(old[2], across)
    w_near = pair_swap(weights, "seq", 1)
    w_far = pair_swap(weights, "seq", 2)
    up_rows, old = lax.optimization_barrier((cotangent[0], old[:2]))
    w_output = tied(w_output, slab)
    upstream_parts = into_slots(up_rows, slot, part_count, part_rows)
    upstream_parts = exchange(upstream_parts)
    n1_all, qkv_t = project(
        (seq_me ^ 3).astype(jnp.int32)[None], across, slab, gain_one, 3 * local, seq_count, old,
    )
    rel = rel_bias.astype(F32)
    bucket = bucket_table[None]
    attended, lse = attend_forward(
        qkv_t, doc_starts, rel, bucket, heads, head, seq_count
    )
    mixed = all_to_all(attended, "seq").reshape(width, span)
    pairs = [list(range(at, at + cores)) for at in range(0, fsdp_count, cores)]
    output_halves = gather_pairs(w_output, "fsdp", groups, pairs, (attended, upstream_parts))

    def of_chip(rows):
        return lax.all_gather(rows, "fsdp", axis=0, tiled=True, axis_index_groups=pairs)

    mixed, output_halves, upstream_parts, w_near, w_far = lax.optimization_barrier(
        (mixed, output_halves, upstream_parts, w_near, w_far)
    )

    hidden, *parts, full_output = rows_into_experts(
        x, mixed, output_halves, gain_two, slot, part_count, part_rows
    )
    w_near, w_far, parts = lax.optimization_barrier((w_near, w_far, parts))
    w_across = [pair_swap(w_near[:width], "seq", 2), pair_swap(w_far[width:], "seq", 1)]
    weights = [weights, w_near, w_far] + w_across
    arrived = exchange(parts)
    kept = ()
    upstream_parts = [of_chip(one) for one in tied(upstream_parts, parts)]
    chip_rows, ys, back, pairs_of_shares = [], [], [], []
    grad_router = []
    steps = part_count // 2
    for part in range(steps):
        some = slice(part * part_count // steps, (part + 1) * part_count // steps)
        rows, some_up = arrived[some], upstream_parts[some]
        if part:
            rows = tied(rows, kept)
        rows = [of_chip(one) for one in rows]
        if not part:
            rows, upstream_parts = lax.optimization_barrier((rows, upstream_parts))
            some_up = upstream_parts[some]
        chip_rows += rows
        ours, theirs, *kept = expert_part(
            part, steps, expert_index, core_index, rows, some_up, full_router, weights, kept,
            experts,
        )
        pairs_of_shares.append((ours, pair_swap(theirs, "fsdp", 1), rows, some_up))
    for ours, theirs, rows, some_up in pairs_of_shares[::-1]:
        ours, theirs = tied((ours, theirs), back)
        some_ys, dns, product = combine_halves(
            expert_index, core_index, ours, theirs, full_router, rows, some_up, experts
        )
        ys = list(some_ys) + ys
        back = list(dns) + back
        grad_router.append(product)
    kept = tied(kept, back)
    back = exchange(back)
    one, two, keep_one, keep_two = expert_grads(kept, chip_rows, quarter)
    back = tied(back, one, two)
    got_one = pair_swap(one, "seq", 1)
    got_two = pair_swap(two, "seq", 2)

    hidden_grads, mixed_grads, grad_gain = rows_from_experts(
        hidden, cotangent[0], full_output, gain_two, slot, back
    )
    ys = exchange(tied(ys, mixed_grads))
    early = early_sums(hidden_grads, mixed, grad_router, grad_gain, experts, seq_count)
    moved = all_to_all(mixed_grads.reshape(seq_count, local, span), "seq")
    settled_sum = [keep[0] + got[0].astype(F32) for keep, got in ((keep_one, got_one), (keep_two, got_two))]
    one, two = settle_step(keep_one, keep_two, got_one, got_two)
    got_one = pair_swap(one, "seq", 2)
    got_two = pair_swap(two, "seq", 1)
    early = all_to_all(tied(early, moved), "seq")
    *shares, distances, weight_grads = attend_backward(
        0, heads, qkv_t, moved, attended, lse, doc_starts, seq_index,
        rel, bucket, n1_all, slab, heads, head,
    )
    shares, distances, weight_grads, got_one, got_two, ys = lax.optimization_barrier(
        (shares, distances, weight_grads, got_one, got_two, ys)
    )
    output = final_output(hidden, gain_two, full_router, chosen, slot, ys, experts)
    shares = [shares[0]] + [
        pair_swap(shares[mask], "seq", mask) for mask in range(1, seq_count)
    ]
    grad_expert_in, grad_expert_out = [
        total + got.astype(F32) for total, got in zip(settled_sum, (got_one, got_two))
    ]
    grad_expert_out = jnp.concatenate(
        [grad_expert_out[at : at + quarter] for at in range(0, width, quarter)], axis=1
    )

    share = experts // seq_count
    rel_count = heads * buckets
    at = local + share + 1
    sums = all_sums(weight_grads, early, distances, bucket, head, buckets, at, fsdp_count)
    summed = scatter_sums(sums, "fsdp", groups)
    summed, shares = lax.optimization_barrier((summed, shares))
    input_grads = rows_out(x, gain_one, hidden_grads, shares)
    by_head = [summed[:, begin : begin + 3 * head] for begin in range(0, 3 * local, 3 * head)]
    summed = summed[:, 3 * local :]
    sum_gain_attn = jnp.sum(summed[:, at + 1 : at + 1 + heads], axis=1) / own_gain
    sum_gain_attn = sum_gain_attn + sum(
        pair_swap(sum_gain_attn, "seq", mask) for mask in range(1, seq_count)
    )
    if rows_here == rel_count:
        sum_rel = summed[:rel_count, local + share + 1].reshape(heads, buckets)
    else:
        onehot = bucket_table[:, None] == jnp.arange(buckets - 1, dtype=jnp.int32)[None, :]
        below = jnp.dot(distances[:, 0], onehot.astype(F32), precision=HIGH)
        grad_rel = jnp.concatenate([below, -jnp.sum(below, axis=1, keepdims=True)], axis=1)
        sum_rel = lax.psum(grad_rel, "fsdp")
    heads_sum = [
        jnp.concatenate([part[:, at : at + head] for part in by_head], axis=1)
        for at in range(0, 3 * head, head)
    ]
    return (
        output[None],
        input_grads[None],
        heads_sum[0],
        heads_sum[1],
        heads_sum[2],
        summed[:, :local],
        summed[:, local : local + share],
        sum_gain_attn,
        summed[:, local + share],
        sum_rel,
        grad_expert_in[None],
        grad_expert_out[None],
    )


def solution(mesh):
    rows = P("fsdp", "seq", None)
    weight = P("fsdp", None)
    shared = P("fsdp", "seq")
    return jax.shard_map(
        per_device,
        mesh=mesh,
        in_specs=(
            rows, rows, weight, shared, P(), weight, weight, weight, weight, weight,
            P("fsdp"), P("fsdp"), P("seq", None), P("fsdp", None, "seq"), rows,
        ),
        out_specs=(
            rows, rows, shared, shared, shared, shared, shared, P("fsdp"), P("fsdp"),
            P("seq", None), P("fsdp", None, "seq"), rows,
        ),
        check_vma=False,
    )
```

```python
import functools

import jax
import jax.numpy as jnp
from jax import lax
from jax.experimental import pallas as pl
from jax.experimental.pallas import tpu as pltpu
from jax.sharding import PartitionSpec as P

EPS = 1e-06
HIGH = lax.Precision.HIGHEST
BIG = 1e30
TILE = 256
LANES = 128
CHUNK = 1024
BF = jnp.bfloat16
F32 = jnp.float32


def contract(left, right, left_dim, right_dim):
    return lax.dot_general(
        left, right, (((left_dim,), (right_dim,)), ((), ())), preferred_element_type=F32
    )


def doc_rows(starts_ref, length, docs):
    pos = lax.broadcasted_iota(jnp.int32, (1, length), 1)
    doc = jnp.zeros((1, length), jnp.int32) - 1
    for index in range(docs):
        doc = doc + (starts_ref[0, index] <= pos).astype(jnp.int32)
    row = lax.broadcasted_iota(jnp.int32, (8, length), 0)
    same = row == doc
    return jnp.where(same, 1.0, 0.0), jnp.where(same, 0.0, jnp.where(row < docs, -BIG, 0.0))


def bias_circle(rel_ref, bucket_ref, head, tile):
    last = rel_ref.shape[1] - 1
    bucket = bucket_ref[...]
    row = jnp.zeros(bucket.shape, F32)
    for index in range(last):
        row = jnp.where(bucket == index, rel_ref[head, index] - rel_ref[head, last], row)
    return pltpu.roll(jnp.broadcast_to(row, (tile, tile)), 0, 1, stride=1, stride_axis=0)


def forward_kernel(
    head, tile, docs, starts_ref, rel_ref, bucket_ref, q_ref, k_ref, v_ref, o_ref, lse_ref,
    kaug, qaug, vaug, band, scores,
):
    length = q_ref.shape[1]
    span = o_ref.shape[2]
    doc_q, doc_k = doc_rows(starts_ref, length, docs)
    qaug[:head, :] = (q_ref[...].astype(F32) * 0.125).astype(BF)
    qaug[head : head + 16, :] = jnp.concatenate([doc_q, jnp.zeros((8, length), F32)], 0).astype(BF)
    qaug[head + 16 :, :] = jnp.zeros((qaug.shape[0] - head - 16, length), BF)
    tail = jnp.zeros((LANES - head - 8, tile), F32)
    for block in range(length // tile):
        cols = slice(block * tile, (block + 1) * tile)
        full = jnp.concatenate([k_ref[:, cols].astype(F32), doc_k[:, cols], tail], 0)
        kaug[cols, :] = full.T.astype(BF)
    vaug[:head, :] = v_ref[...]
    extra = lax.broadcasted_iota(jnp.int32, (vaug.shape[0] - head, length), 0)
    vaug[head:, :] = jnp.where(extra == 0, 1.0, 0.0).astype(BF)
    circle = bias_circle(rel_ref, bucket_ref, pl.program_id(0), tile)
    key_row = lax.broadcasted_iota(jnp.int32, (tile, tile), 0)
    query_col = lax.broadcasted_iota(jnp.int32, (tile, tile), 1)
    band[:tile, :] = jnp.where(key_row > query_col, circle, 0.0)
    band[tile:, :] = jnp.where(key_row <= query_col, circle, -BIG)
    for i in range(length // tile):
        cols = slice(i * tile, (i + 1) * tile)
        queries = qaug[:, cols]
        peak = None
        for j in range(i + 1):
            rows = slice(j * tile, (j + 1) * tile)
            part = contract(kaug[rows, :], queries, 1, 0)
            if j == i:
                part = part + band[tile:, :]
            elif j == i - 1:
                part = part + band[:tile, :]
            scores[rows, :] = part
            most = jnp.max(part.reshape(tile // 8, 8, tile), axis=0)
            peak = most if peak is None else jnp.maximum(peak, most)
        peak = jnp.max(peak, axis=0, keepdims=True)
        summed = jnp.zeros((vaug.shape[0], tile), F32)
        for j in range(i + 1):
            rows = slice(j * tile, (j + 1) * tile)
            expons = jnp.exp(scores[rows, :] - peak).astype(BF)
            summed = summed + contract(vaug[:, rows], expons, 1, 0)
        total = summed[head : head + 1, :]
        start = (i * tile) % span
        o_ref[i * tile // span, :, start : start + tile] = (summed[:head, :] / total).astype(BF)
        lse_ref[0, :, cols] = peak + jnp.log(total)


def attend_forward(qkv_t, starts, rel, bucket, heads, head, spans):
    length = qkv_t.shape[1]
    docs = starts.shape[1]
    span = length // spans

    def rows_of(part):
        return pl.BlockSpec((head, length), lambda h: (3 * h + part, 0))

    return pl.pallas_call(
        functools.partial(forward_kernel, head, TILE, docs),
        grid=(heads,),
        in_specs=[
            pl.BlockSpec(memory_space=pltpu.SMEM),
            pl.BlockSpec(memory_space=pltpu.SMEM),
            pl.BlockSpec((1, TILE), lambda h: (0, 0)),
            rows_of(0),
            rows_of(1),
            rows_of(2),
        ],
        out_specs=[
            pl.BlockSpec((spans, head, span), lambda h: (0, h, 0)),
            pl.BlockSpec((1, 1, length), lambda h: (h, 0, 0)),
        ],
        out_shape=[
            jax.ShapeDtypeStruct((spans, heads * head, span), BF),
            jax.ShapeDtypeStruct((heads, 1, length), F32),
        ],
        scratch_shapes=[
            pltpu.VMEM((length, LANES), BF),
            pltpu.VMEM((LANES, length), BF),
            pltpu.VMEM((head + 16, length), BF),
            pltpu.VMEM((2 * TILE, TILE), F32),
            pltpu.VMEM((length, TILE), F32),
        ],
        compiler_params=pltpu.CompilerParams(vmem_limit_bytes=40 * 2**20),
        name="attend_forward",
    )(starts, rel, bucket, qkv_t, qkv_t, qkv_t)


def backward_kernel(
    count, head, offset, tile, docs, starts_ref, me_ref, rel_ref, bucket_ref, q_ref, k_ref, v_ref, do_ref, o_ref,
    lse_ref, n1_ref, slab_ref, one_ref, two_ref, three_ref, four_ref, dist_ref, weight_ref, qaug, doaug, kaug, vaug, scaled,
    band, dq_sum, diagonal, grads, upstream_all, all_grads, spare,
):
    length = q_ref.shape[1]
    span = o_ref.shape[2]
    doc_q, doc_k = doc_rows(starts_ref, length, docs)
    sub = lax.broadcasted_iota(jnp.int32, (8, tile), 0)

    def minus_split(row):
        row = -row
        high = row.astype(BF).astype(F32)
        rest = row - high
        mid = rest.astype(BF).astype(F32)
        return jnp.where(
            sub == 0, high, jnp.where(sub == 1, mid, jnp.where(sub == 2, rest - mid, 0.0))
        )

    ones3 = jnp.where(lax.broadcasted_iota(jnp.int32, (8, length), 0) < 3, 1.0, 0.0)
    zeros8 = jnp.zeros((8, length), F32)
    blocks = length // tile
    tail = jnp.zeros((LANES - head - 16, tile), F32)
    for block in range(blocks):
        cols = slice(block * tile, (block + 1) * tile)
        begin = (block * tile) % span
        inner = slice(begin, begin + tile)
        upstream_all[:, cols] = do_ref[block * tile // span, :, inner]
        upstream = do_ref[block * tile // span, :, inner].astype(F32)
        attended = o_ref[block * tile // span, :, inner].astype(F32)
        centre = jnp.sum(upstream * attended, axis=0, keepdims=True)
        query = q_ref[:, cols].astype(F32) * 0.125
        scaled[:, cols] = query.astype(BF)
        full = jnp.concatenate([query, doc_q[:, cols], minus_split(lse_ref[0, :, cols]), tail], 0)
        qaug[cols, :] = full.T.astype(BF)
        full = jnp.concatenate([upstream, minus_split(centre), zeros8[:, cols], tail], 0)
        doaug[cols, :] = full.T.astype(BF)
    kaug[:head, :] = k_ref[...]
    kaug[head : head + 16, :] = jnp.concatenate([doc_k, ones3], 0).astype(BF)
    kaug[head + 16 :, :] = jnp.zeros((LANES - head - 16, length), BF)
    vaug[:head, :] = v_ref[...]
    vaug[head : head + 16, :] = jnp.concatenate([ones3, zeros8], 0).astype(BF)
    vaug[head + 16 :, :] = jnp.zeros((LANES - head - 16, length), BF)
    circle = bias_circle(rel_ref, bucket_ref, pl.program_id(0) + offset // (3 * head), tile).T
    query_row = lax.broadcasted_iota(jnp.int32, (tile, tile), 0)
    key_col = lax.broadcasted_iota(jnp.int32, (tile, tile), 1)
    band[:tile, :] = jnp.where(key_col <= query_row, circle, -BIG)
    band[tile:, :] = jnp.where(key_col > query_row, circle, 0.0)
    diagonal[...] = jnp.zeros_like(diagonal)
    for j in range(blocks):
        keys = slice(j * tile, (j + 1) * tile)
        dk = jnp.zeros((head, tile), F32)
        dv = jnp.zeros((head, tile), F32)
        at = j * tile
        while at < length:
            end = min(length, (at // CHUNK + 1) * CHUNK)
            rows = slice(at, end)
            part = contract(qaug[rows, :], kaug[:, keys], 1, 0)
            near = max(0, min(end, (j + 2) * tile) - at)
            if near:
                top = at - j * tile
                part = jnp.concatenate(
                    [part[:near] + band[top : top + near, :]] + ([part[near:]] if at + near < end else []),
                    axis=0,
                )
            probs = jnp.exp(part)
            score_grads = probs * contract(doaug[rows, :], vaug[:, keys], 1, 0)
            if at == j * tile:
                diagonal[...] += score_grads[:tile]
            if at <= (j + 1) * tile < end:
                begin = (j + 1) * tile - at
                diagonal[...] += jnp.where(
                    key_col > query_row, score_grads[begin : begin + tile], 0.0
                )
            weights = probs.astype(BF)
            short = score_grads.astype(BF)
            dv = dv + contract(upstream_all[:, rows], weights, 1, 0)
            dk = dk + contract(scaled[:, rows], short, 1, 0)
            dq = contract(kaug[:head, keys], short, 1, 1)
            if j == 0:
                dq_sum[:, rows] = dq
            else:
                dq_sum[:, rows] += dq
            at = end
        begin = (j * tile) % span
        inner = slice(begin, begin + tile)
        together = jnp.concatenate([dq_sum[:, keys] * 0.125, dk, dv], axis=0).astype(BF)
        grads[:, keys] = together
    step = pl.program_id(0)
    share_refs = (one_ref, two_ref, three_ref, four_ref)
    own = slab_ref[:, offset : offset + 3 * head]
    for later in range(1, count):
        begin = offset + 3 * head * later
        own = jnp.where(pl.program_id(0) == later, slab_ref[:, begin : begin + 3 * head], own)
    here = pl.ds(pl.multiple_of(step * 3 * head, 16), 3 * head)
    all_grads[here, :] = grads[...]

    @pl.when(step == count - 1)
    def _():
        slab = slab_ref[:, offset : offset + 3 * head * count]
        for index in range(length // span):
            spare[index] = contract(
                all_grads[:, index * span : (index + 1) * span], slab, 0, 1
            ).astype(BF)
        for mask, ref in enumerate(share_refs):
            ref[...] = spare[me_ref[0] ^ mask]

    products = contract(grads[...], n1_ref[...], 1, 0).T
    share = jnp.sum(products * own.astype(F32), axis=1, keepdims=True)
    rows, columns = weight_ref.shape
    weight_ref[...] = jnp.concatenate(
        [products, share, jnp.zeros((rows, columns - 3 * head - 1), F32)], axis=1
    ).astype(BF)
    skew = diagonal[...].T
    step = 1
    while step < tile:
        skew = jnp.where((query_row & step) != 0, pltpu.roll(skew, tile - step, 1), skew)
        step *= 2
    dist_ref[0] = jnp.sum(skew, axis=0, keepdims=True)


def attend_backward(
    first, count, qkv_t, upstream, attended, lse, starts, me, rel, bucket, n1, slab, heads, head
):
    length = qkv_t.shape[1]
    docs = starts.shape[1]
    spans, _, span = attended.shape
    width = n1.shape[1]

    def rows_of(part):
        return pl.BlockSpec((head, length), lambda h: (3 * (first + h) + part, 0))

    by_span = pl.BlockSpec((spans, head, span), lambda h: (0, first + h, 0))
    smem = pl.BlockSpec(memory_space=pltpu.SMEM)
    columns = 3 * head + 1
    columns += -columns % LANES
    share = pl.BlockSpec((span, width), lambda h: (0, 0))
    return pl.pallas_call(
        functools.partial(backward_kernel, count, head, 3 * first * head, TILE, docs),
        grid=(count,),
        in_specs=[
            smem,
            smem,
            smem,
            pl.BlockSpec((1, TILE), lambda h: (0, 0)),
            rows_of(0),
            rows_of(1),
            rows_of(2),
            by_span,
            by_span,
            pl.BlockSpec((1, 1, length), lambda h: (first + h, 0, 0)),
            pl.BlockSpec(n1.shape, lambda h: (0, 0)),
            pl.BlockSpec(slab.shape, lambda h: (0, 0)),
        ],
        out_specs=[
            share,
            share,
            share,
            share,
            pl.BlockSpec((1, 1, TILE), lambda h: (h, 0, 0)),
            pl.BlockSpec((width, columns), lambda h: (0, h)),
        ],
        out_shape=[jax.ShapeDtypeStruct((span, width), BF)] * 4
        + [
            jax.ShapeDtypeStruct((count, 1, TILE), F32),
            jax.ShapeDtypeStruct((width, count * columns), BF),
        ],
        scratch_shapes=[
            pltpu.VMEM((length, LANES), BF),
            pltpu.VMEM((length, LANES), BF),
            pltpu.VMEM((LANES, length), BF),
            pltpu.VMEM((LANES, length), BF),
            pltpu.VMEM((head, length), BF),
            pltpu.VMEM((2 * TILE, TILE), F32),
            pltpu.VMEM((head, length), F32),
            pltpu.VMEM((TILE, TILE), F32),
            pltpu.VMEM((3 * head, length), BF),
            pltpu.VMEM((head, length), BF),
            pltpu.VMEM((count * 3 * head, length), BF),
            pltpu.VMEM((spans, span, width), BF),
        ],
        compiler_params=pltpu.CompilerParams(vmem_limit_bytes=60 * 2**20),
        name="attend_backward",
    )(starts, me, rel, bucket, qkv_t, qkv_t, qkv_t, upstream, attended, lse, n1, slab)


def pack_kernel(spans, head, me_ref, q_ref, k_ref, v_ref, router_ref, one_ref, two_ref, slab_ref):
    rows, width = q_ref.shape
    local = width // spans
    for span in range(spans):

        @pl.when(me_ref[0] == span)
        def _():
            pieces = []
            for at in range(span * local, (span + 1) * local, head):
                pieces += [ref[:, at : at + head] for ref in (q_ref, k_ref, v_ref)]
            slab_ref[:, : 3 * local] = jnp.concatenate(pieces, axis=1)

    top = [ref[...].astype(F32) for ref in (router_ref, one_ref, two_ref)]
    used = sum(part.shape[0] for part in top)
    free = slab_ref.shape[1] - 3 * local
    tail = jnp.concatenate(top + [jnp.zeros((free - used, rows), F32)], axis=0)
    tail = jnp.concatenate([tail, jnp.zeros((free, LANES - rows), F32)], axis=1)
    slab_ref[:, 3 * local :] = tail.T[:rows].astype(BF)


def pack_slab(me, w_query, w_key, w_value, w_router, gain_attn, gain_moe, spans, head):
    rows, width = w_query.shape
    columns = 3 * width // spans + w_router.shape[1] + 2
    columns += -columns % LANES
    return pl.pallas_call(
        functools.partial(pack_kernel, spans, head),
        in_specs=[pl.BlockSpec(memory_space=pltpu.SMEM)]
        + [pl.BlockSpec(memory_space=pltpu.VMEM)] * 6,
        out_specs=pl.BlockSpec(memory_space=pltpu.VMEM),
        out_shape=jax.ShapeDtypeStruct((rows, columns), BF),
        name="pack_slab",
    )(me, w_query, w_key, w_value, w_router.T, gain_attn[None], gain_moe[None])


def out_kernel(x_ref, gain_ref, grads_ref, *refs):
    share_refs, out_ref = refs[:-1], refs[-1]
    dn = sum(ref[...].astype(F32) for ref in share_refs)
    x = x_ref[...].astype(F32)
    scale = lax.rsqrt(jnp.mean(x * x, axis=1, keepdims=True) + EPS)
    normed = x * scale
    scaled = dn * gain_ref[...]
    out_ref[...] = grads_ref[...] + scale * (
        scaled - normed * jnp.mean(scaled * normed, axis=1, keepdims=True)
    )


def rows_out(x, gain, grads, shares):
    span, width = x.shape
    part = span // 4
    rows = pl.BlockSpec((part, width), lambda i: (i, 0))
    return pl.pallas_call(
        out_kernel,
        grid=(4,),
        in_specs=[rows, pl.BlockSpec((1, width), lambda i: (0, 0)), rows] + [rows] * len(shares),
        out_specs=rows,
        out_shape=jax.ShapeDtypeStruct(x.shape, F32),
        compiler_params=pltpu.CompilerParams(vmem_limit_bytes=50 * 2**20),
        name="rows_out",
    )(x, gain, grads, *shares)


def project_kernel(wide, pieces, count_old, at_ref, *refs):
    x_refs, slab_ref, gain_ref, refs = refs[:pieces], refs[pieces], refs[pieces + 1], refs[pieces + 2 :]
    if len(refs) == count_old + 5:
        in_ref, w_ref = refs[0], refs[1]
        packed_ref = refs[-1]
        refs = refs[2:-1]
        width, quarter = in_ref.shape
        packed_ref[:width, :] = in_ref[...]
        for at in range(0, width, quarter):
            packed_ref[width + at : width + at + quarter, :] = w_ref[:, at : at + quarter]
    n1_ref, qkv_ref = refs[count_old:]
    x = jnp.concatenate([ref[...].astype(F32) for ref in x_refs], axis=0)
    scale = lax.rsqrt(jnp.mean(x * x, axis=1, keepdims=True) + EPS)
    n1 = (x * scale * gain_ref[...]).astype(BF)
    n1_ref[...] = n1
    qkv_ref[...] = contract(slab_ref[:, :wide], n1, 0, 1).astype(BF)


def project(at, rows, slab, gain, wide, spans, old, expert=()):
    width = rows[0].shape[1]
    span = sum(piece.shape[0] for piece in rows)
    packed = [jax.ShapeDtypeStruct((2 * width, array.shape[1]), BF) for array in expert[:1]]
    first = 3 + len(rows) + len(expert)

    def whole(array):
        return pl.BlockSpec(array.shape, lambda i, at: (0, 0))

    return pl.pallas_call(
        functools.partial(project_kernel, wide, len(rows), len(old)),
        grid_spec=pltpu.PrefetchScalarGridSpec(
            num_scalar_prefetch=1,
            grid=(1,),
            in_specs=[whole(array) for array in (*rows, slab, gain, *expert)]
            + [pl.BlockSpec(memory_space=pl.ANY)] * len(old),
            out_specs=[
                pl.BlockSpec((span, width), lambda i, at: (at[0], 0)),
                pl.BlockSpec((wide, span), lambda i, at: (0, at[0])),
            ]
            + [whole(array) for array in packed],
        ),
        out_shape=[
            jax.ShapeDtypeStruct((spans * span, width), BF),
            jax.ShapeDtypeStruct((wide, spans * span), BF),
        ]
        + packed,
        input_output_aliases={first + index: index for index in range(len(old))},
        compiler_params=pltpu.CompilerParams(vmem_limit_bytes=40 * 2**20),
        name="project",
    )(at, *rows, slab, gain, *expert, *old)


def place_of(slot_ref, part, part_rows):
    slots = lax.broadcasted_iota(jnp.int32, (part_rows, slot_ref.shape[1]), 0) + part * part_rows
    return jnp.where(slots == slot_ref[...], 1.0, 0.0).astype(BF)


def normed_rows(hidden, gain):
    scale = lax.rsqrt(jnp.mean(hidden * hidden, axis=1, keepdims=True) + EPS)
    normed = hidden * scale
    return scale, normed, (normed * gain).astype(BF)


def router_probs(rows, router, experts):
    logits = contract(rows, router, 1, 0)
    lane = lax.broadcasted_iota(jnp.int32, logits.shape, 1)
    logits = jnp.where(lane < experts, logits, -BIG)
    shifted = jnp.exp(logits - jnp.max(logits, axis=1, keepdims=True))
    return shifted / jnp.sum(shifted, axis=1, keepdims=True)


def slots_kernel(rows_ref, slot_ref, *part_refs):
    for part, ref in enumerate(part_refs):
        ref[...] = contract(place_of(slot_ref, part, ref.shape[0]), rows_ref[...], 1, 0).astype(BF)


def into_slots(rows, slot, parts, part_rows):
    vmem = pl.BlockSpec(memory_space=pltpu.VMEM)
    return pl.pallas_call(
        slots_kernel,
        in_specs=[vmem] * 2,
        out_specs=[vmem] * parts,
        out_shape=[jax.ShapeDtypeStruct((part_rows, rows.shape[1]), BF)] * parts,
        name="into_slots",
    )(rows, slot)


def into_kernel(parts, x_ref, mixed_ref, top_ref, low_ref, gain_ref, slot_ref, hidden_ref, *part_refs):
    out_ref = part_refs[-1]
    half, columns = top_ref.shape[1:]
    for begin, ref in ((0, top_ref), (half, low_ref)):
        for core in range(2):
            out_ref[begin : begin + half, core * columns : (core + 1) * columns] = ref[core]
    hidden = x_ref[...].astype(F32) + contract(mixed_ref[...], out_ref[...], 0, 0)
    hidden_ref[...] = hidden
    _, _, n2 = normed_rows(hidden, gain_ref[...])
    for part in range(parts):
        rows = part_refs[part].shape[0]
        part_refs[part][...] = contract(place_of(slot_ref, part, rows), n2, 1, 0).astype(BF)


def rows_into_experts(x, mixed, output_halves, gain, slot, parts, part_rows):
    span, width = x.shape
    if len(output_halves) == 1:
        blocks = output_halves[0].reshape(2, width // 2, 2, width // 2).transpose(0, 2, 1, 3)
        output_halves = [blocks[0], blocks[1]]
    vmem = pl.BlockSpec(memory_space=pltpu.VMEM)
    return pl.pallas_call(
        functools.partial(into_kernel, parts),
        in_specs=[vmem] * 6,
        out_specs=[vmem] * (2 + parts),
        out_shape=[jax.ShapeDtypeStruct((span, width), F32)]
        + [jax.ShapeDtypeStruct((part_rows, width), BF)] * parts
        + [jax.ShapeDtypeStruct((width, width), BF)],
        compiler_params=pltpu.CompilerParams(vmem_limit_bytes=50 * 2**20),
        name="rows_into_experts",
    )(x, mixed, *output_halves, gain, slot)


def back_kernel(hidden_ref, up_ref, out_ref, gain_ref, slot_ref, *refs):
    part_refs = refs[:-3]
    grads_ref, do_ref, grad_gain_ref = refs[-3:]
    dn = None
    for part, part_ref in enumerate(part_refs):
        rows = contract(place_of(slot_ref, part, part_ref.shape[0]), part_ref[...], 0, 0)
        dn = rows if dn is None else dn + rows
    gain = gain_ref[...]
    scale, normed, _ = normed_rows(hidden_ref[...], gain)
    grad_gain_ref[...] = jnp.sum(dn * normed, axis=0, keepdims=True)
    scaled = dn * gain
    grads = up_ref[...].astype(F32) + scale * (
        scaled - normed * jnp.mean(scaled * normed, axis=1, keepdims=True)
    )
    grads_ref[...] = grads
    do_ref[...] = contract(out_ref[...], grads.astype(BF), 1, 1).astype(BF)


def rows_from_experts(hidden, upstream, full_output, gain, slot, back):
    span, width = hidden.shape
    vmem = pl.BlockSpec(memory_space=pltpu.VMEM)
    return pl.pallas_call(
        back_kernel,
        in_specs=[vmem] * (5 + len(back)),
        out_specs=[vmem] * 3,
        out_shape=[
            jax.ShapeDtypeStruct((span, width), F32),
            jax.ShapeDtypeStruct((width, span), BF),
            jax.ShapeDtypeStruct((1, width), F32),
        ],
        compiler_params=pltpu.CompilerParams(vmem_limit_bytes=50 * 2**20),
        name="rows_from_experts",
    )(hidden, upstream, full_output, gain, slot, *back)


def early_kernel(experts, spans, grads_ref, mixed_ref, gain_ref, *refs):
    router_refs, early_ref = refs[:-1], refs[-1]
    grad_output = contract(mixed_ref[...], grads_ref[...].astype(BF), 1, 0)
    width = grad_output.shape[1]
    local = width // spans
    share = experts // spans
    column = jnp.broadcast_to(gain_ref[...], (8, width)).T[:, :1]
    free = early_ref.shape[2] - local - share - 1
    grad_router = sum(ref[...] for ref in router_refs)
    for span in range(spans):
        early_ref[span] = jnp.concatenate(
            [
                grad_output[:, span * local : (span + 1) * local],
                grad_router[:, span * share : (span + 1) * share],
                column,
                jnp.zeros((width, free), F32),
            ],
            axis=1,
        ).astype(BF)


def early_sums(grads, mixed, grad_router, grad_gain, experts, spans):
    width = grads.shape[1]
    columns = width // spans + experts // spans + 1
    columns += -columns % LANES
    vmem = pl.BlockSpec(memory_space=pltpu.VMEM)
    return pl.pallas_call(
        functools.partial(early_kernel, experts, spans),
        in_specs=[vmem] * (3 + len(grad_router)),
        out_specs=vmem,
        out_shape=jax.ShapeDtypeStruct((spans, width, columns), BF),
        compiler_params=pltpu.CompilerParams(vmem_limit_bytes=50 * 2**20),
        name="early_sums",
    )(grads, mixed, grad_gain, *grad_router)


def sums_kernel(heads, head_size, buckets, at, fsdp_count, weights_ref, early_ref, dist_ref, bucket_ref, out_ref):
    width = weights_ref.shape[0]
    columns = weights_ref.shape[1]
    early = early_ref[0].astype(F32)
    for span in range(1, early_ref.shape[0]):
        early = early + early_ref[span].astype(F32)
    index = lax.broadcasted_iota(jnp.int32, (buckets, bucket_ref.shape[1]), 0)
    onehot = jnp.where(index == bucket_ref[...], 1.0, 0.0)
    dist = jnp.concatenate([dist_ref[head] for head in range(heads)], axis=0)
    dist = jnp.concatenate([dist, jnp.zeros((8 - heads, dist.shape[1]), F32)], axis=0)
    rel = lax.dot_general(
        dist, onehot, (((1,), (1,)), ((), ())), precision=HIGH, preferred_element_type=F32
    )
    last = lax.broadcasted_iota(jnp.int32, rel.shape, 1) == buckets - 1
    rel = jnp.where(last, 0.0, rel)
    rel = jnp.where(last, -jnp.sum(rel, axis=1, keepdims=True), rel)
    rows_here = width // fsdp_count
    if heads * buckets == rows_here:
        column = jnp.concatenate([rel.T[:, head : head + 1] for head in range(heads)], axis=0)
        column = jnp.concatenate([column] * fsdp_count, axis=0)
        lane = lax.broadcasted_iota(jnp.int32, early.shape, 1)
        early = jnp.where(lane == at, column, early)
    columns //= heads
    used = 3 * head_size
    parts = [weights_ref[:, head * columns : head * columns + used] for head in range(heads)]
    shares = [
        weights_ref[:, head * columns + used : head * columns + used + 1] for head in range(heads)
    ]
    parts = parts + [early.astype(BF)[:, : at + 1]] + shares
    free = out_ref.shape[1] - sum(part.shape[1] for part in parts)
    out_ref[...] = jnp.concatenate(parts + [jnp.zeros((width, free), BF)], axis=1)


def all_sums(weight_grads, early, distances, bucket, head, buckets, at, fsdp_count):
    width = weight_grads.shape[0]
    heads = distances.shape[0]
    total = heads * (3 * head + 1) + at + 1
    total += -total % LANES
    vmem = pl.BlockSpec(memory_space=pltpu.VMEM)
    return pl.pallas_call(
        functools.partial(sums_kernel, heads, head, buckets, at, fsdp_count),
        in_specs=[vmem] * 4,
        out_specs=vmem,
        out_shape=jax.ShapeDtypeStruct((width, total), BF),
        compiler_params=pltpu.CompilerParams(vmem_limit_bytes=50 * 2**20),
        name="all_sums",
    )(weight_grads, early, distances, bucket)


def final_kernel(experts, hidden_ref, gain_ref, router_ref, chosen_ref, slot_ref, *refs):
    part_refs, output_ref = refs[:-1], refs[-1]
    hidden = hidden_ref[...]
    _, _, n2 = normed_rows(hidden, gain_ref[...])
    probs = router_probs(n2, router_ref[...], experts)
    gate = jnp.sum(probs * chosen_ref[...], axis=1, keepdims=True)
    y = None
    for part, part_ref in enumerate(part_refs):
        rows = contract(place_of(slot_ref, part, part_ref.shape[0]), part_ref[...], 0, 0)
        y = rows if y is None else y + rows
    output_ref[...] = (hidden + gate * y).astype(BF)


def final_output(hidden, gain, router, chosen, slot, parts, experts):
    vmem = pl.BlockSpec(memory_space=pltpu.VMEM)
    return pl.pallas_call(
        functools.partial(final_kernel, experts),
        in_specs=[vmem] * (5 + len(parts)),
        out_specs=vmem,
        out_shape=jax.ShapeDtypeStruct(hidden.shape, BF),
        compiler_params=pltpu.CompilerParams(vmem_limit_bytes=50 * 2**20),
        name="final_output",
    )(hidden, gain, router, chosen, slot, *parts)


def expert_kernel(experts, inputs, count_old, me_ref, core_ref, router_ref, *refs):
    x_refs, up_refs = refs[:inputs], refs[inputs : 2 * inputs]
    own_hbm, near_hbm, far_hbm, in_hbm, out_hbm = refs[2 * inputs : 2 * inputs + 5]
    refs = refs[2 * inputs + 5 + count_old :]
    ours_ref, theirs_ref, act_ref, pre_ref, dy_ref, w_ref, y_sum, dn_sum, sems = refs
    count, width = x_refs[0].shape
    rows = count // 2
    quarter = w_ref.shape[2]
    first = core_ref[0] == 0
    part, pair = pl.program_id(0), pl.program_id(1)
    copies = [
        [
            pltpu.make_async_copy(own_hbm, w_ref.at[0], sems.at[0]),
            pltpu.make_async_copy(near_hbm, w_ref.at[1], sems.at[1]),
        ],
        [
            pltpu.make_async_copy(far_hbm, w_ref.at[2], sems.at[2]),
            pltpu.make_async_copy(in_hbm, w_ref.at[3, pl.ds(0, width)], sems.at[3]),
            pltpu.make_async_copy(out_hbm, w_ref.at[3, pl.ds(width, width)], sems.at[4]),
        ],
    ]

    @pl.when((part == 0) & (pair == 0))
    def _():
        for copy in copies[0] + copies[1]:
            copy.start()

    def parted(index):
        x = x_refs[index][...]

        @pl.when(pair == 0)
        def _():
            probs = router_probs(x, router_ref[...], experts)
            lane = lax.broadcasted_iota(jnp.int32, probs.shape, 1)
            gate = jnp.sum(jnp.where(lane == me_ref[0], probs, 0.0), axis=1, keepdims=True)
            dy_ref[...] = (gate * up_refs[index][...].astype(F32)).astype(BF)

        def blocks(half):
            if index == 0:
                for copy in copies[half]:
                    copy.wait()
            w_in = jnp.concatenate([w_ref[2 * half + b, :width, :] for b in range(2)], axis=1)
            w_out = jnp.concatenate(
                [
                    jnp.concatenate(
                        [
                            w_ref[2 * half + b, at : at + quarter, :]
                            for at in range(width, 2 * width, quarter)
                        ],
                        axis=1,
                    )
                    for b in range(2)
                ],
                axis=0,
            )
            pre = contract(x, w_in, 1, 0)
            root = 0.7978845608028654
            square = pre * pre
            tanh = jnp.tanh(pre * (root + (root * 0.044715) * square))
            upper = 0.5 + 0.5 * tanh
            act = (pre * upper).astype(BF)
            slope = upper + (pre * upper) * (1.0 - tanh) * (root + (root * 0.134145) * square)
            act_ref[...] = act
            pre_grads = (contract(dy_ref[...], w_out, 1, 1) * slope).astype(BF)
            pre_ref[...] = pre_grads
            y = contract(act, w_out, 1, 0)
            dn = contract(pre_grads, w_in, 1, 1)
            if half == 0:
                y_sum[...] = y
                dn_sum[...] = dn
                return
            for some, total in (
                (slice(0, rows), y_sum[...] + y),
                (slice(rows, count), dn_sum[...] + dn),
            ):
                one, two = total[:rows], total[rows:]
                ours_ref[0, some, :] = jnp.where(first, one, two).astype(BF)
                theirs_ref[0, some, :] = jnp.where(first, two, one).astype(BF)

        for half in range(2):
            pl.when(pair == half)(functools.partial(blocks, half))

    for index in range(inputs):
        pl.when(part == index)(functools.partial(parted, index))


def expert_part(part, parts, me, core, rows, upstream, router, weights, old, experts):
    inputs = len(rows)
    count, width = rows[0].shape
    quarter = weights[0].shape[1]
    hidden = 4 * quarter
    total = count * inputs * parts
    begin = part * inputs
    first = 3 + 2 * inputs + len(weights)
    smem = pl.BlockSpec(memory_space=pltpu.SMEM)
    hbm = pl.BlockSpec(memory_space=pl.ANY)
    share = pl.BlockSpec((1, count, width), lambda i, j: (i, 0, 0))
    inner = pl.BlockSpec((count, 2 * quarter), lambda i, j: (begin + i, j))
    return pl.pallas_call(
        functools.partial(expert_kernel, experts, inputs, len(old)),
        grid=(inputs, 2),
        in_specs=[smem] * 2
        + [
            pl.BlockSpec(array.shape, lambda i, j: (0, 0))
            for array in (router, *rows, *upstream)
        ]
        + [hbm] * (len(weights) + len(old)),
        out_specs=[share] * 2
        + [inner] * 2
        + [pl.BlockSpec((count, width), lambda i, j: (begin + i, 0))],
        out_shape=[jax.ShapeDtypeStruct((inputs, count, width), BF)] * 2
        + [jax.ShapeDtypeStruct((total, size), BF) for size in (hidden, hidden, width)],
        scratch_shapes=[
            pltpu.VMEM((4, 2 * width, quarter), BF),
            pltpu.VMEM((count, width), F32),
            pltpu.VMEM((count, width), F32),
            pltpu.SemaphoreType.DMA((5,)),
        ],
        input_output_aliases={first + index: 2 + index for index in range(len(old))},
        compiler_params=pltpu.CompilerParams(vmem_limit_bytes=56 * 2**20),
        name="expert_part",
    )(me, core, router, *rows, *upstream, *weights, *old)


def combine_kernel(inputs, experts, core_ref, me_ref, ours_ref, theirs_ref, router_ref, *refs):
    x_refs, up_refs, refs = refs[:inputs], refs[inputs : 2 * inputs], refs[2 * inputs :]
    y_refs, dn_refs, grad_ref = refs[:inputs], refs[inputs : 2 * inputs], refs[-1]
    rows = y_refs[0].shape[0]
    router = router_ref[...]
    grad_router = None
    for index in range(inputs):
        x = x_refs[index][...]
        y = ours_ref[index, :rows, :].astype(F32) + theirs_ref[index, :rows, :].astype(F32)
        dn = ours_ref[index, rows:, :].astype(F32) + theirs_ref[index, rows:, :].astype(F32)
        probs = router_probs(x, router, experts)
        lane = lax.broadcasted_iota(jnp.int32, probs.shape, 1)
        chosen = jnp.where(lane == me_ref[0], 1.0, 0.0)
        gate = jnp.sum(probs * chosen, axis=1, keepdims=True)
        gate_grads = jnp.sum(up_refs[index][...].astype(F32) * y, axis=1, keepdims=True)
        logit_grads = (probs * (chosen * gate_grads - gate * gate_grads)).astype(BF)
        product = contract(x, logit_grads, 0, 0)
        grad_router = product if grad_router is None else grad_router + product
        y_refs[index][...] = y.astype(BF)
        dn_refs[index][...] = (dn + contract(logit_grads, router, 1, 1)).astype(BF)
    grad_ref[...] = grad_router


def combine_halves(me, core, ours, theirs, router, rows, upstream, experts):
    inputs, count, width = ours.shape

    def whole(array):
        return pl.BlockSpec(array.shape, lambda i, core: (0,) * array.ndim)

    own = pl.BlockSpec((count // 2, width), lambda i, core: (core[0], 0))
    out_shape = [jax.ShapeDtypeStruct((count // 2, width), BF)] * (2 * inputs)
    out_shape.append(jax.ShapeDtypeStruct(router.shape, F32))
    results = pl.pallas_call(
        functools.partial(combine_kernel, inputs, experts),
        grid_spec=pltpu.PrefetchScalarGridSpec(
            num_scalar_prefetch=1,
            grid=(1,),
            in_specs=[pl.BlockSpec(memory_space=pltpu.SMEM)]
            + [whole(array) for array in (ours, theirs, router)]
            + [own] * (2 * inputs),
            out_specs=[
                pl.BlockSpec(array.shape, lambda i, core: (0, 0)) for array in out_shape
            ],
        ),
        out_shape=out_shape,
        compiler_params=pltpu.CompilerParams(vmem_limit_bytes=50 * 2**20),
        name="combine_halves",
    )(core, me, ours, theirs, router, *rows, *upstream)
    return results[:inputs], results[inputs : 2 * inputs], results[-1]


def expert_grads_kernel(act_ref, pre_ref, dy_ref, *refs):
    x_refs = refs[:-4]
    one_ref, two_ref, keep_one, keep_two = refs[-4:]
    width = dy_ref.shape[1]
    quarter = act_ref.shape[1]
    mask = pl.program_id(0)
    rows = jnp.concatenate([ref[...] for ref in x_refs], axis=0)
    grad_in = contract(rows, pre_ref[...], 0, 0)
    grad_out = contract(act_ref[...], dy_ref[...], 0, 0)
    grad_out = jnp.concatenate(
        [grad_out[:, at : at + quarter] for at in range(0, width, quarter)], axis=0
    )
    for at in (1, 3):

        @pl.when(mask == at)
        def _():
            one_ref[0] = grad_in.astype(BF)

    for at in (2, 3):

        @pl.when(mask == at)
        def _():
            two_ref[0] = grad_out.astype(BF)

    for at in (0, 2):

        @pl.when(mask == at)
        def _():
            keep_one[0] = grad_in

    for at in (0, 1):

        @pl.when(mask == at)
        def _():
            keep_two[0] = grad_out


def expert_grads(kept, rows, quarter):
    act, pre, dy = kept
    total, width = dy.shape
    hidden = pl.BlockSpec((total, quarter), lambda f: (0, f))

    def whole(array):
        return pl.BlockSpec(array.shape, lambda f: (0, 0))

    def block(place):
        return pl.BlockSpec((1, width, quarter), lambda f: (place(f), 0, 0))

    return pl.pallas_call(
        expert_grads_kernel,
        grid=(act.shape[1] // quarter,),
        in_specs=[hidden, hidden, whole(dy)] + [whole(part) for part in rows],
        out_specs=[
            block(lambda f: f // 2),
            block(lambda f: jnp.maximum(f - 2, 0)),
            block(lambda f: f // 2),
            block(lambda f: jnp.minimum(f, 1)),
        ],
        out_shape=[jax.ShapeDtypeStruct((2, width, quarter), BF)] * 2
        + [jax.ShapeDtypeStruct((2, width, quarter), F32)] * 2,
        compiler_params=pltpu.CompilerParams(vmem_limit_bytes=50 * 2**20),
        name="expert_grads",
    )(act, pre, dy, *rows)


def settle_kernel(keep_one, keep_two, got_one, got_two, one_ref, two_ref):
    one_ref[...] = (keep_one[0].astype(F32) + got_one[0].astype(F32)).astype(BF)
    two_ref[...] = (keep_two[0].astype(F32) + got_two[0].astype(F32)).astype(BF)


def settle_step(keep_one, keep_two, got_one, got_two):
    _, width, quarter = keep_one.shape
    second = pl.BlockSpec((1, width, quarter), lambda i: (1, 0, 0))
    whole = pl.BlockSpec((width, quarter), lambda i: (0, 0))
    return pl.pallas_call(
        settle_kernel,
        grid=(1,),
        in_specs=[second] * 4,
        out_specs=[whole] * 2,
        out_shape=[jax.ShapeDtypeStruct((width, quarter), BF)] * 2,
        compiler_params=pltpu.CompilerParams(vmem_limit_bytes=50 * 2**20),
        name="settle_step",
    )(keep_one, keep_two, got_one, got_two)


def all_to_all(blocks, axis, groups=None):
    return lax.all_to_all(
        blocks, axis, split_axis=0, concat_axis=0, tiled=True, axis_index_groups=groups
    )


def pair_swap(block, axis, mask):
    count = lax.axis_size(axis)
    return lax.ppermute(block, axis, [(i, i ^ mask) for i in range(count)])


def tied(values, *others):
    return lax.optimization_barrier((values, others))[0]


def gather_pairs(rows, axis, groups, pairs, after):
    count = lax.axis_size(axis)
    if count > 8:
        return [lax.all_gather(rows, axis, axis=0, tiled=True)]
    core = lax.axis_index(axis) % 2
    columns = rows.shape[1] // 2
    low, high = rows[:, :columns], rows[:, columns:]
    mine = jnp.where(core == 0, low, high)
    got = pair_swap(jnp.where(core == 0, high, low), axis, 1)
    chip = jnp.where(core == 0, jnp.stack([mine, got]), jnp.stack([got, mine]))
    whole = all_to_all(jnp.broadcast_to(chip[None], (count // 2,) + chip.shape), axis, groups)
    whole = tied(whole.reshape(2, count * rows.shape[0] // 2, columns), after)
    return [
        lax.all_gather(part, axis, axis=0, tiled=False, axis_index_groups=pairs) for part in whole
    ]


def scatter_sums(rows, axis, groups):
    count = lax.axis_size(axis)
    here = rows.shape[0] // count
    if count > 8:
        blocks = all_to_all(rows.reshape(count, here, rows.shape[1]), axis)
        return jnp.sum(blocks.astype(F32), axis=0)
    core = lax.axis_index(axis) % 2
    split = rows.reshape(count // 2, 2, here, rows.shape[1])
    mine = lax.dynamic_index_in_dim(split, core, 1, keepdims=False)
    other = pair_swap(lax.dynamic_index_in_dim(split, 1 - core, 1, keepdims=False), axis, 1)
    chip = (mine.astype(F32) + other.astype(F32)).astype(BF)
    return jnp.sum(all_to_all(chip, axis, groups).astype(F32), axis=0)


def per_device(
    tokens, cotangent, doc_starts, routes, bucket_table, w_query, w_key, w_value, w_output,
    w_router, gain_attn, gain_moe, rel_bias, expert_in, expert_out,
):
    _, span, width = tokens.shape
    seq_count = lax.axis_size("seq")
    fsdp_count = lax.axis_size("fsdp")
    seq_me = lax.axis_index("seq")
    fsdp_me = lax.axis_index("fsdp")
    heads, buckets = rel_bias.shape
    local = width // seq_count
    head = local // heads
    experts = w_router.shape[1]
    rows_here = w_query.shape[0]
    quarter = expert_in.shape[2]
    cores = 2
    groups = [list(range(core, fsdp_count, cores)) for core in range(cores)]
    x = tokens[0]
    seq_index = seq_me.astype(jnp.int32)[None]
    expert_index = (fsdp_me // cores).astype(jnp.int32)[None]
    core_index = (fsdp_me % cores).astype(jnp.int32)[None]

    near = pair_swap(x, "seq", 1)
    far = pair_swap(x, "seq", 2)
    slab = pack_slab(
        seq_index, w_query, w_key, w_value, w_router, gain_attn, gain_moe, seq_count, head
    )
    slab = lax.all_gather(slab, "fsdp", axis=0, tiled=True)
    half = span // 2
    slab, near_half, far_half = lax.optimization_barrier((slab, near[:half], far[half:]))
    across = [pair_swap(near_half, "seq", 2), pair_swap(far_half, "seq", 1)]
    tail = slab[:, 3 * local :]
    full_router = jnp.pad(tail[:, :experts], ((0, 0), (0, -experts % LANES)))
    gains = tail[:, experts : experts + 2].astype(F32).T
    gain_one, gain_two = gains[:1], gains[1:2]
    own_gain = gain_attn.astype(F32)

    expert_me = fsdp_me // cores
    few = experts <= 4
    route, bucket_table, rel_bias = tied((routes[0], bucket_table[:TILE], rel_bias), slab)
    chosen = (route[:, None] == jnp.arange(LANES, dtype=jnp.int32)[None, :]).astype(F32)
    before = (
        jnp.arange(span, dtype=jnp.int32)[:, None] > jnp.arange(span, dtype=jnp.int32)[None, :]
    ).astype(BF)
    ranks = jnp.dot(before, chosen.astype(BF), preferred_element_type=F32)
    capacity = max(2, 2 * span // experts)
    target = route ^ expert_me if few else route
    slot = target * capacity + jnp.sum(ranks * chosen, axis=1).astype(jnp.int32)
    slot = slot[None]
    part_count = 4
    part_rows = experts * capacity // part_count

    def exchange(parts):
        if few:
            return [parts[0]] + [
                pair_swap(parts[mask], "fsdp", cores * mask) for mask in range(1, part_count)
            ]
        blocks = jnp.concatenate(parts, axis=0).reshape(experts, capacity, width)
        blocks = all_to_all(blocks, "fsdp", groups).reshape(part_count, part_rows, width)
        return [blocks[part] for part in range(part_count)]

    old = ()
    for mask, part in enumerate((x, near, far)):
        old = project(
            (seq_me ^ mask).astype(jnp.int32)[None], (part,), slab, gain_one, 3 * local, seq_count, old,
            () if mask < 2 else (expert_in[0], expert_out[0]),
        )
    weights = tied(old[2], across)
    w_near = pair_swap(weights, "seq", 1)
    w_far = pair_swap(weights, "seq", 2)
    up_rows, old = lax.optimization_barrier((cotangent[0], old[:2]))
    w_output = tied(w_output, slab)
    upstream_parts = into_slots(up_rows, slot, part_count, part_rows)
    upstream_parts = exchange(upstream_parts)
    n1_all, qkv_t = project(
        (seq_me ^ 3).astype(jnp.int32)[None], across, slab, gain_one, 3 * local, seq_count, old,
    )
    rel = rel_bias.astype(F32)
    bucket = bucket_table[None]
    attended, lse = attend_forward(
        qkv_t, doc_starts, rel, bucket, heads, head, seq_count
    )
    mixed = all_to_all(attended, "seq").reshape(width, span)
    pairs = [list(range(at, at + cores)) for at in range(0, fsdp_count, cores)]
    output_halves = gather_pairs(w_output, "fsdp", groups, pairs, (attended, upstream_parts))

    def of_chip(rows):
        return lax.all_gather(rows, "fsdp", axis=0, tiled=True, axis_index_groups=pairs)

    mixed, output_halves, upstream_parts, w_near, w_far = lax.optimization_barrier(
        (mixed, output_halves, upstream_parts, w_near, w_far)
    )

    hidden, *parts, full_output = rows_into_experts(
        x, mixed, output_halves, gain_two, slot, part_count, part_rows
    )
    w_near, w_far, parts = lax.optimization_barrier((w_near, w_far, parts))
    w_across = [pair_swap(w_near[:width], "seq", 2), pair_swap(w_far[width:], "seq", 1)]
    weights = [weights, w_near, w_far] + w_across
    arrived = exchange(parts)
    kept = ()
    upstream_parts = [of_chip(one) for one in tied(upstream_parts, parts)]
    chip_rows, ys, back, pairs_of_shares = [], [], [], []
    grad_router = []
    steps = part_count // 2
    for part in range(steps):
        some = slice(part * part_count // steps, (part + 1) * part_count // steps)
        rows, some_up = arrived[some], upstream_parts[some]
        if part:
            rows = tied(rows, kept)
        rows = [of_chip(one) for one in rows]
        if not part:
            rows, upstream_parts = lax.optimization_barrier((rows, upstream_parts))
            some_up = upstream_parts[some]
        chip_rows += rows
        ours, theirs, *kept = expert_part(
            part, steps, expert_index, core_index, rows, some_up, full_router, weights, kept,
            experts,
        )
        pairs_of_shares.append((ours, pair_swap(theirs, "fsdp", 1), rows, some_up))
    for ours, theirs, rows, some_up in pairs_of_shares[::-1]:
        ours, theirs = tied((ours, theirs), back)
        some_ys, dns, product = combine_halves(
            expert_index, core_index, ours, theirs, full_router, rows, some_up, experts
        )
        ys = list(some_ys) + ys
        back = list(dns) + back
        grad_router.append(product)
    kept = tied(kept, back)
    back = exchange(back)
    one, two, keep_one, keep_two = expert_grads(kept, chip_rows, quarter)
    back = list(back[:2]) + list(tied(back[2:], one, two))
    got_one = pair_swap(one, "seq", 1)
    got_two = pair_swap(two, "seq", 2)

    hidden_grads, mixed_grads, grad_gain = rows_from_experts(
        hidden, cotangent[0], full_output, gain_two, slot, back
    )
    ys = exchange(tied(ys, mixed_grads))
    early = early_sums(hidden_grads, mixed, grad_router, grad_gain, experts, seq_count)
    moved = all_to_all(mixed_grads.reshape(seq_count, local, span), "seq")
    settled_sum = [keep[0] + got[0].astype(F32) for keep, got in ((keep_one, got_one), (keep_two, got_two))]
    one, two = settle_step(keep_one, keep_two, got_one, got_two)
    got_one = pair_swap(one, "seq", 2)
    got_two = pair_swap(two, "seq", 1)
    early = all_to_all(tied(early, moved), "seq")
    *shares, distances, weight_grads = attend_backward(
        0, heads, qkv_t, moved, attended, lse, doc_starts, seq_index,
        rel, bucket, n1_all, slab, heads, head,
    )
    shares, distances, weight_grads, got_one, got_two, ys = lax.optimization_barrier(
        (shares, distances, weight_grads, got_one, got_two, ys)
    )
    output = final_output(hidden, gain_two, full_router, chosen, slot, ys, experts)
    shares = [shares[0]] + [
        pair_swap(shares[mask], "seq", mask) for mask in range(1, seq_count)
    ]
    grad_expert_in, grad_expert_out = [
        total + got.astype(F32) for total, got in zip(settled_sum, (got_one, got_two))
    ]
    grad_expert_out = jnp.concatenate(
        [grad_expert_out[at : at + quarter] for at in range(0, width, quarter)], axis=1
    )

    share = experts // seq_count
    rel_count = heads * buckets
    at = local + share + 1
    sums = all_sums(weight_grads, early, distances, bucket, head, buckets, at, fsdp_count)
    summed = scatter_sums(sums, "fsdp", groups)
    by_head = [summed[:, begin : begin + 3 * head] for begin in range(0, 3 * local, 3 * head)]
    summed = summed[:, 3 * local :]
    sum_gain_attn = jnp.sum(summed[:, at + 1 : at + 1 + heads], axis=1) / own_gain
    sum_gain_attn = sum_gain_attn + sum(
        pair_swap(sum_gain_attn, "seq", mask) for mask in range(1, seq_count)
    )
    if rows_here == rel_count:
        sum_rel = summed[:rel_count, local + share + 1].reshape(heads, buckets)
    else:
        onehot = bucket_table[:, None] == jnp.arange(buckets - 1, dtype=jnp.int32)[None, :]
        below = jnp.dot(distances[:, 0], onehot.astype(F32), precision=HIGH)
        grad_rel = jnp.concatenate([below, -jnp.sum(below, axis=1, keepdims=True)], axis=1)
        sum_rel = lax.psum(grad_rel, "fsdp")
    heads_sum = [
        jnp.concatenate([part[:, at : at + head] for part in by_head], axis=1)
        for at in range(0, 3 * head, head)
    ]
    sums = [*heads_sum, summed[:, :local], summed[:, local : local + share], summed[:, local + share]]
    sums, sum_rel, shares = lax.optimization_barrier((sums, sum_rel, shares))
    input_grads = rows_out(x, gain_one, hidden_grads, shares)
    return (
        output[None],
        input_grads[None],
        *sums[:5],
        sum_gain_attn,
        sums[5],
        sum_rel,
        grad_expert_in[None],
        grad_expert_out[None],
    )


def solution(mesh):
    rows = P("fsdp", "seq", None)
    weight = P("fsdp", None)
    shared = P("fsdp", "seq")
    return jax.shard_map(
        per_device,
        mesh=mesh,
        in_specs=(
            rows, rows, weight, shared, P(), weight, weight, weight, weight, weight,
            P("fsdp"), P("fsdp"), P("seq", None), P("fsdp", None, "seq"), rows,
        ),
        out_specs=(
            rows, rows, shared, shared, shared, shared, shared, P("fsdp"), P("fsdp"),
            P("seq", None), P("fsdp", None, "seq"), rows,
        ),
        check_vma=False,
    )
```

```python
import functools

import jax
import jax.numpy as jnp
from jax import lax
from jax.experimental import pallas as pl
from jax.experimental.pallas import tpu as pltpu
from jax.sharding import PartitionSpec as P

EPS = 1e-06
HIGH = lax.Precision.HIGHEST
BIG = 1e30
TILE = 256
LANES = 128
CHUNK = 1024
BF = jnp.bfloat16
F32 = jnp.float32


def contract(left, right, left_dim, right_dim):
    return lax.dot_general(
        left, right, (((left_dim,), (right_dim,)), ((), ())), preferred_element_type=F32
    )


def doc_rows(starts_ref, length, docs):
    pos = lax.broadcasted_iota(jnp.int32, (1, length), 1)
    doc = jnp.zeros((1, length), jnp.int32) - 1
    for index in range(docs):
        doc = doc + (starts_ref[0, index] <= pos).astype(jnp.int32)
    row = lax.broadcasted_iota(jnp.int32, (8, length), 0)
    same = row == doc
    return jnp.where(same, 1.0, 0.0), jnp.where(same, 0.0, jnp.where(row < docs, -BIG, 0.0))


def bias_circle(rel_ref, bucket_ref, head, tile):
    last = rel_ref.shape[1] - 1
    bucket = bucket_ref[...]
    row = jnp.zeros(bucket.shape, F32)
    for index in range(last):
        row = jnp.where(bucket == index, rel_ref[head, index] - rel_ref[head, last], row)
    return pltpu.roll(jnp.broadcast_to(row, (tile, tile)), 0, 1, stride=1, stride_axis=0)


def forward_kernel(
    head, tile, docs, starts_ref, rel_ref, bucket_ref, q_ref, k_ref, v_ref, o_ref, lse_ref,
    kaug, qaug, vaug, band, scores,
):
    length = q_ref.shape[1]
    span = o_ref.shape[2]
    doc_q, doc_k = doc_rows(starts_ref, length, docs)
    qaug[:head, :] = (q_ref[...].astype(F32) * 0.125).astype(BF)
    qaug[head : head + 16, :] = jnp.concatenate([doc_q, jnp.zeros((8, length), F32)], 0).astype(BF)
    qaug[head + 16 :, :] = jnp.zeros((qaug.shape[0] - head - 16, length), BF)
    tail = jnp.zeros((LANES - head - 8, tile), F32)
    for block in range(length // tile):
        cols = slice(block * tile, (block + 1) * tile)
        full = jnp.concatenate([k_ref[:, cols].astype(F32), doc_k[:, cols], tail], 0)
        kaug[cols, :] = full.T.astype(BF)
    vaug[:head, :] = v_ref[...]
    extra = lax.broadcasted_iota(jnp.int32, (vaug.shape[0] - head, length), 0)
    vaug[head:, :] = jnp.where(extra == 0, 1.0, 0.0).astype(BF)
    circle = bias_circle(rel_ref, bucket_ref, pl.program_id(0), tile)
    key_row = lax.broadcasted_iota(jnp.int32, (tile, tile), 0)
    query_col = lax.broadcasted_iota(jnp.int32, (tile, tile), 1)
    band[:tile, :] = jnp.where(key_row > query_col, circle, 0.0)
    band[tile:, :] = jnp.where(key_row <= query_col, circle, -BIG)
    for i in range(length // tile):
        cols = slice(i * tile, (i + 1) * tile)
        queries = qaug[:, cols]
        peak = None
        for j in range(i + 1):
            rows = slice(j * tile, (j + 1) * tile)
            part = contract(kaug[rows, :], queries, 1, 0)
            if j == i:
                part = part + band[tile:, :]
            elif j == i - 1:
                part = part + band[:tile, :]
            scores[rows, :] = part
            most = jnp.max(part.reshape(tile // 8, 8, tile), axis=0)
            peak = most if peak is None else jnp.maximum(peak, most)
        peak = jnp.max(peak, axis=0, keepdims=True)
        summed = jnp.zeros((vaug.shape[0], tile), F32)
        for j in range(i + 1):
            rows = slice(j * tile, (j + 1) * tile)
            expons = jnp.exp(scores[rows, :] - peak).astype(BF)
            summed = summed + contract(vaug[:, rows], expons, 1, 0)
        total = summed[head : head + 1, :]
        start = (i * tile) % span
        o_ref[i * tile // span, :, start : start + tile] = (summed[:head, :] / total).astype(BF)
        lse_ref[0, :, cols] = peak + jnp.log(total)


def attend_forward(qkv_t, starts, rel, bucket, heads, head, spans):
    length = qkv_t.shape[1]
    docs = starts.shape[1]
    span = length // spans

    def rows_of(part):
        return pl.BlockSpec((head, length), lambda h: (3 * h + part, 0))

    return pl.pallas_call(
        functools.partial(forward_kernel, head, TILE, docs),
        grid=(heads,),
        in_specs=[
            pl.BlockSpec(memory_space=pltpu.SMEM),
            pl.BlockSpec(memory_space=pltpu.SMEM),
            pl.BlockSpec((1, TILE), lambda h: (0, 0)),
            rows_of(0),
            rows_of(1),
            rows_of(2),
        ],
        out_specs=[
            pl.BlockSpec((spans, head, span), lambda h: (0, h, 0)),
            pl.BlockSpec((1, 1, length), lambda h: (h, 0, 0)),
        ],
        out_shape=[
            jax.ShapeDtypeStruct((spans, heads * head, span), BF),
            jax.ShapeDtypeStruct((heads, 1, length), F32),
        ],
        scratch_shapes=[
            pltpu.VMEM((length, LANES), BF),
            pltpu.VMEM((LANES, length), BF),
            pltpu.VMEM((head + 16, length), BF),
            pltpu.VMEM((2 * TILE, TILE), F32),
            pltpu.VMEM((length, TILE), F32),
        ],
        compiler_params=pltpu.CompilerParams(vmem_limit_bytes=40 * 2**20),
        name="attend_forward",
    )(starts, rel, bucket, qkv_t, qkv_t, qkv_t)


def backward_kernel(
    count, head, offset, tile, docs, starts_ref, me_ref, rel_ref, bucket_ref, q_ref, k_ref, v_ref, do_ref, o_ref,
    lse_ref, n1_ref, slab_ref, one_ref, two_ref, three_ref, four_ref, dist_ref, weight_ref, qaug, doaug, kaug, vaug, scaled,
    band, dq_sum, diagonal, grads, upstream_all, all_grads, spare,
):
    length = q_ref.shape[1]
    span = o_ref.shape[2]
    doc_q, doc_k = doc_rows(starts_ref, length, docs)
    sub = lax.broadcasted_iota(jnp.int32, (8, tile), 0)

    def minus_split(row):
        row = -row
        high = row.astype(BF).astype(F32)
        rest = row - high
        mid = rest.astype(BF).astype(F32)
        return jnp.where(
            sub == 0, high, jnp.where(sub == 1, mid, jnp.where(sub == 2, rest - mid, 0.0))
        )

    ones3 = jnp.where(lax.broadcasted_iota(jnp.int32, (8, length), 0) < 3, 1.0, 0.0)
    zeros8 = jnp.zeros((8, length), F32)
    blocks = length // tile
    tail = jnp.zeros((LANES - head - 16, tile), F32)
    for block in range(blocks):
        cols = slice(block * tile, (block + 1) * tile)
        begin = (block * tile) % span
        inner = slice(begin, begin + tile)
        upstream_all[:, cols] = do_ref[block * tile // span, :, inner]
        upstream = do_ref[block * tile // span, :, inner].astype(F32)
        attended = o_ref[block * tile // span, :, inner].astype(F32)
        centre = jnp.sum(upstream * attended, axis=0, keepdims=True)
        query = q_ref[:, cols].astype(F32) * 0.125
        scaled[:, cols] = query.astype(BF)
        full = jnp.concatenate([query, doc_q[:, cols], minus_split(lse_ref[0, :, cols]), tail], 0)
        qaug[cols, :] = full.T.astype(BF)
        full = jnp.concatenate([upstream, minus_split(centre), zeros8[:, cols], tail], 0)
        doaug[cols, :] = full.T.astype(BF)
    kaug[:head, :] = k_ref[...]
    kaug[head : head + 16, :] = jnp.concatenate([doc_k, ones3], 0).astype(BF)
    kaug[head + 16 :, :] = jnp.zeros((LANES - head - 16, length), BF)
    vaug[:head, :] = v_ref[...]
    vaug[head : head + 16, :] = jnp.concatenate([ones3, zeros8], 0).astype(BF)
    vaug[head + 16 :, :] = jnp.zeros((LANES - head - 16, length), BF)
    circle = bias_circle(rel_ref, bucket_ref, pl.program_id(0) + offset // (3 * head), tile).T
    query_row = lax.broadcasted_iota(jnp.int32, (tile, tile), 0)
    key_col = lax.broadcasted_iota(jnp.int32, (tile, tile), 1)
    band[:tile, :] = jnp.where(key_col <= query_row, circle, -BIG)
    band[tile:, :] = jnp.where(key_col > query_row, circle, 0.0)
    diagonal[...] = jnp.zeros_like(diagonal)
    for j in range(blocks):
        keys = slice(j * tile, (j + 1) * tile)
        dk = jnp.zeros((head, tile), F32)
        dv = jnp.zeros((head, tile), F32)
        at = j * tile
        while at < length:
            end = min(length, (at // CHUNK + 1) * CHUNK)
            rows = slice(at, end)
            part = contract(qaug[rows, :], kaug[:, keys], 1, 0)
            near = max(0, min(end, (j + 2) * tile) - at)
            if near:
                top = at - j * tile
                part = jnp.concatenate(
                    [part[:near] + band[top : top + near, :]] + ([part[near:]] if at + near < end else []),
                    axis=0,
                )
            probs = jnp.exp(part)
            score_grads = probs * contract(doaug[rows, :], vaug[:, keys], 1, 0)
            if at == j * tile:
                diagonal[...] += score_grads[:tile]
            if at <= (j + 1) * tile < end:
                begin = (j + 1) * tile - at
                diagonal[...] += jnp.where(
                    key_col > query_row, score_grads[begin : begin + tile], 0.0
                )
            weights = probs.astype(BF)
            short = score_grads.astype(BF)
            dv = dv + contract(upstream_all[:, rows], weights, 1, 0)
            dk = dk + contract(scaled[:, rows], short, 1, 0)
            dq = contract(kaug[:head, keys], short, 1, 1)
            if j == 0:
                dq_sum[:, rows] = dq
            else:
                dq_sum[:, rows] += dq
            at = end
        begin = (j * tile) % span
        inner = slice(begin, begin + tile)
        together = jnp.concatenate([dq_sum[:, keys] * 0.125, dk, dv], axis=0).astype(BF)
        grads[:, keys] = together
    step = pl.program_id(0)
    share_refs = (one_ref, two_ref, three_ref, four_ref)
    own = slab_ref[:, offset : offset + 3 * head]
    for later in range(1, count):
        begin = offset + 3 * head * later
        own = jnp.where(pl.program_id(0) == later, slab_ref[:, begin : begin + 3 * head], own)
    here = pl.ds(pl.multiple_of(step * 3 * head, 16), 3 * head)
    all_grads[here, :] = grads[...]

    @pl.when(step == count - 1)
    def _():
        slab = slab_ref[:, offset : offset + 3 * head * count]
        for index in range(length // span):
            spare[index] = contract(
                all_grads[:, index * span : (index + 1) * span], slab, 0, 1
            ).astype(BF)
        for mask, ref in enumerate(share_refs):
            ref[...] = spare[me_ref[0] ^ mask]

    products = contract(grads[...], n1_ref[...], 1, 0).T
    share = jnp.sum(products * own.astype(F32), axis=1, keepdims=True)
    rows, columns = weight_ref.shape
    weight_ref[...] = jnp.concatenate(
        [products, share, jnp.zeros((rows, columns - 3 * head - 1), F32)], axis=1
    ).astype(BF)
    skew = diagonal[...].T
    step = 1
    while step < tile:
        skew = jnp.where((query_row & step) != 0, pltpu.roll(skew, tile - step, 1), skew)
        step *= 2
    dist_ref[0] = jnp.sum(skew, axis=0, keepdims=True)


def attend_backward(
    first, count, qkv_t, upstream, attended, lse, starts, me, rel, bucket, n1, slab, heads, head
):
    length = qkv_t.shape[1]
    docs = starts.shape[1]
    spans, _, span = attended.shape
    width = n1.shape[1]

    def rows_of(part):
        return pl.BlockSpec((head, length), lambda h: (3 * (first + h) + part, 0))

    by_span = pl.BlockSpec((spans, head, span), lambda h: (0, first + h, 0))
    smem = pl.BlockSpec(memory_space=pltpu.SMEM)
    columns = 3 * head + 1
    columns += -columns % LANES
    share = pl.BlockSpec((span, width), lambda h: (0, 0))
    return pl.pallas_call(
        functools.partial(backward_kernel, count, head, 3 * first * head, TILE, docs),
        grid=(count,),
        in_specs=[
            smem,
            smem,
            smem,
            pl.BlockSpec((1, TILE), lambda h: (0, 0)),
            rows_of(0),
            rows_of(1),
            rows_of(2),
            by_span,
            by_span,
            pl.BlockSpec((1, 1, length), lambda h: (first + h, 0, 0)),
            pl.BlockSpec(n1.shape, lambda h: (0, 0)),
            pl.BlockSpec(slab.shape, lambda h: (0, 0)),
        ],
        out_specs=[
            share,
            share,
            share,
            share,
            pl.BlockSpec((1, 1, TILE), lambda h: (h, 0, 0)),
            pl.BlockSpec((width, columns), lambda h: (0, h)),
        ],
        out_shape=[jax.ShapeDtypeStruct((span, width), BF)] * 4
        + [
            jax.ShapeDtypeStruct((count, 1, TILE), F32),
            jax.ShapeDtypeStruct((width, count * columns), BF),
        ],
        scratch_shapes=[
            pltpu.VMEM((length, LANES), BF),
            pltpu.VMEM((length, LANES), BF),
            pltpu.VMEM((LANES, length), BF),
            pltpu.VMEM((LANES, length), BF),
            pltpu.VMEM((head, length), BF),
            pltpu.VMEM((2 * TILE, TILE), F32),
            pltpu.VMEM((head, length), F32),
            pltpu.VMEM((TILE, TILE), F32),
            pltpu.VMEM((3 * head, length), BF),
            pltpu.VMEM((head, length), BF),
            pltpu.VMEM((count * 3 * head, length), BF),
            pltpu.VMEM((spans, span, width), BF),
        ],
        compiler_params=pltpu.CompilerParams(vmem_limit_bytes=60 * 2**20),
        name="attend_backward",
    )(starts, me, rel, bucket, qkv_t, qkv_t, qkv_t, upstream, attended, lse, n1, slab)


def pack_kernel(spans, head, me_ref, q_ref, k_ref, v_ref, router_ref, one_ref, two_ref, slab_ref):
    rows, width = q_ref.shape
    local = width // spans
    for span in range(spans):

        @pl.when(me_ref[0] == span)
        def _():
            pieces = []
            for at in range(span * local, (span + 1) * local, head):
                pieces += [ref[:, at : at + head] for ref in (q_ref, k_ref, v_ref)]
            slab_ref[:, : 3 * local] = jnp.concatenate(pieces, axis=1)

    top = [ref[...].astype(F32) for ref in (router_ref, one_ref, two_ref)]
    used = sum(part.shape[0] for part in top)
    free = slab_ref.shape[1] - 3 * local
    tail = jnp.concatenate(top + [jnp.zeros((free - used, rows), F32)], axis=0)
    tail = jnp.concatenate([tail, jnp.zeros((free, LANES - rows), F32)], axis=1)
    slab_ref[:, 3 * local :] = tail.T[:rows].astype(BF)


def pack_slab(me, w_query, w_key, w_value, w_router, gain_attn, gain_moe, spans, head):
    rows, width = w_query.shape
    columns = 3 * width // spans + w_router.shape[1] + 2
    columns += -columns % LANES
    return pl.pallas_call(
        functools.partial(pack_kernel, spans, head),
        in_specs=[pl.BlockSpec(memory_space=pltpu.SMEM)]
        + [pl.BlockSpec(memory_space=pltpu.VMEM)] * 6,
        out_specs=pl.BlockSpec(memory_space=pltpu.VMEM),
        out_shape=jax.ShapeDtypeStruct((rows, columns), BF),
        name="pack_slab",
    )(me, w_query, w_key, w_value, w_router.T, gain_attn[None], gain_moe[None])


def out_kernel(x_ref, gain_ref, grads_ref, *refs):
    share_refs, out_ref = refs[:-1], refs[-1]
    dn = sum(ref[...].astype(F32) for ref in share_refs)
    x = x_ref[...].astype(F32)
    scale = lax.rsqrt(jnp.mean(x * x, axis=1, keepdims=True) + EPS)
    normed = x * scale
    scaled = dn * gain_ref[...]
    out_ref[...] = grads_ref[...] + scale * (
        scaled - normed * jnp.mean(scaled * normed, axis=1, keepdims=True)
    )


def rows_out(x, gain, grads, shares):
    span, width = x.shape
    part = span // 4
    rows = pl.BlockSpec((part, width), lambda i: (i, 0))
    return pl.pallas_call(
        out_kernel,
        grid=(4,),
        in_specs=[rows, pl.BlockSpec((1, width), lambda i: (0, 0)), rows] + [rows] * len(shares),
        out_specs=rows,
        out_shape=jax.ShapeDtypeStruct(x.shape, F32),
        compiler_params=pltpu.CompilerParams(vmem_limit_bytes=50 * 2**20),
        name="rows_out",
    )(x, gain, grads, *shares)


def project_kernel(wide, pieces, count_old, at_ref, *refs):
    x_refs, slab_ref, gain_ref, refs = refs[:pieces], refs[pieces], refs[pieces + 1], refs[pieces + 2 :]
    if len(refs) == count_old + 5:
        in_ref, w_ref = refs[0], refs[1]
        packed_ref = refs[-1]
        refs = refs[2:-1]
        width, quarter = in_ref.shape
        packed_ref[:width, :] = in_ref[...]
        for at in range(0, width, quarter):
            packed_ref[width + at : width + at + quarter, :] = w_ref[:, at : at + quarter]
    n1_ref, qkv_ref = refs[count_old:]
    x = jnp.concatenate([ref[...].astype(F32) for ref in x_refs], axis=0)
    scale = lax.rsqrt(jnp.mean(x * x, axis=1, keepdims=True) + EPS)
    n1 = (x * scale * gain_ref[...]).astype(BF)
    n1_ref[...] = n1
    qkv_ref[...] = contract(slab_ref[:, :wide], n1, 0, 1).astype(BF)


def project(at, rows, slab, gain, wide, spans, old, expert=()):
    width = rows[0].shape[1]
    span = sum(piece.shape[0] for piece in rows)
    packed = [jax.ShapeDtypeStruct((2 * width, array.shape[1]), BF) for array in expert[:1]]
    first = 3 + len(rows) + len(expert)

    def whole(array):
        return pl.BlockSpec(array.shape, lambda i, at: (0, 0))

    return pl.pallas_call(
        functools.partial(project_kernel, wide, len(rows), len(old)),
        grid_spec=pltpu.PrefetchScalarGridSpec(
            num_scalar_prefetch=1,
            grid=(1,),
            in_specs=[whole(array) for array in (*rows, slab, gain, *expert)]
            + [pl.BlockSpec(memory_space=pl.ANY)] * len(old),
            out_specs=[
                pl.BlockSpec((span, width), lambda i, at: (at[0], 0)),
                pl.BlockSpec((wide, span), lambda i, at: (0, at[0])),
            ]
            + [whole(array) for array in packed],
        ),
        out_shape=[
            jax.ShapeDtypeStruct((spans * span, width), BF),
            jax.ShapeDtypeStruct((wide, spans * span), BF),
        ]
        + packed,
        input_output_aliases={first + index: index for index in range(len(old))},
        compiler_params=pltpu.CompilerParams(vmem_limit_bytes=40 * 2**20),
        name="project",
    )(at, *rows, slab, gain, *expert, *old)


def place_of(slot_ref, part, part_rows):
    slots = lax.broadcasted_iota(jnp.int32, (part_rows, slot_ref.shape[1]), 0) + part * part_rows
    return jnp.where(slots == slot_ref[...], 1.0, 0.0).astype(BF)


def normed_rows(hidden, gain):
    scale = lax.rsqrt(jnp.mean(hidden * hidden, axis=1, keepdims=True) + EPS)
    normed = hidden * scale
    return scale, normed, (normed * gain).astype(BF)


def router_probs(rows, router, experts):
    logits = contract(rows, router, 1, 0)
    lane = lax.broadcasted_iota(jnp.int32, logits.shape, 1)
    logits = jnp.where(lane < experts, logits, -BIG)
    shifted = jnp.exp(logits - jnp.max(logits, axis=1, keepdims=True))
    return shifted / jnp.sum(shifted, axis=1, keepdims=True)


def slots_kernel(rows_ref, slot_ref, *part_refs):
    for part, ref in enumerate(part_refs):
        ref[...] = contract(place_of(slot_ref, part, ref.shape[0]), rows_ref[...], 1, 0).astype(BF)


def into_slots(rows, slot, parts, part_rows):
    vmem = pl.BlockSpec(memory_space=pltpu.VMEM)
    return pl.pallas_call(
        slots_kernel,
        in_specs=[vmem] * 2,
        out_specs=[vmem] * parts,
        out_shape=[jax.ShapeDtypeStruct((part_rows, rows.shape[1]), BF)] * parts,
        name="into_slots",
    )(rows, slot)


def into_kernel(parts, x_ref, mixed_ref, top_ref, low_ref, gain_ref, slot_ref, hidden_ref, *part_refs):
    out_ref = part_refs[-1]
    half, columns = top_ref.shape[1:]
    for begin, ref in ((0, top_ref), (half, low_ref)):
        for core in range(2):
            out_ref[begin : begin + half, core * columns : (core + 1) * columns] = ref[core]
    hidden = x_ref[...].astype(F32) + contract(mixed_ref[...], out_ref[...], 0, 0)
    hidden_ref[...] = hidden
    _, _, n2 = normed_rows(hidden, gain_ref[...])
    for part in range(parts):
        rows = part_refs[part].shape[0]
        part_refs[part][...] = contract(place_of(slot_ref, part, rows), n2, 1, 0).astype(BF)


def rows_into_experts(x, mixed, output_halves, gain, slot, parts, part_rows):
    span, width = x.shape
    if len(output_halves) == 1:
        blocks = output_halves[0].reshape(2, width // 2, 2, width // 2).transpose(0, 2, 1, 3)
        output_halves = [blocks[0], blocks[1]]
    vmem = pl.BlockSpec(memory_space=pltpu.VMEM)
    return pl.pallas_call(
        functools.partial(into_kernel, parts),
        in_specs=[vmem] * 6,
        out_specs=[vmem] * (2 + parts),
        out_shape=[jax.ShapeDtypeStruct((span, width), F32)]
        + [jax.ShapeDtypeStruct((part_rows, width), BF)] * parts
        + [jax.ShapeDtypeStruct((width, width), BF)],
        compiler_params=pltpu.CompilerParams(vmem_limit_bytes=50 * 2**20),
        name="rows_into_experts",
    )(x, mixed, *output_halves, gain, slot)


def back_kernel(hidden_ref, up_ref, out_ref, gain_ref, slot_ref, *refs):
    part_refs = refs[:-3]
    grads_ref, do_ref, grad_gain_ref = refs[-3:]
    dn = None
    for part, part_ref in enumerate(part_refs):
        rows = contract(place_of(slot_ref, part, part_ref.shape[0]), part_ref[...], 0, 0)
        dn = rows if dn is None else dn + rows
    gain = gain_ref[...]
    scale, normed, _ = normed_rows(hidden_ref[...], gain)
    grad_gain_ref[...] = jnp.sum(dn * normed, axis=0, keepdims=True)
    scaled = dn * gain
    grads = up_ref[...].astype(F32) + scale * (
        scaled - normed * jnp.mean(scaled * normed, axis=1, keepdims=True)
    )
    grads_ref[...] = grads
    do_ref[...] = contract(out_ref[...], grads.astype(BF), 1, 1).astype(BF)


def rows_from_experts(hidden, upstream, full_output, gain, slot, back):
    span, width = hidden.shape
    vmem = pl.BlockSpec(memory_space=pltpu.VMEM)
    return pl.pallas_call(
        back_kernel,
        in_specs=[vmem] * (5 + len(back)),
        out_specs=[vmem] * 3,
        out_shape=[
            jax.ShapeDtypeStruct((span, width), F32),
            jax.ShapeDtypeStruct((width, span), BF),
            jax.ShapeDtypeStruct((1, width), F32),
        ],
        compiler_params=pltpu.CompilerParams(vmem_limit_bytes=50 * 2**20),
        name="rows_from_experts",
    )(hidden, upstream, full_output, gain, slot, *back)


def early_kernel(experts, spans, grads_ref, mixed_ref, gain_ref, *refs):
    router_refs, early_ref = refs[:-1], refs[-1]
    grad_output = contract(mixed_ref[...], grads_ref[...].astype(BF), 1, 0)
    width = grad_output.shape[1]
    local = width // spans
    share = experts // spans
    column = jnp.broadcast_to(gain_ref[...], (8, width)).T[:, :1]
    free = early_ref.shape[2] - local - share - 1
    grad_router = sum(ref[...] for ref in router_refs)
    for span in range(spans):
        early_ref[span] = jnp.concatenate(
            [
                grad_output[:, span * local : (span + 1) * local],
                grad_router[:, span * share : (span + 1) * share],
                column,
                jnp.zeros((width, free), F32),
            ],
            axis=1,
        ).astype(BF)


def early_sums(grads, mixed, grad_router, grad_gain, experts, spans):
    width = grads.shape[1]
    columns = width // spans + experts // spans + 1
    columns += -columns % LANES
    vmem = pl.BlockSpec(memory_space=pltpu.VMEM)
    return pl.pallas_call(
        functools.partial(early_kernel, experts, spans),
        in_specs=[vmem] * (3 + len(grad_router)),
        out_specs=vmem,
        out_shape=jax.ShapeDtypeStruct((spans, width, columns), BF),
        compiler_params=pltpu.CompilerParams(vmem_limit_bytes=50 * 2**20),
        name="early_sums",
    )(grads, mixed, grad_gain, *grad_router)


def sums_kernel(heads, head_size, buckets, at, fsdp_count, weights_ref, early_ref, dist_ref, bucket_ref, out_ref):
    width = weights_ref.shape[0]
    columns = weights_ref.shape[1]
    early = early_ref[0].astype(F32)
    for span in range(1, early_ref.shape[0]):
        early = early + early_ref[span].astype(F32)
    index = lax.broadcasted_iota(jnp.int32, (buckets, bucket_ref.shape[1]), 0)
    onehot = jnp.where(index == bucket_ref[...], 1.0, 0.0)
    dist = jnp.concatenate([dist_ref[head] for head in range(heads)], axis=0)
    dist = jnp.concatenate([dist, jnp.zeros((8 - heads, dist.shape[1]), F32)], axis=0)
    rel = lax.dot_general(
        dist, onehot, (((1,), (1,)), ((), ())), precision=HIGH, preferred_element_type=F32
    )
    last = lax.broadcasted_iota(jnp.int32, rel.shape, 1) == buckets - 1
    rel = jnp.where(last, 0.0, rel)
    rel = jnp.where(last, -jnp.sum(rel, axis=1, keepdims=True), rel)
    rows_here = width // fsdp_count
    if heads * buckets == rows_here:
        column = jnp.concatenate([rel.T[:, head : head + 1] for head in range(heads)], axis=0)
        column = jnp.concatenate([column] * fsdp_count, axis=0)
        lane = lax.broadcasted_iota(jnp.int32, early.shape, 1)
        early = jnp.where(lane == at, column, early)
    columns //= heads
    used = 3 * head_size
    parts = [weights_ref[:, head * columns : head * columns + used] for head in range(heads)]
    shares = [
        weights_ref[:, head * columns + used : head * columns + used + 1] for head in range(heads)
    ]
    parts = parts + [early.astype(BF)[:, : at + 1]] + shares
    free = out_ref.shape[1] - sum(part.shape[1] for part in parts)
    out_ref[...] = jnp.concatenate(parts + [jnp.zeros((width, free), BF)], axis=1)


def all_sums(weight_grads, early, distances, bucket, head, buckets, at, fsdp_count):
    width = weight_grads.shape[0]
    heads = distances.shape[0]
    total = heads * (3 * head + 1) + at + 1
    total += -total % LANES
    vmem = pl.BlockSpec(memory_space=pltpu.VMEM)
    return pl.pallas_call(
        functools.partial(sums_kernel, heads, head, buckets, at, fsdp_count),
        in_specs=[vmem] * 4,
        out_specs=vmem,
        out_shape=jax.ShapeDtypeStruct((width, total), BF),
        compiler_params=pltpu.CompilerParams(vmem_limit_bytes=50 * 2**20),
        name="all_sums",
    )(weight_grads, early, distances, bucket)


def final_kernel(experts, hidden_ref, gain_ref, router_ref, chosen_ref, slot_ref, *refs):
    part_refs, output_ref = refs[:-1], refs[-1]
    hidden = hidden_ref[...]
    _, _, n2 = normed_rows(hidden, gain_ref[...])
    probs = router_probs(n2, router_ref[...], experts)
    gate = jnp.sum(probs * chosen_ref[...], axis=1, keepdims=True)
    y = None
    for part, part_ref in enumerate(part_refs):
        rows = contract(place_of(slot_ref, part, part_ref.shape[0]), part_ref[...], 0, 0)
        y = rows if y is None else y + rows
    output_ref[...] = (hidden + gate * y).astype(BF)


def final_output(hidden, gain, router, chosen, slot, parts, experts):
    vmem = pl.BlockSpec(memory_space=pltpu.VMEM)
    return pl.pallas_call(
        functools.partial(final_kernel, experts),
        in_specs=[vmem] * (5 + len(parts)),
        out_specs=vmem,
        out_shape=jax.ShapeDtypeStruct(hidden.shape, BF),
        compiler_params=pltpu.CompilerParams(vmem_limit_bytes=50 * 2**20),
        name="final_output",
    )(hidden, gain, router, chosen, slot, *parts)


def expert_kernel(experts, inputs, count_old, me_ref, core_ref, router_ref, *refs):
    x_refs, up_refs = refs[:inputs], refs[inputs : 2 * inputs]
    own_hbm, near_hbm, far_hbm, in_hbm, out_hbm = refs[2 * inputs : 2 * inputs + 5]
    refs = refs[2 * inputs + 5 + count_old :]
    ours_ref, theirs_ref, act_ref, pre_ref, dy_ref, w_ref, y_sum, dn_sum, sems = refs
    count, width = x_refs[0].shape
    rows = count // 2
    quarter = w_ref.shape[2]
    first = core_ref[0] == 0
    part, pair = pl.program_id(0), pl.program_id(1)
    copies = [
        [
            pltpu.make_async_copy(own_hbm, w_ref.at[0], sems.at[0]),
            pltpu.make_async_copy(near_hbm, w_ref.at[1], sems.at[1]),
        ],
        [
            pltpu.make_async_copy(far_hbm, w_ref.at[2], sems.at[2]),
            pltpu.make_async_copy(in_hbm, w_ref.at[3, pl.ds(0, width)], sems.at[3]),
            pltpu.make_async_copy(out_hbm, w_ref.at[3, pl.ds(width, width)], sems.at[4]),
        ],
    ]

    @pl.when((part == 0) & (pair == 0))
    def _():
        for copy in copies[0] + copies[1]:
            copy.start()

    def parted(index):
        x = x_refs[index][...]

        @pl.when(pair == 0)
        def _():
            probs = router_probs(x, router_ref[...], experts)
            lane = lax.broadcasted_iota(jnp.int32, probs.shape, 1)
            gate = jnp.sum(jnp.where(lane == me_ref[0], probs, 0.0), axis=1, keepdims=True)
            dy_ref[...] = (gate * up_refs[index][...].astype(F32)).astype(BF)

        def blocks(half):
            if index == 0:
                for copy in copies[half]:
                    copy.wait()
            w_in = jnp.concatenate([w_ref[2 * half + b, :width, :] for b in range(2)], axis=1)
            w_out = jnp.concatenate(
                [
                    jnp.concatenate(
                        [
                            w_ref[2 * half + b, at : at + quarter, :]
                            for at in range(width, 2 * width, quarter)
                        ],
                        axis=1,
                    )
                    for b in range(2)
                ],
                axis=0,
            )
            pre = contract(x, w_in, 1, 0)
            root = 0.7978845608028654
            square = pre * pre
            tanh = jnp.tanh(pre * (root + (root * 0.044715) * square))
            upper = 0.5 + 0.5 * tanh
            act = (pre * upper).astype(BF)
            slope = upper + (pre * upper) * (1.0 - tanh) * (root + (root * 0.134145) * square)
            act_ref[...] = act
            pre_grads = (contract(dy_ref[...], w_out, 1, 1) * slope).astype(BF)
            pre_ref[...] = pre_grads
            y = contract(act, w_out, 1, 0)
            dn = contract(pre_grads, w_in, 1, 1)
            if half == 0:
                y_sum[...] = y
                dn_sum[...] = dn
                return
            for some, total in (
                (slice(0, rows), y_sum[...] + y),
                (slice(rows, count), dn_sum[...] + dn),
            ):
                one, two = total[:rows], total[rows:]
                ours_ref[0, some, :] = jnp.where(first, one, two).astype(BF)
                theirs_ref[0, some, :] = jnp.where(first, two, one).astype(BF)

        for half in range(2):
            pl.when(pair == half)(functools.partial(blocks, half))

    for index in range(inputs):
        pl.when(part == index)(functools.partial(parted, index))


def expert_part(part, parts, me, core, rows, upstream, router, weights, old, experts):
    inputs = len(rows)
    count, width = rows[0].shape
    quarter = weights[0].shape[1]
    hidden = 4 * quarter
    total = count * inputs * parts
    begin = part * inputs
    first = 3 + 2 * inputs + len(weights)
    smem = pl.BlockSpec(memory_space=pltpu.SMEM)
    hbm = pl.BlockSpec(memory_space=pl.ANY)
    share = pl.BlockSpec((1, count, width), lambda i, j: (i, 0, 0))
    inner = pl.BlockSpec((count, 2 * quarter), lambda i, j: (begin + i, j))
    return pl.pallas_call(
        functools.partial(expert_kernel, experts, inputs, len(old)),
        grid=(inputs, 2),
        in_specs=[smem] * 2
        + [
            pl.BlockSpec(array.shape, lambda i, j: (0, 0))
            for array in (router, *rows, *upstream)
        ]
        + [hbm] * (len(weights) + len(old)),
        out_specs=[share] * 2
        + [inner] * 2
        + [pl.BlockSpec((count, width), lambda i, j: (begin + i, 0))],
        out_shape=[jax.ShapeDtypeStruct((inputs, count, width), BF)] * 2
        + [jax.ShapeDtypeStruct((total, size), BF) for size in (hidden, hidden, width)],
        scratch_shapes=[
            pltpu.VMEM((4, 2 * width, quarter), BF),
            pltpu.VMEM((count, width), F32),
            pltpu.VMEM((count, width), F32),
            pltpu.SemaphoreType.DMA((5,)),
        ],
        input_output_aliases={first + index: 2 + index for index in range(len(old))},
        compiler_params=pltpu.CompilerParams(vmem_limit_bytes=56 * 2**20),
        name="expert_part",
    )(me, core, router, *rows, *upstream, *weights, *old)


def combine_kernel(inputs, experts, core_ref, me_ref, ours_ref, theirs_ref, router_ref, *refs):
    x_refs, up_refs, refs = refs[:inputs], refs[inputs : 2 * inputs], refs[2 * inputs :]
    y_refs, dn_refs, grad_ref = refs[:inputs], refs[inputs : 2 * inputs], refs[-1]
    rows = y_refs[0].shape[0]
    router = router_ref[...]
    grad_router = None
    for index in range(inputs):
        x = x_refs[index][...]
        y = ours_ref[index, :rows, :].astype(F32) + theirs_ref[index, :rows, :].astype(F32)
        dn = ours_ref[index, rows:, :].astype(F32) + theirs_ref[index, rows:, :].astype(F32)
        probs = router_probs(x, router, experts)
        lane = lax.broadcasted_iota(jnp.int32, probs.shape, 1)
        chosen = jnp.where(lane == me_ref[0], 1.0, 0.0)
        gate = jnp.sum(probs * chosen, axis=1, keepdims=True)
        gate_grads = jnp.sum(up_refs[index][...].astype(F32) * y, axis=1, keepdims=True)
        logit_grads = (probs * (chosen * gate_grads - gate * gate_grads)).astype(BF)
        product = contract(x, logit_grads, 0, 0)
        grad_router = product if grad_router is None else grad_router + product
        y_refs[index][...] = y.astype(BF)
        dn_refs[index][...] = (dn + contract(logit_grads, router, 1, 1)).astype(BF)
    grad_ref[...] = grad_router


def combine_halves(me, core, ours, theirs, router, rows, upstream, experts):
    inputs, count, width = ours.shape

    def whole(array):
        return pl.BlockSpec(array.shape, lambda i, core: (0,) * array.ndim)

    own = pl.BlockSpec((count // 2, width), lambda i, core: (core[0], 0))
    out_shape = [jax.ShapeDtypeStruct((count // 2, width), BF)] * (2 * inputs)
    out_shape.append(jax.ShapeDtypeStruct(router.shape, F32))
    results = pl.pallas_call(
        functools.partial(combine_kernel, inputs, experts),
        grid_spec=pltpu.PrefetchScalarGridSpec(
            num_scalar_prefetch=1,
            grid=(1,),
            in_specs=[pl.BlockSpec(memory_space=pltpu.SMEM)]
            + [whole(array) for array in (ours, theirs, router)]
            + [own] * (2 * inputs),
            out_specs=[
                pl.BlockSpec(array.shape, lambda i, core: (0, 0)) for array in out_shape
            ],
        ),
        out_shape=out_shape,
        compiler_params=pltpu.CompilerParams(vmem_limit_bytes=50 * 2**20),
        name="combine_halves",
    )(core, me, ours, theirs, router, *rows, *upstream)
    return results[:inputs], results[inputs : 2 * inputs], results[-1]


def expert_grads_kernel(act_ref, pre_ref, dy_ref, *refs):
    x_refs = refs[:-4]
    one_ref, two_ref, keep_one, keep_two = refs[-4:]
    width = dy_ref.shape[1]
    quarter = act_ref.shape[1]
    mask = pl.program_id(0)
    rows = jnp.concatenate([ref[...] for ref in x_refs], axis=0)
    grad_in = contract(rows, pre_ref[...], 0, 0)
    grad_out = contract(act_ref[...], dy_ref[...], 0, 0)
    grad_out = jnp.concatenate(
        [grad_out[:, at : at + quarter] for at in range(0, width, quarter)], axis=0
    )
    for at in (1, 3):

        @pl.when(mask == at)
        def _():
            one_ref[0] = grad_in.astype(BF)

    for at in (2, 3):

        @pl.when(mask == at)
        def _():
            two_ref[0] = grad_out.astype(BF)

    for at in (0, 2):

        @pl.when(mask == at)
        def _():
            keep_one[0] = grad_in

    for at in (0, 1):

        @pl.when(mask == at)
        def _():
            keep_two[0] = grad_out


def expert_grads(kept, rows, quarter):
    act, pre, dy = kept
    total, width = dy.shape
    hidden = pl.BlockSpec((total, quarter), lambda f: (0, f))

    def whole(array):
        return pl.BlockSpec(array.shape, lambda f: (0, 0))

    def block(place):
        return pl.BlockSpec((1, width, quarter), lambda f: (place(f), 0, 0))

    return pl.pallas_call(
        expert_grads_kernel,
        grid=(act.shape[1] // quarter,),
        in_specs=[hidden, hidden, whole(dy)] + [whole(part) for part in rows],
        out_specs=[
            block(lambda f: f // 2),
            block(lambda f: jnp.maximum(f - 2, 0)),
            block(lambda f: f // 2),
            block(lambda f: jnp.minimum(f, 1)),
        ],
        out_shape=[jax.ShapeDtypeStruct((2, width, quarter), BF)] * 2
        + [jax.ShapeDtypeStruct((2, width, quarter), F32)] * 2,
        compiler_params=pltpu.CompilerParams(vmem_limit_bytes=50 * 2**20),
        name="expert_grads",
    )(act, pre, dy, *rows)


def settle_kernel(keep_one, keep_two, got_one, got_two, one_ref, two_ref):
    one_ref[...] = (keep_one[0].astype(F32) + got_one[0].astype(F32)).astype(BF)
    two_ref[...] = (keep_two[0].astype(F32) + got_two[0].astype(F32)).astype(BF)


def settle_step(keep_one, keep_two, got_one, got_two):
    _, width, quarter = keep_one.shape
    second = pl.BlockSpec((1, width, quarter), lambda i: (1, 0, 0))
    whole = pl.BlockSpec((width, quarter), lambda i: (0, 0))
    return pl.pallas_call(
        settle_kernel,
        grid=(1,),
        in_specs=[second] * 4,
        out_specs=[whole] * 2,
        out_shape=[jax.ShapeDtypeStruct((width, quarter), BF)] * 2,
        compiler_params=pltpu.CompilerParams(vmem_limit_bytes=50 * 2**20),
        name="settle_step",
    )(keep_one, keep_two, got_one, got_two)


def all_to_all(blocks, axis, groups=None):
    return lax.all_to_all(
        blocks, axis, split_axis=0, concat_axis=0, tiled=True, axis_index_groups=groups
    )


def pair_swap(block, axis, mask):
    count = lax.axis_size(axis)
    return lax.ppermute(block, axis, [(i, i ^ mask) for i in range(count)])


def tied(values, *others):
    return lax.optimization_barrier((values, others))[0]


def gather_pairs(rows, axis, groups, pairs, after):
    count = lax.axis_size(axis)
    if count > 8:
        return [lax.all_gather(rows, axis, axis=0, tiled=True)]
    core = lax.axis_index(axis) % 2
    columns = rows.shape[1] // 2
    low, high = rows[:, :columns], rows[:, columns:]
    mine = jnp.where(core == 0, low, high)
    got = pair_swap(jnp.where(core == 0, high, low), axis, 1)
    chip = jnp.where(core == 0, jnp.stack([mine, got]), jnp.stack([got, mine]))
    whole = all_to_all(jnp.broadcast_to(chip[None], (count // 2,) + chip.shape), axis, groups)
    whole = tied(whole.reshape(2, count * rows.shape[0] // 2, columns), after)
    return [
        lax.all_gather(part, axis, axis=0, tiled=False, axis_index_groups=pairs) for part in whole
    ]


def scatter_sums(rows, axis, groups):
    count = lax.axis_size(axis)
    here = rows.shape[0] // count
    if count > 8:
        blocks = all_to_all(rows.reshape(count, here, rows.shape[1]), axis)
        return jnp.sum(blocks.astype(F32), axis=0)
    core = lax.axis_index(axis) % 2
    split = rows.reshape(count // 2, 2, here, rows.shape[1])
    mine = lax.dynamic_index_in_dim(split, core, 1, keepdims=False)
    other = pair_swap(lax.dynamic_index_in_dim(split, 1 - core, 1, keepdims=False), axis, 1)
    chip = (mine.astype(F32) + other.astype(F32)).astype(BF)
    return jnp.sum(all_to_all(chip, axis, groups).astype(F32), axis=0)


def per_device(
    tokens, cotangent, doc_starts, routes, bucket_table, w_query, w_key, w_value, w_output,
    w_router, gain_attn, gain_moe, rel_bias, expert_in, expert_out,
):
    _, span, width = tokens.shape
    seq_count = lax.axis_size("seq")
    fsdp_count = lax.axis_size("fsdp")
    seq_me = lax.axis_index("seq")
    fsdp_me = lax.axis_index("fsdp")
    heads, buckets = rel_bias.shape
    local = width // seq_count
    head = local // heads
    experts = w_router.shape[1]
    rows_here = w_query.shape[0]
    quarter = expert_in.shape[2]
    cores = 2
    groups = [list(range(core, fsdp_count, cores)) for core in range(cores)]
    x = tokens[0]
    seq_index = seq_me.astype(jnp.int32)[None]
    expert_index = (fsdp_me // cores).astype(jnp.int32)[None]
    core_index = (fsdp_me % cores).astype(jnp.int32)[None]

    near = pair_swap(x, "seq", 1)
    far = pair_swap(x, "seq", 2)
    slab = pack_slab(
        seq_index, w_query, w_key, w_value, w_router, gain_attn, gain_moe, seq_count, head
    )
    slab = lax.all_gather(slab, "fsdp", axis=0, tiled=True)
    half = span // 2
    slab, near_half, far_half = lax.optimization_barrier((slab, near[:half], far[half:]))
    across = [pair_swap(near_half, "seq", 2), pair_swap(far_half, "seq", 1)]
    tail = slab[:, 3 * local :]
    full_router = jnp.pad(tail[:, :experts], ((0, 0), (0, -experts % LANES)))
    gains = tail[:, experts : experts + 2].astype(F32).T
    gain_one, gain_two = gains[:1], gains[1:2]
    own_gain = gain_attn.astype(F32)

    expert_me = fsdp_me // cores
    few = experts <= 4
    route, bucket_table, rel_bias = tied((routes[0], bucket_table[:TILE], rel_bias), slab)
    chosen = (route[:, None] == jnp.arange(LANES, dtype=jnp.int32)[None, :]).astype(F32)
    before = (
        jnp.arange(span, dtype=jnp.int32)[:, None] > jnp.arange(span, dtype=jnp.int32)[None, :]
    ).astype(BF)
    ranks = jnp.dot(before, chosen.astype(BF), preferred_element_type=F32)
    capacity = max(2, 2 * span // experts)
    target = route ^ expert_me if few else route
    slot = target * capacity + jnp.sum(ranks * chosen, axis=1).astype(jnp.int32)
    slot = slot[None]
    part_count = 4
    part_rows = experts * capacity // part_count

    def exchange(parts):
        if few:
            return [parts[0]] + [
                pair_swap(parts[mask], "fsdp", cores * mask) for mask in range(1, part_count)
            ]
        blocks = jnp.concatenate(parts, axis=0).reshape(experts, capacity, width)
        blocks = all_to_all(blocks, "fsdp", groups).reshape(part_count, part_rows, width)
        return [blocks[part] for part in range(part_count)]

    old = ()
    for mask, part in enumerate((x, near, far)):
        old = project(
            (seq_me ^ mask).astype(jnp.int32)[None], (part,), slab, gain_one, 3 * local, seq_count, old,
            () if mask < 2 else (expert_in[0], expert_out[0]),
        )
    weights = tied(old[2], across)
    w_near = pair_swap(weights, "seq", 1)
    w_far = pair_swap(weights, "seq", 2)
    up_rows, old = lax.optimization_barrier((cotangent[0], old[:2]))
    w_output = tied(w_output, slab)
    upstream_parts = into_slots(up_rows, slot, part_count, part_rows)
    upstream_parts = exchange(upstream_parts)
    n1_all, qkv_t = project(
        (seq_me ^ 3).astype(jnp.int32)[None], across, slab, gain_one, 3 * local, seq_count, old,
    )
    rel = rel_bias.astype(F32)
    bucket = bucket_table[None]
    attended, lse = attend_forward(
        qkv_t, doc_starts, rel, bucket, heads, head, seq_count
    )
    mixed = all_to_all(attended, "seq").reshape(width, span)
    pairs = [list(range(at, at + cores)) for at in range(0, fsdp_count, cores)]

    def of_chip(rows):
        return lax.all_gather(rows, "fsdp", axis=0, tiled=True, axis_index_groups=pairs)

    first_up = [of_chip(one) for one in tied(upstream_parts[:2], attended)]
    output_halves = gather_pairs(
        w_output, "fsdp", groups, pairs, (attended, upstream_parts, first_up)
    )
    mixed, output_halves, upstream_parts, w_near, w_far = lax.optimization_barrier(
        (mixed, output_halves, upstream_parts, w_near, w_far)
    )

    hidden, *parts, full_output = rows_into_experts(
        x, mixed, output_halves, gain_two, slot, part_count, part_rows
    )
    w_near, w_far, parts = lax.optimization_barrier((w_near, w_far, parts))
    w_across = [pair_swap(w_near[:width], "seq", 2), pair_swap(w_far[width:], "seq", 1)]
    weights = [weights, w_near, w_far] + w_across
    arrived = exchange(parts)
    kept = ()
    upstream_parts = first_up + [of_chip(one) for one in tied(upstream_parts[2:], parts)]
    chip_rows, ys, back, pairs_of_shares = [], [], [], []
    grad_router = []
    steps = part_count // 2
    for part in range(steps):
        some = slice(part * part_count // steps, (part + 1) * part_count // steps)
        rows, some_up = arrived[some], upstream_parts[some]
        if part:
            rows = tied(rows, kept)
        rows = [of_chip(one) for one in rows]
        if not part:
            rows, upstream_parts = lax.optimization_barrier((rows, upstream_parts))
            some_up = upstream_parts[some]
        chip_rows += rows
        ours, theirs, *kept = expert_part(
            part, steps, expert_index, core_index, rows, some_up, full_router, weights, kept,
            experts,
        )
        pairs_of_shares.append((ours, pair_swap(theirs, "fsdp", 1), rows, some_up))
    for ours, theirs, rows, some_up in pairs_of_shares[::-1]:
        ours, theirs = tied((ours, theirs), back)
        some_ys, dns, product = combine_halves(
            expert_index, core_index, ours, theirs, full_router, rows, some_up, experts
        )
        ys = list(some_ys) + ys
        back = list(dns) + back
        grad_router.append(product)
    kept = tied(kept, back)
    back = exchange(back)
    one, two, keep_one, keep_two = expert_grads(kept, chip_rows, quarter)
    back = list(back[:2]) + list(tied(back[2:], one, two))
    got_one = pair_swap(one, "seq", 1)
    got_two = pair_swap(two, "seq", 2)

    hidden_grads, mixed_grads, grad_gain = rows_from_experts(
        hidden, cotangent[0], full_output, gain_two, slot, back
    )
    ys = exchange(tied(ys, mixed_grads))
    early = early_sums(hidden_grads, mixed, grad_router, grad_gain, experts, seq_count)
    moved = all_to_all(mixed_grads.reshape(seq_count, local, span), "seq")
    settled_sum = [keep[0] + got[0].astype(F32) for keep, got in ((keep_one, got_one), (keep_two, got_two))]
    one, two = settle_step(keep_one, keep_two, got_one, got_two)
    got_one = pair_swap(one, "seq", 2)
    got_two = pair_swap(two, "seq", 1)
    early = all_to_all(tied(early, moved), "seq")
    *shares, distances, weight_grads = attend_backward(
        0, heads, qkv_t, moved, attended, lse, doc_starts, seq_index,
        rel, bucket, n1_all, slab, heads, head,
    )
    shares, distances, weight_grads, got_one, got_two, ys = lax.optimization_barrier(
        (shares, distances, weight_grads, got_one, got_two, ys)
    )
    output = final_output(hidden, gain_two, full_router, chosen, slot, ys, experts)
    shares = [shares[0]] + [
        pair_swap(shares[mask], "seq", mask) for mask in range(1, seq_count)
    ]
    grad_expert_in, grad_expert_out = [
        total + got.astype(F32) for total, got in zip(settled_sum, (got_one, got_two))
    ]
    grad_expert_out = jnp.concatenate(
        [grad_expert_out[at : at + quarter] for at in range(0, width, quarter)], axis=1
    )

    share = experts // seq_count
    rel_count = heads * buckets
    at = local + share + 1
    sums = all_sums(weight_grads, early, distances, bucket, head, buckets, at, fsdp_count)
    summed = scatter_sums(sums, "fsdp", groups)
    by_head = [summed[:, begin : begin + 3 * head] for begin in range(0, 3 * local, 3 * head)]
    summed = summed[:, 3 * local :]
    sum_gain_attn = jnp.sum(summed[:, at + 1 : at + 1 + heads], axis=1) / own_gain
    sum_gain_attn = sum_gain_attn + sum(
        pair_swap(sum_gain_attn, "seq", mask) for mask in range(1, seq_count)
    )
    if rows_here == rel_count:
        sum_rel = summed[:rel_count, local + share + 1].reshape(heads, buckets)
    else:
        onehot = bucket_table[:, None] == jnp.arange(buckets - 1, dtype=jnp.int32)[None, :]
        below = jnp.dot(distances[:, 0], onehot.astype(F32), precision=HIGH)
        grad_rel = jnp.concatenate([below, -jnp.sum(below, axis=1, keepdims=True)], axis=1)
        sum_rel = lax.psum(grad_rel, "fsdp")
    heads_sum = [
        jnp.concatenate([part[:, at : at + head] for part in by_head], axis=1)
        for at in range(0, 3 * head, head)
    ]
    sums = [*heads_sum, summed[:, :local], summed[:, local : local + share], summed[:, local + share]]
    sums, sum_rel, shares = lax.optimization_barrier((sums, sum_rel, shares))
    input_grads = rows_out(x, gain_one, hidden_grads, shares)
    return (
        output[None],
        input_grads[None],
        *sums[:5],
        sum_gain_attn,
        sums[5],
        sum_rel,
        grad_expert_in[None],
        grad_expert_out[None],
    )


def solution(mesh):
    rows = P("fsdp", "seq", None)
    weight = P("fsdp", None)
    shared = P("fsdp", "seq")
    return jax.shard_map(
        per_device,
        mesh=mesh,
        in_specs=(
            rows, rows, weight, shared, P(), weight, weight, weight, weight, weight,
            P("fsdp"), P("fsdp"), P("seq", None), P("fsdp", None, "seq"), rows,
        ),
        out_specs=(
            rows, rows, shared, shared, shared, shared, shared, P("fsdp"), P("fsdp"),
            P("seq", None), P("fsdp", None, "seq"), rows,
        ),
        check_vma=False,
    )
```

```python
import functools

import jax
import jax.numpy as jnp
from jax import lax
from jax.experimental import pallas as pl
from jax.experimental.pallas import tpu as pltpu
from jax.sharding import PartitionSpec as P

EPS = 1e-06
HIGH = lax.Precision.HIGHEST
BIG = 1e30
TILE = 256
LANES = 128
CHUNK = 1024
BF = jnp.bfloat16
F32 = jnp.float32


def contract(left, right, left_dim, right_dim):
    return lax.dot_general(
        left, right, (((left_dim,), (right_dim,)), ((), ())), preferred_element_type=F32
    )


def doc_rows(starts_ref, length, docs):
    pos = lax.broadcasted_iota(jnp.int32, (1, length), 1)
    doc = jnp.zeros((1, length), jnp.int32) - 1
    for index in range(docs):
        doc = doc + (starts_ref[0, index] <= pos).astype(jnp.int32)
    row = lax.broadcasted_iota(jnp.int32, (8, length), 0)
    same = row == doc
    return jnp.where(same, 1.0, 0.0), jnp.where(same, 0.0, jnp.where(row < docs, -BIG, 0.0))


def bias_circle(rel_ref, bucket_ref, head, tile):
    last = rel_ref.shape[1] - 1
    bucket = bucket_ref[...]
    row = jnp.zeros(bucket.shape, F32)
    for index in range(last):
        row = jnp.where(bucket == index, rel_ref[head, index] - rel_ref[head, last], row)
    return pltpu.roll(jnp.broadcast_to(row, (tile, tile)), 0, 1, stride=1, stride_axis=0)


def forward_kernel(
    head, tile, docs, starts_ref, rel_ref, bucket_ref, q_ref, k_ref, v_ref, o_ref, lse_ref,
    kaug, qaug, vaug, band, scores,
):
    length = q_ref.shape[1]
    span = o_ref.shape[2]
    doc_q, doc_k = doc_rows(starts_ref, length, docs)
    qaug[:head, :] = (q_ref[...].astype(F32) * 0.125).astype(BF)
    qaug[head : head + 16, :] = jnp.concatenate([doc_q, jnp.zeros((8, length), F32)], 0).astype(BF)
    qaug[head + 16 :, :] = jnp.zeros((qaug.shape[0] - head - 16, length), BF)
    tail = jnp.zeros((LANES - head - 8, tile), F32)
    for block in range(length // tile):
        cols = slice(block * tile, (block + 1) * tile)
        full = jnp.concatenate([k_ref[:, cols].astype(F32), doc_k[:, cols], tail], 0)
        kaug[cols, :] = full.T.astype(BF)
    vaug[:head, :] = v_ref[...]
    extra = lax.broadcasted_iota(jnp.int32, (vaug.shape[0] - head, length), 0)
    vaug[head:, :] = jnp.where(extra == 0, 1.0, 0.0).astype(BF)
    circle = bias_circle(rel_ref, bucket_ref, pl.program_id(0), tile)
    key_row = lax.broadcasted_iota(jnp.int32, (tile, tile), 0)
    query_col = lax.broadcasted_iota(jnp.int32, (tile, tile), 1)
    band[:tile, :] = jnp.where(key_row > query_col, circle, 0.0)
    band[tile:, :] = jnp.where(key_row <= query_col, circle, -BIG)
    for i in range(length // tile):
        cols = slice(i * tile, (i + 1) * tile)
        queries = qaug[:, cols]
        peak = None
        for j in range(i + 1):
            rows = slice(j * tile, (j + 1) * tile)
            part = contract(kaug[rows, :], queries, 1, 0)
            if j == i:
                part = part + band[tile:, :]
            elif j == i - 1:
                part = part + band[:tile, :]
            scores[rows, :] = part
            most = jnp.max(part.reshape(tile // 8, 8, tile), axis=0)
            peak = most if peak is None else jnp.maximum(peak, most)
        peak = jnp.max(peak, axis=0, keepdims=True)
        summed = jnp.zeros((vaug.shape[0], tile), F32)
        for j in range(i + 1):
            rows = slice(j * tile, (j + 1) * tile)
            expons = jnp.exp(scores[rows, :] - peak).astype(BF)
            summed = summed + contract(vaug[:, rows], expons, 1, 0)
        total = summed[head : head + 1, :]
        start = (i * tile) % span
        o_ref[i * tile // span, :, start : start + tile] = (summed[:head, :] / total).astype(BF)
        lse_ref[0, :, cols] = peak + jnp.log(total)


def attend_forward(qkv_t, starts, rel, bucket, heads, head, spans):
    length = qkv_t.shape[1]
    docs = starts.shape[1]
    span = length // spans

    def rows_of(part):
        return pl.BlockSpec((head, length), lambda h: (3 * h + part, 0))

    return pl.pallas_call(
        functools.partial(forward_kernel, head, TILE, docs),
        grid=(heads,),
        in_specs=[
            pl.BlockSpec(memory_space=pltpu.SMEM),
            pl.BlockSpec(memory_space=pltpu.SMEM),
            pl.BlockSpec((1, TILE), lambda h: (0, 0)),
            rows_of(0),
            rows_of(1),
            rows_of(2),
        ],
        out_specs=[
            pl.BlockSpec((spans, head, span), lambda h: (0, h, 0)),
            pl.BlockSpec((1, 1, length), lambda h: (h, 0, 0)),
        ],
        out_shape=[
            jax.ShapeDtypeStruct((spans, heads * head, span), BF),
            jax.ShapeDtypeStruct((heads, 1, length), F32),
        ],
        scratch_shapes=[
            pltpu.VMEM((length, LANES), BF),
            pltpu.VMEM((LANES, length), BF),
            pltpu.VMEM((head + 16, length), BF),
            pltpu.VMEM((2 * TILE, TILE), F32),
            pltpu.VMEM((length, TILE), F32),
        ],
        compiler_params=pltpu.CompilerParams(vmem_limit_bytes=40 * 2**20),
        name="attend_forward",
    )(starts, rel, bucket, qkv_t, qkv_t, qkv_t)


def backward_kernel(
    count, head, offset, tile, docs, starts_ref, me_ref, rel_ref, bucket_ref, q_ref, k_ref, v_ref, do_ref, o_ref,
    lse_ref, n1_ref, slab_ref, one_ref, two_ref, three_ref, four_ref, dist_ref, weight_ref, qaug, doaug, kaug, vaug, scaled,
    band, dq_sum, diagonal, grads, upstream_all, all_grads, spare,
):
    length = q_ref.shape[1]
    span = o_ref.shape[2]
    doc_q, doc_k = doc_rows(starts_ref, length, docs)
    sub = lax.broadcasted_iota(jnp.int32, (8, tile), 0)

    def minus_split(row):
        row = -row
        high = row.astype(BF).astype(F32)
        rest = row - high
        mid = rest.astype(BF).astype(F32)
        return jnp.where(
            sub == 0, high, jnp.where(sub == 1, mid, jnp.where(sub == 2, rest - mid, 0.0))
        )

    ones3 = jnp.where(lax.broadcasted_iota(jnp.int32, (8, length), 0) < 3, 1.0, 0.0)
    zeros8 = jnp.zeros((8, length), F32)
    blocks = length // tile
    tail = jnp.zeros((LANES - head - 16, tile), F32)
    for block in range(blocks):
        cols = slice(block * tile, (block + 1) * tile)
        begin = (block * tile) % span
        inner = slice(begin, begin + tile)
        upstream_all[:, cols] = do_ref[block * tile // span, :, inner]
        upstream = do_ref[block * tile // span, :, inner].astype(F32)
        attended = o_ref[block * tile // span, :, inner].astype(F32)
        centre = jnp.sum(upstream * attended, axis=0, keepdims=True)
        query = q_ref[:, cols].astype(F32) * 0.125
        scaled[:, cols] = query.astype(BF)
        full = jnp.concatenate([query, doc_q[:, cols], minus_split(lse_ref[0, :, cols]), tail], 0)
        qaug[cols, :] = full.T.astype(BF)
        full = jnp.concatenate([upstream, minus_split(centre), zeros8[:, cols], tail], 0)
        doaug[cols, :] = full.T.astype(BF)
    kaug[:head, :] = k_ref[...]
    kaug[head : head + 16, :] = jnp.concatenate([doc_k, ones3], 0).astype(BF)
    kaug[head + 16 :, :] = jnp.zeros((LANES - head - 16, length), BF)
    vaug[:head, :] = v_ref[...]
    vaug[head : head + 16, :] = jnp.concatenate([ones3, zeros8], 0).astype(BF)
    vaug[head + 16 :, :] = jnp.zeros((LANES - head - 16, length), BF)
    circle = bias_circle(rel_ref, bucket_ref, pl.program_id(0) + offset // (3 * head), tile).T
    query_row = lax.broadcasted_iota(jnp.int32, (tile, tile), 0)
    key_col = lax.broadcasted_iota(jnp.int32, (tile, tile), 1)
    band[:tile, :] = jnp.where(key_col <= query_row, circle, -BIG)
    band[tile:, :] = jnp.where(key_col > query_row, circle, 0.0)
    diagonal[...] = jnp.zeros_like(diagonal)
    for j in range(blocks):
        keys = slice(j * tile, (j + 1) * tile)
        dk = jnp.zeros((head, tile), F32)
        dv = jnp.zeros((head, tile), F32)
        at = j * tile
        while at < length:
            end = min(length, (at // CHUNK + 1) * CHUNK)
            rows = slice(at, end)
            part = contract(qaug[rows, :], kaug[:, keys], 1, 0)
            near = max(0, min(end, (j + 2) * tile) - at)
            if near:
                top = at - j * tile
                part = jnp.concatenate(
                    [part[:near] + band[top : top + near, :]] + ([part[near:]] if at + near < end else []),
                    axis=0,
                )
            probs = jnp.exp(part)
            score_grads = probs * contract(doaug[rows, :], vaug[:, keys], 1, 0)
            if at == j * tile:
                diagonal[...] += score_grads[:tile]
            if at <= (j + 1) * tile < end:
                begin = (j + 1) * tile - at
                diagonal[...] += jnp.where(
                    key_col > query_row, score_grads[begin : begin + tile], 0.0
                )
            weights = probs.astype(BF)
            short = score_grads.astype(BF)
            dv = dv + contract(upstream_all[:, rows], weights, 1, 0)
            dk = dk + contract(scaled[:, rows], short, 1, 0)
            dq = contract(kaug[:head, keys], short, 1, 1)
            if j == 0:
                dq_sum[:, rows] = dq
            else:
                dq_sum[:, rows] += dq
            at = end
        begin = (j * tile) % span
        inner = slice(begin, begin + tile)
        together = jnp.concatenate([dq_sum[:, keys] * 0.125, dk, dv], axis=0).astype(BF)
        grads[:, keys] = together
    step = pl.program_id(0)
    share_refs = (one_ref, two_ref, three_ref, four_ref)
    own = slab_ref[:, offset : offset + 3 * head]
    for later in range(1, count):
        begin = offset + 3 * head * later
        own = jnp.where(pl.program_id(0) == later, slab_ref[:, begin : begin + 3 * head], own)
    here = pl.ds(pl.multiple_of(step * 3 * head, 16), 3 * head)
    all_grads[here, :] = grads[...]

    @pl.when(step == count - 1)
    def _():
        slab = slab_ref[:, offset : offset + 3 * head * count]
        for index in range(length // span):
            spare[index] = contract(
                all_grads[:, index * span : (index + 1) * span], slab, 0, 1
            ).astype(BF)
        for mask, ref in enumerate(share_refs):
            ref[...] = spare[me_ref[0] ^ mask]

    products = contract(grads[...], n1_ref[...], 1, 0).T
    share = jnp.sum(products * own.astype(F32), axis=1, keepdims=True)
    rows, columns = weight_ref.shape
    weight_ref[...] = jnp.concatenate(
        [products, share, jnp.zeros((rows, columns - 3 * head - 1), F32)], axis=1
    ).astype(BF)
    skew = diagonal[...].T
    step = 1
    while step < tile:
        skew = jnp.where((query_row & step) != 0, pltpu.roll(skew, tile - step, 1), skew)
        step *= 2
    dist_ref[0] = jnp.sum(skew, axis=0, keepdims=True)


def attend_backward(
    first, count, qkv_t, upstream, attended, lse, starts, me, rel, bucket, n1, slab, heads, head
):
    length = qkv_t.shape[1]
    docs = starts.shape[1]
    spans, _, span = attended.shape
    width = n1.shape[1]

    def rows_of(part):
        return pl.BlockSpec((head, length), lambda h: (3 * (first + h) + part, 0))

    by_span = pl.BlockSpec((spans, head, span), lambda h: (0, first + h, 0))
    smem = pl.BlockSpec(memory_space=pltpu.SMEM)
    columns = 3 * head + 1
    columns += -columns % LANES
    share = pl.BlockSpec((span, width), lambda h: (0, 0))
    return pl.pallas_call(
        functools.partial(backward_kernel, count, head, 3 * first * head, TILE, docs),
        grid=(count,),
        in_specs=[
            smem,
            smem,
            smem,
            pl.BlockSpec((1, TILE), lambda h: (0, 0)),
            rows_of(0),
            rows_of(1),
            rows_of(2),
            by_span,
            by_span,
            pl.BlockSpec((1, 1, length), lambda h: (first + h, 0, 0)),
            pl.BlockSpec(n1.shape, lambda h: (0, 0)),
            pl.BlockSpec(slab.shape, lambda h: (0, 0)),
        ],
        out_specs=[
            share,
            share,
            share,
            share,
            pl.BlockSpec((1, 1, TILE), lambda h: (h, 0, 0)),
            pl.BlockSpec((width, columns), lambda h: (0, h)),
        ],
        out_shape=[jax.ShapeDtypeStruct((span, width), BF)] * 4
        + [
            jax.ShapeDtypeStruct((count, 1, TILE), F32),
            jax.ShapeDtypeStruct((width, count * columns), BF),
        ],
        scratch_shapes=[
            pltpu.VMEM((length, LANES), BF),
            pltpu.VMEM((length, LANES), BF),
            pltpu.VMEM((LANES, length), BF),
            pltpu.VMEM((LANES, length), BF),
            pltpu.VMEM((head, length), BF),
            pltpu.VMEM((2 * TILE, TILE), F32),
            pltpu.VMEM((head, length), F32),
            pltpu.VMEM((TILE, TILE), F32),
            pltpu.VMEM((3 * head, length), BF),
            pltpu.VMEM((head, length), BF),
            pltpu.VMEM((count * 3 * head, length), BF),
            pltpu.VMEM((spans, span, width), BF),
        ],
        compiler_params=pltpu.CompilerParams(vmem_limit_bytes=60 * 2**20),
        name="attend_backward",
    )(starts, me, rel, bucket, qkv_t, qkv_t, qkv_t, upstream, attended, lse, n1, slab)


def pack_kernel(spans, head, me_ref, q_ref, k_ref, v_ref, router_ref, one_ref, two_ref, slab_ref):
    rows, width = q_ref.shape
    local = width // spans
    for span in range(spans):

        @pl.when(me_ref[0] == span)
        def _():
            pieces = []
            for at in range(span * local, (span + 1) * local, head):
                pieces += [ref[:, at : at + head] for ref in (q_ref, k_ref, v_ref)]
            slab_ref[:, : 3 * local] = jnp.concatenate(pieces, axis=1)

    top = [ref[...].astype(F32) for ref in (router_ref, one_ref, two_ref)]
    used = sum(part.shape[0] for part in top)
    free = slab_ref.shape[1] - 3 * local
    tail = jnp.concatenate(top + [jnp.zeros((free - used, rows), F32)], axis=0)
    tail = jnp.concatenate([tail, jnp.zeros((free, LANES - rows), F32)], axis=1)
    slab_ref[:, 3 * local :] = tail.T[:rows].astype(BF)


def pack_slab(me, w_query, w_key, w_value, w_router, gain_attn, gain_moe, spans, head):
    rows, width = w_query.shape
    columns = 3 * width // spans + w_router.shape[1] + 2
    columns += -columns % LANES
    return pl.pallas_call(
        functools.partial(pack_kernel, spans, head),
        in_specs=[pl.BlockSpec(memory_space=pltpu.SMEM)]
        + [pl.BlockSpec(memory_space=pltpu.VMEM)] * 6,
        out_specs=pl.BlockSpec(memory_space=pltpu.VMEM),
        out_shape=jax.ShapeDtypeStruct((rows, columns), BF),
        name="pack_slab",
    )(me, w_query, w_key, w_value, w_router.T, gain_attn[None], gain_moe[None])


def out_kernel(x_ref, gain_ref, grads_ref, *refs):
    share_refs, out_ref = refs[:-1], refs[-1]
    dn = sum(ref[...].astype(F32) for ref in share_refs)
    x = x_ref[...].astype(F32)
    scale = lax.rsqrt(jnp.mean(x * x, axis=1, keepdims=True) + EPS)
    normed = x * scale
    scaled = dn * gain_ref[...]
    out_ref[...] = grads_ref[...] + scale * (
        scaled - normed * jnp.mean(scaled * normed, axis=1, keepdims=True)
    )


def rows_out(x, gain, grads, shares):
    span, width = x.shape
    part = span // 4
    rows = pl.BlockSpec((part, width), lambda i: (i, 0))
    return pl.pallas_call(
        out_kernel,
        grid=(4,),
        in_specs=[rows, pl.BlockSpec((1, width), lambda i: (0, 0)), rows] + [rows] * len(shares),
        out_specs=rows,
        out_shape=jax.ShapeDtypeStruct(x.shape, F32),
        compiler_params=pltpu.CompilerParams(vmem_limit_bytes=50 * 2**20),
        name="rows_out",
    )(x, gain, grads, *shares)


def project_kernel(wide, pieces, count_old, at_ref, *refs):
    x_refs, slab_ref, gain_ref, refs = refs[:pieces], refs[pieces], refs[pieces + 1], refs[pieces + 2 :]
    if len(refs) == count_old + 5:
        in_ref, w_ref = refs[0], refs[1]
        packed_ref = refs[-1]
        refs = refs[2:-1]
        width, quarter = in_ref.shape
        packed_ref[:width, :] = in_ref[...]
        for at in range(0, width, quarter):
            packed_ref[width + at : width + at + quarter, :] = w_ref[:, at : at + quarter]
    n1_ref, qkv_ref = refs[count_old:]
    x = jnp.concatenate([ref[...].astype(F32) for ref in x_refs], axis=0)
    scale = lax.rsqrt(jnp.mean(x * x, axis=1, keepdims=True) + EPS)
    n1 = (x * scale * gain_ref[...]).astype(BF)
    n1_ref[...] = n1
    qkv_ref[...] = contract(slab_ref[:, :wide], n1, 0, 1).astype(BF)


def project(at, rows, slab, gain, wide, spans, old, expert=()):
    width = rows[0].shape[1]
    span = sum(piece.shape[0] for piece in rows)
    packed = [jax.ShapeDtypeStruct((2 * width, array.shape[1]), BF) for array in expert[:1]]
    first = 3 + len(rows) + len(expert)

    def whole(array):
        return pl.BlockSpec(array.shape, lambda i, at: (0, 0))

    return pl.pallas_call(
        functools.partial(project_kernel, wide, len(rows), len(old)),
        grid_spec=pltpu.PrefetchScalarGridSpec(
            num_scalar_prefetch=1,
            grid=(1,),
            in_specs=[whole(array) for array in (*rows, slab, gain, *expert)]
            + [pl.BlockSpec(memory_space=pl.ANY)] * len(old),
            out_specs=[
                pl.BlockSpec((span, width), lambda i, at: (at[0], 0)),
                pl.BlockSpec((wide, span), lambda i, at: (0, at[0])),
            ]
            + [whole(array) for array in packed],
        ),
        out_shape=[
            jax.ShapeDtypeStruct((spans * span, width), BF),
            jax.ShapeDtypeStruct((wide, spans * span), BF),
        ]
        + packed,
        input_output_aliases={first + index: index for index in range(len(old))},
        compiler_params=pltpu.CompilerParams(vmem_limit_bytes=60 * 2**20),
        name="project",
    )(at, *rows, slab, gain, *expert, *old)


def place_of(slot_ref, part, part_rows):
    slots = lax.broadcasted_iota(jnp.int32, (part_rows, slot_ref.shape[1]), 0) + part * part_rows
    return jnp.where(slots == slot_ref[...], 1.0, 0.0).astype(BF)


def normed_rows(hidden, gain):
    scale = lax.rsqrt(jnp.mean(hidden * hidden, axis=1, keepdims=True) + EPS)
    normed = hidden * scale
    return scale, normed, (normed * gain).astype(BF)


def router_probs(rows, router, experts):
    logits = contract(rows, router, 1, 0)
    lane = lax.broadcasted_iota(jnp.int32, logits.shape, 1)
    logits = jnp.where(lane < experts, logits, -BIG)
    shifted = jnp.exp(logits - jnp.max(logits, axis=1, keepdims=True))
    return shifted / jnp.sum(shifted, axis=1, keepdims=True)


def slots_kernel(rows_ref, slot_ref, *part_refs):
    for part, ref in enumerate(part_refs):
        ref[...] = contract(place_of(slot_ref, part, ref.shape[0]), rows_ref[...], 1, 0).astype(BF)


def into_slots(rows, slot, parts, part_rows):
    vmem = pl.BlockSpec(memory_space=pltpu.VMEM)
    return pl.pallas_call(
        slots_kernel,
        in_specs=[vmem] * 2,
        out_specs=[vmem] * parts,
        out_shape=[jax.ShapeDtypeStruct((part_rows, rows.shape[1]), BF)] * parts,
        name="into_slots",
    )(rows, slot)


def into_kernel(parts, x_ref, mixed_ref, top_ref, low_ref, gain_ref, slot_ref, hidden_ref, *part_refs):
    out_ref = part_refs[-1]
    half, columns = top_ref.shape[1:]
    for begin, ref in ((0, top_ref), (half, low_ref)):
        for core in range(2):
            out_ref[begin : begin + half, core * columns : (core + 1) * columns] = ref[core]
    hidden = x_ref[...].astype(F32) + contract(mixed_ref[...], out_ref[...], 0, 0)
    hidden_ref[...] = hidden
    _, _, n2 = normed_rows(hidden, gain_ref[...])
    for part in range(parts):
        rows = part_refs[part].shape[0]
        part_refs[part][...] = contract(place_of(slot_ref, part, rows), n2, 1, 0).astype(BF)


def rows_into_experts(x, mixed, output_halves, gain, slot, parts, part_rows):
    span, width = x.shape
    if len(output_halves) == 1:
        blocks = output_halves[0].reshape(2, width // 2, 2, width // 2).transpose(0, 2, 1, 3)
        output_halves = [blocks[0], blocks[1]]
    vmem = pl.BlockSpec(memory_space=pltpu.VMEM)
    return pl.pallas_call(
        functools.partial(into_kernel, parts),
        in_specs=[vmem] * 6,
        out_specs=[vmem] * (2 + parts),
        out_shape=[jax.ShapeDtypeStruct((span, width), F32)]
        + [jax.ShapeDtypeStruct((part_rows, width), BF)] * parts
        + [jax.ShapeDtypeStruct((width, width), BF)],
        compiler_params=pltpu.CompilerParams(vmem_limit_bytes=50 * 2**20),
        name="rows_into_experts",
    )(x, mixed, *output_halves, gain, slot)


def back_kernel(hidden_ref, up_ref, out_ref, gain_ref, slot_ref, *refs):
    part_refs = refs[:-3]
    grads_ref, do_ref, grad_gain_ref = refs[-3:]
    dn = None
    for part, part_ref in enumerate(part_refs):
        rows = contract(place_of(slot_ref, part, part_ref.shape[0]), part_ref[...], 0, 0)
        dn = rows if dn is None else dn + rows
    gain = gain_ref[...]
    scale, normed, _ = normed_rows(hidden_ref[...], gain)
    grad_gain_ref[...] = jnp.sum(dn * normed, axis=0, keepdims=True)
    scaled = dn * gain
    grads = up_ref[...].astype(F32) + scale * (
        scaled - normed * jnp.mean(scaled * normed, axis=1, keepdims=True)
    )
    grads_ref[...] = grads
    do_ref[...] = contract(out_ref[...], grads.astype(BF), 1, 1).astype(BF)


def rows_from_experts(hidden, upstream, full_output, gain, slot, back):
    span, width = hidden.shape
    vmem = pl.BlockSpec(memory_space=pltpu.VMEM)
    return pl.pallas_call(
        back_kernel,
        in_specs=[vmem] * (5 + len(back)),
        out_specs=[vmem] * 3,
        out_shape=[
            jax.ShapeDtypeStruct((span, width), F32),
            jax.ShapeDtypeStruct((width, span), BF),
            jax.ShapeDtypeStruct((1, width), F32),
        ],
        compiler_params=pltpu.CompilerParams(vmem_limit_bytes=50 * 2**20),
        name="rows_from_experts",
    )(hidden, upstream, full_output, gain, slot, *back)


def early_kernel(experts, spans, grads_ref, mixed_ref, gain_ref, *refs):
    router_refs, early_ref = refs[:-1], refs[-1]
    grad_output = contract(mixed_ref[...], grads_ref[...].astype(BF), 1, 0)
    width = grad_output.shape[1]
    local = width // spans
    share = experts // spans
    column = jnp.broadcast_to(gain_ref[...], (8, width)).T[:, :1]
    free = early_ref.shape[2] - local - share - 1
    grad_router = sum(ref[...] for ref in router_refs)
    for span in range(spans):
        early_ref[span] = jnp.concatenate(
            [
                grad_output[:, span * local : (span + 1) * local],
                grad_router[:, span * share : (span + 1) * share],
                column,
                jnp.zeros((width, free), F32),
            ],
            axis=1,
        ).astype(BF)


def early_sums(grads, mixed, grad_router, grad_gain, experts, spans):
    width = grads.shape[1]
    columns = width // spans + experts // spans + 1
    columns += -columns % LANES
    vmem = pl.BlockSpec(memory_space=pltpu.VMEM)
    return pl.pallas_call(
        functools.partial(early_kernel, experts, spans),
        in_specs=[vmem] * (3 + len(grad_router)),
        out_specs=vmem,
        out_shape=jax.ShapeDtypeStruct((spans, width, columns), BF),
        compiler_params=pltpu.CompilerParams(vmem_limit_bytes=50 * 2**20),
        name="early_sums",
    )(grads, mixed, grad_gain, *grad_router)


def sums_kernel(heads, head_size, buckets, at, fsdp_count, weights_ref, early_ref, dist_ref, bucket_ref, out_ref):
    width = weights_ref.shape[0]
    columns = weights_ref.shape[1]
    early = early_ref[0].astype(F32)
    for span in range(1, early_ref.shape[0]):
        early = early + early_ref[span].astype(F32)
    index = lax.broadcasted_iota(jnp.int32, (buckets, bucket_ref.shape[1]), 0)
    onehot = jnp.where(index == bucket_ref[...], 1.0, 0.0)
    dist = jnp.concatenate([dist_ref[head] for head in range(heads)], axis=0)
    dist = jnp.concatenate([dist, jnp.zeros((8 - heads, dist.shape[1]), F32)], axis=0)
    rel = lax.dot_general(
        dist, onehot, (((1,), (1,)), ((), ())), precision=HIGH, preferred_element_type=F32
    )
    last = lax.broadcasted_iota(jnp.int32, rel.shape, 1) == buckets - 1
    rel = jnp.where(last, 0.0, rel)
    rel = jnp.where(last, -jnp.sum(rel, axis=1, keepdims=True), rel)
    rows_here = width // fsdp_count
    if heads * buckets == rows_here:
        column = jnp.concatenate([rel.T[:, head : head + 1] for head in range(heads)], axis=0)
        column = jnp.concatenate([column] * fsdp_count, axis=0)
        lane = lax.broadcasted_iota(jnp.int32, early.shape, 1)
        early = jnp.where(lane == at, column, early)
    columns //= heads
    used = 3 * head_size
    parts = [weights_ref[:, head * columns : head * columns + used] for head in range(heads)]
    shares = [
        weights_ref[:, head * columns + used : head * columns + used + 1] for head in range(heads)
    ]
    parts = parts + [early.astype(BF)[:, : at + 1]] + shares
    free = out_ref.shape[1] - sum(part.shape[1] for part in parts)
    out_ref[...] = jnp.concatenate(parts + [jnp.zeros((width, free), BF)], axis=1)


def all_sums(weight_grads, early, distances, bucket, head, buckets, at, fsdp_count):
    width = weight_grads.shape[0]
    heads = distances.shape[0]
    total = heads * (3 * head + 1) + at + 1
    total += -total % LANES
    vmem = pl.BlockSpec(memory_space=pltpu.VMEM)
    return pl.pallas_call(
        functools.partial(sums_kernel, heads, head, buckets, at, fsdp_count),
        in_specs=[vmem] * 4,
        out_specs=vmem,
        out_shape=jax.ShapeDtypeStruct((width, total), BF),
        compiler_params=pltpu.CompilerParams(vmem_limit_bytes=50 * 2**20),
        name="all_sums",
    )(weight_grads, early, distances, bucket)


def final_kernel(experts, hidden_ref, gain_ref, router_ref, chosen_ref, slot_ref, *refs):
    part_refs, output_ref = refs[:-1], refs[-1]
    hidden = hidden_ref[...]
    _, _, n2 = normed_rows(hidden, gain_ref[...])
    probs = router_probs(n2, router_ref[...], experts)
    gate = jnp.sum(probs * chosen_ref[...], axis=1, keepdims=True)
    y = None
    for part, part_ref in enumerate(part_refs):
        rows = contract(place_of(slot_ref, part, part_ref.shape[0]), part_ref[...], 0, 0)
        y = rows if y is None else y + rows
    output_ref[...] = (hidden + gate * y).astype(BF)


def final_output(hidden, gain, router, chosen, slot, parts, experts):
    vmem = pl.BlockSpec(memory_space=pltpu.VMEM)
    return pl.pallas_call(
        functools.partial(final_kernel, experts),
        in_specs=[vmem] * (5 + len(parts)),
        out_specs=vmem,
        out_shape=jax.ShapeDtypeStruct(hidden.shape, BF),
        compiler_params=pltpu.CompilerParams(vmem_limit_bytes=50 * 2**20),
        name="final_output",
    )(hidden, gain, router, chosen, slot, *parts)


def expert_kernel(experts, inputs, count_old, me_ref, core_ref, router_ref, *refs):
    x_refs, up_refs = refs[:inputs], refs[inputs : 2 * inputs]
    own_hbm, near_hbm, far_hbm, in_hbm, out_hbm = refs[2 * inputs : 2 * inputs + 5]
    refs = refs[2 * inputs + 5 + count_old :]
    ours_ref, theirs_ref, act_ref, pre_ref, dy_ref, w_ref, y_sum, dn_sum, sems = refs
    count, width = x_refs[0].shape
    rows = count // 2
    quarter = w_ref.shape[2]
    first = core_ref[0] == 0
    part, pair = pl.program_id(0), pl.program_id(1)
    copies = [
        [
            pltpu.make_async_copy(own_hbm, w_ref.at[0], sems.at[0]),
            pltpu.make_async_copy(near_hbm, w_ref.at[1], sems.at[1]),
        ],
        [
            pltpu.make_async_copy(far_hbm, w_ref.at[2], sems.at[2]),
            pltpu.make_async_copy(in_hbm, w_ref.at[3, pl.ds(0, width)], sems.at[3]),
            pltpu.make_async_copy(out_hbm, w_ref.at[3, pl.ds(width, width)], sems.at[4]),
        ],
    ]

    @pl.when((part == 0) & (pair == 0))
    def _():
        for copy in copies[0] + copies[1]:
            copy.start()

    def parted(index):
        x = x_refs[index][...]

        @pl.when(pair == 0)
        def _():
            probs = router_probs(x, router_ref[...], experts)
            lane = lax.broadcasted_iota(jnp.int32, probs.shape, 1)
            gate = jnp.sum(jnp.where(lane == me_ref[0], probs, 0.0), axis=1, keepdims=True)
            dy_ref[...] = (gate * up_refs[index][...].astype(F32)).astype(BF)

        def blocks(half):
            if index == 0:
                for copy in copies[half]:
                    copy.wait()
            w_in = jnp.concatenate([w_ref[2 * half + b, :width, :] for b in range(2)], axis=1)
            w_out = jnp.concatenate(
                [
                    jnp.concatenate(
                        [
                            w_ref[2 * half + b, at : at + quarter, :]
                            for at in range(width, 2 * width, quarter)
                        ],
                        axis=1,
                    )
                    for b in range(2)
                ],
                axis=0,
            )
            pre = contract(x, w_in, 1, 0)
            root = 0.7978845608028654
            square = pre * pre
            tanh = jnp.tanh(pre * (root + (root * 0.044715) * square))
            upper = 0.5 + 0.5 * tanh
            act = (pre * upper).astype(BF)
            slope = upper + (pre * upper) * (1.0 - tanh) * (root + (root * 0.134145) * square)
            act_ref[...] = act
            pre_grads = (contract(dy_ref[...], w_out, 1, 1) * slope).astype(BF)
            pre_ref[...] = pre_grads
            y = contract(act, w_out, 1, 0)
            dn = contract(pre_grads, w_in, 1, 1)
            if half == 0:
                y_sum[...] = y
                dn_sum[...] = dn
                return
            for some, total in (
                (slice(0, rows), y_sum[...] + y),
                (slice(rows, count), dn_sum[...] + dn),
            ):
                one, two = total[:rows], total[rows:]
                ours_ref[0, some, :] = jnp.where(first, one, two).astype(BF)
                theirs_ref[0, some, :] = jnp.where(first, two, one).astype(BF)

        for half in range(2):
            pl.when(pair == half)(functools.partial(blocks, half))

    for index in range(inputs):
        pl.when(part == index)(functools.partial(parted, index))


def expert_part(part, parts, me, core, rows, upstream, router, weights, old, experts):
    inputs = len(rows)
    count, width = rows[0].shape
    quarter = weights[0].shape[1]
    hidden = 4 * quarter
    total = count * inputs * parts
    begin = part * inputs
    first = 3 + 2 * inputs + len(weights)
    smem = pl.BlockSpec(memory_space=pltpu.SMEM)
    hbm = pl.BlockSpec(memory_space=pl.ANY)
    share = pl.BlockSpec((1, count, width), lambda i, j: (i, 0, 0))
    inner = pl.BlockSpec((count, 2 * quarter), lambda i, j: (begin + i, j))
    return pl.pallas_call(
        functools.partial(expert_kernel, experts, inputs, len(old)),
        grid=(inputs, 2),
        in_specs=[smem] * 2
        + [
            pl.BlockSpec(array.shape, lambda i, j: (0, 0))
            for array in (router, *rows, *upstream)
        ]
        + [hbm] * (len(weights) + len(old)),
        out_specs=[share] * 2
        + [inner] * 2
        + [pl.BlockSpec((count, width), lambda i, j: (begin + i, 0))],
        out_shape=[jax.ShapeDtypeStruct((inputs, count, width), BF)] * 2
        + [jax.ShapeDtypeStruct((total, size), BF) for size in (hidden, hidden, width)],
        scratch_shapes=[
            pltpu.VMEM((4, 2 * width, quarter), BF),
            pltpu.VMEM((count, width), F32),
            pltpu.VMEM((count, width), F32),
            pltpu.SemaphoreType.DMA((5,)),
        ],
        input_output_aliases={first + index: 2 + index for index in range(len(old))},
        compiler_params=pltpu.CompilerParams(vmem_limit_bytes=56 * 2**20),
        name="expert_part",
    )(me, core, router, *rows, *upstream, *weights, *old)


def combine_kernel(inputs, experts, core_ref, me_ref, ours_ref, theirs_ref, router_ref, *refs):
    x_refs, up_refs, refs = refs[:inputs], refs[inputs : 2 * inputs], refs[2 * inputs :]
    y_refs, dn_refs, grad_ref = refs[:inputs], refs[inputs : 2 * inputs], refs[-1]
    rows = y_refs[0].shape[0]
    router = router_ref[...]
    grad_router = None
    for index in range(inputs):
        x = x_refs[index][...]
        y = ours_ref[index, :rows, :].astype(F32) + theirs_ref[index, :rows, :].astype(F32)
        dn = ours_ref[index, rows:, :].astype(F32) + theirs_ref[index, rows:, :].astype(F32)
        probs = router_probs(x, router, experts)
        lane = lax.broadcasted_iota(jnp.int32, probs.shape, 1)
        chosen = jnp.where(lane == me_ref[0], 1.0, 0.0)
        gate = jnp.sum(probs * chosen, axis=1, keepdims=True)
        gate_grads = jnp.sum(up_refs[index][...].astype(F32) * y, axis=1, keepdims=True)
        logit_grads = (probs * (chosen * gate_grads - gate * gate_grads)).astype(BF)
        product = contract(x, logit_grads, 0, 0)
        grad_router = product if grad_router is None else grad_router + product
        y_refs[index][...] = y.astype(BF)
        dn_refs[index][...] = (dn + contract(logit_grads, router, 1, 1)).astype(BF)
    grad_ref[...] = grad_router


def combine_halves(me, core, ours, theirs, router, rows, upstream, experts):
    inputs, count, width = ours.shape

    def whole(array):
        return pl.BlockSpec(array.shape, lambda i, core: (0,) * array.ndim)

    own = pl.BlockSpec((count // 2, width), lambda i, core: (core[0], 0))
    out_shape = [jax.ShapeDtypeStruct((count // 2, width), BF)] * (2 * inputs)
    out_shape.append(jax.ShapeDtypeStruct(router.shape, F32))
    results = pl.pallas_call(
        functools.partial(combine_kernel, inputs, experts),
        grid_spec=pltpu.PrefetchScalarGridSpec(
            num_scalar_prefetch=1,
            grid=(1,),
            in_specs=[pl.BlockSpec(memory_space=pltpu.SMEM)]
            + [whole(array) for array in (ours, theirs, router)]
            + [own] * (2 * inputs),
            out_specs=[
                pl.BlockSpec(array.shape, lambda i, core: (0, 0)) for array in out_shape
            ],
        ),
        out_shape=out_shape,
        compiler_params=pltpu.CompilerParams(vmem_limit_bytes=50 * 2**20),
        name="combine_halves",
    )(core, me, ours, theirs, router, *rows, *upstream)
    return results[:inputs], results[inputs : 2 * inputs], results[-1]


def expert_grads_kernel(act_ref, pre_ref, dy_ref, *refs):
    x_refs = refs[:-4]
    one_ref, two_ref, keep_one, keep_two = refs[-4:]
    width = dy_ref.shape[1]
    quarter = act_ref.shape[1]
    mask = pl.program_id(0)
    rows = jnp.concatenate([ref[...] for ref in x_refs], axis=0)
    grad_in = contract(rows, pre_ref[...], 0, 0)
    grad_out = contract(act_ref[...], dy_ref[...], 0, 0)
    grad_out = jnp.concatenate(
        [grad_out[:, at : at + quarter] for at in range(0, width, quarter)], axis=0
    )
    for at in (1, 3):

        @pl.when(mask == at)
        def _():
            one_ref[0] = grad_in.astype(BF)

    for at in (2, 3):

        @pl.when(mask == at)
        def _():
            two_ref[0] = grad_out.astype(BF)

    for at in (0, 2):

        @pl.when(mask == at)
        def _():
            keep_one[0] = grad_in

    for at in (0, 1):

        @pl.when(mask == at)
        def _():
            keep_two[0] = grad_out


def expert_grads(kept, rows, quarter):
    act, pre, dy = kept
    total, width = dy.shape
    hidden = pl.BlockSpec((total, quarter), lambda f: (0, f))

    def whole(array):
        return pl.BlockSpec(array.shape, lambda f: (0, 0))

    def block(place):
        return pl.BlockSpec((1, width, quarter), lambda f: (place(f), 0, 0))

    return pl.pallas_call(
        expert_grads_kernel,
        grid=(act.shape[1] // quarter,),
        in_specs=[hidden, hidden, whole(dy)] + [whole(part) for part in rows],
        out_specs=[
            block(lambda f: f // 2),
            block(lambda f: jnp.maximum(f - 2, 0)),
            block(lambda f: f // 2),
            block(lambda f: jnp.minimum(f, 1)),
        ],
        out_shape=[jax.ShapeDtypeStruct((2, width, quarter), BF)] * 2
        + [jax.ShapeDtypeStruct((2, width, quarter), F32)] * 2,
        compiler_params=pltpu.CompilerParams(vmem_limit_bytes=50 * 2**20),
        name="expert_grads",
    )(act, pre, dy, *rows)


def settle_kernel(keep_one, keep_two, got_one, got_two, one_ref, two_ref):
    one_ref[...] = (keep_one[0].astype(F32) + got_one[0].astype(F32)).astype(BF)
    two_ref[...] = (keep_two[0].astype(F32) + got_two[0].astype(F32)).astype(BF)


def settle_step(keep_one, keep_two, got_one, got_two):
    _, width, quarter = keep_one.shape
    second = pl.BlockSpec((1, width, quarter), lambda i: (1, 0, 0))
    whole = pl.BlockSpec((width, quarter), lambda i: (0, 0))
    return pl.pallas_call(
        settle_kernel,
        grid=(1,),
        in_specs=[second] * 4,
        out_specs=[whole] * 2,
        out_shape=[jax.ShapeDtypeStruct((width, quarter), BF)] * 2,
        compiler_params=pltpu.CompilerParams(vmem_limit_bytes=50 * 2**20),
        name="settle_step",
    )(keep_one, keep_two, got_one, got_two)


def all_to_all(blocks, axis, groups=None):
    return lax.all_to_all(
        blocks, axis, split_axis=0, concat_axis=0, tiled=True, axis_index_groups=groups
    )


def pair_swap(block, axis, mask):
    count = lax.axis_size(axis)
    return lax.ppermute(block, axis, [(i, i ^ mask) for i in range(count)])


def tied(values, *others):
    return lax.optimization_barrier((values, others))[0]


def gather_pairs(rows, axis, groups, pairs, after):
    count = lax.axis_size(axis)
    if count > 8:
        return [lax.all_gather(rows, axis, axis=0, tiled=True)]
    core = lax.axis_index(axis) % 2
    columns = rows.shape[1] // 2
    low, high = rows[:, :columns], rows[:, columns:]
    mine = jnp.where(core == 0, low, high)
    got = pair_swap(jnp.where(core == 0, high, low), axis, 1)
    chip = jnp.where(core == 0, jnp.stack([mine, got]), jnp.stack([got, mine]))
    whole = all_to_all(jnp.broadcast_to(chip[None], (count // 2,) + chip.shape), axis, groups)
    whole = tied(whole.reshape(2, count * rows.shape[0] // 2, columns), after)
    return [
        lax.all_gather(part, axis, axis=0, tiled=False, axis_index_groups=pairs) for part in whole
    ]


def scatter_sums(rows, axis, groups):
    count = lax.axis_size(axis)
    here = rows.shape[0] // count
    if count > 8:
        blocks = all_to_all(rows.reshape(count, here, rows.shape[1]), axis)
        return jnp.sum(blocks.astype(F32), axis=0)
    core = lax.axis_index(axis) % 2
    split = rows.reshape(count // 2, 2, here, rows.shape[1])
    mine = lax.dynamic_index_in_dim(split, core, 1, keepdims=False)
    other = pair_swap(lax.dynamic_index_in_dim(split, 1 - core, 1, keepdims=False), axis, 1)
    chip = (mine.astype(F32) + other.astype(F32)).astype(BF)
    return jnp.sum(all_to_all(chip, axis, groups).astype(F32), axis=0)


def per_device(
    tokens, cotangent, doc_starts, routes, bucket_table, w_query, w_key, w_value, w_output,
    w_router, gain_attn, gain_moe, rel_bias, expert_in, expert_out,
):
    _, span, width = tokens.shape
    seq_count = lax.axis_size("seq")
    fsdp_count = lax.axis_size("fsdp")
    seq_me = lax.axis_index("seq")
    fsdp_me = lax.axis_index("fsdp")
    heads, buckets = rel_bias.shape
    local = width // seq_count
    head = local // heads
    experts = w_router.shape[1]
    rows_here = w_query.shape[0]
    quarter = expert_in.shape[2]
    cores = 2
    groups = [list(range(core, fsdp_count, cores)) for core in range(cores)]
    x = tokens[0]
    seq_index = seq_me.astype(jnp.int32)[None]
    expert_index = (fsdp_me // cores).astype(jnp.int32)[None]
    core_index = (fsdp_me % cores).astype(jnp.int32)[None]

    near = pair_swap(x, "seq", 1)
    far = pair_swap(x, "seq", 2)
    slab = pack_slab(
        seq_index, w_query, w_key, w_value, w_router, gain_attn, gain_moe, seq_count, head
    )
    slab = lax.all_gather(slab, "fsdp", axis=0, tiled=True)
    half = span // 2
    slab, near_half, far_half = lax.optimization_barrier((slab, near[:half], far[half:]))
    across = [pair_swap(near_half, "seq", 2), pair_swap(far_half, "seq", 1)]
    tail = slab[:, 3 * local :]
    full_router = jnp.pad(tail[:, :experts], ((0, 0), (0, -experts % LANES)))
    gains = tail[:, experts : experts + 2].astype(F32).T
    gain_one, gain_two = gains[:1], gains[1:2]
    own_gain = gain_attn.astype(F32)

    expert_me = fsdp_me // cores
    few = experts <= 4
    route, bucket_table, rel_bias = tied((routes[0], bucket_table[:TILE], rel_bias), slab)
    chosen = (route[:, None] == jnp.arange(LANES, dtype=jnp.int32)[None, :]).astype(F32)
    before = (
        jnp.arange(span, dtype=jnp.int32)[:, None] > jnp.arange(span, dtype=jnp.int32)[None, :]
    ).astype(BF)
    ranks = jnp.dot(before, chosen.astype(BF), preferred_element_type=F32)
    capacity = max(2, 2 * span // experts)
    target = route ^ expert_me if few else route
    slot = target * capacity + jnp.sum(ranks * chosen, axis=1).astype(jnp.int32)
    slot = slot[None]
    part_count = 4
    part_rows = experts * capacity // part_count

    def exchange(parts):
        if few:
            return [parts[0]] + [
                pair_swap(parts[mask], "fsdp", cores * mask) for mask in range(1, part_count)
            ]
        blocks = jnp.concatenate(parts, axis=0).reshape(experts, capacity, width)
        blocks = all_to_all(blocks, "fsdp", groups).reshape(part_count, part_rows, width)
        return [blocks[part] for part in range(part_count)]

    old = ()
    for mask, part in enumerate((x, near, far)):
        old = project(
            (seq_me ^ mask).astype(jnp.int32)[None], (part,), slab, gain_one, 3 * local, seq_count, old,
            () if mask < 2 else (expert_in[0], expert_out[0]),
        )
    weights = tied(old[2], across)
    w_near = pair_swap(weights, "seq", 1)
    w_far = pair_swap(weights, "seq", 2)
    up_rows, old = lax.optimization_barrier((cotangent[0], old[:2]))
    w_output = tied(w_output, slab)
    upstream_parts = into_slots(up_rows, slot, part_count, part_rows)
    upstream_parts = exchange(upstream_parts)
    n1_all, qkv_t = project(
        (seq_me ^ 3).astype(jnp.int32)[None], across, slab, gain_one, 3 * local, seq_count, old,
    )
    rel = rel_bias.astype(F32)
    bucket = bucket_table[None]
    attended, lse = attend_forward(
        qkv_t, doc_starts, rel, bucket, heads, head, seq_count
    )
    mixed = all_to_all(attended, "seq").reshape(width, span)
    pairs = [list(range(at, at + cores)) for at in range(0, fsdp_count, cores)]

    def of_chip(rows):
        return lax.all_gather(rows, "fsdp", axis=0, tiled=True, axis_index_groups=pairs)

    first_up = [of_chip(one) for one in tied(upstream_parts[:2], attended)]
    output_halves = gather_pairs(
        w_output, "fsdp", groups, pairs, (attended, upstream_parts, first_up)
    )
    mixed, output_halves, upstream_parts, w_near, w_far = lax.optimization_barrier(
        (mixed, output_halves, upstream_parts, w_near, w_far)
    )

    hidden, *parts, full_output = rows_into_experts(
        x, mixed, output_halves, gain_two, slot, part_count, part_rows
    )
    w_near, w_far, parts = lax.optimization_barrier((w_near, w_far, parts))
    w_across = [pair_swap(w_near[:width], "seq", 2), pair_swap(w_far[width:], "seq", 1)]
    weights = [weights, w_near, w_far] + w_across
    arrived = exchange(parts)
    kept = ()
    upstream_parts = first_up + [of_chip(one) for one in tied(upstream_parts[2:], parts)]
    chip_rows, ys, back, pairs_of_shares = [], [], [], []
    grad_router = []
    steps = part_count // 2
    for part in range(steps):
        some = slice(part * part_count // steps, (part + 1) * part_count // steps)
        rows, some_up = arrived[some], upstream_parts[some]
        if part:
            rows = tied(rows, kept)
        rows = [of_chip(one) for one in rows]
        if not part:
            rows, upstream_parts = lax.optimization_barrier((rows, upstream_parts))
            some_up = upstream_parts[some]
        chip_rows += rows
        ours, theirs, *kept = expert_part(
            part, steps, expert_index, core_index, rows, some_up, full_router, weights, kept,
            experts,
        )
        pairs_of_shares.append((ours, pair_swap(theirs, "fsdp", 1), rows, some_up))
    for ours, theirs, rows, some_up in pairs_of_shares[::-1]:
        ours, theirs = tied((ours, theirs), back)
        some_ys, dns, product = combine_halves(
            expert_index, core_index, ours, theirs, full_router, rows, some_up, experts
        )
        ys = list(some_ys) + ys
        back = list(dns) + back
        grad_router.append(product)
    kept = tied(kept, back)
    back = exchange(back)
    one, two, keep_one, keep_two = expert_grads(kept, chip_rows, quarter)
    back = list(back[:2]) + list(tied(back[2:], one, two))
    got_one = pair_swap(one, "seq", 1)
    got_two = pair_swap(two, "seq", 2)

    hidden_grads, mixed_grads, grad_gain = rows_from_experts(
        hidden, cotangent[0], full_output, gain_two, slot, back
    )
    ys = exchange(tied(ys, mixed_grads))
    early = early_sums(hidden_grads, mixed, grad_router, grad_gain, experts, seq_count)
    moved = all_to_all(mixed_grads.reshape(seq_count, local, span), "seq")
    settled_sum = [keep[0] + got[0].astype(F32) for keep, got in ((keep_one, got_one), (keep_two, got_two))]
    one, two = settle_step(keep_one, keep_two, got_one, got_two)
    got_one = pair_swap(one, "seq", 2)
    got_two = pair_swap(two, "seq", 1)
    early = all_to_all(tied(early, moved), "seq")
    *shares, distances, weight_grads = attend_backward(
        0, heads, qkv_t, moved, attended, lse, doc_starts, seq_index,
        rel, bucket, n1_all, slab, heads, head,
    )
    shares, distances, weight_grads, got_one, got_two, ys = lax.optimization_barrier(
        (shares, distances, weight_grads, got_one, got_two, ys)
    )
    output = final_output(hidden, gain_two, full_router, chosen, slot, ys, experts)
    shares = [shares[0]] + [
        pair_swap(shares[mask], "seq", mask) for mask in range(1, seq_count)
    ]
    grad_expert_in, grad_expert_out = [
        total + got.astype(F32) for total, got in zip(settled_sum, (got_one, got_two))
    ]
    grad_expert_out = jnp.concatenate(
        [grad_expert_out[at : at + quarter] for at in range(0, width, quarter)], axis=1
    )

    share = experts // seq_count
    rel_count = heads * buckets
    at = local + share + 1
    sums = all_sums(weight_grads, early, distances, bucket, head, buckets, at, fsdp_count)
    summed = scatter_sums(sums, "fsdp", groups)
    by_head = [summed[:, begin : begin + 3 * head] for begin in range(0, 3 * local, 3 * head)]
    summed = summed[:, 3 * local :]
    sum_gain_attn = jnp.sum(summed[:, at + 1 : at + 1 + heads], axis=1) / own_gain
    sum_gain_attn = sum_gain_attn + sum(
        pair_swap(sum_gain_attn, "seq", mask) for mask in range(1, seq_count)
    )
    if rows_here == rel_count:
        sum_rel = summed[:rel_count, local + share + 1].reshape(heads, buckets)
    else:
        onehot = bucket_table[:, None] == jnp.arange(buckets - 1, dtype=jnp.int32)[None, :]
        below = jnp.dot(distances[:, 0], onehot.astype(F32), precision=HIGH)
        grad_rel = jnp.concatenate([below, -jnp.sum(below, axis=1, keepdims=True)], axis=1)
        sum_rel = lax.psum(grad_rel, "fsdp")
    heads_sum = [
        jnp.concatenate([part[:, at : at + head] for part in by_head], axis=1)
        for at in range(0, 3 * head, head)
    ]
    sums = [*heads_sum, summed[:, :local], summed[:, local : local + share], summed[:, local + share]]
    sums, sum_rel, shares = lax.optimization_barrier((sums, sum_rel, shares))
    input_grads = rows_out(x, gain_one, hidden_grads, shares)
    return (
        output[None],
        input_grads[None],
        *sums[:5],
        sum_gain_attn,
        sums[5],
        sum_rel,
        grad_expert_in[None],
        grad_expert_out[None],
    )


def solution(mesh):
    rows = P("fsdp", "seq", None)
    weight = P("fsdp", None)
    shared = P("fsdp", "seq")
    return jax.shard_map(
        per_device,
        mesh=mesh,
        in_specs=(
            rows, rows, weight, shared, P(), weight, weight, weight, weight, weight,
            P("fsdp"), P("fsdp"), P("seq", None), P("fsdp", None, "seq"), rows,
        ),
        out_specs=(
            rows, rows, shared, shared, shared, shared, shared, P("fsdp"), P("fsdp"),
            P("seq", None), P("fsdp", None, "seq"), rows,
        ),
        check_vma=False,
    )
```
